128 devices in a mesh: dp: 32 (over z_lo, y, x), tensor: 4 (over z_hi, core).
Axes of the slice: x: 4, y: 4, z: 4 (z_hi: 2, z_lo: 2; z = z_hi * 2 + z_lo), core: 2. Of those that a mesh axis runs over, the one named last changes fastest.
Arguments:
- hidden_in: bfloat16 [4096, 2048], P('dp'), may hold values from -6 to 6
- cotangent: bfloat16 [4096, 2048], P('dp'), may hold values from -6 to 6
- attn_gain: float32 [2048], replicated, may hold values from 0.1 to 1.9
- attn_router: bfloat16 [2048, 4], replicated, may hold values from -0.125 to 0.125
- qkv_weight: bfloat16 [2048, 6, 2048], P('dp', None, 'tensor'), may hold values from -0.125 to 0.125
- out_weight: bfloat16 [2048, 4, 2048], P('dp', None, 'tensor'), may hold values from -0.75 to 0.75
- mlp_gain: float32 [2048], replicated, may hold values from 0.1 to 1.9
- mlp_router: bfloat16 [2048, 4], replicated, may hold values from -0.125 to 0.125
- gate_up_weight: bfloat16 [2048, 4, 2, 5632], P('dp', None, None, 'tensor'), may hold values from -0.125 to 0.125
- down_weight: bfloat16 [2048, 4, 5632], P('dp', None, 'tensor'), may hold values from -0.15625 to 0.15625
- attn_route: int32 [4096, 2], P('dp'), may hold values from 0 to 3, as said below
- attn_slot: int32 [4096, 2], P('dp'), may hold values from 0 to 127, as said below
- mlp_route: int32 [4096, 2], P('dp'), may hold values from 0 to 3, as said below
- mlp_slot: int32 [4096, 2], P('dp'), may hold values from 0 to 127, as said below
Outputs:
- out_hidden: bfloat16 [4096, 2048], P('dp')
- grad_in: float32 [4096, 2048], P('dp')
- attn_gain_grad: float32 [2048], replicated
- attn_router_grad: float32 [2048, 4], replicated
- qkv_grad: float32 [2048, 6, 2048], P('dp', None, 'tensor')
- out_grad: float32 [2048, 4, 2048], P('dp', None, 'tensor')
- mlp_gain_grad: float32 [2048], replicated
- mlp_router_grad: float32 [2048, 4], replicated
- gate_up_grad: float32 [2048, 4, 2, 5632], P('dp', None, None, 'tensor')
- down_grad: float32 [2048, 4, 5632], P('dp', None, 'tensor')
The draws below stay inside these ranges and needn't reach their ends.
Inputs may be any that keep to these rules, and one draw needn't show every extreme that they name: `attn_route`: each row names two different attention experts; among the rows of one sequence no expert is named more than 128 times, and in some sequence one expert is named by every row. `attn_slot`: within one sequence the pairs (expert, slot) of all rows and choices are distinct, and an expert named n times there holds slots 0 to n - 1. `mlp_route`: each row names two different feed-forward experts; among the rows of one sequence no expert is named more than 128 times, and in some sequence one expert is named by every row. `mlp_slot`: within one sequence the pairs (expert, slot) of all rows and choices are distinct, and an expert named n times there holds slots 0 to n - 1.
All inputs are finite; a program needn't handle non-finite values.
Results may differ from the reference program's by a relative error of at most 0.029.
Values may be sent and summed in bfloat16 or wider, within the bound.
A program may use at most 384 MiB of HBM per device.

```python
import jax
import jax.numpy as jnp
from jax import lax

D = 2048
KEY_VALUE_HEADS = 16
HEAD_SIZE = 128
FF = 5632
ATTN_EXPERTS = 4
EM = 4
TOK_DEV = 128
QKW = 2048
EXPERT_SLOTS = 128
TOKENS = 4096


def routing_block(key, experts, token_rows, full):
    keys = jax.random.split(key, 5)
    least = (2 * token_rows + experts - 1) // experts + 1
    drawn = jax.random.randint(keys[0], (), least, token_rows + 1)
    busiest = jnp.where(full, token_rows, drawn).astype(jnp.int32)
    remaining = 2 * token_rows - busiest
    base_load = remaining // (experts - 1)
    extra = remaining - base_load * (experts - 1)
    others = base_load + (jnp.arange(experts - 1) < extra).astype(jnp.int32)
    limit = jnp.minimum(busiest - base_load - 1, base_load - 1)
    jitter = jax.random.randint(keys[1], (), 0, limit + 1)
    others = others.at[0].add(jitter).at[1].add(-jitter)
    ordered = jnp.concatenate([busiest[None], others]).astype(jnp.int32)
    owners = jax.random.permutation(keys[2], experts)
    loads = jnp.zeros((experts,), jnp.int32).at[owners].set(ordered)
    ends = jnp.cumsum(loads)
    starts = ends - loads
    places = jnp.arange(2 * token_rows)
    labels = jnp.sum((ends[None, :] <= places[:, None]).astype(jnp.int32), axis=1)
    slots = places - starts[labels]
    pair_labels = jnp.stack([labels[:token_rows], labels[token_rows:]], axis=1)
    pair_slots = jnp.stack([slots[:token_rows], slots[token_rows:]], axis=1)
    order = jax.random.permutation(keys[3], token_rows)
    pair_labels = pair_labels[order]
    pair_slots = pair_slots[order]
    flips = jax.random.randint(keys[4], (token_rows, 1), 0, 2)
    pair_labels = jnp.where(flips == 1, pair_labels[:, ::-1], pair_labels)
    pair_slots = jnp.where(flips == 1, pair_slots[:, ::-1], pair_slots)
    return (pair_labels.astype(jnp.int32), pair_slots.astype(jnp.int32))


def routing_tables(key, experts, salt):
    key = jax.random.fold_in(key, salt)
    blocks = TOKENS // TOK_DEV
    pick_key, rest_key = jax.random.split(key)
    full_block = jax.random.randint(pick_key, (), 0, blocks)
    block_keys = jax.random.split(rest_key, blocks)
    labels, slots = jax.vmap(lambda block_key, index: routing_block(block_key, experts, TOK_DEV, index == full_block))(block_keys, jnp.arange(blocks))
    return (labels.reshape(TOKENS, 2), slots.reshape(TOKENS, 2))


def draw_attn_route(key, part):
    return routing_tables(key, ATTN_EXPERTS, 21)[0]


def draw_attn_slot(key, part):
    return routing_tables(key, ATTN_EXPERTS, 21)[1]


def draw_mlp_route(key, part):
    return routing_tables(key, EM, 22)[0]


def draw_mlp_slot(key, part):
    return routing_tables(key, EM, 22)[1]


def steps_of(key, extent, cuts, smallest, largest):
    def one(axis_at, parts):
        draws = jax.random.uniform(jax.random.fold_in(jax.random.fold_in(key, 6), axis_at), (parts,), jnp.float32, smallest / len(cuts), largest / len(cuts))
        return jnp.repeat(jnp.exp(draws), extent[axis_at] // parts).reshape((-1,) + (1,) * (len(extent) - axis_at - 1))

    level = one(*cuts[0])
    for cut in cuts[1:]:
        level = level * one(*cut)
    return level


def normal_values(rng, extent, deviation, reach, cuts=(), dtype=jnp.bfloat16):
    values = jax.random.normal(rng, extent, jnp.float32) * deviation
    if len(cuts) > 0:
        values = steps_of(rng, extent, cuts, -0.22, 0.18) * values
    return jnp.clip(values, min=-reach, max=reach).astype(dtype)


def setup_inputs(seed: int = 0) -> dict:
    streams_of = jax.random.split(jax.random.key(seed), 15)
    hidden_in = normal_values(streams_of[0], (TOKENS, D), 1.0, 6.0, ((0, 32),))
    cotangent = normal_values(streams_of[1], (TOKENS, D), 1.0, 6.0, ((0, 32),))
    attn_gain = jnp.clip(1.0 + 0.18 * jax.random.normal(streams_of[2], (D,), jnp.float32), 0.1, 1.9)
    attn_router = normal_values(streams_of[3], (D, ATTN_EXPERTS), D ** -0.5, 0.125)
    qkv_weight = normal_values(streams_of[4], (D, ATTN_EXPERTS + 2, QKW), D ** -0.5, 0.125, ((0, 32), (2, 4)))
    out_weight = normal_values(streams_of[5], (D, ATTN_EXPERTS, QKW), (QKW // 32) ** -0.5, 0.75, ((0, 32), (2, 4)))
    mlp_gain = jnp.clip(1.0 + 0.18 * jax.random.normal(streams_of[6], (D,), jnp.float32), 0.1, 1.9)
    mlp_router = normal_values(streams_of[7], (D, EM), D ** -0.5, 0.125)
    gate_up_weight = normal_values(streams_of[8], (D, EM, 2, FF), D ** -0.5, 0.125, ((0, 32), (3, 4)))
    down_weight = normal_values(streams_of[9], (D, EM, FF), (FF // 4) ** -0.5, 0.15625, ((0, 32), (2, 4)))
    attn_route = draw_attn_route(jax.random.fold_in(streams_of[14], 71), 0)
    attn_slot = draw_attn_slot(jax.random.fold_in(streams_of[14], 71), 0)
    mlp_route = draw_mlp_route(jax.random.fold_in(streams_of[14], 71), 0)
    mlp_slot = draw_mlp_slot(jax.random.fold_in(streams_of[14], 71), 0)
    return dict(hidden_in=hidden_in, cotangent=cotangent, attn_gain=attn_gain, attn_router=attn_router, qkv_weight=qkv_weight, out_weight=out_weight, mlp_gain=mlp_gain, mlp_router=mlp_router, gate_up_weight=gate_up_weight, down_weight=down_weight, attn_route=attn_route, attn_slot=attn_slot, mlp_route=mlp_route, mlp_slot=mlp_slot)


EPS = 1e-05
THETA = 10000.0
NEG = -1e+30
HIGHEST = lax.Precision.HIGHEST

@jax.custom_vjp
def lower_half(v):
    return lax.optimization_barrier(v.astype(jnp.bfloat16)).astype(jnp.float32)

@jax.custom_vjp
def low_back(v):
    return v

def low_keep(v):
    return (lower_half(v), None)

def low_pass(kept, grad):
    return (grad,)

def back_keep(v):
    return (v, None)

def back_low(kept, grad):
    return (lower_half(grad),)
lower_half.defvjp(low_keep, low_pass)
low_back.defvjp(back_keep, back_low)

def rms_scale(values):
    return lax.rsqrt(lax.optimization_barrier(jnp.mean(values * values, axis=-1, keepdims=True)) + EPS)

def rope_tables(positions):
    half_dim = HEAD_SIZE // 2
    frequency = THETA ** (-(jnp.arange(half_dim).astype(jnp.float32) * 2.0 / HEAD_SIZE))
    angles = positions[:, None] * frequency[None, :]
    return (jnp.cos(angles)[:, None, :], jnp.sin(angles)[:, None, :])

def apply_rotary(values, cosines, sines):
    half_dim = values.shape[-1] // 2
    first = values[..., :half_dim]
    second = values[..., half_dim:]
    return jnp.concatenate([first * cosines - second * sines, second * cosines + first * sines], axis=-1)

def pair_gates(logits, route):
    chosen = jnp.take_along_axis(logits, route, axis=1)
    row_top = lax.optimization_barrier(jnp.max(chosen, axis=1, keepdims=True))
    expon = jnp.exp(chosen - row_top)
    return expon / lax.optimization_barrier(jnp.sum(expon, axis=1, keepdims=True))

def slot_table(route, slot, experts, capacity):
    token_rows = route.shape[0]
    flat_index = route * capacity + slot
    owners = jnp.broadcast_to(jnp.arange(token_rows).astype(jnp.int32)[:, None], route.shape)
    token_of = jnp.zeros((experts * capacity,), jnp.int32).at[flat_index.reshape(-1)].set(owners.reshape(-1))
    filled = jnp.zeros((experts * capacity,), jnp.float32).at[flat_index.reshape(-1)].set(1.0)
    return (token_of, filled, flat_index)

def combine(branch, flat_index, gate_weights):
    token_rows = flat_index.shape[0]
    picked = jnp.take(branch.reshape(-1, D), flat_index.reshape(-1), axis=0).reshape(token_rows, 2, D)
    return lax.optimization_barrier(jnp.sum(gate_weights[:, :, None] * picked, axis=1))

def attention_branch(inputs, gain, router, qkv_w, out_w, route, slot):
    token_rows = inputs.shape[0]
    normed = lower_half(inputs * rms_scale(inputs) * gain)
    gate_weights = pair_gates(jnp.dot(normed, router, precision=HIGHEST), route)
    token_of, filled, flat_index = slot_table(route, slot, ATTN_EXPERTS, EXPERT_SLOTS)
    block_rows = (jnp.take(normed, token_of, axis=0) * filled[:, None]).reshape(ATTN_EXPERTS, EXPERT_SLOTS, D)
    positions = jnp.arange(token_rows).astype(jnp.float32)
    row_pos = jnp.take(positions, token_of)
    query_rows = low_back(jnp.einsum('ecd,dew->ecw', block_rows, qkv_w[:, :ATTN_EXPERTS], precision=HIGHEST))
    key_value_pair = low_back(jnp.einsum('td,dcw->tcw', normed, qkv_w[:, ATTN_EXPERTS:], precision=HIGHEST))
    cosine_row, sine_row = rope_tables(row_pos)
    cosine_token, sine_token = rope_tables(positions)
    rotated_query = lower_half(apply_rotary(query_rows.reshape(ATTN_EXPERTS * EXPERT_SLOTS, KEY_VALUE_HEADS, HEAD_SIZE), cosine_row, sine_row))
    rotated_key = lower_half(apply_rotary(key_value_pair[:, 0].reshape(token_rows, KEY_VALUE_HEADS, HEAD_SIZE), cosine_token, sine_token))
    value_block = lower_half(key_value_pair[:, 1].reshape(token_rows, KEY_VALUE_HEADS, HEAD_SIZE))
    scores = low_back(jnp.einsum('rhk,thk->hrt', rotated_query, rotated_key, precision=HIGHEST)) * HEAD_SIZE ** (-0.5)
    allowed = positions[None, None, :] <= row_pos[None, :, None]
    scores = jnp.where(allowed, scores, NEG)
    row_top = lax.optimization_barrier(jnp.max(scores, axis=2, keepdims=True))
    expon = jnp.exp(scores - row_top)
    probs = expon / lax.optimization_barrier(jnp.sum(expon, axis=2, keepdims=True))
    attention_output = low_back(jnp.einsum('hrt,thk->rhk', lower_half(probs), value_block, precision=HIGHEST))
    attention_output_block = lower_half(attention_output).reshape(ATTN_EXPERTS, EXPERT_SLOTS, KEY_VALUE_HEADS * HEAD_SIZE)
    branch = low_back(jnp.einsum('ecw,dew->ecd', attention_output_block, out_w, precision=HIGHEST))
    return combine(branch, flat_index, gate_weights)

def expert_branch(inputs, gain, router, gate_up_w, down_w, route, slot):
    normed = lower_half(inputs * rms_scale(inputs) * gain)
    gate_weights = pair_gates(jnp.dot(normed, router, precision=HIGHEST), route)
    token_of, filled, flat_index = slot_table(route, slot, EM, EXPERT_SLOTS)
    block_rows = (jnp.take(normed, token_of, axis=0) * filled[:, None]).reshape(EM, EXPERT_SLOTS, D)
    gate_up = low_back(jnp.einsum('ecd,degf->ecgf', block_rows, gate_up_w, precision=HIGHEST))
    activated = lower_half(jax.nn.silu(gate_up[:, :, 0]) * gate_up[:, :, 1])
    branch = low_back(jnp.einsum('ecf,def->ecd', activated, down_w, precision=HIGHEST))
    return combine(branch, flat_index, gate_weights)

def layer(inputs, params, attn_route, attn_slot, mlp_route, mlp_slot):
    attn_gain, attn_router, qkv_w, out_w, mlp_gain, mlp_router, gate_up_w, down_w = params
    after_attn = inputs + attention_branch(inputs, attn_gain, attn_router, qkv_w, out_w, attn_route, attn_slot)
    return after_attn + expert_branch(after_attn, mlp_gain, mlp_router, gate_up_w, down_w, mlp_route, mlp_slot)

def reference(hidden_in, cotangent, attn_gain, attn_router, qkv_weight, out_weight, mlp_gain, mlp_router, gate_up_weight, down_weight, attn_route, attn_slot, mlp_route, mlp_slot):
    weights = tuple((weight.astype(jnp.float32) for weight in (attn_gain, attn_router, qkv_weight, out_weight, mlp_gain, mlp_router, gate_up_weight, down_weight)))
    blocks = TOKENS // TOK_DEV
    seq_inputs = hidden_in.astype(jnp.float32).reshape(blocks, TOK_DEV, D)
    routing = tuple((table.reshape(blocks, TOK_DEV, 2) for table in (attn_route, attn_slot, mlp_route, mlp_slot)))

    def forward(seq_in, *params):

        def single_seq(members):
            return layer(members[0], params, members[1], members[2], members[3], members[4])
        return lax.map(jax.checkpoint(single_seq), (seq_in,) + routing)
    outputs, pullback = jax.vjp(forward, seq_inputs, *weights)
    grads = pullback(cotangent.astype(jnp.float32).reshape(blocks, TOK_DEV, D))
    return (outputs.reshape(TOKENS, D).astype(jnp.bfloat16), grads[0].reshape(TOKENS, D), grads[1], grads[2], grads[3], grads[4], grads[5], grads[6], grads[7], grads[8])
```

```python
import jax
import jax.numpy as jnp
from jax import lax
from jax.sharding import Mesh, PartitionSpec as P

HEAD = 128
LANE = 128
EPS = 1e-05
THETA = 10000.0
NEG = -1e30
EXPERTS = 4
GROUP = ("zl", "x")
TEAM = ("zl", "x", "zh", "c")
ALL = ("zl", "y", "x", "zh", "c")
BF = jnp.bfloat16
F32 = jnp.float32


def dot(a, b, dims):
    return lax.dot_general(a, b, (dims, ((), ())), preferred_element_type=F32)


def mm(a, b):
    return dot(a, b, ((1,), (0,)))


def mm_nt(a, b):
    return dot(a, b, ((1,), (1,)))


def mm_tn(a, b):
    return dot(a, b, ((0,), (0,)))


def rms_scale(values):
    return lax.rsqrt(jnp.mean(values * values, axis=-1, keepdims=True) + EPS)


def chosen_mask(route):
    columns = jnp.arange(EXPERTS)[None, :]
    return (route[:, :1] == columns) | (route[:, 1:] == columns)


def dense_gates(logits, mask):
    top = jnp.max(jnp.where(mask, logits, NEG), axis=1, keepdims=True)
    expon = jnp.where(mask, jnp.exp(jnp.where(mask, logits - top, 0.0)), 0.0)
    return expon / jnp.sum(expon, axis=1, keepdims=True)


def gates_back(gates, dots):
    return gates * (dots - jnp.sum(gates * dots, axis=1, keepdims=True))


def rope_tables(count):
    frequency = THETA ** (-(jnp.arange(HEAD // 2).astype(F32) * 2.0 / HEAD))
    angles = jnp.arange(count).astype(F32)[:, None] * frequency[None, :]
    cosines, sines = jnp.cos(angles), jnp.sin(angles)
    return (
        jnp.concatenate([cosines, cosines], axis=1),
        jnp.concatenate([-sines, sines], axis=1),
    )


def rotate(values, cosines, sines):
    half = HEAD // 2
    swapped = jnp.concatenate([values[..., half:], values[..., :half]], axis=-1)
    return values * cosines + swapped * sines


def norm_back(inputs, scale, gain, grad_normed):
    scaled = inputs * scale
    grad_scaled = grad_normed * gain
    grad_inputs = scale * (
        grad_scaled - scaled * jnp.mean(grad_scaled * scaled, axis=-1, keepdims=True)
    )
    return grad_inputs, jnp.sum(grad_normed * scaled, axis=0)


def gather_rows(blocks):
    _, count, rows, cols = blocks.shape
    got = lax.all_to_all(blocks, GROUP, split_axis=0, concat_axis=0, tiled=True)
    got = lax.all_gather(got, "y", axis=0, tiled=False)
    got = got.reshape(4, 2, 4, count, rows, cols)
    return got.transpose(3, 1, 0, 2, 4, 5).reshape(count, 32 * rows, cols)


def scatter_rows(grads):
    count, all_rows, cols = grads.shape
    rows = all_rows // 32
    parts = grads.reshape(count, 2, 4, 4, rows, cols).transpose(2, 1, 3, 0, 4, 5)
    parts = parts.reshape(4, 8, count, rows, cols)
    mine = lax.psum_scatter(parts, "y", scatter_dimension=0, tiled=False)
    return lax.all_to_all(mine, GROUP, split_axis=0, concat_axis=0, tiled=True)


def local(
    hidden,
    cotangent,
    attn_gain,
    attn_router,
    qkv_weight,
    out_weight,
    mlp_gain,
    mlp_router,
    gate_up_weight,
    down_weight,
    attn_route,
    attn_slot,
    mlp_route,
    mlp_slot,
):
    seq, width = hidden.shape
    rows = qkv_weight.shape[0]
    features = down_weight.shape[2]
    tiles = features // LANE
    part = (tiles + 1) // 2 * LANE
    low = features - part
    zl, x = lax.axis_index("zl"), lax.axis_index("x")
    quarter = lax.axis_index("zh") * 2 + lax.axis_index("c")
    own = seq // 4
    scale = HEAD ** (-0.5)
    group = 8 * seq

    query_blocks = qkv_weight[:, :EXPERTS].reshape(rows, 2, 2, 4, HEAD).transpose(1, 3, 2, 0, 4)
    kv_blocks = qkv_weight[:, EXPERTS:].reshape(rows, 2, 4, HEAD).transpose(2, 1, 0, 3)
    kv_blocks = jnp.broadcast_to(kv_blocks[None], (2,) + kv_blocks.shape)
    out_blocks = out_weight.reshape(rows, 2, 2, 4, HEAD).transpose(1, 3, 2, 0, 4)
    attn_blocks = jnp.concatenate([query_blocks, kv_blocks, out_blocks], axis=2)
    attn_w = gather_rows(attn_blocks.reshape(8, 6, rows, HEAD))
    mlp_all = jnp.concatenate([gate_up_weight, down_weight[:, :, None]], axis=2)
    mlp_all = mlp_all.transpose(1, 2, 0, 3)
    mlp_blocks = jnp.stack([mlp_all[..., :part], mlp_all[..., low:]], axis=0)
    mlp_w = gather_rows(mlp_blocks.reshape(8, 3, rows, part))

    masks = jnp.concatenate([chosen_mask(attn_route), chosen_mask(mlp_route)], axis=1)
    packed = jnp.concatenate(
        [hidden, cotangent, jnp.pad(masks.astype(BF), ((0, 0), (0, LANE - 2 * EXPERTS)))], axis=1
    )
    packed = lax.all_gather(packed, GROUP, axis=0, tiled=True)
    group_in = packed[:, :width]
    group_cot = packed[:, width : 2 * width]
    mask_a = packed[:, 2 * width : 2 * width + EXPERTS] > 0.5
    mask_m = packed[:, 2 * width + EXPERTS : 2 * width + 2 * EXPERTS] > 0.5
    start = (zl * 4 + x) * seq + quarter * own

    def mine(array):
        return lax.dynamic_slice_in_dim(array, start, own, axis=0)

    inputs = group_in.astype(F32)
    scale_a = rms_scale(inputs)
    normed_a = (inputs * scale_a * attn_gain).astype(BF)
    gates_a = dense_gates(mm(normed_a, attn_router), mask_a)
    pair_a = lax.dynamic_slice_in_dim(gates_a, zl * 2, 2, axis=1)
    cosines, sines = rope_tables(seq)
    proj = jnp.einsum("td,ndw->ntw", normed_a, attn_w[:4], preferred_element_type=F32)
    proj = proj.reshape(4, 8, seq, HEAD)
    turned = rotate(proj[:3], cosines, sines).astype(BF)
    query, key, value = turned[:2], turned[2], proj[3].astype(BF)
    scores = jnp.einsum("nsrk,stk->nsrt", query, key, preferred_element_type=F32) * scale
    causal = jnp.arange(seq)[None, :] <= jnp.arange(seq)[:, None]
    scores = jnp.where(causal, scores, NEG)
    expon = jnp.exp(scores - jnp.max(scores, axis=-1, keepdims=True))
    probs = expon / jnp.sum(expon, axis=-1, keepdims=True)
    probs_b = probs.astype(BF)
    attended = jnp.einsum("nsrt,stk->nsrk", probs_b, value, preferred_element_type=F32)
    attended = attended.reshape(2, group, HEAD)
    gate_cols = pair_a.T[:, :, None]
    gated_att = (attended * gate_cols).astype(BF)
    branch_a = jnp.einsum("ntw,ndw->td", gated_att, attn_w[4:], preferred_element_type=F32)
    branch_a = lax.psum_scatter(branch_a.astype(BF), TEAM, scatter_dimension=0, tiled=True)
    own_in = mine(inputs)
    after_attn = own_in + branch_a.astype(F32)

    scale_m = rms_scale(after_attn)
    normed_own = (after_attn * scale_m * mlp_gain).astype(BF)
    normed_m = lax.all_gather(normed_own, TEAM, axis=0, tiled=True)
    gates_m = dense_gates(mm(normed_m, mlp_router), mask_m)
    col_ok = (jnp.arange(part)[None, :] >= zl * (2 * part - features)).astype(F32)
    gate_m = lax.dynamic_slice_in_dim(gates_m, x, 1, axis=1) * col_ok
    gate_part = mm(normed_m, mlp_w[0])
    up_part = mm(normed_m, mlp_w[1])
    sigma = jax.nn.sigmoid(gate_part)
    silu = gate_part * sigma
    activated = silu * up_part
    gated_act = (activated * gate_m).astype(BF)
    branch_m = mm_nt(gated_act, mlp_w[2])
    branch_m = lax.psum_scatter(branch_m.astype(BF), TEAM, scatter_dimension=0, tiled=True)
    out_own = (after_attn + branch_m.astype(F32)).astype(BF)

    cot_down = mm(group_cot, mlp_w[2])
    dots_m = jnp.sum(activated * col_ok * cot_down, axis=1, keepdims=True)
    grad_act = cot_down * gate_m
    grad_gate = (grad_act * up_part * sigma * (1.0 + gate_part * (1.0 - sigma))).astype(BF)
    grad_up = (grad_act * silu).astype(BF)
    grad_rows = mm_nt(grad_gate, mlp_w[0]) + mm_nt(grad_up, mlp_w[1])
    one_hot_x = (jnp.arange(LANE) == x).astype(F32)
    back_m = jnp.concatenate([grad_rows, dots_m * one_hot_x], axis=1).astype(BF)
    back_m = lax.psum_scatter(back_m, TEAM, scatter_dimension=0, tiled=True).astype(F32)
    mlp_grads = jnp.stack(
        [mm_tn(normed_m, grad_gate), mm_tn(normed_m, grad_up), mm_tn(group_cot, gated_act)]
    )
    mlp_grads = scatter_rows(mlp_grads.astype(BF)).astype(F32)
    own_gates_m = mine(gates_m)
    logits_back_m = gates_back(own_gates_m, back_m[:, width : width + EXPERTS])
    router_grad_m = mm_tn(normed_own.astype(F32), logits_back_m)
    full_m = back_m[:, :width] + mm_nt(logits_back_m, mlp_router.astype(F32))
    inner_m, gain_grad_m = norm_back(after_attn, scale_m, mlp_gain, full_m)
    grad_mid_own = mine(group_cot).astype(F32) + inner_m

    grad_mid = lax.all_gather(grad_mid_own.astype(BF), TEAM, axis=0, tiled=True)
    grad_att = jnp.einsum("td,ndw->ntw", grad_mid, attn_w[4:], preferred_element_type=F32)
    dots_a = jnp.sum(attended * grad_att, axis=2).T
    grad_att = (grad_att * gate_cols).astype(BF).reshape(2, 8, seq, HEAD)
    grad_probs = jnp.einsum("nsrk,stk->nsrt", grad_att, value, preferred_element_type=F32)
    inner = jnp.sum(probs * grad_probs, axis=-1, keepdims=True)
    grad_scores = (probs * (grad_probs - inner) * scale).astype(BF)
    grad_query = jnp.einsum("nsrt,stk->nsrk", grad_scores, key, preferred_element_type=F32)
    grad_key = jnp.einsum("nsrt,nsrk->stk", grad_scores, query, preferred_element_type=F32)
    grad_value = jnp.einsum("nsrt,nsrk->stk", probs_b, grad_att, preferred_element_type=F32)
    turned_back = rotate(
        jnp.concatenate([grad_query, grad_key[None]], axis=0), cosines, -sines
    )
    grad_proj = jnp.concatenate([turned_back, grad_value[None]], axis=0).astype(BF)
    grad_proj = grad_proj.reshape(4, group, HEAD)
    grad_rows_a = jnp.einsum("ntw,ndw->td", grad_proj, attn_w[:4], preferred_element_type=F32)
    pair_hot = (jnp.arange(LANE)[None, :] == (zl * 2 + jnp.arange(2))[:, None]).astype(F32)
    back_a = jnp.concatenate([grad_rows_a, mm(dots_a, pair_hot)], axis=1).astype(BF)
    back_a = lax.psum_scatter(back_a, TEAM, scatter_dimension=0, tiled=True).astype(F32)
    attn_grads = jnp.concatenate(
        [
            jnp.einsum("td,ntw->ndw", normed_a, grad_proj, preferred_element_type=F32),
            jnp.einsum("td,ntw->ndw", grad_mid, gated_att, preferred_element_type=F32),
        ],
        axis=0,
    )
    attn_grads = scatter_rows(attn_grads.astype(BF)).astype(F32)
    logits_back_a = gates_back(mine(gates_a), back_a[:, width : width + EXPERTS])
    own_normed_a = mine(normed_a).astype(F32)
    router_grad_a = mm_tn(own_normed_a, logits_back_a)
    full_a = back_a[:, :width] + mm_nt(logits_back_a, attn_router.astype(F32))
    inner_a, gain_grad_a = norm_back(own_in, mine(scale_a), attn_gain, full_a)
    grad_in_own = grad_mid_own + inner_a

    out_hidden = lax.all_gather(out_own, ("zh", "c"), axis=0, tiled=True)
    grad_in = lax.all_gather(grad_in_own, ("zh", "c"), axis=0, tiled=True)
    small = jnp.concatenate(
        [gain_grad_a[None], gain_grad_m[None], router_grad_a.T, router_grad_m.T], axis=0
    )
    small = lax.psum(small, ALL)

    attn_grads = attn_grads.reshape(2, 4, 6, rows, HEAD)
    query_grad = attn_grads[:, :, :2].transpose(3, 0, 2, 1, 4).reshape(rows, EXPERTS, 4 * HEAD)
    kv_grad = jnp.sum(attn_grads[:, :, 2:4], axis=0).transpose(2, 1, 0, 3).reshape(rows, 2, 4 * HEAD)
    qkv_grad = jnp.concatenate([query_grad, kv_grad], axis=1)
    out_grad = attn_grads[:, :, 4:].transpose(3, 0, 2, 1, 4).reshape(rows, EXPERTS, 4 * HEAD)
    mlp_grads = mlp_grads.reshape(2, EXPERTS, 3, rows, part)
    whole = jnp.concatenate([mlp_grads[0], mlp_grads[1][..., 2 * part - features :]], axis=-1)
    whole = whole.transpose(2, 0, 1, 3)
    return (
        out_hidden,
        grad_in,
        small[0],
        small[2 : 2 + EXPERTS].T,
        qkv_grad,
        out_grad,
        small[1],
        small[2 + EXPERTS :].T,
        whole[:, :, :2],
        whole[:, :, 2],
    )


def solution(mesh):
    fine = Mesh(mesh.devices.reshape(2, 4, 4, 2, 2), ALL)
    dp, tensor = ("zl", "y", "x"), ("zh", "c")
    placed = (
        P(dp, None),
        P(dp, None),
        P(),
        P(),
        P(dp, None, tensor),
        P(dp, None, tensor),
        P(),
        P(),
        P(dp, None, None, tensor),
        P(dp, None, tensor),
        P(dp, None),
        P(dp, None),
        P(dp, None),
        P(dp, None),
    )
    return jax.shard_map(
        local,
        mesh=fine,
        in_specs=placed,
        out_specs=(
            P(dp, None),
            P(dp, None),
            P(),
            P(),
            P(dp, None, tensor),
            P(dp, None, tensor),
            P(),
            P(),
            P(dp, None, None, tensor),
            P(dp, None, tensor),
        ),
        check_vma=False,
    )
```

```python
import itertools

import jax
import jax.numpy as jnp
from jax import lax
from jax.experimental import pallas as pl
from jax.experimental.pallas import tpu as pltpu
from jax.sharding import Mesh, PartitionSpec as P

HEAD = 128
LANE = 128
EPS = 1e-05
THETA = 10000.0
NEG = -1e30
EXPERTS = 4
GROUP = ("zl", "x")
TEAM = ("zl", "x", "zh", "c")
ALL = ("zl", "y", "x", "zh", "c")
SIZES = dict(zl=2, y=4, x=4, zh=2, c=2)
BF = jnp.bfloat16
F32 = jnp.float32
MESH = pl.DeviceIdType.MESH
ANY = pl.BlockSpec(memory_space=pl.ANY)
VMEM = pl.BlockSpec(memory_space=pltpu.VMEM)


def dot(a, b, dims):
    return lax.dot_general(a, b, (dims, ((), ())), preferred_element_type=F32)


def mm(a, b):
    return dot(a, b, ((1,), (0,)))


def mm_nt(a, b):
    return dot(a, b, ((1,), (1,)))


def mm_tn(a, b):
    return dot(a, b, ((0,), (0,)))


def rms_scale(values):
    return lax.rsqrt(jnp.mean(values * values, axis=-1, keepdims=True) + EPS)


def chosen_mask(route):
    columns = jnp.arange(EXPERTS)[None, :]
    return (route[:, :1] == columns) | (route[:, 1:] == columns)


def dense_gates(logits, mask):
    top = jnp.max(jnp.where(mask, logits, NEG), axis=1, keepdims=True)
    expon = jnp.where(mask, jnp.exp(jnp.where(mask, logits - top, 0.0)), 0.0)
    return expon / jnp.sum(expon, axis=1, keepdims=True)


def gates_back(gates, dots):
    return gates * (dots - jnp.sum(gates * dots, axis=1, keepdims=True))


def rope_tables(count):
    frequency = THETA ** (-(jnp.arange(HEAD // 2).astype(F32) * 2.0 / HEAD))
    angles = jnp.arange(count).astype(F32)[:, None] * frequency[None, :]
    cosines, sines = jnp.cos(angles), jnp.sin(angles)
    return (
        jnp.concatenate([cosines, cosines], axis=1),
        jnp.concatenate([-sines, sines], axis=1),
    )


def rotate(values, cosines, sines):
    half = HEAD // 2
    swapped = jnp.concatenate([values[..., half:], values[..., :half]], axis=-1)
    return values * cosines + swapped * sines


def norm_back(inputs, scale, gain, grad_normed):
    scaled = inputs * scale
    grad_scaled = grad_normed * gain
    grad_inputs = scale * (
        grad_scaled - scaled * jnp.mean(grad_scaled * scaled, axis=-1, keepdims=True)
    )
    return grad_inputs, jnp.sum(grad_normed * scaled, axis=0)


def moves(*axes):
    return [dict(zip(axes, steps)) for steps in itertools.product(*[range(SIZES[a]) for a in axes])]


def place(move, sign=1):
    return {a: lax.rem(lax.axis_index(a) + sign * v + SIZES[a], SIZES[a]) for a, v in move.items()}


def number(coords):
    total = 0
    for axis, value in coords.items():
        total = total * SIZES[axis] + value
    return total


def meet(partners):
    barrier = pltpu.get_barrier_semaphore()
    for partner in partners:
        pl.semaphore_signal(barrier, inc=1, device_id=partner, device_id_type=MESH)
    pl.semaphore_wait(barrier, len(partners))


def push(src, dst, send, recv, to):
    return pltpu.make_async_remote_copy(
        src_ref=src, dst_ref=dst, send_sem=send, recv_sem=recv, device_id=to, device_id_type=MESH
    )


def settings(number, moved):
    return dict(
        compiler_params=pltpu.CompilerParams(
            collective_id=number, has_side_effects=True, vmem_limit_bytes=32 << 20
        ),
        cost_estimate=pl.CostEstimate(flops=0, bytes_accessed=moved, transcendentals=0),
    )


GROUP_MOVES = moves("zl", "x")
TEAM_MOVES = moves("zl", "x", "zh")
Y_MOVES = moves("y")


def sibling():
    return {"c": 1 - lax.axis_index("c")}


class Spread:
    sems = [pltpu.SemaphoreType.DMA((8,))] * 4

    def __init__(self, src, dst, sems):
        self.src, self.dst = src, dst
        self.send, self.recv, self.fsend, self.frecv = sems
        rows = src.shape[0] // 2
        self.half = pl.ds(pl.multiple_of(lax.axis_index("c") * rows, rows), rows)
        self.me = number(place(GROUP_MOVES[0]))

    def start(self):
        self.copies = [pltpu.make_async_copy(self.src, self.dst.at[self.me], self.send.at[0])]
        for k, move in enumerate(GROUP_MOVES):
            if k:
                self.copies.append(
                    push(
                        self.src.at[self.half],
                        self.dst.at[self.me, self.half],
                        self.send.at[k],
                        self.recv.at[k],
                        place(move),
                    )
                )
        for copy in self.copies:
            copy.start()

    def finish(self):
        forwards = []
        for k, move in enumerate(GROUP_MOVES):
            if k:
                self.copies[k].wait_recv()
                block = self.dst.at[number(place(move, -1)), self.half]
                forwards.append(push(block, block, self.fsend.at[k], self.frecv.at[k], sibling()))
                forwards[-1].start()
        for forward in forwards:
            forward.wait()
        self.copies[0].wait()
        for copy in self.copies[1:]:
            copy.wait_send()


class Swap:
    sems = [pltpu.SemaphoreType.DMA((8,))] * 2

    def __init__(self, src, dst, sems):
        self.src, self.dst = src, dst
        self.send, self.recv = sems

    def start(self):
        me = number(place(GROUP_MOVES[0]))
        self.copies = [
            pltpu.make_async_copy(self.src.at[me], self.dst.at[:, me], self.send.at[0])
        ]
        for k, move in enumerate(GROUP_MOVES):
            if k:
                to = place(move)
                self.copies.append(
                    push(
                        self.src.at[number(to)],
                        self.dst.at[:, me],
                        self.send.at[k],
                        self.recv.at[k],
                        to,
                    )
                )
        for copy in self.copies:
            copy.start()

    def finish(self):
        for copy in self.copies:
            copy.wait()


def enter(collective, hidden, masks, blocks):
    rows, width = hidden.shape
    count, shard, cols = blocks.shape[1:]

    def kernel(hidden_ref, mask_ref, block_ref, hidden_out, mask_out, block_out, *sems):
        meet([place(m) for m in GROUP_MOVES[1:]] + [sibling()])
        swap = Swap(block_ref, block_out, sems[0:2])
        first = Spread(mask_ref, mask_out, sems[2:6])
        second = Spread(hidden_ref, hidden_out, sems[6:10])
        swap.start()
        first.start()
        second.start()
        first.finish()
        second.finish()
        swap.finish()

    return pl.pallas_call(
        kernel,
        out_shape=[
            jax.ShapeDtypeStruct((8, rows, width), hidden.dtype),
            jax.ShapeDtypeStruct((8,) + masks.shape, masks.dtype),
            jax.ShapeDtypeStruct((count, 8, shard, cols), blocks.dtype),
        ],
        in_specs=[ANY] * 3,
        out_specs=[ANY] * 3,
        scratch_shapes=Swap.sems + Spread.sems * 2,
        name="enter",
        **settings(collective, 90 << 20),
    )(hidden, masks, blocks)


def along_y(collective, rows_a, blocks_m, cotangent):
    count, all_rows, cols = rows_a.shape
    count_m, shard, cols_m = blocks_m.shape[1:]

    def kernel(a_ref, m_ref, cot_ref, a_out, m_out, cot_out, *sems):
        meet([place(m) for m in GROUP_MOVES[1:] + Y_MOVES[1:]] + [sibling()])
        y = lax.axis_index("y")
        copies = [pltpu.make_async_copy(a_ref, a_out.at[:, y], sems[0].at[0])]
        for k, move in enumerate(Y_MOVES):
            if k:
                copies.append(
                    push(a_ref, a_out.at[:, y], sems[0].at[k], sems[1].at[k], place(move))
                )
        for copy in copies:
            copy.start()
        swap = Swap(m_ref, m_out, sems[2:4])
        spread = Spread(cot_ref, cot_out, sems[4:8])
        swap.start()
        spread.start()
        for copy in copies:
            copy.wait()
        swap.finish()
        spread.finish()

    return pl.pallas_call(
        kernel,
        out_shape=[
            jax.ShapeDtypeStruct((count, 4, all_rows, cols), rows_a.dtype),
            jax.ShapeDtypeStruct((count_m, 8, shard, cols_m), blocks_m.dtype),
            jax.ShapeDtypeStruct((8,) + cotangent.shape, cotangent.dtype),
        ],
        in_specs=[ANY] * 3,
        out_specs=[ANY] * 3,
        scratch_shapes=[pltpu.SemaphoreType.DMA((4,))] * 2 + Swap.sems + Spread.sems,
        name="along_y",
        **settings(collective, 120 << 20),
    )(rows_a, blocks_m, cotangent)


def swap_back(collective, name, blocks):
    count, shard, cols = blocks.shape[1:]

    def kernel(m_ref, m_out, *sems):
        meet([place(m) for m in GROUP_MOVES[1:]])
        swap = Swap(m_ref, m_out, sems)
        swap.start()
        swap.finish()

    return pl.pallas_call(
        kernel,
        out_shape=jax.ShapeDtypeStruct((count, 8, shard, cols), blocks.dtype),
        in_specs=[ANY],
        out_specs=ANY,
        scratch_shapes=Swap.sems,
        name=name,
        **settings(collective, 80 << 20),
    )(blocks)


def team_sum(collective, name, parts):
    width = parts.shape[1]
    own = parts.shape[0] // 32
    parts = parts.reshape(16, 2, own, width)

    def kernel(part_ref, out_ref, held, other, got, lsem, ssem, rsem, dsend, drecv):
        meet([place(m) for m in TEAM_MOVES[1:]] + [sibling()])
        c = lax.axis_index("c")
        loads, swaps = [], []
        for k, move in enumerate(TEAM_MOVES):
            tile = number(place(move))
            loads.append(
                pltpu.make_async_copy(part_ref.at[tile, c], held.at[k], lsem.at[k])
            )
            swaps.append(
                push(part_ref.at[tile, 1 - c], other.at[k], ssem.at[k], rsem.at[k], sibling())
            )
        order = list(range(1, 16)) + [0]
        for k in order:
            swaps[k].start()
            loads[k].start()
        sends = []
        for k in order:
            loads[k].wait()
            swaps[k].wait_recv()
            total = held[k].astype(F32) + other[k].astype(F32)
            if k:
                held[k] = total.astype(BF)
                sends.append(
                    push(
                        held.at[k],
                        got.at[k - 1],
                        dsend.at[k - 1],
                        drecv.at[k - 1],
                        place(TEAM_MOVES[k]),
                    )
                )
                sends[-1].start()
            else:
                out_ref[...] = total
        for k in range(15):
            sends[k].wait_recv()
            out_ref[...] += got[k].astype(F32)
        for k in range(16):
            swaps[k].wait_send()
        for send in sends:
            send.wait_send()

    return pl.pallas_call(
        kernel,
        out_shape=jax.ShapeDtypeStruct((own, width), F32),
        in_specs=[ANY],
        out_specs=VMEM,
        scratch_shapes=[
            pltpu.VMEM((16, own, width), BF),
            pltpu.VMEM((16, own, width), BF),
            pltpu.VMEM((15, own, width), BF),
        ]
        + [pltpu.SemaphoreType.DMA((16,))] * 5,
        name=name,
        **settings(collective, 90 << 20),
    )(parts)


def team_spread(collective, name, rows):
    own, width = rows.shape

    def kernel(row_ref, out_ref, send, recv, fsend, frecv):
        meet([place(m) for m in TEAM_MOVES[1:]] + [sibling()])
        c = lax.axis_index("c")
        mine = out_ref.at[number(place(TEAM_MOVES[0])), c]
        stay = pltpu.make_async_copy(row_ref, mine, send.at[0])
        stay.start()
        pushes = [
            push(row_ref, mine, send.at[k], recv.at[k], place(TEAM_MOVES[k])) for k in range(1, 16)
        ]
        for copy in pushes:
            copy.start()
        forwards = [push(row_ref, mine, fsend.at[0], frecv.at[0], sibling())]
        forwards[0].start()
        for k in range(1, 16):
            pushes[k - 1].wait_recv()
            tile = out_ref.at[number(place(TEAM_MOVES[k], -1)), c]
            forwards.append(push(tile, tile, fsend.at[k], frecv.at[k], sibling()))
            forwards[-1].start()
        for copy in forwards:
            copy.wait()
        stay.wait()
        for copy in pushes:
            copy.wait_send()

    return pl.pallas_call(
        kernel,
        out_shape=jax.ShapeDtypeStruct((16, 2, own, width), rows.dtype),
        in_specs=[ANY],
        out_specs=ANY,
        scratch_shapes=[pltpu.SemaphoreType.DMA((16,))] * 4,
        name=name,
        **settings(collective, 90 << 20),
    )(rows).reshape(32 * own, width)


def leave(collective, out_own, grad_own, small):
    own, width = out_own.shape
    stages = [moves("c"), moves("x"), moves("y"), moves("zl", "zh")]
    near = moves("zh", "c")

    def kernel(out_ref, grad_ref, small_ref, out_all, grad_all, small_out, got, send, recv, ssend, srecv):
        partners = [place(m) for m in near[1:]] + [place(m) for m in stages[1][1:] + stages[2][1:]]
        partners += [place(m) for m in stages[3][1:] if m["zl"]]
        meet(partners)
        me = number(place(near[0]))
        copies = []
        for i, (src, dst) in enumerate(((out_ref, out_all), (grad_ref, grad_all))):
            copies.append(pltpu.make_async_copy(src, dst.at[me], send.at[i, 0]))
            for k in range(1, 4):
                copies.append(
                    push(src, dst.at[me], send.at[i, k], recv.at[i, k], place(near[k]))
                )
        for copy in copies:
            copy.start()
        small_out[...] = small_ref[...]
        for s, stage in enumerate(stages):
            swaps = [
                push(small_out, got.at[s, k - 1], ssend.at[s, k], srecv.at[s, k], place(stage[k]))
                for k in range(1, len(stage))
            ]
            for swap in swaps:
                swap.start()
            for swap in swaps:
                swap.wait()
            total = small_out[...]
            for k in range(1, len(stage)):
                total += got[s, k - 1]
            small_out[...] = total
        for copy in copies:
            copy.wait()

    return pl.pallas_call(
        kernel,
        out_shape=[
            jax.ShapeDtypeStruct((4, own, width), out_own.dtype),
            jax.ShapeDtypeStruct((4, own, width), grad_own.dtype),
            jax.ShapeDtypeStruct(small.shape, F32),
        ],
        in_specs=[ANY, ANY, VMEM],
        out_specs=[ANY, ANY, VMEM],
        scratch_shapes=[pltpu.VMEM((4, 3) + small.shape, F32)]
        + [pltpu.SemaphoreType.DMA((2, 4))] * 2
        + [pltpu.SemaphoreType.DMA((4, 4))] * 2,
        name="leave",
        **settings(collective, 60 << 20),
    )(out_own, grad_own, small)


def reorder(array, axis):
    shape = array.shape
    split = shape[:axis] + (2, 4, shape[axis] // 8) + shape[axis + 1 :]
    return jnp.swapaxes(array.reshape(split), axis, axis + 1).reshape(shape)


def restore(array, axis):
    shape = array.shape
    split = shape[:axis] + (4, 2, shape[axis] // 8) + shape[axis + 1 :]
    return jnp.swapaxes(array.reshape(split), axis, axis + 1).reshape(shape)


def gather_y(blocks):
    return [lax.all_gather(block, "y", axis=0, tiled=True) for block in blocks]


def sum_y(grads):
    summed = [lax.psum_scatter(g.astype(BF), "y", scatter_dimension=0, tiled=True) for g in grads]
    return jnp.stack([s.reshape(8, s.shape[0] // 8, s.shape[1]) for s in summed], axis=1)


def local(
    hidden,
    cotangent,
    attn_gain,
    attn_router,
    qkv_weight,
    out_weight,
    mlp_gain,
    mlp_router,
    gate_up_weight,
    down_weight,
    attn_route,
    attn_slot,
    mlp_route,
    mlp_slot,
):
    seq, width = hidden.shape
    rows = qkv_weight.shape[0]
    features = down_weight.shape[2]
    tiles = features // LANE
    part = (tiles + 1) // 2 * LANE
    low = features - part
    zl, x = lax.axis_index("zl"), lax.axis_index("x")
    quarter = lax.axis_index("zh") * 2 + lax.axis_index("c")
    own = seq // 4
    scale = HEAD ** (-0.5)
    group = 8 * seq

    query_blocks = qkv_weight[:, :EXPERTS].reshape(rows, 2, 2, 4, HEAD).transpose(1, 3, 2, 0, 4)
    kv_blocks = qkv_weight[:, EXPERTS:].reshape(rows, 2, 4, HEAD).transpose(2, 1, 0, 3)
    kv_blocks = jnp.broadcast_to(kv_blocks[None], (2,) + kv_blocks.shape)
    out_blocks = out_weight.reshape(rows, 2, 2, 4, HEAD).transpose(1, 3, 2, 0, 4)
    attn_blocks = jnp.concatenate([query_blocks, kv_blocks, out_blocks], axis=2)
    attn_blocks = attn_blocks.reshape(8, 6, rows, HEAD)
    mlp_all = jnp.concatenate([gate_up_weight, down_weight[:, :, None]], axis=2)
    mlp_all = mlp_all.transpose(1, 2, 0, 3)
    mlp_blocks = jnp.stack([mlp_all[..., :part], mlp_all[..., low:]], axis=0)
    mlp_blocks = mlp_blocks.reshape(8, 3, rows, part)

    masks = jnp.concatenate([chosen_mask(attn_route), chosen_mask(mlp_route)], axis=1)
    masks = jnp.pad(masks.astype(BF), ((0, 0), (0, LANE - 2 * EXPERTS)))
    attn_gain, mlp_gain = reorder(attn_gain, 0), reorder(mlp_gain, 0)
    attn_router, mlp_router = reorder(attn_router, 0), reorder(mlp_router, 0)
    group_in, masks, attn_rows = enter(1, reorder(hidden, 1), masks, attn_blocks)
    attn_w, mlp_rows, group_cot = along_y(
        2, attn_rows.reshape(6, 8 * rows, HEAD), mlp_blocks, reorder(cotangent, 1)
    )
    attn_w = attn_w.reshape(6, width, HEAD)
    mlp_w = gather_y(mlp_rows.reshape(3, 8 * rows, part))
    group_in = group_in.reshape(group, width)
    group_cot = group_cot.reshape(group, width)
    masks = masks.reshape(group, LANE)
    mask_a = masks[:, :EXPERTS] > 0.5
    mask_m = masks[:, EXPERTS : 2 * EXPERTS] > 0.5
    start = (zl * 4 + x) * seq + quarter * own

    def mine(array):
        return lax.dynamic_slice_in_dim(array, start, own, axis=0)

    inputs = group_in.astype(F32)
    scale_a = rms_scale(inputs)
    normed_a = (inputs * scale_a * attn_gain).astype(BF)
    gates_a = dense_gates(mm(normed_a, attn_router), mask_a)
    pair_a = lax.dynamic_slice_in_dim(gates_a, zl * 2, 2, axis=1)
    cosines, sines = rope_tables(seq)
    proj = jnp.einsum("td,ndw->ntw", normed_a, attn_w[:4], preferred_element_type=F32)
    proj = proj.reshape(4, 8, seq, HEAD)
    turned = rotate(proj[:3], cosines, sines).astype(BF)
    query, key, value = turned[:2], turned[2], proj[3].astype(BF)
    scores = jnp.einsum("nsrk,stk->nsrt", query, key, preferred_element_type=F32) * scale
    causal = jnp.arange(seq)[None, :] <= jnp.arange(seq)[:, None]
    scores = jnp.where(causal, scores, NEG)
    expon = jnp.exp(scores - jnp.max(scores, axis=-1, keepdims=True))
    probs = expon / jnp.sum(expon, axis=-1, keepdims=True)
    probs_b = probs.astype(BF)
    attended = jnp.einsum("nsrt,stk->nsrk", probs_b, value, preferred_element_type=F32)
    attended = attended.reshape(2, group, HEAD)
    gate_cols = pair_a.T[:, :, None]
    gated_att = (attended * gate_cols).astype(BF)
    branch_a = jnp.einsum("ntw,ndw->td", gated_att, attn_w[4:], preferred_element_type=F32)
    branch_a = team_sum(3, "sum_attn", branch_a.astype(BF))
    own_in = mine(inputs)
    after_attn = own_in + branch_a

    scale_m = rms_scale(after_attn)
    normed_own = (after_attn * scale_m * mlp_gain).astype(BF)
    normed_m = team_spread(4, "spread_normed", normed_own)
    gates_m = dense_gates(mm(normed_m, mlp_router), mask_m)
    col_ok = (jnp.arange(part)[None, :] >= zl * (2 * part - features)).astype(F32)
    gate_m = lax.dynamic_slice_in_dim(gates_m, x, 1, axis=1) * col_ok
    gate_part = mm(normed_m, mlp_w[0])
    up_part = mm(normed_m, mlp_w[1])
    sigma = jax.nn.sigmoid(gate_part)
    silu = gate_part * sigma
    activated = silu * up_part
    gated_act = (activated * gate_m).astype(BF)
    branch_m = mm_nt(gated_act, mlp_w[2])
    branch_m = team_sum(5, "sum_mlp", branch_m.astype(BF))
    out_own = (after_attn + branch_m).astype(BF)

    cot_down = mm(group_cot, mlp_w[2])
    dots_m = jnp.sum(activated * col_ok * cot_down, axis=1, keepdims=True)
    grad_act = cot_down * gate_m
    grad_gate = (grad_act * up_part * sigma * (1.0 + gate_part * (1.0 - sigma))).astype(BF)
    grad_up = (grad_act * silu).astype(BF)
    grad_rows = mm_nt(grad_gate, mlp_w[0]) + mm_nt(grad_up, mlp_w[1])
    one_hot_x = (jnp.arange(LANE) == x).astype(F32)
    back_m = jnp.concatenate([grad_rows, dots_m * one_hot_x], axis=1).astype(BF)
    back_m = team_sum(6, "sum_mlp_back", back_m)
    mlp_grads = sum_y(
        [mm_tn(normed_m, grad_gate), mm_tn(normed_m, grad_up), mm_tn(group_cot, gated_act)]
    )
    mlp_grads = swap_back(7, "swap_mlp", mlp_grads).astype(F32)
    own_gates_m = mine(gates_m)
    logits_back_m = gates_back(own_gates_m, back_m[:, width : width + EXPERTS])
    router_grad_m = mm_tn(normed_own.astype(F32), logits_back_m)
    full_m = back_m[:, :width] + mm_nt(logits_back_m, mlp_router.astype(F32))
    inner_m, gain_grad_m = norm_back(after_attn, scale_m, mlp_gain, full_m)
    grad_mid_own = mine(group_cot).astype(F32) + inner_m

    grad_mid = team_spread(8, "spread_mid", grad_mid_own.astype(BF))
    grad_att = jnp.einsum("td,ndw->ntw", grad_mid, attn_w[4:], preferred_element_type=F32)
    dots_a = jnp.sum(attended * grad_att, axis=2).T
    grad_att = (grad_att * gate_cols).astype(BF).reshape(2, 8, seq, HEAD)
    grad_probs = jnp.einsum("nsrk,stk->nsrt", grad_att, value, preferred_element_type=F32)
    inner = jnp.sum(probs * grad_probs, axis=-1, keepdims=True)
    grad_scores = (probs * (grad_probs - inner) * scale).astype(BF)
    grad_query = jnp.einsum("nsrt,stk->nsrk", grad_scores, key, preferred_element_type=F32)
    grad_key = jnp.einsum("nsrt,nsrk->stk", grad_scores, query, preferred_element_type=F32)
    grad_value = jnp.einsum("nsrt,nsrk->stk", probs_b, grad_att, preferred_element_type=F32)
    turned_back = rotate(
        jnp.concatenate([grad_query, grad_key[None]], axis=0), cosines, -sines
    )
    grad_proj = jnp.concatenate([turned_back, grad_value[None]], axis=0).astype(BF)
    grad_proj = grad_proj.reshape(4, group, HEAD)
    grad_rows_a = jnp.einsum("ntw,ndw->td", grad_proj, attn_w[:4], preferred_element_type=F32)
    pair_hot = (jnp.arange(LANE)[None, :] == (zl * 2 + jnp.arange(2))[:, None]).astype(F32)
    back_a = jnp.concatenate([grad_rows_a, mm(dots_a, pair_hot)], axis=1).astype(BF)
    back_a = team_sum(9, "sum_attn_back", back_a)
    proj_grads = jnp.einsum("td,ntw->dnw", normed_a, grad_proj, preferred_element_type=F32)
    back_grads = jnp.einsum("td,ntw->dnw", grad_mid, gated_att, preferred_element_type=F32)
    attn_grads = jnp.concatenate(
        [proj_grads.reshape(width, 4 * HEAD), back_grads.reshape(width, 2 * HEAD)], axis=1
    )
    attn_grads = sum_y([attn_grads])
    attn_grads = swap_back(10, "swap_attn", attn_grads).astype(F32)
    logits_back_a = gates_back(mine(gates_a), back_a[:, width : width + EXPERTS])
    own_normed_a = mine(normed_a).astype(F32)
    router_grad_a = mm_tn(own_normed_a, logits_back_a)
    full_a = back_a[:, :width] + mm_nt(logits_back_a, attn_router.astype(F32))
    inner_a, gain_grad_a = norm_back(own_in, mine(scale_a), attn_gain, full_a)
    grad_in_own = grad_mid_own + inner_a

    small = jnp.concatenate(
        [gain_grad_a[None], gain_grad_m[None], router_grad_a.T, router_grad_m.T], axis=0
    )
    small = jnp.pad(small, ((0, 6), (0, 0)))
    out_hidden, grad_in, small = leave(11, out_own, grad_in_own.astype(BF), small)
    out_hidden = restore(out_hidden.reshape(seq, width), 1)
    grad_in = restore(grad_in.reshape(seq, width), 1).astype(F32)
    small = restore(small, 1)

    attn_grads = attn_grads.reshape(2, 4, rows, 6, HEAD).transpose(2, 0, 3, 1, 4)
    attn_grads = attn_grads.reshape(rows, 2, 6, 4 * HEAD)
    query_grad = attn_grads[:, :, :2].reshape(rows, EXPERTS, 4 * HEAD)
    kv_grad = attn_grads[:, 0, 2:4] + attn_grads[:, 1, 2:4]
    qkv_grad = jnp.concatenate([query_grad, kv_grad], axis=1)
    out_grad = attn_grads[:, :, 4:].reshape(rows, EXPERTS, 4 * HEAD)
    mlp_grads = mlp_grads.reshape(3, 2, EXPERTS, rows, part)
    whole = jnp.concatenate([mlp_grads[:, 0], mlp_grads[:, 1, ..., 2 * part - features :]], axis=-1)
    whole = whole.transpose(2, 1, 0, 3)
    return (
        out_hidden,
        grad_in,
        small[0],
        small[2 : 2 + EXPERTS].T,
        qkv_grad,
        out_grad,
        small[1],
        small[2 + EXPERTS : 2 + 2 * EXPERTS].T,
        whole[:, :, :2],
        whole[:, :, 2],
    )


def solution(mesh):
    fine = Mesh(mesh.devices.reshape(2, 4, 4, 2, 2), ALL)
    dp, tensor = ("zl", "y", "x"), ("zh", "c")
    placed = (
        P(dp, None),
        P(dp, None),
        P(),
        P(),
        P(dp, None, tensor),
        P(dp, None, tensor),
        P(),
        P(),
        P(dp, None, None, tensor),
        P(dp, None, tensor),
        P(dp, None),
        P(dp, None),
        P(dp, None),
        P(dp, None),
    )
    return jax.shard_map(
        local,
        mesh=fine,
        in_specs=placed,
        out_specs=(
            P(dp, None),
            P(dp, None),
            P(),
            P(),
            P(dp, None, tensor),
            P(dp, None, tensor),
            P(),
            P(),
            P(dp, None, None, tensor),
            P(dp, None, tensor),
        ),
        check_vma=False,
    )
```

```python
import itertools

import jax
import jax.numpy as jnp
import numpy as np
from jax import lax
from jax.experimental import pallas as pl
from jax.experimental.pallas import tpu as pltpu
from jax.sharding import Mesh, PartitionSpec as P

HEAD = 128
LANE = 128
EPS = 1e-05
THETA = 10000.0
NEG = -1e30
EXPERTS = 4
GROUP = ("zl", "x")
TEAM = ("zl", "x", "zh", "c")
ALL = ("zl", "y", "x", "zh", "c")
SIZES = dict(zl=2, y=4, x=4, zh=2, c=2)
BF = jnp.bfloat16
F32 = jnp.float32
MESH = pl.DeviceIdType.MESH
ANY = pl.BlockSpec(memory_space=pl.ANY)
VMEM = pl.BlockSpec(memory_space=pltpu.VMEM)


def dot(a, b, dims):
    return lax.dot_general(a, b, (dims, ((), ())), preferred_element_type=F32)


def mm(a, b):
    return dot(a, b, ((1,), (0,)))


def mm_nt(a, b):
    return dot(a, b, ((1,), (1,)))


def mm_tn(a, b):
    return dot(a, b, ((0,), (0,)))


def rms_scale(values):
    return lax.rsqrt(jnp.mean(values * values, axis=-1, keepdims=True) + EPS)


def chosen_mask(route):
    columns = jnp.arange(EXPERTS)[None, :]
    return (route[:, :1] == columns) | (route[:, 1:] == columns)


def lanes(rows):
    return lax.broadcasted_iota(jnp.int32, (rows, LANE), 1)


def dense_gates(logits, mask):
    top = jnp.max(jnp.where(mask, logits, NEG), axis=1, keepdims=True)
    expon = jnp.where(mask, jnp.exp(jnp.where(mask, logits - top, 0.0)), 0.0)
    return expon / jnp.sum(expon, axis=1, keepdims=True)


def pick(values, lane):
    return jnp.sum(jnp.where(lanes(values.shape[0]) == lane, values, 0.0), axis=1, keepdims=True)


def gates_back(gates, dots):
    return gates * (dots - jnp.sum(gates * dots, axis=1, keepdims=True))


def rope_tables(count):
    frequency = THETA ** (-(np.arange(HEAD // 2).astype(np.float32) * 2.0 / HEAD))
    angles = np.arange(count).astype(np.float32)[:, None] * frequency[None, :].astype(np.float32)
    cosines, sines = np.cos(angles), np.sin(angles)
    return (
        jnp.asarray(np.concatenate([cosines, cosines], axis=1), F32),
        jnp.asarray(np.concatenate([-sines, sines], axis=1), F32),
    )


def rotate(values, cosines, sines):
    return values * cosines + pltpu.roll(values, HEAD // 2, 1) * sines


def norm_back(inputs, gain, grad_normed):
    scale = rms_scale(inputs)
    scaled = inputs * scale
    grad_scaled = grad_normed * gain
    grad_inputs = scale * (
        grad_scaled - scaled * jnp.mean(grad_scaled * scaled, axis=-1, keepdims=True)
    )
    return grad_inputs, jnp.sum(grad_normed * scaled, axis=0, keepdims=True)


def moves(*axes):
    return [dict(zip(axes, steps)) for steps in itertools.product(*[range(SIZES[a]) for a in axes])]


def place(move, sign=1):
    return {a: lax.rem(lax.axis_index(a) + sign * v + SIZES[a], SIZES[a]) for a, v in move.items()}


def number(coords):
    total = 0
    for axis, value in coords.items():
        total = total * SIZES[axis] + value
    return total


def meet(partners):
    barrier = pltpu.get_barrier_semaphore()
    for partner in partners:
        pl.semaphore_signal(barrier, inc=1, device_id=partner, device_id_type=MESH)
    pl.semaphore_wait(barrier, len(partners))


def push(src, dst, send, recv, to):
    return pltpu.make_async_remote_copy(
        src_ref=src, dst_ref=dst, send_sem=send, recv_sem=recv, device_id=to, device_id_type=MESH
    )


def settings(number, moved, vmem=32):
    return dict(
        compiler_params=pltpu.CompilerParams(
            collective_id=number, has_side_effects=True, vmem_limit_bytes=vmem << 20
        ),
        cost_estimate=pl.CostEstimate(flops=0, bytes_accessed=moved, transcendentals=0),
    )


GROUP_MOVES = moves("zl", "x")
TEAM_MOVES = moves("zl", "x", "zh")
Y_MOVES = moves("y")


def sibling():
    return {"c": 1 - lax.axis_index("c")}


class Spread:
    sems = [pltpu.SemaphoreType.DMA((8,))] * 4

    def __init__(self, src, dst, sems):
        self.src, self.dst = src, dst
        self.send, self.recv, self.fsend, self.frecv = sems
        rows = src.shape[0] // 2
        self.half = pl.ds(pl.multiple_of(lax.axis_index("c") * rows, rows), rows)
        self.me = number(place(GROUP_MOVES[0]))

    def start(self):
        self.copies = [pltpu.make_async_copy(self.src, self.dst.at[self.me], self.send.at[0])]
        for k, move in enumerate(GROUP_MOVES):
            if k:
                self.copies.append(
                    push(
                        self.src.at[self.half],
                        self.dst.at[self.me, self.half],
                        self.send.at[k],
                        self.recv.at[k],
                        place(move),
                    )
                )
        for copy in self.copies:
            copy.start()

    def finish(self):
        forwards = []
        for k, move in enumerate(GROUP_MOVES):
            if k:
                self.copies[k].wait_recv()
                block = self.dst.at[number(place(move, -1)), self.half]
                forwards.append(push(block, block, self.fsend.at[k], self.frecv.at[k], sibling()))
                forwards[-1].start()
        for forward in forwards:
            forward.wait()
        self.copies[0].wait()
        for copy in self.copies[1:]:
            copy.wait_send()


class Swap:
    sems = [pltpu.SemaphoreType.DMA((8,))] * 2

    def __init__(self, src, dst, sems):
        self.src, self.dst = src, dst
        self.send, self.recv = sems

    def start(self):
        me = number(place(GROUP_MOVES[0]))
        self.copies = [
            pltpu.make_async_copy(self.src.at[me], self.dst.at[me], self.send.at[0])
        ]
        for k, move in enumerate(GROUP_MOVES):
            if k:
                to = place(move)
                self.copies.append(
                    push(
                        self.src.at[number(to)],
                        self.dst.at[me],
                        self.send.at[k],
                        self.recv.at[k],
                        to,
                    )
                )
        for copy in self.copies:
            copy.start()

    def finish(self):
        for copy in self.copies:
            copy.wait()


def enter(collective, hidden, masks, blocks):
    rows, width = hidden.shape

    def kernel(hidden_ref, mask_ref, block_ref, hidden_out, mask_out, block_out, *sems):
        meet([place(m) for m in GROUP_MOVES[1:]] + [sibling()])
        swap = Swap(block_ref, block_out, sems[0:2])
        first = Spread(mask_ref, mask_out, sems[2:6])
        second = Spread(hidden_ref, hidden_out, sems[6:10])
        swap.start()
        first.start()
        second.start()
        first.finish()
        second.finish()
        swap.finish()

    return pl.pallas_call(
        kernel,
        out_shape=[
            jax.ShapeDtypeStruct((8, rows, width), hidden.dtype),
            jax.ShapeDtypeStruct((8,) + masks.shape, masks.dtype),
            jax.ShapeDtypeStruct(blocks.shape, blocks.dtype),
        ],
        in_specs=[ANY] * 3,
        out_specs=[ANY] * 3,
        scratch_shapes=Swap.sems + Spread.sems * 2,
        name="enter",
        **settings(collective, 90 << 20),
    )(hidden, masks, blocks)


def along_y(collective, rows_a, blocks_m, cotangent):
    def kernel(a_ref, *refs):
        m_refs, cot_ref, a_out, m_outs, cot_out = refs[:3], refs[3], refs[4], refs[5:8], refs[8]
        sems = refs[9:]
        meet([place(m) for m in GROUP_MOVES[1:] + Y_MOVES[1:]] + [sibling()])
        y = lax.axis_index("y")
        copies = [pltpu.make_async_copy(a_ref, a_out.at[y], sems[0].at[0])]
        for k, move in enumerate(Y_MOVES):
            if k:
                copies.append(push(a_ref, a_out.at[y], sems[0].at[k], sems[1].at[k], place(move)))
        for copy in copies:
            copy.start()
        swaps = [Swap(m_refs[i], m_outs[i], sems[2 + 2 * i : 4 + 2 * i]) for i in range(3)]
        spread = Spread(cot_ref, cot_out, sems[8:12])
        for swap in swaps:
            swap.start()
        spread.start()
        for copy in copies:
            copy.wait()
        for swap in swaps:
            swap.finish()
        spread.finish()

    return pl.pallas_call(
        kernel,
        out_shape=[jax.ShapeDtypeStruct((4,) + rows_a.shape, rows_a.dtype)]
        + [jax.ShapeDtypeStruct(b.shape, b.dtype) for b in blocks_m]
        + [jax.ShapeDtypeStruct((8,) + cotangent.shape, cotangent.dtype)],
        in_specs=[ANY] * 5,
        out_specs=[ANY] * 5,
        scratch_shapes=[pltpu.SemaphoreType.DMA((4,))] * 2 + Swap.sems * 3 + Spread.sems,
        name="along_y",
        **settings(collective, 120 << 20),
    )(rows_a, *blocks_m, cotangent)


def swap_back(collective, name, blocks):
    count = len(blocks)

    def kernel(*refs):
        sems = refs[2 * count :]
        meet([place(m) for m in GROUP_MOVES[1:]])
        swaps = [Swap(refs[i], refs[count + i], sems[2 * i : 2 * i + 2]) for i in range(count)]
        for swap in swaps:
            swap.start()
        for swap in swaps:
            swap.finish()

    return pl.pallas_call(
        kernel,
        out_shape=[jax.ShapeDtypeStruct(b.shape, b.dtype) for b in blocks],
        in_specs=[ANY] * count,
        out_specs=[ANY] * count,
        scratch_shapes=Swap.sems * count,
        name=name,
        **settings(collective, 80 << 20),
    )(*blocks)


class TeamSum:
    @staticmethod
    def scratch(own, width):
        return [
            pltpu.VMEM((8, 2, own, width), BF),
            pltpu.VMEM((16, own, width), BF),
            pltpu.SemaphoreType.DMA((8,)),
            pltpu.SemaphoreType.DMA((8,)),
            pltpu.SemaphoreType.DMA((16,)),
            pltpu.SemaphoreType.DMA((16,)),
        ]

    def __init__(self, part, scratch):
        self.part = part
        self.other, self.got, self.ssem, self.rsem, self.dsend, self.drecv = scratch
        self.zl, self.x, self.zh, self.c = (lax.axis_index(a) for a in TEAM)
        self.seq = self.zl * 4 + self.x
        self.chip = self.seq * 2 + self.zh

    def swap(self, seq):
        return push(
            self.part.at[seq, :, 1 - self.c],
            self.other.at[seq],
            self.ssem.at[seq],
            self.rsem.at[seq],
            sibling(),
        )

    def send(self, seq, zh):
        chip = seq * 2 + zh
        return push(
            self.part.at[seq, zh, self.c],
            self.got.at[self.chip],
            self.dsend.at[chip],
            self.drecv.at[self.chip],
            {"zl": seq // 4, "x": lax.rem(seq, 4), "zh": zh},
        )

    def both(self, seq, zh):
        return self.part[seq, zh, self.c].astype(F32) + self.other[seq, zh].astype(F32)

    def forward(self, seq):
        self.swap(seq).wait_recv()
        for zh in range(2):
            self.part[seq, zh, self.c] = self.both(seq, zh).astype(BF)
            self.send(seq, zh).start()

    def pair(self, step):
        back = 3 - step
        return lax.rem(self.zl + back // 2, 2) * 2 + lax.rem(self.x // 2 + back, 2)

    def last(self):
        beside = self.seq + 1 - 2 * lax.rem(self.x, 2)
        self.forward(beside)
        self.swap(self.seq).wait_recv()
        away = 1 - self.zh
        self.part[self.seq, away, self.c] = self.both(self.seq, away).astype(BF)
        self.send(self.seq, away).start()

    def total(self, total_ref):
        total_ref[...] = self.both(self.seq, self.zh)
        for move in TEAM_MOVES[1:]:
            chip = number(place(move, -1))
            pltpu.make_async_copy(self.got.at[chip], self.got.at[chip], self.drecv.at[chip]).wait()
            total_ref[...] += self.got[chip].astype(F32)

    def close(self):
        for seq in range(8):
            self.swap(seq).wait_send()
        for move in TEAM_MOVES[1:]:
            to = place(move)
            self.send(to["zl"] * 4 + to["x"], to["zh"]).wait_send()

    def run(self):
        for step in range(4):
            for j in range(2):
                self.swap(self.pair(step) * 2 + j).start()
        for step in range(3):
            for j in range(2):
                self.forward(self.pair(step) * 2 + j)
        self.last()


class TeamSpread:
    sems = [pltpu.SemaphoreType.DMA((16,))] * 4

    def __init__(self, rows, out, sems):
        self.rows, self.out = rows, out
        self.send, self.recv, self.fsend, self.frecv = sems

    def run(self):
        c = lax.axis_index("c")
        mine = self.out.at[number(place(TEAM_MOVES[0])), c]
        stay = pltpu.make_async_copy(self.rows, mine, self.send.at[0])
        stay.start()
        pushes = [
            push(self.rows, mine, self.send.at[k], self.recv.at[k], place(TEAM_MOVES[k]))
            for k in range(1, 16)
        ]
        for copy in pushes:
            copy.start()
        forwards = [push(self.rows, mine, self.fsend.at[0], self.frecv.at[0], sibling())]
        forwards[0].start()
        for k in range(1, 16):
            pushes[k - 1].wait_recv()
            tile = self.out.at[number(place(TEAM_MOVES[k], -1)), c]
            forwards.append(push(tile, tile, self.fsend.at[k], self.frecv.at[k], sibling()))
            forwards[-1].start()
        for copy in forwards:
            copy.wait()
        stay.wait()
        for copy in pushes:
            copy.wait_send()


def meet_team():
    meet([place(m) for m in TEAM_MOVES[1:]] + [sibling()])


def soft(scores, causal):
    scores = jnp.where(causal, scores, NEG)
    expon = jnp.exp(scores - jnp.max(scores, axis=-1, keepdims=True))
    return expon / jnp.sum(expon, axis=-1, keepdims=True)


def causal_mask(copies, seq):
    rows = lax.rem(lax.broadcasted_iota(jnp.int32, (copies * seq, seq), 0), seq)
    return lax.broadcasted_iota(jnp.int32, (copies * seq, seq), 1) <= rows


def attn_forward(collective, hidden, masks, weights, gain, routers, cosines, sines, mlp_gain, hidden_own):
    _, seq, width = hidden.shape
    own = hidden_own.shape[0]
    scale = HEAD ** (-0.5)

    def kernel(
        hid, mask, w_ref, gain_ref, router_ref, cos_ref, sin_ref, gain_m_ref, own_ref,
        normed_out, qkv_out, gated_out, gates_out, after_out, spread_out,
        part, total, row, *rest,
    ):
        meet_team()
        team = TeamSum(part, rest[:6])
        first = 2 * team.zl
        causal = causal_mask(2, seq)

        def step(i, _):
            pair = team.pair(i)
            for j in range(2):
                values = hid[pair * 2 + j].astype(F32)
                normed_out[pair * 2 + j] = (values * rms_scale(values) * gain_ref[...]).astype(BF)
            normed = normed_out[pl.ds(pair * 2, 2)].reshape(2 * seq, width)
            logits = mm(normed, router_ref[...])
            proj = mm(normed, w_ref[:, : 4 * HEAD])
            allowed = mask[pl.ds(pair * 2, 2)].reshape(2 * seq, LANE).astype(F32) > 0.5
            gates = dense_gates(logits, allowed & (lanes(2 * seq) < EXPERTS))
            gates_out[pl.ds(pair * 2, 2)] = gates.reshape(2, seq, LANE)
            gated = []
            for j in range(2):
                rows = slice(j * seq, (j + 1) * seq)
                query = [
                    rotate(proj[rows, e * HEAD : (e + 1) * HEAD], cos_ref[...], sin_ref[...]).astype(BF)
                    for e in range(2)
                ]
                key = rotate(proj[rows, 2 * HEAD : 3 * HEAD], cos_ref[...], sin_ref[...]).astype(BF)
                value = proj[rows, 3 * HEAD :].astype(BF)
                probs = soft(mm_nt(jnp.concatenate(query, axis=0), key) * scale, causal)
                attended = mm(probs.astype(BF), value)
                out = [
                    (attended[e * seq : (e + 1) * seq] * pick(gates[rows], first + e)).astype(BF)
                    for e in range(2)
                ]
                qkv_out[pair * 2 + j] = jnp.concatenate(query + [key, value], axis=1)
                gated.append(jnp.concatenate(out, axis=1))
                gated_out[pair * 2 + j] = gated[-1]
            branch = mm_nt(jnp.concatenate(gated, axis=0), w_ref[:, 4 * HEAD :])
            part[pl.ds(pair * 2, 2)] = branch.astype(BF).reshape(2, 2, 2, own, width)
            for j in range(2):
                team.swap(pair * 2 + j).start()

            @pl.when(i > 0)
            def _():
                for j in range(2):
                    team.forward(team.pair(i - 1) * 2 + j)

            return 0

        lax.fori_loop(0, 4, step, 0)
        team.last()
        team.total(total)
        after = total[...] + own_ref[...].astype(F32)
        after_out[...] = after
        row[...] = (after * rms_scale(after) * gain_m_ref[...]).astype(BF)
        TeamSpread(row, spread_out, rest[6:]).run()
        team.close()

    return pl.pallas_call(
        kernel,
        out_shape=[
            jax.ShapeDtypeStruct((8, seq, width), BF),
            jax.ShapeDtypeStruct((8, seq, 4 * HEAD), BF),
            jax.ShapeDtypeStruct((8, seq, 2 * HEAD), BF),
            jax.ShapeDtypeStruct((8, seq, LANE), F32),
            jax.ShapeDtypeStruct((own, width), F32),
            jax.ShapeDtypeStruct((16, 2, own, width), BF),
        ],
        in_specs=[VMEM] * 9,
        out_specs=[VMEM] * 5 + [ANY],
        scratch_shapes=[
            pltpu.VMEM((8, 2, 2, own, width), BF),
            pltpu.VMEM((own, width), F32),
            pltpu.VMEM((own, width), BF),
        ]
        + TeamSum.scratch(own, width)
        + TeamSpread.sems,
        name="attn_forward",
        **settings(collective, 200 << 20, 48),
    )(hidden, masks, weights, gain, routers, cosines, sines, mlp_gain, hidden_own)


def experts(normed, cotangent, masks, routers, weights, extra):
    rows, width = normed.shape
    part = weights[0].shape[1]
    tile = rows // 4

    def kernel(x_ref, cot_ref, mask, router_ref, wg, wu, wd, h_out, dg_out, du_out, branch_out, back_out, gates_out):
        lane = EXPERTS + lax.axis_index("x")
        skip = lax.axis_index("zl") * extra
        x = x_ref[...]
        logits = mm(x, router_ref[...])
        index = lanes(tile)
        allowed = (mask[...].astype(F32) > 0.5) & (index >= EXPERTS) & (index < 2 * EXPERTS)
        gates = dense_gates(logits, allowed)
        gates_out[...] = gates
        valid = (lax.broadcasted_iota(jnp.int32, (1, part), 1) >= skip).astype(F32)
        gate = pick(gates, lane) * valid
        gate_part = mm(x, wg[...])
        up_part = mm(x, wu[...])
        sigma = 1.0 / (1.0 + jnp.exp(-gate_part))
        silu = gate_part * sigma
        activated = silu * up_part
        h = (activated * gate).astype(BF)
        h_out[...] = h
        branch_out[...] = mm_nt(h, wd[...]).astype(BF)
        cot_down = mm(cot_ref[...], wd[...])
        dots = jnp.sum(activated * valid * cot_down, axis=1, keepdims=True)
        grad_act = cot_down * gate
        grad_gate = (grad_act * up_part * sigma * (1.0 + gate_part * (1.0 - sigma))).astype(BF)
        grad_up = (grad_act * silu).astype(BF)
        dg_out[...] = grad_gate
        du_out[...] = grad_up
        back_out[:, :width] = (mm_nt(grad_gate, wg[...]) + mm_nt(grad_up, wu[...])).astype(BF)
        back_out[:, width:] = jnp.where(index == lane, dots, 0.0).astype(BF)

    def tiled(cols):
        return pl.BlockSpec((tile, cols), lambda i: (i, 0))

    def whole(array):
        return pl.BlockSpec(array.shape, lambda i: (0, 0), pipeline_mode=pl.Buffered(1))

    cols = [part, part, part, width, width + LANE]
    return pl.pallas_call(
        kernel,
        grid=(4,),
        out_shape=[jax.ShapeDtypeStruct((rows, c), BF) for c in cols]
        + [jax.ShapeDtypeStruct((rows, LANE), F32)],
        in_specs=[tiled(width), tiled(width), tiled(LANE), whole(routers)]
        + [whole(w) for w in weights],
        out_specs=[tiled(c) for c in cols] + [tiled(LANE)],
        compiler_params=pltpu.CompilerParams(vmem_limit_bytes=48 << 20),
        cost_estimate=pl.CostEstimate(
            flops=12 * rows * width * part, bytes_accessed=40 << 20, transcendentals=rows * part
        ),
        name="experts",
    )(normed, cotangent, masks, routers, *weights)


def attn_backward(grad_mid, qkv, gates, weights, cosines, sines):
    rows, width = grad_mid.shape
    tile = rows // 4
    seq = tile // 2
    scale = HEAD ** (-0.5)

    def kernel(gm_ref, qkv_ref, gates_ref, w_ref, cos_ref, sin_ref, proj_out, back_out):
        first = 2 * lax.axis_index("zl")
        causal = causal_mask(2, seq)
        grads = mm(gm_ref[...], w_ref[:, 4 * HEAD :])
        gates = gates_ref[...]
        index = lanes(tile)
        dots = jnp.zeros((tile, LANE), F32)
        for j in range(2):
            here = slice(j * seq, (j + 1) * seq)
            query = jnp.concatenate(
                [qkv_ref[here, e * HEAD : (e + 1) * HEAD] for e in range(2)], axis=0
            )
            key = qkv_ref[here, 2 * HEAD : 3 * HEAD]
            value = qkv_ref[here, 3 * HEAD :]
            probs = soft(mm_nt(query, key) * scale, causal)
            probs_b = probs.astype(BF)
            attended = mm(probs_b, value)
            grad = jnp.concatenate(
                [grads[here, e * HEAD : (e + 1) * HEAD] for e in range(2)], axis=0
            )
            gate = jnp.concatenate([pick(gates[here], first + e) for e in range(2)], axis=0)
            each = jnp.sum(attended * grad, axis=1, keepdims=True)
            spread = jnp.where(lanes(seq) == first, each[:seq], 0.0)
            spread += jnp.where(lanes(seq) == first + 1, each[seq:], 0.0)
            grad = (grad * gate).astype(BF)
            grad_probs = mm_nt(grad, value)
            inner = jnp.sum(probs * grad_probs, axis=1, keepdims=True)
            grad_scores = (probs * (grad_probs - inner) * scale).astype(BF)
            grad_query = mm(grad_scores, key)
            grad_key = mm_tn(grad_scores, query)
            grad_value = mm_tn(probs_b, grad)
            proj_out[here, :HEAD] = rotate(grad_query[:seq], cos_ref[...], -sin_ref[...]).astype(BF)
            proj_out[here, HEAD : 2 * HEAD] = rotate(
                grad_query[seq:], cos_ref[...], -sin_ref[...]
            ).astype(BF)
            proj_out[here, 2 * HEAD : 3 * HEAD] = rotate(
                grad_key, cos_ref[...], -sin_ref[...]
            ).astype(BF)
            proj_out[here, 3 * HEAD :] = grad_value.astype(BF)
            back_out[here, width:] = spread.astype(BF)
        back_out[:, :width] = mm_nt(proj_out[...], w_ref[:, : 4 * HEAD]).astype(BF)

    def tiled(cols):
        return pl.BlockSpec((tile, cols), lambda i: (i, 0))

    def whole(array):
        return pl.BlockSpec(array.shape, lambda i: (0, 0), pipeline_mode=pl.Buffered(1))

    return pl.pallas_call(
        kernel,
        grid=(4,),
        out_shape=[
            jax.ShapeDtypeStruct((rows, 4 * HEAD), BF),
            jax.ShapeDtypeStruct((rows, width + LANE), BF),
        ],
        in_specs=[tiled(width), tiled(4 * HEAD), tiled(LANE)]
        + [whole(a) for a in (weights, cosines, sines)],
        out_specs=[tiled(4 * HEAD), tiled(width + LANE)],
        compiler_params=pltpu.CompilerParams(vmem_limit_bytes=48 << 20),
        cost_estimate=pl.CostEstimate(
            flops=2 * rows * width * 6 * HEAD, bytes_accessed=20 << 20, transcendentals=0
        ),
        name="attn_backward",
    )(grad_mid, qkv, gates, weights, cosines, sines)


def back_through_norm(total, inputs, gain, gates, normed, routers):
    width = inputs.shape[1]
    logits_back = gates_back(gates, total[:, width:])
    full = total[:, :width] + mm_nt(logits_back.astype(BF), routers)
    inner, gain_grad = norm_back(inputs, gain, full)
    return inner, gain_grad, mm_tn(logits_back.astype(BF), normed)[:8]


def middle(collective, back, after, gain, gates_own, routers, cot_own):
    own, width = after.shape

    def kernel(part_ref, after_ref, gain_ref, gates_ref, router_ref, cot_ref, mid_out, small_out, spread_out, part, load, total, row, *rest):
        fetch = pltpu.make_async_copy(part_ref, part, load.at[0])
        fetch.start()
        meet_team()
        fetch.wait()
        team = TeamSum(part, rest[:6])
        team.run()
        after = after_ref[...]
        normed = (after * rms_scale(after) * gain_ref[...]).astype(BF)
        team.total(total)
        inner, gain_grad, router_grad = back_through_norm(
            total[...], after, gain_ref[...], gates_ref[...], normed, router_ref[...]
        )
        grad_mid = cot_ref[...].astype(F32) + inner
        mid_out[...] = grad_mid
        row[...] = grad_mid.astype(BF)
        small_out[:8] = jnp.zeros((8, width), F32)
        small_out[0:1] = gain_grad
        small_out[8:] = router_grad
        TeamSpread(row, spread_out, rest[6:]).run()
        team.close()

    return pl.pallas_call(
        kernel,
        out_shape=[
            jax.ShapeDtypeStruct((own, width), F32),
            jax.ShapeDtypeStruct((16, width), F32),
            jax.ShapeDtypeStruct((16, 2, own, width), BF),
        ],
        in_specs=[ANY] + [VMEM] * 5,
        out_specs=[VMEM] * 2 + [ANY],
        scratch_shapes=[
            pltpu.VMEM((8, 2, 2, own, width + LANE), BF),
            pltpu.SemaphoreType.DMA((1,)),
            pltpu.VMEM((own, width + LANE), F32),
            pltpu.VMEM((own, width), BF),
        ]
        + TeamSum.scratch(own, width + LANE)
        + TeamSpread.sems,
        name="middle",
        **settings(collective, 160 << 20, 48),
    )(back.reshape(8, 2, 2, own, width + LANE), after, gain, gates_own, routers, cot_own)


def leave(collective, back, branch, after, grad_mid, inputs, gain, gates_own, routers, small):
    own, width = after.shape
    stages = [moves("c"), moves("x"), moves("y"), moves("zl", "zh")]
    near = moves("zh", "c")

    def kernel(
        back_ref, branch_ref, after_ref, mid_ref, in_ref, gain_ref, gates_ref, router_ref, small_ref,
        out_all, grad_all, small_out,
        part_a, part_b, load, total_a, total_b, row_a, row_b, got, send, recv, ssend, srecv, *rest,
    ):
        fetches = [
            pltpu.make_async_copy(back_ref, part_a, load.at[0]),
            pltpu.make_async_copy(branch_ref, part_b, load.at[1]),
        ]
        for fetch in fetches:
            fetch.start()
        meet([place(m) for m in TEAM_MOVES[1:] + Y_MOVES[1:]] + [place(m) for m in near[1:] if m["c"]])
        team_a, team_b = TeamSum(part_a, rest[:6]), TeamSum(part_b, rest[6:])
        fetches[0].wait()
        team_a.run()
        fetches[1].wait()
        team_b.run()
        inputs = in_ref[...].astype(F32)
        normed = (inputs * rms_scale(inputs) * gain_ref[...]).astype(BF)
        team_a.total(total_a)
        inner, gain_grad, router_grad = back_through_norm(
            total_a[...], inputs, gain_ref[...], gates_ref[...], normed, router_ref[...]
        )
        row_a[...] = (mid_ref[...] + inner).astype(BF)
        small_out[...] = small_ref[...]
        small_out[1:2] = gain_grad
        small_out[8:] += router_grad
        me = number(place(near[0]))
        copies = []

        def spread(i, src, dst):
            new = [pltpu.make_async_copy(src, dst.at[me], send.at[i, 0])]
            for k in range(1, 4):
                new.append(push(src, dst.at[me], send.at[i, k], recv.at[i, k], place(near[k])))
            for copy in new:
                copy.start()
            copies.extend(new)

        spread(0, row_a, grad_all)
        for s, stage in enumerate(stages):
            swaps = [
                push(small_out, got.at[s, k - 1], ssend.at[s, k], srecv.at[s, k], place(stage[k]))
                for k in range(1, len(stage))
            ]
            for swap in swaps:
                swap.start()
            if s == 0:
                team_b.total(total_b)
                row_b[...] = (after_ref[...] + total_b[...]).astype(BF)
                spread(1, row_b, out_all)
            for swap in swaps:
                swap.wait()
            total = small_out[...]
            for k in range(1, len(stage)):
                total += got[s, k - 1]
            small_out[...] = total
        for copy in copies:
            copy.wait()
        team_a.close()
        team_b.close()

    return pl.pallas_call(
        kernel,
        out_shape=[jax.ShapeDtypeStruct((4, own, width), BF)] * 2
        + [jax.ShapeDtypeStruct((16, width), F32)],
        in_specs=[ANY, ANY] + [VMEM] * 7,
        out_specs=[ANY, ANY, VMEM],
        scratch_shapes=[
            pltpu.VMEM((8, 2, 2, own, width + LANE), BF),
            pltpu.VMEM((8, 2, 2, own, width), BF),
            pltpu.SemaphoreType.DMA((2,)),
            pltpu.VMEM((own, width + LANE), F32),
            pltpu.VMEM((own, width), F32),
            pltpu.VMEM((own, width), BF),
            pltpu.VMEM((own, width), BF),
            pltpu.VMEM((4, 3, 16, width), F32),
        ]
        + [pltpu.SemaphoreType.DMA((2, 4))] * 2
        + [pltpu.SemaphoreType.DMA((4, 4))] * 2
        + TeamSum.scratch(own, width + LANE)
        + TeamSum.scratch(own, width),
        name="leave",
        **settings(collective, 200 << 20, 48),
    )(
        back.reshape(8, 2, 2, own, width + LANE),
        branch.reshape(8, 2, 2, own, width),
        after, grad_mid, inputs, gain, gates_own, routers, small,
    )


def reorder(array, axis):
    shape = array.shape
    split = shape[:axis] + (2, 4, shape[axis] // 8) + shape[axis + 1 :]
    return jnp.swapaxes(array.reshape(split), axis, axis + 1).reshape(shape)


def restore(array, axis):
    shape = array.shape
    split = shape[:axis] + (4, 2, shape[axis] // 8) + shape[axis + 1 :]
    return jnp.swapaxes(array.reshape(split), axis, axis + 1).reshape(shape)


def gather_y(block):
    return lax.all_gather(block.reshape(-1, block.shape[2]), "y", axis=0, tiled=True)


def sum_y(grad):
    summed = lax.psum_scatter(grad.astype(BF), "y", scatter_dimension=0, tiled=True)
    return summed.reshape(8, -1, grad.shape[1])


def local(
    hidden,
    cotangent,
    attn_gain,
    attn_router,
    qkv_weight,
    out_weight,
    mlp_gain,
    mlp_router,
    gate_up_weight,
    down_weight,
    attn_route,
    attn_slot,
    mlp_route,
    mlp_slot,
):
    seq, width = hidden.shape
    rows = qkv_weight.shape[0]
    features = down_weight.shape[2]
    part = (features // LANE + 1) // 2 * LANE
    low = features - part
    zl, x = lax.axis_index("zl"), lax.axis_index("x")
    quarter = lax.axis_index("zh") * 2 + lax.axis_index("c")
    own = seq // 4
    group = 8 * seq
    cosines, sines = rope_tables(seq)

    query_blocks = qkv_weight[:, :EXPERTS].reshape(rows, 2, 2, 4, HEAD).transpose(1, 3, 0, 2, 4)
    kv_blocks = qkv_weight[:, EXPERTS:].reshape(rows, 2, 4, HEAD).transpose(2, 0, 1, 3)
    kv_blocks = jnp.broadcast_to(kv_blocks[None], (2,) + kv_blocks.shape)
    out_blocks = out_weight.reshape(rows, 2, 2, 4, HEAD).transpose(1, 3, 0, 2, 4)
    attn_blocks = jnp.concatenate([query_blocks, kv_blocks, out_blocks], axis=3)
    attn_blocks = attn_blocks.reshape(8, rows, 6 * HEAD)

    def by_target(weight):
        weight = weight.transpose(1, 0, 2)
        return jnp.stack([weight[..., :part], weight[..., low:]], axis=0).reshape(8, rows, part)

    mlp_blocks = [
        by_target(w) for w in (gate_up_weight[:, :, 0], gate_up_weight[:, :, 1], down_weight)
    ]

    masks = jnp.concatenate([chosen_mask(attn_route), chosen_mask(mlp_route)], axis=1)
    masks = jnp.pad(masks.astype(BF), ((0, 0), (0, LANE - 2 * EXPERTS)))
    attn_gain, mlp_gain = reorder(attn_gain, 0)[None], reorder(mlp_gain, 0)[None]
    routers = reorder(jnp.concatenate([attn_router, mlp_router], axis=1), 0)
    routers = jnp.pad(routers, ((0, 0), (0, LANE - 2 * EXPERTS)))
    hidden = reorder(hidden, 1)
    cotangent = reorder(cotangent, 1)
    hidden_own = lax.dynamic_slice_in_dim(hidden, quarter * own, own, axis=0)
    cot_own = lax.dynamic_slice_in_dim(cotangent, quarter * own, own, axis=0)
    start = (zl * 4 + x) * seq + quarter * own

    def mine(array):
        return lax.dynamic_slice_in_dim(array, start, own, axis=0)

    group_in, masks, attn_rows = enter(1, hidden, masks, attn_blocks)
    attn_w, *mlp_rows, group_cot = along_y(
        2, attn_rows.reshape(8 * rows, 6 * HEAD), mlp_blocks, cotangent
    )
    attn_w = attn_w.reshape(width, 6 * HEAD)
    mlp_w = [gather_y(block) for block in mlp_rows]
    group_cot = group_cot.reshape(group, width)

    normed_a, qkv, gated_att, gates_a, after, normed_m = attn_forward(
        3, group_in, masks, attn_w, attn_gain, routers, cosines, sines, mlp_gain, hidden_own
    )
    normed_a = normed_a.reshape(group, width)
    normed_m = normed_m.reshape(group, width)
    gates_a = gates_a.reshape(group, LANE)

    h, grad_gate, grad_up, branch_m, back_m, gates_m = experts(
        normed_m, group_cot, masks.reshape(group, LANE), routers, mlp_w, 2 * part - features
    )
    mlp_grads = [
        sum_y(mm_tn(normed_m, grad_gate)),
        sum_y(mm_tn(normed_m, grad_up)),
        sum_y(mm_tn(group_cot, h)),
    ]
    grad_mid_own, small_m, grad_mid = middle(
        4, back_m, after, mlp_gain, mine(gates_m), routers, cot_own
    )
    grad_mid = grad_mid.reshape(group, width)
    grad_proj, back_a = attn_backward(
        grad_mid, qkv.reshape(group, 4 * HEAD), gates_a, attn_w, cosines, sines
    )
    attn_grads = sum_y(
        jnp.concatenate(
            [
                mm_tn(normed_a, grad_proj).astype(BF),
                mm_tn(grad_mid, gated_att.reshape(group, 2 * HEAD)).astype(BF),
            ],
            axis=1,
        )
    )
    out_hidden, grad_in, small = leave(
        5, back_a, branch_m, after, grad_mid_own, hidden_own, attn_gain, mine(gates_a), routers, small_m
    )
    out_hidden = restore(out_hidden.reshape(seq, width), 1)
    grad_in = restore(grad_in.reshape(seq, width), 1).astype(F32)
    small = restore(small, 1)

    *mlp_grads, attn_grads = swap_back(6, "swap_back", mlp_grads + [attn_grads])
    attn_grads = attn_grads.astype(F32).reshape(2, 4, rows, 6, HEAD).transpose(2, 0, 3, 1, 4)
    attn_grads = attn_grads.reshape(rows, 2, 6, 4 * HEAD)
    query_grad = attn_grads[:, :, :2].reshape(rows, EXPERTS, 4 * HEAD)
    kv_grad = attn_grads[:, 0, 2:4] + attn_grads[:, 1, 2:4]
    qkv_grad = jnp.concatenate([query_grad, kv_grad], axis=1)
    out_grad = attn_grads[:, :, 4:].reshape(rows, EXPERTS, 4 * HEAD)

    def placed_back(grad):
        grad = grad.reshape(2, EXPERTS, rows, part)
        return jnp.concatenate([grad[0], grad[1, ..., 2 * part - features :]], axis=-1).transpose(1, 0, 2)

    gate_grad, up_grad, down_grad = [placed_back(g) for g in mlp_grads]
    return (
        out_hidden,
        grad_in,
        small[1],
        small[8 : 8 + EXPERTS].T,
        qkv_grad,
        out_grad,
        small[0],
        small[8 + EXPERTS :].T,
        jnp.stack([gate_grad, up_grad], axis=2).astype(F32),
        down_grad.astype(F32),
    )


def solution(mesh):
    fine = Mesh(mesh.devices.reshape(2, 4, 4, 2, 2), ALL)
    dp, tensor = ("zl", "y", "x"), ("zh", "c")
    placed = (
        P(dp, None),
        P(dp, None),
        P(),
        P(),
        P(dp, None, tensor),
        P(dp, None, tensor),
        P(),
        P(),
        P(dp, None, None, tensor),
        P(dp, None, tensor),
        P(dp, None),
        P(dp, None),
        P(dp, None),
        P(dp, None),
    )
    return jax.shard_map(
        local,
        mesh=fine,
        in_specs=placed,
        out_specs=(
            P(dp, None),
            P(dp, None),
            P(),
            P(),
            P(dp, None, tensor),
            P(dp, None, tensor),
            P(),
            P(),
            P(dp, None, None, tensor),
            P(dp, None, tensor),
        ),
        check_vma=False,
    )
```

```python
import itertools

import jax
import jax.numpy as jnp
import numpy as np
from jax import lax
from jax.experimental import pallas as pl
from jax.experimental.pallas import tpu as pltpu
from jax.sharding import Mesh, PartitionSpec as P

HEAD = 128
LANE = 128
EPS = 1e-05
THETA = 10000.0
NEG = -1e30
EXPERTS = 4
GROUP = ("zl", "x")
TEAM = ("zl", "x", "zh", "c")
ALL = ("zl", "y", "x", "zh", "c")
SIZES = dict(zl=2, y=4, x=4, zh=2, c=2)
BF = jnp.bfloat16
F32 = jnp.float32
MESH = pl.DeviceIdType.MESH
ANY = pl.BlockSpec(memory_space=pl.ANY)
VMEM = pl.BlockSpec(memory_space=pltpu.VMEM)


def dot(a, b, dims):
    return lax.dot_general(a, b, (dims, ((), ())), preferred_element_type=F32)


def mm(a, b):
    return dot(a, b, ((1,), (0,)))


def mm_nt(a, b):
    return dot(a, b, ((1,), (1,)))


def mm_tn(a, b):
    return dot(a, b, ((0,), (0,)))


def rms_scale(values):
    return lax.rsqrt(jnp.mean(values * values, axis=-1, keepdims=True) + EPS)


def chosen_mask(route):
    columns = jnp.arange(EXPERTS)[None, :]
    return (route[:, :1] == columns) | (route[:, 1:] == columns)


def lanes(rows):
    return lax.broadcasted_iota(jnp.int32, (rows, LANE), 1)


def dense_gates(logits, mask):
    top = jnp.max(jnp.where(mask, logits, NEG), axis=1, keepdims=True)
    expon = jnp.where(mask, jnp.exp(jnp.where(mask, logits - top, 0.0)), 0.0)
    return expon / jnp.sum(expon, axis=1, keepdims=True)


def pick(values, lane):
    return jnp.sum(jnp.where(lanes(values.shape[0]) == lane, values, 0.0), axis=1, keepdims=True)


def gates_back(gates, dots):
    return gates * (dots - jnp.sum(gates * dots, axis=1, keepdims=True))


def rope_tables(count):
    frequency = THETA ** (-(np.arange(HEAD // 2).astype(np.float32) * 2.0 / HEAD))
    angles = np.arange(count).astype(np.float32)[:, None] * frequency[None, :].astype(np.float32)
    cosines, sines = np.cos(angles), np.sin(angles)
    return (
        jnp.asarray(np.concatenate([cosines, cosines], axis=1), F32),
        jnp.asarray(np.concatenate([-sines, sines], axis=1), F32),
    )


def rotate(values, cosines, sines):
    return values * cosines + pltpu.roll(values, HEAD // 2, 1) * sines


def norm_back(inputs, gain, grad_normed):
    scale = rms_scale(inputs)
    scaled = inputs * scale
    grad_scaled = grad_normed * gain
    grad_inputs = scale * (
        grad_scaled - scaled * jnp.mean(grad_scaled * scaled, axis=-1, keepdims=True)
    )
    return grad_inputs, jnp.sum(grad_normed * scaled, axis=0, keepdims=True)


def moves(*axes):
    return [dict(zip(axes, steps)) for steps in itertools.product(*[range(SIZES[a]) for a in axes])]


def place(move, sign=1):
    return {a: lax.rem(lax.axis_index(a) + sign * v + SIZES[a], SIZES[a]) for a, v in move.items()}


def number(coords):
    total = 0
    for axis, value in coords.items():
        total = total * SIZES[axis] + value
    return total


def meet(partners):
    barrier = pltpu.get_barrier_semaphore()
    for partner in partners:
        pl.semaphore_signal(barrier, inc=1, device_id=partner, device_id_type=MESH)
    pl.semaphore_wait(barrier, len(partners))


def push(src, dst, send, recv, to):
    return pltpu.make_async_remote_copy(
        src_ref=src, dst_ref=dst, send_sem=send, recv_sem=recv, device_id=to, device_id_type=MESH
    )


def settings(number, moved, vmem=32):
    return dict(
        compiler_params=pltpu.CompilerParams(
            collective_id=number, has_side_effects=True, vmem_limit_bytes=vmem << 20
        ),
        cost_estimate=pl.CostEstimate(flops=0, bytes_accessed=moved, transcendentals=0),
    )


GROUP_MOVES = moves("zl", "x")
TEAM_MOVES = moves("zl", "x", "zh")
Y_MOVES = moves("y")


def sibling():
    return {"c": 1 - lax.axis_index("c")}


class Spread:
    sems = [pltpu.SemaphoreType.DMA((8,))] * 4

    def __init__(self, src, dst, sems):
        self.src, self.dst = src, dst
        self.send, self.recv, self.fsend, self.frecv = sems
        rows = src.shape[0] // 2
        self.half = pl.ds(pl.multiple_of(lax.axis_index("c") * rows, rows), rows)
        self.me = number(place(GROUP_MOVES[0]))

    def start(self):
        self.copies = [pltpu.make_async_copy(self.src, self.dst.at[self.me], self.send.at[0])]
        for k, move in enumerate(GROUP_MOVES):
            if k:
                self.copies.append(
                    push(
                        self.src.at[self.half],
                        self.dst.at[self.me, self.half],
                        self.send.at[k],
                        self.recv.at[k],
                        place(move),
                    )
                )
        for copy in self.copies:
            copy.start()

    def finish(self):
        forwards = []
        for k, move in enumerate(GROUP_MOVES):
            if k:
                self.copies[k].wait_recv()
                block = self.dst.at[number(place(move, -1)), self.half]
                forwards.append(push(block, block, self.fsend.at[k], self.frecv.at[k], sibling()))
                forwards[-1].start()
        for forward in forwards:
            forward.wait()
        self.copies[0].wait()
        for copy in self.copies[1:]:
            copy.wait_send()


class Swap:
    sems = [pltpu.SemaphoreType.DMA((8,))] * 2

    def __init__(self, src, dst, sems):
        self.src, self.dst = src, dst
        self.send, self.recv = sems

    def start(self):
        me = number(place(GROUP_MOVES[0]))
        self.copies = [
            pltpu.make_async_copy(self.src.at[me], self.dst.at[me], self.send.at[0])
        ]
        for k, move in enumerate(GROUP_MOVES):
            if k:
                to = place(move)
                self.copies.append(
                    push(
                        self.src.at[number(to)],
                        self.dst.at[me],
                        self.send.at[k],
                        self.recv.at[k],
                        to,
                    )
                )
        for copy in self.copies:
            copy.start()

    def finish(self):
        for copy in self.copies:
            copy.wait()


def enter(collective, attn_blocks, blocks):
    def kernel(a_ref, *refs):
        m_refs, a_mid, a_out, m_outs, sems = refs[:3], refs[3], refs[4], refs[5:8], refs[8:]
        meet([place(m) for m in GROUP_MOVES[1:] + Y_MOVES[1:]])
        first = Swap(a_ref, a_mid, sems[2:4])
        first.start()
        swaps = [Swap(m_refs[i], m_outs[i], sems[4 + 2 * i : 6 + 2 * i]) for i in range(3)]
        for swap in swaps:
            swap.start()
        first.finish()
        mine = a_out.at[lax.axis_index("y")]
        copies = [pltpu.make_async_copy(a_mid, mine, sems[0].at[0])]
        for k in range(1, 4):
            copies.append(push(a_mid, mine, sems[0].at[k], sems[1].at[k], place(Y_MOVES[k])))
        for copy in copies:
            copy.start()
        for swap in swaps:
            swap.finish()
        for copy in copies:
            copy.wait()

    like = jax.ShapeDtypeStruct(attn_blocks.shape, attn_blocks.dtype)
    return pl.pallas_call(
        kernel,
        out_shape=[like, jax.ShapeDtypeStruct((4,) + like.shape, like.dtype)]
        + [jax.ShapeDtypeStruct(b.shape, b.dtype) for b in blocks],
        in_specs=[ANY] * 4,
        out_specs=[ANY] * 5,
        scratch_shapes=[pltpu.SemaphoreType.DMA((4,))] * 2 + Swap.sems * 4,
        name="enter",
        **settings(collective, 120 << 20),
    )(attn_blocks, *blocks)[1:]


def spread_in(collective, hidden, masks):
    def kernel(hidden_ref, mask_ref, hidden_out, mask_out, *sems):
        meet([place(m) for m in GROUP_MOVES[1:]] + [sibling()])
        first = Spread(mask_ref, mask_out, sems[0:4])
        second = Spread(hidden_ref, hidden_out, sems[4:8])
        first.start()
        second.start()
        first.finish()
        second.finish()

    return pl.pallas_call(
        kernel,
        out_shape=[
            jax.ShapeDtypeStruct((8,) + hidden.shape, hidden.dtype),
            jax.ShapeDtypeStruct((8,) + masks.shape, masks.dtype),
        ],
        in_specs=[ANY] * 2,
        out_specs=[ANY] * 2,
        scratch_shapes=Spread.sems * 2,
        name="spread_in",
        **settings(collective, 90 << 20),
    )(hidden, masks)


def swap_back(collective, name, blocks):
    count = len(blocks)

    def kernel(*refs):
        sems = refs[2 * count :]
        meet([place(m) for m in GROUP_MOVES[1:]])
        swaps = [Swap(refs[i], refs[count + i], sems[2 * i : 2 * i + 2]) for i in range(count)]
        for swap in swaps:
            swap.start()
        for swap in swaps:
            swap.finish()

    return pl.pallas_call(
        kernel,
        out_shape=[jax.ShapeDtypeStruct(b.shape, b.dtype) for b in blocks],
        in_specs=[ANY] * count,
        out_specs=[ANY] * count,
        scratch_shapes=Swap.sems * count,
        name=name,
        **settings(collective, 80 << 20),
    )(*blocks)


class TeamSum:
    @staticmethod
    def scratch(own, width):
        return [
            pltpu.VMEM((8, 2, own, width), BF),
            pltpu.VMEM((16, own, width), BF),
            pltpu.SemaphoreType.DMA((8,)),
            pltpu.SemaphoreType.DMA((8,)),
            pltpu.SemaphoreType.DMA((16,)),
            pltpu.SemaphoreType.DMA((16,)),
        ]

    def __init__(self, part, scratch):
        self.part = part
        self.other, self.got, self.ssem, self.rsem, self.dsend, self.drecv = scratch
        self.zl, self.x, self.zh, self.c = (lax.axis_index(a) for a in TEAM)
        self.seq = self.zl * 4 + self.x
        self.chip = self.seq * 2 + self.zh

    def swap(self, seq):
        return push(
            self.part.at[seq, :, 1 - self.c],
            self.other.at[seq],
            self.ssem.at[seq],
            self.rsem.at[seq],
            sibling(),
        )

    def send(self, seq, zh):
        chip = seq * 2 + zh
        return push(
            self.part.at[seq, zh, self.c],
            self.got.at[self.chip],
            self.dsend.at[chip],
            self.drecv.at[self.chip],
            {"zl": seq // 4, "x": lax.rem(seq, 4), "zh": zh},
        )

    def both(self, seq, zh):
        return self.part[seq, zh, self.c].astype(F32) + self.other[seq, zh].astype(F32)

    def forward(self, seq):
        self.swap(seq).wait_recv()
        for zh in range(2):
            self.part[seq, zh, self.c] = self.both(seq, zh).astype(BF)
            self.send(seq, zh).start()

    def pair(self, step):
        back = 3 - step
        return lax.rem(self.zl + back // 2, 2) * 2 + lax.rem(self.x // 2 + back, 2)

    def last(self):
        beside = self.seq + 1 - 2 * lax.rem(self.x, 2)
        self.forward(beside)
        self.swap(self.seq).wait_recv()
        away = 1 - self.zh
        self.part[self.seq, away, self.c] = self.both(self.seq, away).astype(BF)
        self.send(self.seq, away).start()

    def total(self, total_ref):
        total_ref[...] = self.both(self.seq, self.zh)
        for move in TEAM_MOVES[1:]:
            chip = number(place(move, -1))
            pltpu.make_async_copy(self.got.at[chip], self.got.at[chip], self.drecv.at[chip]).wait()
            total_ref[...] += self.got[chip].astype(F32)

    def close(self):
        for seq in range(8):
            self.swap(seq).wait_send()
        for move in TEAM_MOVES[1:]:
            to = place(move)
            self.send(to["zl"] * 4 + to["x"], to["zh"]).wait_send()

    def run(self):
        for step in range(4):
            for j in range(2):
                self.swap(self.pair(step) * 2 + j).start()
        for step in range(3):
            for j in range(2):
                self.forward(self.pair(step) * 2 + j)
        self.last()


class TeamSpread:
    sems = [pltpu.SemaphoreType.DMA((16,))] * 4

    def __init__(self, rows, out, sems):
        self.rows, self.out = rows, out
        self.send, self.recv, self.fsend, self.frecv = sems

    def run(self):
        c = lax.axis_index("c")
        mine = self.out.at[number(place(TEAM_MOVES[0])), c]
        stay = pltpu.make_async_copy(self.rows, mine, self.send.at[0])
        stay.start()
        pushes = [
            push(self.rows, mine, self.send.at[k], self.recv.at[k], place(TEAM_MOVES[k]))
            for k in range(1, 16)
        ]
        for copy in pushes:
            copy.start()
        forwards = [push(self.rows, mine, self.fsend.at[0], self.frecv.at[0], sibling())]
        forwards[0].start()
        for k in range(1, 16):
            pushes[k - 1].wait_recv()
            tile = self.out.at[number(place(TEAM_MOVES[k], -1)), c]
            forwards.append(push(tile, tile, self.fsend.at[k], self.frecv.at[k], sibling()))
            forwards[-1].start()
        for copy in forwards:
            copy.wait()
        stay.wait()
        for copy in pushes:
            copy.wait_send()


def meet_team():
    meet([place(m) for m in TEAM_MOVES[1:]] + [sibling()])


def soft(scores, causal):
    scores = jnp.where(causal, scores, NEG)
    expon = jnp.exp(scores - jnp.max(scores, axis=-1, keepdims=True))
    return expon / jnp.sum(expon, axis=-1, keepdims=True)


def causal_mask(copies, seq):
    rows = lax.rem(lax.broadcasted_iota(jnp.int32, (copies * seq, seq), 0), seq)
    return lax.broadcasted_iota(jnp.int32, (copies * seq, seq), 1) <= rows


def attn_forward(
    collective, hidden, masks, weights, gain, routers, cosines, sines, mlp_gain, hidden_own, cotangent
):
    _, seq, width = hidden.shape
    own = hidden_own.shape[0]
    scale = HEAD ** (-0.5)

    def kernel(
        hid, mask, w_ref, gain_ref, router_ref, cos_ref, sin_ref, gain_m_ref, own_ref, cot_ref,
        normed_out, qkv_out, gated_out, gates_out, after_out, spread_out, cot_out,
        part, total, row, *rest,
    ):
        meet_team()
        team = TeamSum(part, rest[:6])
        cot = Spread(cot_ref, cot_out, rest[10:])
        cot.start()
        first = 2 * team.zl
        causal = causal_mask(2, seq)

        def step(i, _):
            pair = team.pair(i)
            for j in range(2):
                values = hid[pair * 2 + j].astype(F32)
                normed_out[pair * 2 + j] = (values * rms_scale(values) * gain_ref[...]).astype(BF)
            normed = normed_out[pl.ds(pair * 2, 2)].reshape(2 * seq, width)
            logits = mm(normed, router_ref[...])
            proj = mm(normed, w_ref[:, : 4 * HEAD])
            allowed = mask[pl.ds(pair * 2, 2)].reshape(2 * seq, LANE).astype(F32) > 0.5
            gates = dense_gates(logits, allowed & (lanes(2 * seq) < EXPERTS))
            gates_out[pl.ds(pair * 2, 2)] = gates.reshape(2, seq, LANE)
            gated = []
            for j in range(2):
                rows = slice(j * seq, (j + 1) * seq)
                query = [
                    rotate(proj[rows, e * HEAD : (e + 1) * HEAD], cos_ref[...], sin_ref[...]).astype(BF)
                    for e in range(2)
                ]
                key = rotate(proj[rows, 2 * HEAD : 3 * HEAD], cos_ref[...], sin_ref[...]).astype(BF)
                value = proj[rows, 3 * HEAD :].astype(BF)
                probs = soft(mm_nt(jnp.concatenate(query, axis=0), key) * scale, causal)
                attended = mm(probs.astype(BF), value)
                out = [
                    (attended[e * seq : (e + 1) * seq] * pick(gates[rows], first + e)).astype(BF)
                    for e in range(2)
                ]
                qkv_out[pair * 2 + j] = jnp.concatenate(query + [key, value], axis=1)
                gated.append(jnp.concatenate(out, axis=1))
                gated_out[pair * 2 + j] = gated[-1]
            branch = mm_nt(jnp.concatenate(gated, axis=0), w_ref[:, 4 * HEAD :])
            part[pl.ds(pair * 2, 2)] = branch.astype(BF).reshape(2, 2, 2, own, width)
            for j in range(2):
                team.swap(pair * 2 + j).start()

            @pl.when(i > 0)
            def _():
                for j in range(2):
                    team.forward(team.pair(i - 1) * 2 + j)

            return 0

        lax.fori_loop(0, 4, step, 0)
        team.last()
        cot.finish()
        team.total(total)
        after = total[...] + own_ref[...].astype(F32)
        after_out[...] = after
        row[...] = (after * rms_scale(after) * gain_m_ref[...]).astype(BF)
        TeamSpread(row, spread_out, rest[6:10]).run()
        team.close()

    return pl.pallas_call(
        kernel,
        out_shape=[
            jax.ShapeDtypeStruct((8, seq, width), BF),
            jax.ShapeDtypeStruct((8, seq, 4 * HEAD), BF),
            jax.ShapeDtypeStruct((8, seq, 2 * HEAD), BF),
            jax.ShapeDtypeStruct((8, seq, LANE), F32),
            jax.ShapeDtypeStruct((own, width), F32),
            jax.ShapeDtypeStruct((16, 2, own, width), BF),
            jax.ShapeDtypeStruct((8, seq, width), BF),
        ],
        in_specs=[VMEM] * 9 + [ANY],
        out_specs=[VMEM] * 5 + [ANY] * 2,
        scratch_shapes=[
            pltpu.VMEM((8, 2, 2, own, width), BF),
            pltpu.VMEM((own, width), F32),
            pltpu.VMEM((own, width), BF),
        ]
        + TeamSum.scratch(own, width)
        + TeamSpread.sems
        + Spread.sems,
        name="attn_forward",
        **settings(collective, 200 << 20, 48),
    )(hidden, masks, weights, gain, routers, cosines, sines, mlp_gain, hidden_own, cotangent)


def experts(normed, cotangent, masks, routers, weights, extra):
    rows, width = normed.shape
    part = weights[0].shape[1]
    tile = rows // 4

    def kernel(x_ref, cot_ref, mask, router_ref, wg, wu, wd, h_out, dg_out, du_out, branch_out, back_out, gates_out):
        lane = EXPERTS + lax.axis_index("x")
        skip = lax.axis_index("zl") * extra
        x = x_ref[...]
        logits = mm(x, router_ref[...])
        index = lanes(tile)
        allowed = (mask[...].astype(F32) > 0.5) & (index >= EXPERTS) & (index < 2 * EXPERTS)
        gates = dense_gates(logits, allowed)
        gates_out[...] = gates
        valid = (lax.broadcasted_iota(jnp.int32, (1, part), 1) >= skip).astype(F32)
        gate = pick(gates, lane) * valid
        gate_part = mm(x, wg[...])
        up_part = mm(x, wu[...])
        sigma = 1.0 / (1.0 + jnp.exp(-gate_part))
        silu = gate_part * sigma
        activated = silu * up_part
        h = (activated * gate).astype(BF)
        h_out[...] = h
        branch_out[...] = mm_nt(h, wd[...]).astype(BF)
        cot_down = mm(cot_ref[...], wd[...])
        dots = jnp.sum(activated * valid * cot_down, axis=1, keepdims=True)
        grad_act = cot_down * gate
        grad_gate = (grad_act * up_part * sigma * (1.0 + gate_part * (1.0 - sigma))).astype(BF)
        grad_up = (grad_act * silu).astype(BF)
        dg_out[...] = grad_gate
        du_out[...] = grad_up
        back_out[:, :width] = (mm_nt(grad_gate, wg[...]) + mm_nt(grad_up, wu[...])).astype(BF)
        back_out[:, width:] = jnp.where(index == lane, dots, 0.0).astype(BF)

    def tiled(cols):
        return pl.BlockSpec((tile, cols), lambda i: (i, 0))

    def whole(array):
        return pl.BlockSpec(array.shape, lambda i: (0, 0), pipeline_mode=pl.Buffered(1))

    cols = [part, part, part, width, width + LANE]
    return pl.pallas_call(
        kernel,
        grid=(4,),
        out_shape=[jax.ShapeDtypeStruct((rows, c), BF) for c in cols]
        + [jax.ShapeDtypeStruct((rows, LANE), F32)],
        in_specs=[tiled(width), tiled(width), tiled(LANE), whole(routers)]
        + [whole(w) for w in weights],
        out_specs=[tiled(c) for c in cols] + [tiled(LANE)],
        compiler_params=pltpu.CompilerParams(vmem_limit_bytes=48 << 20),
        cost_estimate=pl.CostEstimate(
            flops=12 * rows * width * part, bytes_accessed=40 << 20, transcendentals=rows * part
        ),
        name="experts",
    )(normed, cotangent, masks, routers, *weights)


def attn_backward(grad_mid, qkv, gates, weights, cosines, sines):
    rows, width = grad_mid.shape
    tile = rows // 4
    seq = tile // 2
    scale = HEAD ** (-0.5)

    def kernel(gm_ref, qkv_ref, gates_ref, w_ref, cos_ref, sin_ref, proj_out, back_out):
        first = 2 * lax.axis_index("zl")
        causal = causal_mask(2, seq)
        grads = mm(gm_ref[...], w_ref[:, 4 * HEAD :])
        gates = gates_ref[...]
        index = lanes(tile)
        dots = jnp.zeros((tile, LANE), F32)
        for j in range(2):
            here = slice(j * seq, (j + 1) * seq)
            query = jnp.concatenate(
                [qkv_ref[here, e * HEAD : (e + 1) * HEAD] for e in range(2)], axis=0
            )
            key = qkv_ref[here, 2 * HEAD : 3 * HEAD]
            value = qkv_ref[here, 3 * HEAD :]
            probs = soft(mm_nt(query, key) * scale, causal)
            probs_b = probs.astype(BF)
            attended = mm(probs_b, value)
            grad = jnp.concatenate(
                [grads[here, e * HEAD : (e + 1) * HEAD] for e in range(2)], axis=0
            )
            gate = jnp.concatenate([pick(gates[here], first + e) for e in range(2)], axis=0)
            each = jnp.sum(attended * grad, axis=1, keepdims=True)
            spread = jnp.where(lanes(seq) == first, each[:seq], 0.0)
            spread += jnp.where(lanes(seq) == first + 1, each[seq:], 0.0)
            grad = (grad * gate).astype(BF)
            grad_probs = mm_nt(grad, value)
            inner = jnp.sum(probs * grad_probs, axis=1, keepdims=True)
            grad_scores = (probs * (grad_probs - inner) * scale).astype(BF)
            grad_query = mm(grad_scores, key)
            grad_key = mm_tn(grad_scores, query)
            grad_value = mm_tn(probs_b, grad)
            proj_out[here, :HEAD] = rotate(grad_query[:seq], cos_ref[...], -sin_ref[...]).astype(BF)
            proj_out[here, HEAD : 2 * HEAD] = rotate(
                grad_query[seq:], cos_ref[...], -sin_ref[...]
            ).astype(BF)
            proj_out[here, 2 * HEAD : 3 * HEAD] = rotate(
                grad_key, cos_ref[...], -sin_ref[...]
            ).astype(BF)
            proj_out[here, 3 * HEAD :] = grad_value.astype(BF)
            back_out[here, width:] = spread.astype(BF)
        back_out[:, :width] = mm_nt(proj_out[...], w_ref[:, : 4 * HEAD]).astype(BF)

    def tiled(cols):
        return pl.BlockSpec((tile, cols), lambda i: (i, 0))

    def whole(array):
        return pl.BlockSpec(array.shape, lambda i: (0, 0), pipeline_mode=pl.Buffered(1))

    return pl.pallas_call(
        kernel,
        grid=(4,),
        out_shape=[
            jax.ShapeDtypeStruct((rows, 4 * HEAD), BF),
            jax.ShapeDtypeStruct((rows, width + LANE), BF),
        ],
        in_specs=[tiled(width), tiled(4 * HEAD), tiled(LANE)]
        + [whole(a) for a in (weights, cosines, sines)],
        out_specs=[tiled(4 * HEAD), tiled(width + LANE)],
        compiler_params=pltpu.CompilerParams(vmem_limit_bytes=48 << 20),
        cost_estimate=pl.CostEstimate(
            flops=2 * rows * width * 6 * HEAD, bytes_accessed=20 << 20, transcendentals=0
        ),
        name="attn_backward",
    )(grad_mid, qkv, gates, weights, cosines, sines)


def back_through_norm(total, inputs, gain, gates, normed, routers):
    width = inputs.shape[1]
    logits_back = gates_back(gates, total[:, width:])
    full = total[:, :width] + mm_nt(logits_back.astype(BF), routers)
    inner, gain_grad = norm_back(inputs, gain, full)
    return inner, gain_grad, mm_tn(logits_back.astype(BF), normed)[:8]


def middle(collective, back, after, gain, gates_own, routers, cot_own):
    own, width = after.shape

    def kernel(part_ref, after_ref, gain_ref, gates_ref, router_ref, cot_ref, mid_out, small_out, spread_out, part, load, total, row, *rest):
        fetch = pltpu.make_async_copy(part_ref, part, load.at[0])
        fetch.start()
        meet_team()
        fetch.wait()
        team = TeamSum(part, rest[:6])
        team.run()
        after = after_ref[...]
        normed = (after * rms_scale(after) * gain_ref[...]).astype(BF)
        team.total(total)
        inner, gain_grad, router_grad = back_through_norm(
            total[...], after, gain_ref[...], gates_ref[...], normed, router_ref[...]
        )
        grad_mid = cot_ref[...].astype(F32) + inner
        mid_out[...] = grad_mid
        row[...] = grad_mid.astype(BF)
        small_out[:8] = jnp.zeros((8, width), F32)
        small_out[0:1] = gain_grad
        small_out[8:] = router_grad
        TeamSpread(row, spread_out, rest[6:]).run()
        team.close()

    return pl.pallas_call(
        kernel,
        out_shape=[
            jax.ShapeDtypeStruct((own, width), F32),
            jax.ShapeDtypeStruct((16, width), F32),
            jax.ShapeDtypeStruct((16, 2, own, width), BF),
        ],
        in_specs=[ANY] + [VMEM] * 5,
        out_specs=[VMEM] * 2 + [ANY],
        scratch_shapes=[
            pltpu.VMEM((8, 2, 2, own, width + LANE), BF),
            pltpu.SemaphoreType.DMA((1,)),
            pltpu.VMEM((own, width + LANE), F32),
            pltpu.VMEM((own, width), BF),
        ]
        + TeamSum.scratch(own, width + LANE)
        + TeamSpread.sems,
        name="middle",
        **settings(collective, 160 << 20, 48),
    )(back.reshape(8, 2, 2, own, width + LANE), after, gain, gates_own, routers, cot_own)


def leave(collective, back, branch, after, grad_mid, inputs, gain, gates_own, routers, small, grads):
    own, width = after.shape
    stages = [moves("c"), moves("x"), moves("y"), moves("zl", "zh")]
    near = moves("zh", "c")

    def kernel(
        back_ref, branch_ref, after_ref, mid_ref, in_ref, gain_ref, gates_ref, router_ref, small_ref,
        g0, g1, g2, out_all, grad_all, small_out, s0, s1, s2,
        part_a, part_b, load, total_a, total_b, row_a, row_b, got, send, recv, ssend, srecv, *rest,
    ):
        fetches = [
            pltpu.make_async_copy(back_ref, part_a, load.at[0]),
            pltpu.make_async_copy(branch_ref, part_b, load.at[1]),
        ]
        for fetch in fetches:
            fetch.start()
        meet([place(m) for m in TEAM_MOVES[1:] + Y_MOVES[1:]] + [place(m) for m in near[1:] if m["c"]])
        team_a, team_b = TeamSum(part_a, rest[:6]), TeamSum(part_b, rest[6:12])
        fetches[0].wait()
        team_a.run()
        fetches[1].wait()
        team_b.run()
        grad_swaps = [
            Swap(g, s, rest[12 + 2 * i : 14 + 2 * i])
            for i, (g, s) in enumerate(((g0, s0), (g1, s1), (g2, s2)))
        ]
        for swap in grad_swaps:
            swap.start()
        inputs = in_ref[...].astype(F32)
        normed = (inputs * rms_scale(inputs) * gain_ref[...]).astype(BF)
        team_a.total(total_a)
        inner, gain_grad, router_grad = back_through_norm(
            total_a[...], inputs, gain_ref[...], gates_ref[...], normed, router_ref[...]
        )
        row_a[...] = (mid_ref[...] + inner).astype(BF)
        small_out[...] = small_ref[...]
        small_out[1:2] = gain_grad
        small_out[8:] += router_grad
        me = number(place(near[0]))
        copies = []

        def spread(i, src, dst):
            new = [pltpu.make_async_copy(src, dst.at[me], send.at[i, 0])]
            for k in range(1, 4):
                new.append(push(src, dst.at[me], send.at[i, k], recv.at[i, k], place(near[k])))
            for copy in new:
                copy.start()
            copies.extend(new)

        spread(0, row_a, grad_all)
        for s, stage in enumerate(stages):
            swaps = [
                push(small_out, got.at[s, k - 1], ssend.at[s, k], srecv.at[s, k], place(stage[k]))
                for k in range(1, len(stage))
            ]
            for swap in swaps:
                swap.start()
            if s == 0:
                team_b.total(total_b)
                row_b[...] = (after_ref[...] + total_b[...]).astype(BF)
                spread(1, row_b, out_all)
            for swap in swaps:
                swap.wait()
            total = small_out[...]
            for k in range(1, len(stage)):
                total += got[s, k - 1]
            small_out[...] = total
        for copy in copies:
            copy.wait()
        for swap in grad_swaps:
            swap.finish()
        team_a.close()
        team_b.close()

    return pl.pallas_call(
        kernel,
        out_shape=[jax.ShapeDtypeStruct((4, own, width), BF)] * 2
        + [jax.ShapeDtypeStruct((16, width), F32)]
        + [jax.ShapeDtypeStruct(g.shape, g.dtype) for g in grads],
        in_specs=[ANY, ANY] + [VMEM] * 7 + [ANY] * 3,
        out_specs=[ANY, ANY, VMEM] + [ANY] * 3,
        scratch_shapes=[
            pltpu.VMEM((8, 2, 2, own, width + LANE), BF),
            pltpu.VMEM((8, 2, 2, own, width), BF),
            pltpu.SemaphoreType.DMA((2,)),
            pltpu.VMEM((own, width + LANE), F32),
            pltpu.VMEM((own, width), F32),
            pltpu.VMEM((own, width), BF),
            pltpu.VMEM((own, width), BF),
            pltpu.VMEM((4, 3, 16, width), F32),
        ]
        + [pltpu.SemaphoreType.DMA((2, 4))] * 2
        + [pltpu.SemaphoreType.DMA((4, 4))] * 2
        + TeamSum.scratch(own, width + LANE)
        + TeamSum.scratch(own, width)
        + Swap.sems * 3,
        name="leave",
        **settings(collective, 200 << 20, 48),
    )(
        back.reshape(8, 2, 2, own, width + LANE),
        branch.reshape(8, 2, 2, own, width),
        after, grad_mid, inputs, gain, gates_own, routers, small, *grads,
    )


def reorder(array, axis):
    shape = array.shape
    split = shape[:axis] + (2, 4, shape[axis] // 8) + shape[axis + 1 :]
    return jnp.swapaxes(array.reshape(split), axis, axis + 1).reshape(shape)


def restore(array, axis):
    shape = array.shape
    split = shape[:axis] + (4, 2, shape[axis] // 8) + shape[axis + 1 :]
    return jnp.swapaxes(array.reshape(split), axis, axis + 1).reshape(shape)


def gather_y(block):
    return lax.all_gather(block.reshape(-1, block.shape[2]), "y", axis=0, tiled=True)


def sum_y(grad):
    summed = lax.psum_scatter(grad.astype(BF), "y", scatter_dimension=0, tiled=True)
    return summed.reshape(8, -1, grad.shape[1])


def local(
    hidden,
    cotangent,
    attn_gain,
    attn_router,
    qkv_weight,
    out_weight,
    mlp_gain,
    mlp_router,
    gate_up_weight,
    down_weight,
    attn_route,
    attn_slot,
    mlp_route,
    mlp_slot,
):
    seq, width = hidden.shape
    rows = qkv_weight.shape[0]
    features = down_weight.shape[2]
    part = (features // LANE + 1) // 2 * LANE
    low = features - part
    zl, x = lax.axis_index("zl"), lax.axis_index("x")
    quarter = lax.axis_index("zh") * 2 + lax.axis_index("c")
    own = seq // 4
    group = 8 * seq
    cosines, sines = rope_tables(seq)

    query_blocks = qkv_weight[:, :EXPERTS].reshape(rows, 2, 2, 4, HEAD).transpose(1, 3, 0, 2, 4)
    kv_blocks = qkv_weight[:, EXPERTS:].reshape(rows, 2, 4, HEAD).transpose(2, 0, 1, 3)
    kv_blocks = jnp.broadcast_to(kv_blocks[None], (2,) + kv_blocks.shape)
    out_blocks = out_weight.reshape(rows, 2, 2, 4, HEAD).transpose(1, 3, 0, 2, 4)
    attn_blocks = jnp.concatenate([query_blocks, kv_blocks, out_blocks], axis=3)
    attn_blocks = attn_blocks.reshape(8, rows, 6 * HEAD)

    def by_target(weight):
        weight = weight.transpose(1, 0, 2)
        return jnp.stack([weight[..., :part], weight[..., low:]], axis=0).reshape(8, rows, part)

    mlp_blocks = [
        by_target(w) for w in (gate_up_weight[:, :, 0], gate_up_weight[:, :, 1], down_weight)
    ]

    masks = jnp.concatenate([chosen_mask(attn_route), chosen_mask(mlp_route)], axis=1)
    masks = jnp.pad(masks.astype(BF), ((0, 0), (0, LANE - 2 * EXPERTS)))
    attn_gain, mlp_gain = reorder(attn_gain, 0)[None], reorder(mlp_gain, 0)[None]
    routers = reorder(jnp.concatenate([attn_router, mlp_router], axis=1), 0)
    routers = jnp.pad(routers, ((0, 0), (0, LANE - 2 * EXPERTS)))
    hidden = reorder(hidden, 1)
    cotangent = reorder(cotangent, 1)
    hidden_own = lax.dynamic_slice_in_dim(hidden, quarter * own, own, axis=0)
    cot_own = lax.dynamic_slice_in_dim(cotangent, quarter * own, own, axis=0)
    start = (zl * 4 + x) * seq + quarter * own

    def mine(array):
        return lax.dynamic_slice_in_dim(array, start, own, axis=0)

    attn_w, *mlp_rows = enter(1, attn_blocks, mlp_blocks)
    attn_w = attn_w.reshape(width, 6 * HEAD)
    mlp_w = [gather_y(block) for block in mlp_rows]
    hidden, _ = lax.optimization_barrier((hidden, attn_w))
    group_in, masks = spread_in(2, hidden, masks)

    normed_a, qkv, gated_att, gates_a, after, normed_m, group_cot = attn_forward(
        3, group_in, masks, attn_w, attn_gain, routers, cosines, sines, mlp_gain, hidden_own, cotangent
    )
    group_cot = group_cot.reshape(group, width)
    normed_a = normed_a.reshape(group, width)
    normed_m = normed_m.reshape(group, width)
    gates_a = gates_a.reshape(group, LANE)

    h, grad_gate, grad_up, branch_m, back_m, gates_m = experts(
        normed_m, group_cot, masks.reshape(group, LANE), routers, mlp_w, 2 * part - features
    )
    mlp_grads = [
        mm_tn(normed_m, grad_gate).astype(BF),
        mm_tn(normed_m, grad_up).astype(BF),
        mm_tn(group_cot, h).astype(BF),
    ]
    back_m = lax.optimization_barrier((back_m, *mlp_grads))[0]
    mlp_grads = [sum_y(grad) for grad in mlp_grads]
    grad_mid_own, small_m, grad_mid = middle(
        4, back_m, after, mlp_gain, mine(gates_m), routers, cot_own
    )
    grad_mid = lax.optimization_barrier((grad_mid, mlp_grads[0], mlp_grads[1]))[0]
    grad_mid = grad_mid.reshape(group, width)
    grad_proj, back_a = attn_backward(
        grad_mid, qkv.reshape(group, 4 * HEAD), gates_a, attn_w, cosines, sines
    )
    attn_grads = jnp.concatenate(
        [
            mm_tn(normed_a, grad_proj).astype(BF),
            mm_tn(grad_mid, gated_att.reshape(group, 2 * HEAD)).astype(BF),
        ],
        axis=1,
    )
    attn_grads = sum_y(lax.optimization_barrier((attn_grads, mlp_grads[2]))[0])
    out_hidden, grad_in, small, *mlp_grads = leave(
        5, back_a, branch_m, after, grad_mid_own, hidden_own, attn_gain, mine(gates_a), routers, small_m,
        mlp_grads,
    )
    out_hidden = restore(out_hidden.reshape(seq, width), 1)
    grad_in = restore(grad_in.reshape(seq, width), 1).astype(F32)
    small = restore(small, 1)

    attn_grads = lax.optimization_barrier((attn_grads, small))[0]
    (attn_grads,) = swap_back(6, "swap_back", [attn_grads])
    attn_grads = attn_grads.astype(F32).reshape(2, 4, rows, 6, HEAD).transpose(2, 0, 3, 1, 4)
    attn_grads = attn_grads.reshape(rows, 2, 6, 4 * HEAD)
    query_grad = attn_grads[:, :, :2].reshape(rows, EXPERTS, 4 * HEAD)
    kv_grad = attn_grads[:, 0, 2:4] + attn_grads[:, 1, 2:4]
    qkv_grad = jnp.concatenate([query_grad, kv_grad], axis=1)
    out_grad = attn_grads[:, :, 4:].reshape(rows, EXPERTS, 4 * HEAD)

    def placed_back(grad):
        grad = grad.reshape(2, EXPERTS, rows, part)
        return jnp.concatenate([grad[0], grad[1, ..., 2 * part - features :]], axis=-1).transpose(1, 0, 2)

    gate_grad, up_grad, down_grad = [placed_back(g) for g in mlp_grads]
    return (
        out_hidden,
        grad_in,
        small[1],
        small[8 : 8 + EXPERTS].T,
        qkv_grad,
        out_grad,
        small[0],
        small[8 + EXPERTS :].T,
        jnp.stack([gate_grad, up_grad], axis=2).astype(F32),
        down_grad.astype(F32),
    )


def solution(mesh):
    fine = Mesh(mesh.devices.reshape(2, 4, 4, 2, 2), ALL)
    dp, tensor = ("zl", "y", "x"), ("zh", "c")
    placed = (
        P(dp, None),
        P(dp, None),
        P(),
        P(),
        P(dp, None, tensor),
        P(dp, None, tensor),
        P(),
        P(),
        P(dp, None, None, tensor),
        P(dp, None, tensor),
        P(dp, None),
        P(dp, None),
        P(dp, None),
        P(dp, None),
    )
    return jax.shard_map(
        local,
        mesh=fine,
        in_specs=placed,
        out_specs=(
            P(dp, None),
            P(dp, None),
            P(),
            P(),
            P(dp, None, tensor),
            P(dp, None, tensor),
            P(),
            P(),
            P(dp, None, None, tensor),
            P(dp, None, tensor),
        ),
        check_vma=False,
    )
```

```python
import itertools

import jax
import jax.numpy as jnp
import numpy as np
from jax import lax
from jax.experimental import pallas as pl
from jax.experimental.pallas import tpu as pltpu
from jax.sharding import Mesh, PartitionSpec as P

HEAD = 128
LANE = 128
EPS = 1e-05
THETA = 10000.0
NEG = -1e30
EXPERTS = 4
GROUP = ("zl", "x")
TEAM = ("zl", "x", "zh", "c")
ALL = ("zl", "y", "x", "zh", "c")
SIZES = dict(zl=2, y=4, x=4, zh=2, c=2)
BF = jnp.bfloat16
F32 = jnp.float32
MESH = pl.DeviceIdType.MESH
ANY = pl.BlockSpec(memory_space=pl.ANY)
VMEM = pl.BlockSpec(memory_space=pltpu.VMEM)


def dot(a, b, dims):
    return lax.dot_general(a, b, (dims, ((), ())), preferred_element_type=F32)


def mm(a, b):
    return dot(a, b, ((1,), (0,)))


def mm_nt(a, b):
    return dot(a, b, ((1,), (1,)))


def mm_tn(a, b):
    return dot(a, b, ((0,), (0,)))


def rms_scale(values):
    return lax.rsqrt(jnp.mean(values * values, axis=-1, keepdims=True) + EPS)


def chosen_mask(route):
    columns = jnp.arange(EXPERTS)[None, :]
    return (route[:, :1] == columns) | (route[:, 1:] == columns)


def lanes(rows):
    return lax.broadcasted_iota(jnp.int32, (rows, LANE), 1)


def dense_gates(logits, mask):
    top = jnp.max(jnp.where(mask, logits, NEG), axis=1, keepdims=True)
    expon = jnp.where(mask, jnp.exp(jnp.where(mask, logits - top, 0.0)), 0.0)
    return expon / jnp.sum(expon, axis=1, keepdims=True)


def pick(values, lane):
    return jnp.sum(jnp.where(lanes(values.shape[0]) == lane, values, 0.0), axis=1, keepdims=True)


def gates_back(gates, dots):
    return gates * (dots - jnp.sum(gates * dots, axis=1, keepdims=True))


def rope_tables(count):
    frequency = THETA ** (-(np.arange(HEAD // 2).astype(np.float32) * 2.0 / HEAD))
    angles = np.arange(count).astype(np.float32)[:, None] * frequency[None, :].astype(np.float32)
    cosines, sines = np.cos(angles), np.sin(angles)
    return (
        jnp.asarray(np.concatenate([cosines, cosines], axis=1), F32),
        jnp.asarray(np.concatenate([-sines, sines], axis=1), F32),
    )


def rotate(values, cosines, sines):
    return values * cosines + pltpu.roll(values, HEAD // 2, 1) * sines


def norm_back(inputs, gain, grad_normed):
    scale = rms_scale(inputs)
    scaled = inputs * scale
    grad_scaled = grad_normed * gain
    grad_inputs = scale * (
        grad_scaled - scaled * jnp.mean(grad_scaled * scaled, axis=-1, keepdims=True)
    )
    return grad_inputs, jnp.sum(grad_normed * scaled, axis=0, keepdims=True)


def moves(*axes):
    return [dict(zip(axes, steps)) for steps in itertools.product(*[range(SIZES[a]) for a in axes])]


def place(move, sign=1):
    return {a: lax.rem(lax.axis_index(a) + sign * v + SIZES[a], SIZES[a]) for a, v in move.items()}


def number(coords):
    total = 0
    for axis, value in coords.items():
        total = total * SIZES[axis] + value
    return total


def meet(partners):
    barrier = pltpu.get_barrier_semaphore()
    for partner in partners:
        pl.semaphore_signal(barrier, inc=1, device_id=partner, device_id_type=MESH)
    pl.semaphore_wait(barrier, len(partners))


def push(src, dst, send, recv, to):
    return pltpu.make_async_remote_copy(
        src_ref=src, dst_ref=dst, send_sem=send, recv_sem=recv, device_id=to, device_id_type=MESH
    )


def settings(number, moved, vmem=32):
    return dict(
        compiler_params=pltpu.CompilerParams(
            collective_id=number, has_side_effects=True, vmem_limit_bytes=vmem << 20
        ),
        cost_estimate=pl.CostEstimate(flops=0, bytes_accessed=moved, transcendentals=0),
    )


GROUP_MOVES = moves("zl", "x")
TEAM_MOVES = moves("zl", "x", "zh")
X_MOVES = moves("x")
Y_MOVES = moves("y")
Z_MOVES = moves("zl", "zh")


def sibling():
    return {"c": 1 - lax.axis_index("c")}


class RingY:
    sems = [pltpu.SemaphoreType.DMA((5,)), pltpu.SemaphoreType.DMA((5,))]

    def __init__(self, src, out, sems):
        self.src, self.out = src, out
        self.send, self.recv = sems
        self.y = lax.axis_index("y")
        self.half = src.shape[0] // 2

    def line(self, step):
        return lax.rem(self.y + step, 4)

    def copy(self, k):
        y = self.y
        if k < 2:
            src, dst, to = self.src, self.out.at[y], self.line((1, 3)[k])
        else:
            half = pl.ds((k - 2) * self.half, self.half)
            src = dst = self.out.at[self.line((3, 1)[k - 2]), half]
            to = self.line((1, 3)[k - 2])
        return push(src, dst, self.send.at[k], self.recv.at[k], {"y": to})

    def start(self):
        self.stay = pltpu.make_async_copy(self.src, self.out.at[self.y], self.send.at[4])
        for k in range(2):
            self.copy(k).start()
        self.stay.start()

    def forward(self):
        for k in range(2):
            self.copy(k).wait_recv()
            self.copy(k + 2).start()

    def finish(self):
        for k in range(2):
            self.copy(k + 2).wait_recv()
        for k in range(4):
            self.copy(k).wait_send()
        self.stay.wait()


class Swap:
    sems = [pltpu.SemaphoreType.DMA((8,))] * 2

    def __init__(self, src, dst, sems):
        self.src, self.dst = src, dst
        self.send, self.recv = sems

    def start(self):
        me = number(place(GROUP_MOVES[0]))
        self.copies = [
            pltpu.make_async_copy(self.src.at[me], self.dst.at[me], self.send.at[0])
        ]
        for k, move in enumerate(GROUP_MOVES):
            if k:
                to = place(move)
                self.copies.append(
                    push(
                        self.src.at[number(to)],
                        self.dst.at[me],
                        self.send.at[k],
                        self.recv.at[k],
                        to,
                    )
                )
        for copy in self.copies:
            copy.start()

    def finish(self):
        for copy in self.copies:
            copy.wait()


def enter(collective, attn_blocks, blocks):
    def kernel(a_ref, *refs):
        m_refs, a_mid, a_out, m_outs, sems = refs[:3], refs[3], refs[4], refs[5:8], refs[8:]
        meet([place(m) for m in GROUP_MOVES[1:] + [Y_MOVES[1], Y_MOVES[3]]])
        first = Swap(a_ref, a_mid, sems[2:4])
        first.start()
        swaps = [Swap(m_refs[i], m_outs[i], sems[4 + 2 * i : 6 + 2 * i]) for i in range(3)]
        for swap in swaps:
            swap.start()
        first.finish()
        ring = RingY(a_mid, a_out, sems[0:2])
        ring.start()
        ring.forward()
        for swap in swaps:
            swap.finish()
        ring.finish()

    like = jax.ShapeDtypeStruct(attn_blocks.shape, attn_blocks.dtype)
    return pl.pallas_call(
        kernel,
        out_shape=[like, jax.ShapeDtypeStruct((4,) + like.shape, like.dtype)]
        + [jax.ShapeDtypeStruct(b.shape, b.dtype) for b in blocks],
        in_specs=[ANY] * 4,
        out_specs=[ANY] * 5,
        scratch_shapes=RingY.sems + Swap.sems * 4,
        name="enter",
        **settings(collective, 120 << 20),
    )(attn_blocks, *blocks)[1:]


def spread_in(collective, rows):
    own, width = rows.shape

    def kernel(row_ref, out_ref, *sems):
        meet_team()
        spread = TeamSpread(row_ref, out_ref, sems)
        spread.start()
        spread.middle()
        spread.finish()

    return pl.pallas_call(
        kernel,
        out_shape=jax.ShapeDtypeStruct((2, 4, 2, 2, own, width), rows.dtype),
        in_specs=[ANY],
        out_specs=ANY,
        scratch_shapes=TeamSpread.sems,
        name="spread_in",
        **settings(collective, 90 << 20),
    )(rows)


def swap_back(collective, name, blocks):
    count = len(blocks)

    def kernel(*refs):
        sems = refs[2 * count :]
        meet([place(m) for m in GROUP_MOVES[1:]])
        swaps = [Swap(refs[i], refs[count + i], sems[2 * i : 2 * i + 2]) for i in range(count)]
        for swap in swaps:
            swap.start()
        for swap in swaps:
            swap.finish()

    return pl.pallas_call(
        kernel,
        out_shape=[jax.ShapeDtypeStruct(b.shape, b.dtype) for b in blocks],
        in_specs=[ANY] * count,
        out_specs=[ANY] * count,
        scratch_shapes=Swap.sems * count,
        name=name,
        **settings(collective, 80 << 20),
    )(*blocks)


class TeamSum:
    @staticmethod
    def scratch(own, width):
        half = own // 2
        return [
            pltpu.VMEM((8, 2, own, width), BF),
            pltpu.VMEM((3, 2, 2, half, width), BF),
            pltpu.VMEM((3, 4, half, width), BF),
            pltpu.VMEM((6, half, width), BF),
            pltpu.SemaphoreType.DMA((8,)),
            pltpu.SemaphoreType.DMA((8,)),
            pltpu.SemaphoreType.DMA((6,)),
            pltpu.SemaphoreType.DMA((6,)),
            pltpu.SemaphoreType.DMA((6,)),
            pltpu.SemaphoreType.DMA((6,)),
        ]

    count = 10

    def __init__(self, part, scratch):
        self.part = part
        self.other, self.got_x, self.got_z, self.late = scratch[:4]
        self.ssem, self.rsem, self.send1, self.recv1, self.send2, self.recv2 = scratch[4:]
        self.zl, self.x, self.zh, self.c = (lax.axis_index(a) for a in TEAM)
        self.half = part.shape[4] // 2
        self.top, self.low = pl.ds(0, self.half), pl.ds(self.half, self.half)

    def swap(self, seq):
        return push(
            self.part.at[seq // 4, lax.rem(seq, 4), :, 1 - self.c],
            self.other.at[seq],
            self.ssem.at[seq],
            self.rsem.at[seq],
            sibling(),
        )

    def send_x(self, x):
        slot = lax.rem(x - self.x + 4, 4) - 1
        return push(
            self.part.at[:, x, :, self.c, self.top],
            self.got_x.at[slot],
            self.send1.at[slot],
            self.recv1.at[slot],
            {"x": x},
        )

    def send_z(self, zl, zh):
        slot = lax.rem(zl - self.zl + 2, 2) * 2 + lax.rem(zh - self.zh + 2, 2) - 1
        return push(
            self.part.at[zl, :, zh, self.c, self.low],
            self.got_z.at[slot],
            self.send1.at[3 + slot],
            self.recv1.at[3 + slot],
            {"zl": zl, "zh": zh},
        )

    def late_z(self, k):
        to = place(Z_MOVES[k])
        return push(
            self.part.at[to["zl"], self.x, to["zh"], self.c, self.top],
            self.late.at[k - 1],
            self.send2.at[k - 1],
            self.recv2.at[k - 1],
            to,
        )

    def late_x(self, k):
        to = place(X_MOVES[k])
        return push(
            self.part.at[self.zl, to["x"], self.zh, self.c, self.low],
            self.late.at[2 + k],
            self.send2.at[2 + k],
            self.recv2.at[2 + k],
            to,
        )

    def add(self, seq):
        self.swap(seq).wait_recv()
        zl, x = seq // 4, lax.rem(seq, 4)
        for zh in range(2):
            mine = self.part[zl, x, zh, self.c].astype(F32)
            self.part[zl, x, zh, self.c] = (mine + self.other[seq, zh].astype(F32)).astype(BF)

    def pair(self, step):
        back = 3 - step
        return lax.rem(self.zl + back // 2, 2) * 2 + lax.rem(self.x // 2 + back, 2)

    def add_pair(self, step):
        for j in range(2):
            self.add(self.pair(step) * 2 + j)

    def send_far_z(self):
        for zh in range(2):
            self.send_z(1 - self.zl, zh).start()

    def send_far_x(self):
        for j in range(2):
            self.send_x((1 - self.x // 2) * 2 + j).start()

    def last(self):
        self.add_pair(3)
        self.send_x(self.x + 1 - 2 * lax.rem(self.x, 2)).start()
        self.send_z(self.zl, 1 - self.zh).start()

    def got(self, ref, sem):
        pltpu.make_async_copy(ref, ref, sem).wait()

    def total(self, total_ref):
        half, c = self.half, self.c
        for k in range(3):
            self.got(self.got_x.at[k], self.recv1.at[k])
        for k, move in reversed(list(enumerate(Z_MOVES))):
            at = place(move)
            rows = self.part[at["zl"], self.x, at["zh"], c, :half].astype(F32)
            for j in range(3):
                rows += self.got_x[j, at["zl"], at["zh"]].astype(F32)
            if k:
                self.part[at["zl"], self.x, at["zh"], c, :half] = rows.astype(BF)
                self.late_z(k).start()
            else:
                total_ref[:half] = rows
        for k in range(3):
            self.got(self.got_z.at[k], self.recv1.at[3 + k])
        for k, move in reversed(list(enumerate(X_MOVES))):
            at = place(move)
            rows = self.part[self.zl, at["x"], self.zh, c, half:].astype(F32)
            for j in range(3):
                rows += self.got_z[j, at["x"]].astype(F32)
            if k:
                self.part[self.zl, at["x"], self.zh, c, half:] = rows.astype(BF)
                self.late_x(k).start()
            else:
                total_ref[half:] = rows
        for k in range(3):
            self.got(self.late.at[k], self.recv2.at[k])
            total_ref[:half] += self.late[k].astype(F32)
        for k in range(3):
            self.got(self.late.at[3 + k], self.recv2.at[3 + k])
            total_ref[half:] += self.late[3 + k].astype(F32)

    def close(self):
        for seq in range(8):
            self.swap(seq).wait_send()
        for k in range(1, 4):
            x, z = place(X_MOVES[k])["x"], place(Z_MOVES[k])
            self.send_x(x).wait_send()
            self.send_z(z["zl"], z["zh"]).wait_send()
            self.late_z(k).wait_send()
            self.late_x(k).wait_send()

    def run(self):
        for step in range(4):
            for j in range(2):
                self.swap(self.pair(step) * 2 + j).start()
        self.add_pair(0)
        self.add_pair(1)
        self.send_far_z()
        self.add_pair(2)
        self.send_far_x()
        self.last()


class TeamSpread:
    sems = [pltpu.SemaphoreType.DMA((12,))] * 2 + [pltpu.SemaphoreType.DMA((9,))] * 2

    def __init__(self, rows, out, sems):
        self.rows, self.out = rows, out
        self.send, self.recv, self.fsend, self.frecv = sems
        self.zl, self.x, self.zh, self.c = (lax.axis_index(a) for a in TEAM)
        self.half = rows.shape[0] // 2
        self.top, self.low = pl.ds(0, self.half), pl.ds(self.half, self.half)

    def tops(self, zl, zh):
        return self.out.at[zl, :, zh, self.c, self.top]

    def lows(self, x):
        return self.out.at[:, x, :, self.c, self.low]

    def hop(self, k, src, dst, to):
        return push(src, dst, self.send.at[k], self.recv.at[k], to)

    def first(self, k):
        here = (self.zl, self.x, self.zh, self.c)
        if k < 3:
            return self.hop(k, self.rows.at[self.top], self.out.at[(*here, self.top)], place(X_MOVES[k + 1]))
        return self.hop(k, self.rows.at[self.low], self.out.at[(*here, self.low)], place(Z_MOVES[k - 2]))

    def second(self, k):
        if k < 3:
            block = self.tops(self.zl, self.zh)
            return self.hop(6 + k, block, block, place(Z_MOVES[k + 1]))
        block = self.lows(self.x)
        return self.hop(6 + k, block, block, place(X_MOVES[k - 2]))

    def forward(self, k, block):
        return push(block, block, self.fsend.at[k], self.frecv.at[k], sibling())

    def start(self):
        self.stay = pltpu.make_async_copy(
            self.rows, self.out.at[self.zl, self.x, self.zh, self.c], self.fsend.at[8]
        )
        for k in range(6):
            self.first(k).start()
        self.stay.start()

    def middle(self):
        self.stay.wait()
        for k in range(3):
            self.first(k).wait_recv()
        for k in range(3):
            self.second(k).start()
        self.forward(0, self.tops(self.zl, self.zh)).start()
        for k in range(3, 6):
            self.first(k).wait_recv()
        for k in range(3, 6):
            self.second(k).start()
        self.forward(1, self.lows(self.x)).start()

    def block(self, k):
        if k < 3:
            at = place(Z_MOVES[k + 1], -1)
            return self.tops(at["zl"], at["zh"])
        return self.lows(place(X_MOVES[k - 2], -1)["x"])

    def finish(self):
        for k in range(6):
            self.second(k).wait_recv()
            self.forward(2 + k, self.block(k)).start()
        blocks = [self.tops(self.zl, self.zh), self.lows(self.x)] + [self.block(k) for k in range(6)]
        for k in range(8):
            self.forward(k, blocks[k]).wait()
        for k in range(6):
            self.first(k).wait_send()
            self.second(k).wait_send()


def meet_team():
    meet([place(m) for m in TEAM_MOVES[1:]] + [sibling()])


def soft(scores, causal):
    scores = jnp.where(causal, scores, NEG)
    expon = jnp.exp(scores - jnp.max(scores, axis=-1, keepdims=True))
    return expon / jnp.sum(expon, axis=-1, keepdims=True)


def causal_mask(copies, seq):
    rows = lax.rem(lax.broadcasted_iota(jnp.int32, (copies * seq, seq), 0), seq)
    return lax.broadcasted_iota(jnp.int32, (copies * seq, seq), 1) <= rows


def attn_forward(
    collective, hidden, weights, gain, routers, cosines, sines, mlp_gain, hidden_own, cot_own
):
    own, width = hidden_own.shape
    seq = hidden.shape[1]
    scale = HEAD ** (-0.5)

    def kernel(
        hid, w_ref, gain_ref, router_ref, cos_ref, sin_ref, gain_m_ref, own_ref, cot_ref,
        normed_out, qkv_out, gated_out, gates_out, after_out, spread_out, cot_out,
        part, total, row, *rest,
    ):
        meet_team()
        team = TeamSum(part, rest[: TeamSum.count])
        cot = TeamSpread(cot_ref, cot_out, rest[TeamSum.count : TeamSum.count + 4])
        cot.start()
        first = 2 * team.zl
        causal = causal_mask(2, seq)

        def step(i, _):
            pair = team.pair(i)
            for j in range(2):
                values = hid[pair * 2 + j, :, :width].astype(F32)
                normed_out[pair * 2 + j] = (values * rms_scale(values) * gain_ref[...]).astype(BF)
            normed = normed_out[pl.ds(pair * 2, 2)].reshape(2 * seq, width)
            logits = mm(normed, router_ref[...])
            proj = mm(normed, w_ref[:, : 4 * HEAD])
            allowed = hid[pl.ds(pair * 2, 2), :, width:].reshape(2 * seq, LANE).astype(F32) > 0.5
            gates = dense_gates(logits, allowed & (lanes(2 * seq) < EXPERTS))
            gates_out[pl.ds(pair * 2, 2)] = gates.reshape(2, seq, LANE)
            gated = []
            for j in range(2):
                rows = slice(j * seq, (j + 1) * seq)
                query = [
                    rotate(proj[rows, e * HEAD : (e + 1) * HEAD], cos_ref[...], sin_ref[...]).astype(BF)
                    for e in range(2)
                ]
                key = rotate(proj[rows, 2 * HEAD : 3 * HEAD], cos_ref[...], sin_ref[...]).astype(BF)
                value = proj[rows, 3 * HEAD :].astype(BF)
                probs = soft(mm_nt(jnp.concatenate(query, axis=0), key) * scale, causal)
                attended = mm(probs.astype(BF), value)
                out = [
                    (attended[e * seq : (e + 1) * seq] * pick(gates[rows], first + e)).astype(BF)
                    for e in range(2)
                ]
                qkv_out[pair * 2 + j] = jnp.concatenate(query + [key, value], axis=1)
                gated.append(jnp.concatenate(out, axis=1))
                gated_out[pair * 2 + j] = gated[-1]
            branch = mm_nt(jnp.concatenate(gated, axis=0), w_ref[:, 4 * HEAD :])
            part[pair // 2, pl.ds(lax.rem(pair, 2) * 2, 2)] = branch.astype(BF).reshape(
                2, 2, 2, own, width
            )
            for j in range(2):
                team.swap(pair * 2 + j).start()

            @pl.when(i == 0)
            def _():
                cot.middle()

            @pl.when(i > 0)
            def _():
                team.add_pair(i - 1)

            @pl.when(i == 2)
            def _():
                team.send_far_z()

            @pl.when(i == 3)
            def _():
                team.send_far_x()

            return 0

        lax.fori_loop(0, 4, step, 0)
        team.last()
        cot.finish()
        team.total(total)
        after = total[...] + own_ref[...].astype(F32)
        after_out[...] = after
        row[...] = (after * rms_scale(after) * gain_m_ref[...]).astype(BF)
        spread = TeamSpread(row, spread_out, rest[TeamSum.count + 4 :])
        spread.start()
        spread.middle()
        spread.finish()
        team.close()

    return pl.pallas_call(
        kernel,
        out_shape=[
            jax.ShapeDtypeStruct((8, seq, width), BF),
            jax.ShapeDtypeStruct((8, seq, 4 * HEAD), BF),
            jax.ShapeDtypeStruct((8, seq, 2 * HEAD), BF),
            jax.ShapeDtypeStruct((8, seq, LANE), F32),
            jax.ShapeDtypeStruct((own, width), F32),
            jax.ShapeDtypeStruct((2, 4, 2, 2, own, width), BF),
            jax.ShapeDtypeStruct((2, 4, 2, 2, own, width), BF),
        ],
        in_specs=[VMEM] * 8 + [ANY],
        out_specs=[VMEM] * 5 + [ANY] * 2,
        scratch_shapes=[
            pltpu.VMEM((2, 4, 2, 2, own, width), BF),
            pltpu.VMEM((own, width), F32),
            pltpu.VMEM((own, width), BF),
        ]
        + TeamSum.scratch(own, width)
        + TeamSpread.sems * 2,
        name="attn_forward",
        **settings(collective, 200 << 20, 48),
    )(hidden, weights, gain, routers, cosines, sines, mlp_gain, hidden_own, cot_own)


def experts(normed, cotangent, masks, routers, weights, extra):
    rows, width = normed.shape
    part = weights[0].shape[1]
    tile = rows // 4

    def kernel(x_ref, cot_ref, mask, router_ref, wg, wu, wd, h_out, dg_out, du_out, branch_out, back_out, gates_out):
        lane = EXPERTS + lax.axis_index("x")
        skip = lax.axis_index("zl") * extra
        x = x_ref[...]
        logits = mm(x, router_ref[...])
        index = lanes(tile)
        allowed = (mask[...].astype(F32) > 0.5) & (index >= EXPERTS) & (index < 2 * EXPERTS)
        gates = dense_gates(logits, allowed)
        gates_out[...] = gates
        valid = (lax.broadcasted_iota(jnp.int32, (1, part), 1) >= skip).astype(F32)
        gate = pick(gates, lane) * valid
        gate_part = mm(x, wg[...])
        up_part = mm(x, wu[...])
        sigma = 1.0 / (1.0 + jnp.exp(-gate_part))
        silu = gate_part * sigma
        activated = silu * up_part
        h = (activated * gate).astype(BF)
        h_out[...] = h
        branch_out[...] = mm_nt(h, wd[...]).astype(BF)
        cot_down = mm(cot_ref[...], wd[...])
        dots = jnp.sum(activated * valid * cot_down, axis=1, keepdims=True)
        grad_act = cot_down * gate
        grad_gate = (grad_act * up_part * sigma * (1.0 + gate_part * (1.0 - sigma))).astype(BF)
        grad_up = (grad_act * silu).astype(BF)
        dg_out[...] = grad_gate
        du_out[...] = grad_up
        back_out[:, :width] = (mm_nt(grad_gate, wg[...]) + mm_nt(grad_up, wu[...])).astype(BF)
        back_out[:, width:] = jnp.where(index == lane, dots, 0.0).astype(BF)

    def tiled(cols):
        return pl.BlockSpec((tile, cols), lambda i: (i, 0))

    def whole(array):
        return pl.BlockSpec(array.shape, lambda i: (0, 0), pipeline_mode=pl.Buffered(1))

    cols = [part, part, part, width, width + LANE]
    return pl.pallas_call(
        kernel,
        grid=(4,),
        out_shape=[jax.ShapeDtypeStruct((rows, c), BF) for c in cols]
        + [jax.ShapeDtypeStruct((rows, LANE), F32)],
        in_specs=[tiled(width), tiled(width)]
        + [pl.BlockSpec((tile, LANE), lambda i: (i, width // LANE)), whole(routers)]
        + [whole(w) for w in weights],
        out_specs=[tiled(c) for c in cols] + [tiled(LANE)],
        compiler_params=pltpu.CompilerParams(vmem_limit_bytes=48 << 20),
        cost_estimate=pl.CostEstimate(
            flops=12 * rows * width * part, bytes_accessed=40 << 20, transcendentals=rows * part
        ),
        name="experts",
    )(normed, cotangent, masks, routers, *weights)


def attn_backward(grad_mid, qkv, gates, weights, cosines, sines):
    rows, width = grad_mid.shape
    tile = rows // 4
    seq = tile // 2
    scale = HEAD ** (-0.5)

    def kernel(gm_ref, qkv_ref, gates_ref, w_ref, cos_ref, sin_ref, proj_out, back_out):
        first = 2 * lax.axis_index("zl")
        causal = causal_mask(2, seq)
        grads = mm(gm_ref[...], w_ref[:, 4 * HEAD :])
        gates = gates_ref[...]
        index = lanes(tile)
        dots = jnp.zeros((tile, LANE), F32)
        for j in range(2):
            here = slice(j * seq, (j + 1) * seq)
            query = jnp.concatenate(
                [qkv_ref[here, e * HEAD : (e + 1) * HEAD] for e in range(2)], axis=0
            )
            key = qkv_ref[here, 2 * HEAD : 3 * HEAD]
            value = qkv_ref[here, 3 * HEAD :]
            probs = soft(mm_nt(query, key) * scale, causal)
            probs_b = probs.astype(BF)
            attended = mm(probs_b, value)
            grad = jnp.concatenate(
                [grads[here, e * HEAD : (e + 1) * HEAD] for e in range(2)], axis=0
            )
            gate = jnp.concatenate([pick(gates[here], first + e) for e in range(2)], axis=0)
            each = jnp.sum(attended * grad, axis=1, keepdims=True)
            spread = jnp.where(lanes(seq) == first, each[:seq], 0.0)
            spread += jnp.where(lanes(seq) == first + 1, each[seq:], 0.0)
            grad = (grad * gate).astype(BF)
            grad_probs = mm_nt(grad, value)
            inner = jnp.sum(probs * grad_probs, axis=1, keepdims=True)
            grad_scores = (probs * (grad_probs - inner) * scale).astype(BF)
            grad_query = mm(grad_scores, key)
            grad_key = mm_tn(grad_scores, query)
            grad_value = mm_tn(probs_b, grad)
            proj_out[here, :HEAD] = rotate(grad_query[:seq], cos_ref[...], -sin_ref[...]).astype(BF)
            proj_out[here, HEAD : 2 * HEAD] = rotate(
                grad_query[seq:], cos_ref[...], -sin_ref[...]
            ).astype(BF)
            proj_out[here, 2 * HEAD : 3 * HEAD] = rotate(
                grad_key, cos_ref[...], -sin_ref[...]
            ).astype(BF)
            proj_out[here, 3 * HEAD :] = grad_value.astype(BF)
            back_out[here, width:] = spread.astype(BF)
        back_out[:, :width] = mm_nt(proj_out[...], w_ref[:, : 4 * HEAD]).astype(BF)

    def tiled(cols):
        return pl.BlockSpec((tile, cols), lambda i: (i, 0))

    def whole(array):
        return pl.BlockSpec(array.shape, lambda i: (0, 0), pipeline_mode=pl.Buffered(1))

    return pl.pallas_call(
        kernel,
        grid=(4,),
        out_shape=[
            jax.ShapeDtypeStruct((rows, 4 * HEAD), BF),
            jax.ShapeDtypeStruct((rows, width + LANE), BF),
        ],
        in_specs=[tiled(width), tiled(4 * HEAD), tiled(LANE)]
        + [whole(a) for a in (weights, cosines, sines)],
        out_specs=[tiled(4 * HEAD), tiled(width + LANE)],
        compiler_params=pltpu.CompilerParams(vmem_limit_bytes=48 << 20),
        cost_estimate=pl.CostEstimate(
            flops=2 * rows * width * 6 * HEAD, bytes_accessed=20 << 20, transcendentals=0
        ),
        name="attn_backward",
    )(grad_mid, qkv, gates, weights, cosines, sines)


def back_through_norm(total, inputs, gain, gates, normed, routers):
    width = inputs.shape[1]
    logits_back = gates_back(gates, total[:, width:])
    full = total[:, :width] + mm_nt(logits_back.astype(BF), routers)
    inner, gain_grad = norm_back(inputs, gain, full)
    return inner, gain_grad, mm_tn(logits_back.astype(BF), normed)[:8]


def middle(collective, back, after, gain, gates_own, routers, cot_own):
    own, width = after.shape

    def kernel(part_ref, after_ref, gain_ref, gates_ref, router_ref, cot_ref, mid_out, small_out, spread_out, part, load, total, row, *rest):
        fetch = pltpu.make_async_copy(part_ref, part, load.at[0])
        fetch.start()
        meet_team()
        fetch.wait()
        team = TeamSum(part, rest[: TeamSum.count])
        team.run()
        after = after_ref[...]
        normed = (after * rms_scale(after) * gain_ref[...]).astype(BF)
        team.total(total)
        inner, gain_grad, router_grad = back_through_norm(
            total[...], after, gain_ref[...], gates_ref[...], normed, router_ref[...]
        )
        grad_mid = cot_ref[...].astype(F32) + inner
        mid_out[...] = grad_mid
        row[...] = grad_mid.astype(BF)
        small_out[:8] = jnp.zeros((8, width), F32)
        small_out[0:1] = gain_grad
        small_out[8:] = router_grad
        spread = TeamSpread(row, spread_out, rest[TeamSum.count :])
        spread.start()
        spread.middle()
        spread.finish()
        team.close()

    return pl.pallas_call(
        kernel,
        out_shape=[
            jax.ShapeDtypeStruct((own, width), F32),
            jax.ShapeDtypeStruct((16, width), F32),
            jax.ShapeDtypeStruct((2, 4, 2, 2, own, width), BF),
        ],
        in_specs=[ANY] + [VMEM] * 5,
        out_specs=[VMEM] * 2 + [ANY],
        scratch_shapes=[
            pltpu.VMEM((2, 4, 2, 2, own, width + LANE), BF),
            pltpu.SemaphoreType.DMA((1,)),
            pltpu.VMEM((own, width + LANE), F32),
            pltpu.VMEM((own, width), BF),
        ]
        + TeamSum.scratch(own, width + LANE)
        + TeamSpread.sems,
        name="middle",
        **settings(collective, 160 << 20, 48),
    )(back.reshape(2, 4, 2, 2, own, width + LANE), after, gain, gates_own, routers, cot_own)


def leave(collective, back, branch, after, grad_mid, inputs, gain, gates_own, routers, small, grads):
    own, width = after.shape
    stages = [X_MOVES, Y_MOVES, Z_MOVES]

    def kernel(
        back_ref, branch_ref, after_ref, mid_ref, in_ref, gain_ref, gates_ref, router_ref, small_ref,
        g0, g1, g2, out_all, grad_all, small_out, s0, s1, s2,
        part_a, part_b, load, total_a, total_b, row_a, row_b, got, other, rest_rows, csem, send, recv, ssend, srecv, *rest,
    ):
        fetches = [
            pltpu.make_async_copy(back_ref, part_a, load.at[0]),
            pltpu.make_async_copy(branch_ref, part_b, load.at[1]),
        ]
        for fetch in fetches:
            fetch.start()
        meet([place(m) for m in TEAM_MOVES[1:] + Y_MOVES[1:]] + [sibling()])
        count = TeamSum.count
        team_a, team_b = TeamSum(part_a, rest[:count]), TeamSum(part_b, rest[count : 2 * count])
        fetches[0].wait()
        team_a.run()
        fetches[1].wait()
        team_b.run()
        grad_swaps = [
            Swap(g, s, rest[2 * count + 2 * i : 2 * count + 2 * i + 2])
            for i, (g, s) in enumerate(((g0, s0), (g1, s1), (g2, s2)))
        ]
        for swap in grad_swaps:
            swap.start()
        inputs = in_ref[...].astype(F32)
        normed = (inputs * rms_scale(inputs) * gain_ref[...]).astype(BF)
        team_a.total(total_a)
        inner, gain_grad, router_grad = back_through_norm(
            total_a[...], inputs, gain_ref[...], gates_ref[...], normed, router_ref[...]
        )
        row_a[...] = (mid_ref[...] + inner).astype(BF)
        small_out[...] = small_ref[...]
        small_out[1:2] = gain_grad
        small_out[8:] += router_grad
        zh, c = lax.axis_index("zh"), lax.axis_index("c")

        def spread(i, src, dst):
            mine, far = dst.at[zh, c], dst.at[1 - zh, c]
            copies = [
                pltpu.make_async_copy(src, mine, send.at[i, 0]),
                push(src, mine, send.at[i, 1], recv.at[i, 1], {"zh": 1 - zh}),
                push(src, mine, send.at[i, 2], recv.at[i, 2], sibling()),
                push(far, far, send.at[i, 3], recv.at[i, 3], sibling()),
            ]
            for copy in copies[:3]:
                copy.start()
            return copies

        def settle(copies):
            copies[1].wait_recv()
            copies[3].start()
            copies[0].wait()
            copies[1].wait_send()
            copies[2].wait()
            copies[3].wait()

        first = spread(0, row_a, grad_all)
        half = pl.ds(pl.multiple_of(c * 8, 8), 8)
        rest_half = pl.ds(pl.multiple_of((1 - c) * 8, 8), 8)
        over = push(small_out.at[rest_half], other, csem.at[0], csem.at[1], sibling())
        over.start()
        team_b.total(total_b)
        row_b[...] = (after_ref[...] + total_b[...]).astype(BF)
        second = spread(1, row_b, out_all)
        over.wait()
        small_out[half] = small_out[half] + other[...]
        for s, stage in enumerate(stages):
            swaps = [
                push(small_out.at[half], got.at[s, k - 1], ssend.at[s, k], srecv.at[s, k], place(stage[k]))
                for k in range(1, 4)
            ]
            for swap in swaps:
                swap.start()
            for swap in swaps:
                swap.wait()
            small_out[half] = small_out[half] + got[s, 0] + got[s, 1] + got[s, 2]
        back_over = push(small_out.at[half], rest_rows, csem.at[2], csem.at[3], sibling())
        back_over.start()
        settle(first)
        settle(second)
        back_over.wait()
        small_out[rest_half] = rest_rows[...]
        for swap in grad_swaps:
            swap.finish()
        team_a.close()
        team_b.close()

    return pl.pallas_call(
        kernel,
        out_shape=[jax.ShapeDtypeStruct((2, 2, own, width), BF)] * 2
        + [jax.ShapeDtypeStruct((16, width), F32)]
        + [jax.ShapeDtypeStruct(g.shape, g.dtype) for g in grads],
        in_specs=[ANY, ANY] + [VMEM] * 7 + [ANY] * 3,
        out_specs=[ANY, ANY, VMEM] + [ANY] * 3,
        scratch_shapes=[
            pltpu.VMEM((2, 4, 2, 2, own, width + LANE), BF),
            pltpu.VMEM((2, 4, 2, 2, own, width), BF),
            pltpu.SemaphoreType.DMA((2,)),
            pltpu.VMEM((own, width + LANE), F32),
            pltpu.VMEM((own, width), F32),
            pltpu.VMEM((own, width), BF),
            pltpu.VMEM((own, width), BF),
            pltpu.VMEM((3, 3, 8, width), F32),
            pltpu.VMEM((8, width), F32),
            pltpu.VMEM((8, width), F32),
            pltpu.SemaphoreType.DMA((4,)),
        ]
        + [pltpu.SemaphoreType.DMA((2, 4))] * 2
        + [pltpu.SemaphoreType.DMA((4, 4))] * 2
        + TeamSum.scratch(own, width + LANE)
        + TeamSum.scratch(own, width)
        + Swap.sems * 3,
        name="leave",
        **settings(collective, 200 << 20, 48),
    )(
        back.reshape(2, 4, 2, 2, own, width + LANE),
        branch.reshape(2, 4, 2, 2, own, width),
        after, grad_mid, inputs, gain, gates_own, routers, small, *grads,
    )


def reorder(array, axis):
    shape = array.shape
    split = shape[:axis] + (2, 4, shape[axis] // 8) + shape[axis + 1 :]
    return jnp.swapaxes(array.reshape(split), axis, axis + 1).reshape(shape)


def restore(array, axis):
    shape = array.shape
    split = shape[:axis] + (4, 2, shape[axis] // 8) + shape[axis + 1 :]
    return jnp.swapaxes(array.reshape(split), axis, axis + 1).reshape(shape)


def gather_y(block):
    return lax.all_gather(block.reshape(-1, block.shape[2]), "y", axis=0, tiled=True)


def sum_y(grad):
    summed = lax.psum_scatter(grad.astype(BF), "y", scatter_dimension=0, tiled=True)
    return summed.reshape(8, -1, grad.shape[1])


def local(
    hidden,
    cotangent,
    attn_gain,
    attn_router,
    qkv_weight,
    out_weight,
    mlp_gain,
    mlp_router,
    gate_up_weight,
    down_weight,
    attn_route,
    attn_slot,
    mlp_route,
    mlp_slot,
):
    seq, width = hidden.shape
    rows = qkv_weight.shape[0]
    features = down_weight.shape[2]
    part = (features // LANE + 1) // 2 * LANE
    low = features - part
    zl, x = lax.axis_index("zl"), lax.axis_index("x")
    quarter = lax.axis_index("zh") * 2 + lax.axis_index("c")
    own = seq // 4
    group = 8 * seq
    cosines, sines = rope_tables(seq)

    query_blocks = qkv_weight[:, :EXPERTS].reshape(rows, 2, 2, 4, HEAD).transpose(1, 3, 0, 2, 4)
    kv_blocks = qkv_weight[:, EXPERTS:].reshape(rows, 2, 4, HEAD).transpose(2, 0, 1, 3)
    kv_blocks = jnp.broadcast_to(kv_blocks[None], (2,) + kv_blocks.shape)
    out_blocks = out_weight.reshape(rows, 2, 2, 4, HEAD).transpose(1, 3, 0, 2, 4)
    attn_blocks = jnp.concatenate([query_blocks, kv_blocks, out_blocks], axis=3)
    attn_blocks = attn_blocks.reshape(8, rows, 6 * HEAD)

    def by_target(weight):
        weight = weight.transpose(1, 0, 2)
        return jnp.stack([weight[..., :part], weight[..., low:]], axis=0).reshape(8, rows, part)

    mlp_blocks = [
        by_target(w) for w in (gate_up_weight[:, :, 0], gate_up_weight[:, :, 1], down_weight)
    ]

    masks = jnp.concatenate([chosen_mask(attn_route), chosen_mask(mlp_route)], axis=1)
    masks = jnp.pad(masks.astype(BF), ((0, 0), (0, LANE - 2 * EXPERTS)))
    attn_gain, mlp_gain = reorder(attn_gain, 0)[None], reorder(mlp_gain, 0)[None]
    routers = reorder(jnp.concatenate([attn_router, mlp_router], axis=1), 0)
    routers = jnp.pad(routers, ((0, 0), (0, LANE - 2 * EXPERTS)))

    def quarter_of(array):
        return lax.dynamic_slice_in_dim(array, quarter * own, own, axis=0)

    hidden_own = reorder(quarter_of(hidden), 1)
    cot_own = reorder(quarter_of(cotangent), 1)
    start = (zl * 4 + x) * seq + quarter * own

    def mine(array):
        return lax.dynamic_slice_in_dim(array, start, own, axis=0)

    attn_w, *mlp_rows = enter(1, attn_blocks, mlp_blocks)
    attn_w = attn_w.reshape(width, 6 * HEAD)
    mlp_w = [gather_y(block) for block in mlp_rows]
    entering = jnp.concatenate([hidden_own, quarter_of(masks)], axis=1)
    entering = lax.optimization_barrier((entering, attn_w))[0]
    group_in = spread_in(2, entering).reshape(8, seq, width + LANE)

    normed_a, qkv, gated_att, gates_a, after, normed_m, group_cot = attn_forward(
        3, group_in, attn_w, attn_gain, routers, cosines, sines, mlp_gain, hidden_own, cot_own
    )
    group_cot = group_cot.reshape(group, width)
    normed_a = normed_a.reshape(group, width)
    normed_m = normed_m.reshape(group, width)
    gates_a = gates_a.reshape(group, LANE)

    h, grad_gate, grad_up, branch_m, back_m, gates_m = experts(
        normed_m, group_cot, group_in.reshape(group, width + LANE), routers, mlp_w, 2 * part - features
    )
    mlp_grads = [
        mm_tn(normed_m, grad_gate).astype(BF),
        mm_tn(normed_m, grad_up).astype(BF),
        mm_tn(group_cot, h).astype(BF),
    ]
    back_m = lax.optimization_barrier((back_m, *mlp_grads))[0]
    mlp_grads = [sum_y(grad) for grad in mlp_grads]
    grad_mid_own, small_m, grad_mid = middle(
        4, back_m, after, mlp_gain, mine(gates_m), routers, cot_own
    )
    grad_mid = lax.optimization_barrier((grad_mid, mlp_grads[0], mlp_grads[1]))[0]
    grad_mid = grad_mid.reshape(group, width)
    grad_proj, back_a = attn_backward(
        grad_mid, qkv.reshape(group, 4 * HEAD), gates_a, attn_w, cosines, sines
    )
    attn_grads = jnp.concatenate(
        [
            mm_tn(normed_a, grad_proj).astype(BF),
            mm_tn(grad_mid, gated_att.reshape(group, 2 * HEAD)).astype(BF),
        ],
        axis=1,
    )
    attn_grads = sum_y(lax.optimization_barrier((attn_grads, mlp_grads[2]))[0])
    out_hidden, grad_in, small, *mlp_grads = leave(
        5, back_a, branch_m, after, grad_mid_own, hidden_own, attn_gain, mine(gates_a), routers, small_m,
        mlp_grads,
    )
    out_hidden = restore(out_hidden.reshape(seq, width), 1)
    grad_in = restore(grad_in.reshape(seq, width), 1).astype(F32)
    small = restore(small, 1)

    attn_grads = lax.optimization_barrier((attn_grads, small))[0]
    (attn_grads,) = swap_back(6, "swap_back", [attn_grads])
    attn_grads = attn_grads.astype(F32).reshape(2, 4, rows, 6, HEAD).transpose(2, 0, 3, 1, 4)
    attn_grads = attn_grads.reshape(rows, 2, 6, 4 * HEAD)
    query_grad = attn_grads[:, :, :2].reshape(rows, EXPERTS, 4 * HEAD)
    kv_grad = attn_grads[:, 0, 2:4] + attn_grads[:, 1, 2:4]
    qkv_grad = jnp.concatenate([query_grad, kv_grad], axis=1)
    out_grad = attn_grads[:, :, 4:].reshape(rows, EXPERTS, 4 * HEAD)

    def placed_back(grad):
        grad = grad.reshape(2, EXPERTS, rows, part)
        return jnp.concatenate([grad[0], grad[1, ..., 2 * part - features :]], axis=-1).transpose(1, 0, 2)

    gate_grad, up_grad, down_grad = [placed_back(g) for g in mlp_grads]
    return (
        out_hidden,
        grad_in,
        small[1],
        small[8 : 8 + EXPERTS].T,
        qkv_grad,
        out_grad,
        small[0],
        small[8 + EXPERTS :].T,
        jnp.stack([gate_grad, up_grad], axis=2).astype(F32),
        down_grad.astype(F32),
    )


def solution(mesh):
    fine = Mesh(mesh.devices.reshape(2, 4, 4, 2, 2), ALL)
    dp, tensor = ("zl", "y", "x"), ("zh", "c")
    placed = (
        P(dp, None),
        P(dp, None),
        P(),
        P(),
        P(dp, None, tensor),
        P(dp, None, tensor),
        P(),
        P(),
        P(dp, None, None, tensor),
        P(dp, None, tensor),
        P(dp, None),
        P(dp, None),
        P(dp, None),
        P(dp, None),
    )
    return jax.shard_map(
        local,
        mesh=fine,
        in_specs=placed,
        out_specs=(
            P(dp, None),
            P(dp, None),
            P(),
            P(),
            P(dp, None, tensor),
            P(dp, None, tensor),
            P(),
            P(),
            P(dp, None, None, tensor),
            P(dp, None, tensor),
        ),
        check_vma=False,
    )
```

```python
import itertools

import jax
import jax.numpy as jnp
import numpy as np
from jax import lax
from jax.experimental import pallas as pl
from jax.experimental.pallas import tpu as pltpu
from jax.sharding import Mesh, PartitionSpec as P

HEAD = 128
LANE = 128
EPS = 1e-05
THETA = 10000.0
NEG = -1e30
EXPERTS = 4
GROUP = ("zl", "x")
TEAM = ("zl", "x", "zh", "c")
ALL = ("zl", "y", "x", "zh", "c")
SIZES = dict(zl=2, y=4, x=4, zh=2, c=2)
BF = jnp.bfloat16
F32 = jnp.float32
MESH = pl.DeviceIdType.MESH
ANY = pl.BlockSpec(memory_space=pl.ANY)
VMEM = pl.BlockSpec(memory_space=pltpu.VMEM)


def dot(a, b, dims):
    return lax.dot_general(a, b, (dims, ((), ())), preferred_element_type=F32)


def mm(a, b):
    return dot(a, b, ((1,), (0,)))


def mm_nt(a, b):
    return dot(a, b, ((1,), (1,)))


def mm_tn(a, b):
    return dot(a, b, ((0,), (0,)))


def rms_scale(values):
    return lax.rsqrt(jnp.mean(values * values, axis=-1, keepdims=True) + EPS)


def chosen_mask(route):
    columns = jnp.arange(EXPERTS)[None, :]
    return (route[:, :1] == columns) | (route[:, 1:] == columns)


def lanes(rows):
    return lax.broadcasted_iota(jnp.int32, (rows, LANE), 1)


def dense_gates(logits, mask):
    top = jnp.max(jnp.where(mask, logits, NEG), axis=1, keepdims=True)
    expon = jnp.where(mask, jnp.exp(jnp.where(mask, logits - top, 0.0)), 0.0)
    return expon / jnp.sum(expon, axis=1, keepdims=True)


def pick(values, lane):
    return jnp.sum(jnp.where(lanes(values.shape[0]) == lane, values, 0.0), axis=1, keepdims=True)


def gates_back(gates, dots):
    return gates * (dots - jnp.sum(gates * dots, axis=1, keepdims=True))


def rope_tables(count):
    frequency = THETA ** (-(np.arange(HEAD // 2).astype(np.float32) * 2.0 / HEAD))
    angles = np.arange(count).astype(np.float32)[:, None] * frequency[None, :].astype(np.float32)
    cosines, sines = np.cos(angles), np.sin(angles)
    return (
        jnp.asarray(np.concatenate([cosines, cosines], axis=1), F32),
        jnp.asarray(np.concatenate([-sines, sines], axis=1), F32),
    )


def rotate(values, cosines, sines):
    return values * cosines + pltpu.roll(values, HEAD // 2, 1) * sines


def norm_back(inputs, gain, grad_normed):
    scale = rms_scale(inputs)
    scaled = inputs * scale
    grad_scaled = grad_normed * gain
    grad_inputs = scale * (
        grad_scaled - scaled * jnp.mean(grad_scaled * scaled, axis=-1, keepdims=True)
    )
    return grad_inputs, jnp.sum(grad_normed * scaled, axis=0, keepdims=True)


def moves(*axes):
    return [dict(zip(axes, steps)) for steps in itertools.product(*[range(SIZES[a]) for a in axes])]


def place(move, sign=1):
    return {a: lax.rem(lax.axis_index(a) + sign * v + SIZES[a], SIZES[a]) for a, v in move.items()}


def number(coords):
    total = 0
    for axis, value in coords.items():
        total = total * SIZES[axis] + value
    return total


def meet(partners):
    barrier = pltpu.get_barrier_semaphore()
    for partner in partners:
        pl.semaphore_signal(barrier, inc=1, device_id=partner, device_id_type=MESH)
    pl.semaphore_wait(barrier, len(partners))


def push(src, dst, send, recv, to):
    return pltpu.make_async_remote_copy(
        src_ref=src, dst_ref=dst, send_sem=send, recv_sem=recv, device_id=to, device_id_type=MESH
    )


def settings(number, moved, vmem=32):
    return dict(
        compiler_params=pltpu.CompilerParams(
            collective_id=number, has_side_effects=True, vmem_limit_bytes=vmem << 20
        ),
        cost_estimate=pl.CostEstimate(flops=0, bytes_accessed=moved, transcendentals=0),
    )


GROUP_MOVES = moves("zl", "x")
TEAM_MOVES = moves("zl", "x", "zh")
X_MOVES = moves("x")
Y_MOVES = moves("y")
Z_MOVES = moves("zl", "zh")


def sibling():
    return {"c": 1 - lax.axis_index("c")}


class RingY:
    sems = [pltpu.SemaphoreType.DMA((5,)), pltpu.SemaphoreType.DMA((5,))]

    def __init__(self, src, out, sems):
        self.src, self.out = src, out
        self.send, self.recv = sems
        self.y = lax.axis_index("y")
        self.half = src.shape[0] // 2

    def line(self, step):
        return lax.rem(self.y + step, 4)

    def copy(self, k):
        y = self.y
        if k < 2:
            src, dst, to = self.src, self.out.at[y], self.line((1, 3)[k])
        else:
            half = pl.ds((k - 2) * self.half, self.half)
            src = dst = self.out.at[self.line((3, 1)[k - 2]), half]
            to = self.line((1, 3)[k - 2])
        return push(src, dst, self.send.at[k], self.recv.at[k], {"y": to})

    def start(self):
        self.stay = pltpu.make_async_copy(self.src, self.out.at[self.y], self.send.at[4])
        for k in range(2):
            self.copy(k).start()
        self.stay.start()

    def forward(self):
        for k in range(2):
            self.copy(k).wait_recv()
            self.copy(k + 2).start()

    def finish(self):
        for k in range(2):
            self.copy(k + 2).wait_recv()
        for k in range(4):
            self.copy(k).wait_send()
        self.stay.wait()


class Swap:
    sems = [pltpu.SemaphoreType.DMA((8,))] * 2

    def __init__(self, src, dst, sems):
        self.src, self.dst = src, dst
        self.send, self.recv = sems

    def start(self):
        me = number(place(GROUP_MOVES[0]))
        self.copies = [
            pltpu.make_async_copy(self.src.at[me], self.dst.at[me], self.send.at[0])
        ]
        for k, move in enumerate(GROUP_MOVES):
            if k:
                to = place(move)
                self.copies.append(
                    push(
                        self.src.at[number(to)],
                        self.dst.at[me],
                        self.send.at[k],
                        self.recv.at[k],
                        to,
                    )
                )
        for copy in self.copies:
            copy.start()

    def finish(self):
        for copy in self.copies:
            copy.wait()


def enter(collective, attn_blocks, blocks, rows):
    own, width = rows.shape

    def kernel(a_ref, *refs):
        m_refs, row_ref, a_mid, a_out, m_outs, row_out, sems = (
            refs[:3], refs[3], refs[4], refs[5], refs[6:9], refs[9], refs[10:],
        )
        meet([place(m) for m in TEAM_MOVES[1:] + [Y_MOVES[1], Y_MOVES[3]]] + [sibling()])
        first = Swap(a_ref, a_mid, sems[2:4])
        first.start()
        spread = TeamSpread(row_ref, row_out, sems[10:14])
        spread.start()
        first.finish()
        ring = RingY(a_mid, a_out, sems[0:2])
        ring.start()
        spread.middle()
        swaps = [Swap(m_refs[i], m_outs[i], sems[4 + 2 * i : 6 + 2 * i]) for i in range(3)]
        for swap in swaps:
            swap.start()
        spread.finish()
        ring.forward()
        for swap in swaps:
            swap.finish()
        ring.finish()

    like = jax.ShapeDtypeStruct(attn_blocks.shape, attn_blocks.dtype)
    return pl.pallas_call(
        kernel,
        out_shape=[like, jax.ShapeDtypeStruct((4,) + like.shape, like.dtype)]
        + [jax.ShapeDtypeStruct(b.shape, b.dtype) for b in blocks]
        + [jax.ShapeDtypeStruct((2, 4, 2, 2, own, width), rows.dtype)],
        in_specs=[ANY] * 5,
        out_specs=[ANY] * 6,
        scratch_shapes=RingY.sems + Swap.sems * 4 + TeamSpread.sems,
        name="enter",
        **settings(collective, 120 << 20),
    )(attn_blocks, *blocks, rows)[1:]


class RingSum:
    @staticmethod
    def scratch(rows, cols):
        return [
            pltpu.VMEM((2, rows // 2, cols), BF),
            pltpu.VMEM((2, rows // 2, cols), BF),
            pltpu.VMEM((2, rows, cols), BF),
            pltpu.SemaphoreType.DMA((6,)),
            pltpu.SemaphoreType.DMA((6,)),
        ]

    count = 5

    def __init__(self, part, scratch):
        self.part = part
        self.got, self.mix, self.sums, self.send, self.recv = scratch
        self.y = lax.axis_index("y")
        half = part.shape[1] // 2
        self.halves = [pl.ds(0, half), pl.ds(half, half)]

    def line(self, step):
        return lax.rem(self.y + step, 4)

    def copy(self, k):
        kind, way = k // 2, k % 2
        step = (1, 3)[way]
        top, low = self.halves[way], self.halves[1 - way]
        if kind == 0:
            src, dst = self.part.at[self.line(2), top], self.got.at[way]
        elif kind == 1:
            src, dst = self.part.at[self.line(step), low], self.sums.at[way, low]
        else:
            src, dst = self.mix.at[way], self.sums.at[way, top]
        return push(src, dst, self.send.at[k], self.recv.at[k], {"y": self.line(step)})

    def start(self):
        for k in range(4):
            self.copy(k).start()

    def middle(self):
        for way in range(2):
            self.copy(way).wait_recv()
            mine = self.part[self.line((1, 3)[way]), self.halves[way]].astype(F32)
            self.mix[way] = (mine + self.got[way].astype(F32)).astype(BF)
            self.copy(4 + way).start()

    def finish(self, out):
        for k in range(2, 6):
            self.copy(k).wait_recv()
        total = self.part[self.y].astype(F32) + self.sums[0].astype(F32) + self.sums[1].astype(F32)
        out[...] = total.astype(BF).reshape(out.shape)
        for k in range(6):
            self.copy(k).wait_send()


class TeamSum:
    @staticmethod
    def scratch(own, width):
        half = own // 2
        return [
            pltpu.VMEM((8, 2, own, width), BF),
            pltpu.VMEM((3, 2, 2, half, width), BF),
            pltpu.VMEM((3, 4, half, width), BF),
            pltpu.VMEM((6, half, width), BF),
            pltpu.SemaphoreType.DMA((8,)),
            pltpu.SemaphoreType.DMA((8,)),
            pltpu.SemaphoreType.DMA((6,)),
            pltpu.SemaphoreType.DMA((6,)),
            pltpu.SemaphoreType.DMA((6,)),
            pltpu.SemaphoreType.DMA((6,)),
        ]

    count = 10

    def __init__(self, part, scratch):
        self.part = part
        self.other, self.got_x, self.got_z, self.late = scratch[:4]
        self.ssem, self.rsem, self.send1, self.recv1, self.send2, self.recv2 = scratch[4:]
        self.zl, self.x, self.zh, self.c = (lax.axis_index(a) for a in TEAM)
        self.half = part.shape[4] // 2
        self.top, self.low = pl.ds(0, self.half), pl.ds(self.half, self.half)

    def swap(self, seq):
        return push(
            self.part.at[seq // 4, lax.rem(seq, 4), :, 1 - self.c],
            self.other.at[seq],
            self.ssem.at[seq],
            self.rsem.at[seq],
            sibling(),
        )

    def send_x(self, x):
        slot = lax.rem(x - self.x + 4, 4) - 1
        return push(
            self.part.at[:, x, :, self.c, self.top],
            self.got_x.at[slot],
            self.send1.at[slot],
            self.recv1.at[slot],
            {"x": x},
        )

    def send_z(self, zl, zh):
        slot = lax.rem(zl - self.zl + 2, 2) * 2 + lax.rem(zh - self.zh + 2, 2) - 1
        return push(
            self.part.at[zl, :, zh, self.c, self.low],
            self.got_z.at[slot],
            self.send1.at[3 + slot],
            self.recv1.at[3 + slot],
            {"zl": zl, "zh": zh},
        )

    def late_z(self, k):
        to = place(Z_MOVES[k])
        return push(
            self.part.at[to["zl"], self.x, to["zh"], self.c, self.top],
            self.late.at[k - 1],
            self.send2.at[k - 1],
            self.recv2.at[k - 1],
            to,
        )

    def late_x(self, k):
        to = place(X_MOVES[k])
        return push(
            self.part.at[self.zl, to["x"], self.zh, self.c, self.low],
            self.late.at[2 + k],
            self.send2.at[2 + k],
            self.recv2.at[2 + k],
            to,
        )

    def add(self, seq):
        self.swap(seq).wait_recv()
        zl, x = seq // 4, lax.rem(seq, 4)
        for zh in range(2):
            mine = self.part[zl, x, zh, self.c].astype(F32)
            self.part[zl, x, zh, self.c] = (mine + self.other[seq, zh].astype(F32)).astype(BF)

    def pair(self, step):
        back = 3 - step
        return lax.rem(self.zl + back // 2, 2) * 2 + lax.rem(self.x // 2 + back, 2)

    def add_pair(self, step):
        for j in range(2):
            self.add(self.pair(step) * 2 + j)

    def send_far_z(self):
        for zh in range(2):
            self.send_z(1 - self.zl, zh).start()

    def send_far_x(self):
        for j in range(2):
            self.send_x((1 - self.x // 2) * 2 + j).start()

    def last(self):
        self.add_pair(3)
        self.send_x(self.x + 1 - 2 * lax.rem(self.x, 2)).start()
        self.send_z(self.zl, 1 - self.zh).start()

    def got(self, ref, sem):
        pltpu.make_async_copy(ref, ref, sem).wait()

    def total(self, total_ref):
        half, c = self.half, self.c
        for k in range(3):
            self.got(self.got_x.at[k], self.recv1.at[k])
        for k, move in reversed(list(enumerate(Z_MOVES))):
            at = place(move)
            rows = self.part[at["zl"], self.x, at["zh"], c, :half].astype(F32)
            for j in range(3):
                rows += self.got_x[j, at["zl"], at["zh"]].astype(F32)
            if k:
                self.part[at["zl"], self.x, at["zh"], c, :half] = rows.astype(BF)
                self.late_z(k).start()
            else:
                total_ref[:half] = rows
        for k in range(3):
            self.got(self.got_z.at[k], self.recv1.at[3 + k])
        for k, move in reversed(list(enumerate(X_MOVES))):
            at = place(move)
            rows = self.part[self.zl, at["x"], self.zh, c, half:].astype(F32)
            for j in range(3):
                rows += self.got_z[j, at["x"]].astype(F32)
            if k:
                self.part[self.zl, at["x"], self.zh, c, half:] = rows.astype(BF)
                self.late_x(k).start()
            else:
                total_ref[half:] = rows
        for k in range(3):
            self.got(self.late.at[k], self.recv2.at[k])
            total_ref[:half] += self.late[k].astype(F32)
        for k in range(3):
            self.got(self.late.at[3 + k], self.recv2.at[3 + k])
            total_ref[half:] += self.late[3 + k].astype(F32)

    def close(self):
        for seq in range(8):
            self.swap(seq).wait_send()
        for k in range(1, 4):
            x, z = place(X_MOVES[k])["x"], place(Z_MOVES[k])
            self.send_x(x).wait_send()
            self.send_z(z["zl"], z["zh"]).wait_send()
            self.late_z(k).wait_send()
            self.late_x(k).wait_send()

    def run(self):
        for step in range(4):
            for j in range(2):
                self.swap(self.pair(step) * 2 + j).start()
        self.add_pair(0)
        self.add_pair(1)
        self.send_far_z()
        self.add_pair(2)
        self.send_far_x()
        self.last()


class TeamSpread:
    sems = [pltpu.SemaphoreType.DMA((12,))] * 2 + [pltpu.SemaphoreType.DMA((9,))] * 2

    def __init__(self, rows, out, sems):
        self.rows, self.out = rows, out
        self.send, self.recv, self.fsend, self.frecv = sems
        self.zl, self.x, self.zh, self.c = (lax.axis_index(a) for a in TEAM)
        self.half = rows.shape[0] // 2
        self.top, self.low = pl.ds(0, self.half), pl.ds(self.half, self.half)

    def tops(self, zl, zh):
        return self.out.at[zl, :, zh, self.c, self.top]

    def lows(self, x):
        return self.out.at[:, x, :, self.c, self.low]

    def hop(self, k, src, dst, to):
        return push(src, dst, self.send.at[k], self.recv.at[k], to)

    def first(self, k):
        here = (self.zl, self.x, self.zh, self.c)
        if k < 3:
            return self.hop(k, self.rows.at[self.top], self.out.at[(*here, self.top)], place(X_MOVES[k + 1]))
        return self.hop(k, self.rows.at[self.low], self.out.at[(*here, self.low)], place(Z_MOVES[k - 2]))

    def second(self, k):
        if k < 3:
            block = self.tops(self.zl, self.zh)
            return self.hop(6 + k, block, block, place(Z_MOVES[k + 1]))
        block = self.lows(self.x)
        return self.hop(6 + k, block, block, place(X_MOVES[k - 2]))

    def forward(self, k, block):
        return push(block, block, self.fsend.at[k], self.frecv.at[k], sibling())

    def start(self):
        self.stay = pltpu.make_async_copy(
            self.rows, self.out.at[self.zl, self.x, self.zh, self.c], self.fsend.at[8]
        )
        for k in range(6):
            self.first(k).start()
        self.stay.start()

    def middle(self):
        self.stay.wait()
        for k in range(3):
            self.first(k).wait_recv()
        for k in range(3):
            self.second(k).start()
        self.forward(0, self.tops(self.zl, self.zh)).start()
        for k in range(3, 6):
            self.first(k).wait_recv()
        for k in range(3, 6):
            self.second(k).start()
        self.forward(1, self.lows(self.x)).start()

    def block(self, k):
        if k < 3:
            at = place(Z_MOVES[k + 1], -1)
            return self.tops(at["zl"], at["zh"])
        return self.lows(place(X_MOVES[k - 2], -1)["x"])

    def finish(self):
        for k in range(6):
            self.second(k).wait_recv()
            self.forward(2 + k, self.block(k)).start()
        blocks = [self.tops(self.zl, self.zh), self.lows(self.x)] + [self.block(k) for k in range(6)]
        for k in range(8):
            self.forward(k, blocks[k]).wait()
        for k in range(6):
            self.first(k).wait_send()
            self.second(k).wait_send()


def meet_team():
    meet([place(m) for m in TEAM_MOVES[1:]] + [sibling()])


def soft(scores, causal):
    scores = jnp.where(causal, scores, NEG)
    expon = jnp.exp(scores - jnp.max(scores, axis=-1, keepdims=True))
    return expon / jnp.sum(expon, axis=-1, keepdims=True)


def causal_mask(copies, seq):
    rows = lax.rem(lax.broadcasted_iota(jnp.int32, (copies * seq, seq), 0), seq)
    return lax.broadcasted_iota(jnp.int32, (copies * seq, seq), 1) <= rows


def attn_forward(
    collective, hidden, weights, gain, routers, cosines, sines, mlp_gain, hidden_own, cot_own, blocks
):
    own, width = hidden_own.shape
    seq = hidden.shape[1]
    scale = HEAD ** (-0.5)

    def kernel(
        hid, w_ref, gain_ref, router_ref, cos_ref, sin_ref, gain_m_ref, own_ref, cot_ref, b0, b1, b2,
        normed_out, qkv_out, gated_out, gates_out, after_out, spread_out, cot_out, w0, w1, w2,
        part, total, row, *rest,
    ):
        meet([place(m) for m in TEAM_MOVES[1:] + [Y_MOVES[1], Y_MOVES[3]]] + [sibling()])
        count = TeamSum.count
        team = TeamSum(part, rest[:count])
        cot = TeamSpread(cot_ref, cot_out, rest[count : count + 4])
        cot.start()
        rings = [
            RingY(b, w, rest[count + 8 + 2 * k : count + 10 + 2 * k])
            for k, (b, w) in enumerate(((b0, w0), (b1, w1), (b2, w2)))
        ]
        for ring in rings:
            ring.start()
        first = 2 * team.zl
        causal = causal_mask(2, seq)

        def step(i, _):
            pair = team.pair(i)
            for j in range(2):
                values = hid[pair * 2 + j, :, :width].astype(F32)
                normed_out[pair * 2 + j] = (values * rms_scale(values) * gain_ref[...]).astype(BF)
            normed = normed_out[pl.ds(pair * 2, 2)].reshape(2 * seq, width)
            logits = mm(normed, router_ref[...])
            proj = mm(normed, w_ref[:, : 4 * HEAD])
            allowed = hid[pl.ds(pair * 2, 2), :, width:].reshape(2 * seq, LANE).astype(F32) > 0.5
            gates = dense_gates(logits, allowed & (lanes(2 * seq) < EXPERTS))
            gates_out[pl.ds(pair * 2, 2)] = gates.reshape(2, seq, LANE)
            gated = []
            for j in range(2):
                rows = slice(j * seq, (j + 1) * seq)
                query = [
                    rotate(proj[rows, e * HEAD : (e + 1) * HEAD], cos_ref[...], sin_ref[...]).astype(BF)
                    for e in range(2)
                ]
                key = rotate(proj[rows, 2 * HEAD : 3 * HEAD], cos_ref[...], sin_ref[...]).astype(BF)
                value = proj[rows, 3 * HEAD :].astype(BF)
                probs = soft(mm_nt(jnp.concatenate(query, axis=0), key) * scale, causal)
                attended = mm(probs.astype(BF), value)
                out = [
                    (attended[e * seq : (e + 1) * seq] * pick(gates[rows], first + e)).astype(BF)
                    for e in range(2)
                ]
                qkv_out[pair * 2 + j] = jnp.concatenate(query + [key, value], axis=1)
                gated.append(jnp.concatenate(out, axis=1))
                gated_out[pair * 2 + j] = gated[-1]
            branch = mm_nt(jnp.concatenate(gated, axis=0), w_ref[:, 4 * HEAD :])
            part[pair // 2, pl.ds(lax.rem(pair, 2) * 2, 2)] = branch.astype(BF).reshape(
                2, 2, 2, own, width
            )
            for j in range(2):
                team.swap(pair * 2 + j).start()

            @pl.when(i == 0)
            def _():
                cot.middle()

            @pl.when(i > 0)
            def _():
                team.add_pair(i - 1)

            @pl.when(i == 2)
            def _():
                team.send_far_z()

            @pl.when(i == 3)
            def _():
                team.send_far_x()

            return 0

        lax.fori_loop(0, 4, step, 0)
        team.last()
        cot.finish()
        team.total(total)
        after = total[...] + own_ref[...].astype(F32)
        after_out[...] = after
        row[...] = (after * rms_scale(after) * gain_m_ref[...]).astype(BF)
        spread = TeamSpread(row, spread_out, rest[count + 4 : count + 8])
        spread.start()
        rings[0].forward()
        spread.middle()
        rings[1].forward()
        spread.finish()
        rings[2].forward()
        team.close()
        for ring in rings:
            ring.finish()

    return pl.pallas_call(
        kernel,
        out_shape=[
            jax.ShapeDtypeStruct((8, seq, width), BF),
            jax.ShapeDtypeStruct((8, seq, 4 * HEAD), BF),
            jax.ShapeDtypeStruct((8, seq, 2 * HEAD), BF),
            jax.ShapeDtypeStruct((8, seq, LANE), F32),
            jax.ShapeDtypeStruct((own, width), F32),
            jax.ShapeDtypeStruct((2, 4, 2, 2, own, width), BF),
            jax.ShapeDtypeStruct((2, 4, 2, 2, own, width), BF),
        ]
        + [jax.ShapeDtypeStruct((4,) + b.shape, b.dtype) for b in blocks],
        in_specs=[VMEM] * 8 + [ANY] * 4,
        out_specs=[VMEM] * 5 + [ANY] * 5,
        scratch_shapes=[
            pltpu.VMEM((2, 4, 2, 2, own, width), BF),
            pltpu.VMEM((own, width), F32),
            pltpu.VMEM((own, width), BF),
        ]
        + TeamSum.scratch(own, width)
        + TeamSpread.sems * 2
        + RingY.sems * 3,
        name="attn_forward",
        **settings(collective, 200 << 20, 48),
    )(hidden, weights, gain, routers, cosines, sines, mlp_gain, hidden_own, cot_own, *blocks)


def experts(normed, cotangent, masks, routers, weights, extra):
    rows, width = normed.shape
    part = weights[0].shape[1]
    tile = rows // 4

    def kernel(x_ref, cot_ref, mask, router_ref, wg, wu, wd, h_out, dg_out, du_out, branch_out, back_out, gates_out):
        lane = EXPERTS + lax.axis_index("x")
        skip = lax.axis_index("zl") * extra
        x = x_ref[...]
        logits = mm(x, router_ref[...])
        index = lanes(tile)
        allowed = (mask[...].astype(F32) > 0.5) & (index >= EXPERTS) & (index < 2 * EXPERTS)
        gates = dense_gates(logits, allowed)
        gates_out[...] = gates
        valid = (lax.broadcasted_iota(jnp.int32, (1, part), 1) >= skip).astype(F32)
        gate = pick(gates, lane) * valid
        gate_part = mm(x, wg[...])
        up_part = mm(x, wu[...])
        sigma = 1.0 / (1.0 + jnp.exp(-gate_part))
        silu = gate_part * sigma
        activated = silu * up_part
        h = (activated * gate).astype(BF)
        h_out[...] = h
        branch_out[...] = mm_nt(h, wd[...]).astype(BF)
        cot_down = mm(cot_ref[...], wd[...])
        dots = jnp.sum(activated * valid * cot_down, axis=1, keepdims=True)
        grad_act = cot_down * gate
        grad_gate = (grad_act * up_part * sigma * (1.0 + gate_part * (1.0 - sigma))).astype(BF)
        grad_up = (grad_act * silu).astype(BF)
        dg_out[...] = grad_gate
        du_out[...] = grad_up
        back_out[:, :width] = (mm_nt(grad_gate, wg[...]) + mm_nt(grad_up, wu[...])).astype(BF)
        back_out[:, width:] = jnp.where(index == lane, dots, 0.0).astype(BF)

    def tiled(cols):
        return pl.BlockSpec((tile, cols), lambda i: (i, 0))

    def whole(array):
        return pl.BlockSpec(array.shape, lambda i: (0, 0), pipeline_mode=pl.Buffered(1))

    cols = [part, part, part, width, width + LANE]
    return pl.pallas_call(
        kernel,
        grid=(4,),
        out_shape=[jax.ShapeDtypeStruct((rows, c), BF) for c in cols]
        + [jax.ShapeDtypeStruct((rows, LANE), F32)],
        in_specs=[tiled(width), tiled(width)]
        + [pl.BlockSpec((tile, LANE), lambda i: (i, width // LANE)), whole(routers)]
        + [whole(w) for w in weights],
        out_specs=[tiled(c) for c in cols] + [tiled(LANE)],
        compiler_params=pltpu.CompilerParams(vmem_limit_bytes=48 << 20),
        cost_estimate=pl.CostEstimate(
            flops=12 * rows * width * part, bytes_accessed=40 << 20, transcendentals=rows * part
        ),
        name="experts",
    )(normed, cotangent, masks, routers, *weights)


def attn_backward(grad_mid, qkv, gates, weights, cosines, sines):
    rows, width = grad_mid.shape
    tile = rows // 4
    seq = tile // 2
    scale = HEAD ** (-0.5)

    def kernel(gm_ref, qkv_ref, gates_ref, w_ref, cos_ref, sin_ref, proj_out, back_out):
        first = 2 * lax.axis_index("zl")
        causal = causal_mask(2, seq)
        grads = mm(gm_ref[...], w_ref[:, 4 * HEAD :])
        gates = gates_ref[...]
        index = lanes(tile)
        dots = jnp.zeros((tile, LANE), F32)
        for j in range(2):
            here = slice(j * seq, (j + 1) * seq)
            query = jnp.concatenate(
                [qkv_ref[here, e * HEAD : (e + 1) * HEAD] for e in range(2)], axis=0
            )
            key = qkv_ref[here, 2 * HEAD : 3 * HEAD]
            value = qkv_ref[here, 3 * HEAD :]
            probs = soft(mm_nt(query, key) * scale, causal)
            probs_b = probs.astype(BF)
            attended = mm(probs_b, value)
            grad = jnp.concatenate(
                [grads[here, e * HEAD : (e + 1) * HEAD] for e in range(2)], axis=0
            )
            gate = jnp.concatenate([pick(gates[here], first + e) for e in range(2)], axis=0)
            each = jnp.sum(attended * grad, axis=1, keepdims=True)
            spread = jnp.where(lanes(seq) == first, each[:seq], 0.0)
            spread += jnp.where(lanes(seq) == first + 1, each[seq:], 0.0)
            grad = (grad * gate).astype(BF)
            grad_probs = mm_nt(grad, value)
            inner = jnp.sum(probs * grad_probs, axis=1, keepdims=True)
            grad_scores = (probs * (grad_probs - inner) * scale).astype(BF)
            grad_query = mm(grad_scores, key)
            grad_key = mm_tn(grad_scores, query)
            grad_value = mm_tn(probs_b, grad)
            proj_out[here, :HEAD] = rotate(grad_query[:seq], cos_ref[...], -sin_ref[...]).astype(BF)
            proj_out[here, HEAD : 2 * HEAD] = rotate(
                grad_query[seq:], cos_ref[...], -sin_ref[...]
            ).astype(BF)
            proj_out[here, 2 * HEAD : 3 * HEAD] = rotate(
                grad_key, cos_ref[...], -sin_ref[...]
            ).astype(BF)
            proj_out[here, 3 * HEAD :] = grad_value.astype(BF)
            back_out[here, width:] = spread.astype(BF)
        back_out[:, :width] = mm_nt(proj_out[...], w_ref[:, : 4 * HEAD]).astype(BF)

    def tiled(cols):
        return pl.BlockSpec((tile, cols), lambda i: (i, 0))

    def whole(array):
        return pl.BlockSpec(array.shape, lambda i: (0, 0), pipeline_mode=pl.Buffered(1))

    return pl.pallas_call(
        kernel,
        grid=(4,),
        out_shape=[
            jax.ShapeDtypeStruct((rows, 4 * HEAD), BF),
            jax.ShapeDtypeStruct((rows, width + LANE), BF),
        ],
        in_specs=[tiled(width), tiled(4 * HEAD), tiled(LANE)]
        + [whole(a) for a in (weights, cosines, sines)],
        out_specs=[tiled(4 * HEAD), tiled(width + LANE)],
        compiler_params=pltpu.CompilerParams(vmem_limit_bytes=48 << 20),
        cost_estimate=pl.CostEstimate(
            flops=2 * rows * width * 6 * HEAD, bytes_accessed=20 << 20, transcendentals=0
        ),
        name="attn_backward",
    )(grad_mid, qkv, gates, weights, cosines, sines)


def back_through_norm(total, inputs, gain, gates, normed, routers):
    width = inputs.shape[1]
    logits_back = gates_back(gates, total[:, width:])
    full = total[:, :width] + mm_nt(logits_back.astype(BF), routers)
    inner, gain_grad = norm_back(inputs, gain, full)
    return inner, gain_grad, mm_tn(logits_back.astype(BF), normed)[:8]


def middle(collective, back, after, gain, gates_own, routers, cot_own, grads):
    own, width = after.shape
    rows, cols = grads[0].shape[0] // 4, grads[0].shape[1]

    def kernel(
        part_ref, after_ref, gain_ref, gates_ref, router_ref, cot_ref, g0, g1,
        mid_out, small_out, spread_out, s0, s1,
        part, load, total, row, *rest,
    ):
        fetch = pltpu.make_async_copy(part_ref, part, load.at[0])
        fetch.start()
        meet([place(m) for m in TEAM_MOVES[1:] + [Y_MOVES[1], Y_MOVES[3]]] + [sibling()])
        count = TeamSum.count
        team = TeamSum(part, rest[:count])
        rings = [
            RingSum(g, rest[count + 4 + RingSum.count * k : count + 4 + RingSum.count * (k + 1)])
            for k, g in enumerate((g0, g1))
        ]
        for ring in rings:
            ring.start()
        fetch.wait()
        team.run()
        rings[0].middle()
        after = after_ref[...]
        normed = (after * rms_scale(after) * gain_ref[...]).astype(BF)
        team.total(total)
        inner, gain_grad, router_grad = back_through_norm(
            total[...], after, gain_ref[...], gates_ref[...], normed, router_ref[...]
        )
        grad_mid = cot_ref[...].astype(F32) + inner
        mid_out[...] = grad_mid
        row[...] = grad_mid.astype(BF)
        small_out[:8] = jnp.zeros((8, width), F32)
        small_out[0:1] = gain_grad
        small_out[8:] = router_grad
        spread = TeamSpread(row, spread_out, rest[count : count + 4])
        spread.start()
        rings[1].middle()
        spread.middle()
        spread.finish()
        rings[0].finish(s0)
        rings[1].finish(s1)
        team.close()

    return pl.pallas_call(
        kernel,
        out_shape=[
            jax.ShapeDtypeStruct((own, width), F32),
            jax.ShapeDtypeStruct((16, width), F32),
            jax.ShapeDtypeStruct((2, 4, 2, 2, own, width), BF),
        ]
        + [jax.ShapeDtypeStruct((8, rows // 8, cols), BF)] * 2,
        in_specs=[ANY] + [VMEM] * 7,
        out_specs=[VMEM] * 2 + [ANY] + [VMEM] * 2,
        scratch_shapes=[
            pltpu.VMEM((2, 4, 2, 2, own, width + LANE), BF),
            pltpu.SemaphoreType.DMA((1,)),
            pltpu.VMEM((own, width + LANE), F32),
            pltpu.VMEM((own, width), BF),
        ]
        + TeamSum.scratch(own, width + LANE)
        + TeamSpread.sems
        + RingSum.scratch(rows, cols) * 2,
        name="middle",
        **settings(collective, 160 << 20, 48),
    )(back.reshape(2, 4, 2, 2, own, width + LANE), after, gain, gates_own, routers, cot_own, *[
        g.reshape(4, rows, cols) for g in grads
    ])


def leave(collective, back, branch, after, grad_mid, inputs, gain, gates_own, routers, small, summed, grads):
    own, width = after.shape
    rows, cols = grads[0].shape[0] // 4, grads[0].shape[1]
    stages = [X_MOVES, Y_MOVES, Z_MOVES]

    def kernel(
        back_ref, branch_ref, after_ref, mid_ref, in_ref, gain_ref, gates_ref, router_ref, small_ref,
        y0, y1, g2, g3, out_all, grad_all, small_out, s0, s1, s2, s3, y2, y3,
        part_a, part_b, load, total_a, total_b, row_a, row_b, got, other, rest_rows, csem, send, recv, ssend, srecv, *rest,
    ):
        fetches = [
            pltpu.make_async_copy(back_ref, part_a, load.at[0]),
            pltpu.make_async_copy(branch_ref, part_b, load.at[1]),
        ]
        for fetch in fetches:
            fetch.start()
        meet([place(m) for m in TEAM_MOVES[1:] + Y_MOVES[1:]] + [sibling()])
        count = TeamSum.count
        team_a, team_b = TeamSum(part_a, rest[:count]), TeamSum(part_b, rest[count : 2 * count])
        count = 2 * count
        swaps_back = [
            Swap(y, s, rest[count + 2 * k : count + 2 * k + 2])
            for k, (y, s) in enumerate(((y0, s0), (y1, s1), (y2, s2), (y3, s3)))
        ]
        count += 8
        rings = [
            RingSum(g, rest[count + RingSum.count * k : count + RingSum.count * (k + 1)])
            for k, g in enumerate((g2, g3))
        ]
        for ring in rings:
            ring.start()
        fetches[0].wait()
        team_a.run()
        fetches[1].wait()
        team_b.run()
        rings[0].middle()
        swaps_back[0].start()
        swaps_back[1].start()
        inputs = in_ref[...].astype(F32)
        normed = (inputs * rms_scale(inputs) * gain_ref[...]).astype(BF)
        team_a.total(total_a)
        inner, gain_grad, router_grad = back_through_norm(
            total_a[...], inputs, gain_ref[...], gates_ref[...], normed, router_ref[...]
        )
        row_a[...] = (mid_ref[...] + inner).astype(BF)
        small_out[...] = small_ref[...]
        small_out[1:2] = gain_grad
        small_out[8:] += router_grad
        zh, c = lax.axis_index("zh"), lax.axis_index("c")

        def spread(i, src, dst):
            mine, far = dst.at[zh, c], dst.at[1 - zh, c]
            copies = [
                pltpu.make_async_copy(src, mine, send.at[i, 0]),
                push(src, mine, send.at[i, 1], recv.at[i, 1], {"zh": 1 - zh}),
                push(src, mine, send.at[i, 2], recv.at[i, 2], sibling()),
                push(far, far, send.at[i, 3], recv.at[i, 3], sibling()),
            ]
            for copy in copies[:3]:
                copy.start()
            return copies

        def settle(copies):
            copies[1].wait_recv()
            copies[3].start()
            copies[0].wait()
            copies[1].wait_send()
            copies[2].wait()
            copies[3].wait()

        first = spread(0, row_a, grad_all)
        half = pl.ds(pl.multiple_of(c * 8, 8), 8)
        rest_half = pl.ds(pl.multiple_of((1 - c) * 8, 8), 8)
        over = push(small_out.at[rest_half], other, csem.at[0], csem.at[1], sibling())
        over.start()
        team_b.total(total_b)
        row_b[...] = (after_ref[...] + total_b[...]).astype(BF)
        second = spread(1, row_b, out_all)
        rings[1].middle()
        over.wait()
        small_out[half] = small_out[half] + other[...]
        rings[0].finish(y2)
        swaps_back[2].start()
        for s, stage in enumerate(stages):
            swaps = [
                push(small_out.at[half], got.at[s, k - 1], ssend.at[s, k], srecv.at[s, k], place(stage[k]))
                for k in range(1, 4)
            ]
            for swap in swaps:
                swap.start()
            for swap in swaps:
                swap.wait()
            small_out[half] = small_out[half] + got[s, 0] + got[s, 1] + got[s, 2]
            if s == 0:
                rings[1].finish(y3)
                swaps_back[3].start()
        back_over = push(small_out.at[half], rest_rows, csem.at[2], csem.at[3], sibling())
        back_over.start()
        settle(first)
        settle(second)
        back_over.wait()
        small_out[rest_half] = rest_rows[...]
        for swap in swaps_back:
            swap.finish()
        team_a.close()
        team_b.close()

    return pl.pallas_call(
        kernel,
        out_shape=[jax.ShapeDtypeStruct((2, 2, own, width), BF)] * 2
        + [jax.ShapeDtypeStruct((16, width), F32)]
        + [jax.ShapeDtypeStruct((8, rows // 8, cols), BF)] * 4,
        in_specs=[ANY, ANY] + [VMEM] * 7 + [ANY] * 2 + [VMEM] * 2,
        out_specs=[ANY, ANY, VMEM] + [ANY] * 4,
        scratch_shapes=[pltpu.VMEM((8, rows // 8, cols), BF)] * 2
        + [
            pltpu.VMEM((2, 4, 2, 2, own, width + LANE), BF),
            pltpu.VMEM((2, 4, 2, 2, own, width), BF),
            pltpu.SemaphoreType.DMA((2,)),
            pltpu.VMEM((own, width + LANE), F32),
            pltpu.VMEM((own, width), F32),
            pltpu.VMEM((own, width), BF),
            pltpu.VMEM((own, width), BF),
            pltpu.VMEM((3, 3, 8, width), F32),
            pltpu.VMEM((8, width), F32),
            pltpu.VMEM((8, width), F32),
            pltpu.SemaphoreType.DMA((4,)),
        ]
        + [pltpu.SemaphoreType.DMA((2, 4))] * 2
        + [pltpu.SemaphoreType.DMA((4, 4))] * 2
        + TeamSum.scratch(own, width + LANE)
        + TeamSum.scratch(own, width)
        + Swap.sems * 4
        + RingSum.scratch(rows, cols) * 2,
        name="leave",
        **settings(collective, 200 << 20, 48),
    )(
        back.reshape(2, 4, 2, 2, own, width + LANE),
        branch.reshape(2, 4, 2, 2, own, width),
        after, grad_mid, inputs, gain, gates_own, routers, small, *summed,
        *[g.reshape(4, rows, cols) for g in grads],
    )


def reorder(array, axis):
    shape = array.shape
    split = shape[:axis] + (2, 4, shape[axis] // 8) + shape[axis + 1 :]
    return jnp.swapaxes(array.reshape(split), axis, axis + 1).reshape(shape)


def restore(array, axis):
    shape = array.shape
    split = shape[:axis] + (4, 2, shape[axis] // 8) + shape[axis + 1 :]
    return jnp.swapaxes(array.reshape(split), axis, axis + 1).reshape(shape)


def local(
    hidden,
    cotangent,
    attn_gain,
    attn_router,
    qkv_weight,
    out_weight,
    mlp_gain,
    mlp_router,
    gate_up_weight,
    down_weight,
    attn_route,
    attn_slot,
    mlp_route,
    mlp_slot,
):
    seq, width = hidden.shape
    rows = qkv_weight.shape[0]
    features = down_weight.shape[2]
    part = (features // LANE + 1) // 2 * LANE
    low = features - part
    zl, x = lax.axis_index("zl"), lax.axis_index("x")
    quarter = lax.axis_index("zh") * 2 + lax.axis_index("c")
    own = seq // 4
    group = 8 * seq
    cosines, sines = rope_tables(seq)

    query_blocks = qkv_weight[:, :EXPERTS].reshape(rows, 2, 2, 4, HEAD).transpose(1, 3, 0, 2, 4)
    kv_blocks = qkv_weight[:, EXPERTS:].reshape(rows, 2, 4, HEAD).transpose(2, 0, 1, 3)
    kv_blocks = jnp.broadcast_to(kv_blocks[None], (2,) + kv_blocks.shape)
    out_blocks = out_weight.reshape(rows, 2, 2, 4, HEAD).transpose(1, 3, 0, 2, 4)
    attn_blocks = jnp.concatenate([query_blocks, kv_blocks, out_blocks], axis=3)
    attn_blocks = attn_blocks.reshape(8, rows, 6 * HEAD)

    def by_target(weight):
        weight = weight.transpose(1, 0, 2)
        return jnp.stack([weight[..., :part], weight[..., low:]], axis=0).reshape(8, rows, part)

    mlp_blocks = [
        by_target(w) for w in (gate_up_weight[:, :, 0], gate_up_weight[:, :, 1], down_weight)
    ]

    masks = jnp.concatenate([chosen_mask(attn_route), chosen_mask(mlp_route)], axis=1)
    masks = jnp.pad(masks.astype(BF), ((0, 0), (0, LANE - 2 * EXPERTS)))
    attn_gain, mlp_gain = reorder(attn_gain, 0)[None], reorder(mlp_gain, 0)[None]
    routers = reorder(jnp.concatenate([attn_router, mlp_router], axis=1), 0)
    routers = jnp.pad(routers, ((0, 0), (0, LANE - 2 * EXPERTS)))

    def quarter_of(array):
        return lax.dynamic_slice_in_dim(array, quarter * own, own, axis=0)

    hidden_own = reorder(quarter_of(hidden), 1)
    cot_own = reorder(quarter_of(cotangent), 1)
    start = (zl * 4 + x) * seq + quarter * own

    def mine(array):
        return lax.dynamic_slice_in_dim(array, start, own, axis=0)

    entering = jnp.concatenate([hidden_own, quarter_of(masks)], axis=1)
    attn_w, *mlp_rows, group_in = enter(1, attn_blocks, mlp_blocks, entering)
    attn_w = attn_w.reshape(width, 6 * HEAD)
    group_in = group_in.reshape(8, seq, width + LANE)

    normed_a, qkv, gated_att, gates_a, after, normed_m, group_cot, *mlp_w = attn_forward(
        2, group_in, attn_w, attn_gain, routers, cosines, sines, mlp_gain, hidden_own, cot_own, mlp_rows
    )
    mlp_w = [w.reshape(width, part) for w in mlp_w]
    group_cot = group_cot.reshape(group, width)
    normed_a = normed_a.reshape(group, width)
    normed_m = normed_m.reshape(group, width)
    gates_a = gates_a.reshape(group, LANE)

    h, grad_gate, grad_up, branch_m, back_m, gates_m = experts(
        normed_m, group_cot, group_in.reshape(group, width + LANE), routers, mlp_w, 2 * part - features
    )
    grad_mid_own, small_m, grad_mid, *summed = middle(
        3, back_m, after, mlp_gain, mine(gates_m), routers, cot_own,
        [mm_tn(normed_m, grad_gate).astype(BF), mm_tn(normed_m, grad_up).astype(BF)],
    )
    grad_mid = grad_mid.reshape(group, width)
    grad_proj, back_a = attn_backward(
        grad_mid, qkv.reshape(group, 4 * HEAD), gates_a, attn_w, cosines, sines
    )
    attn_grads = jnp.concatenate(
        [
            mm_tn(normed_a, grad_proj).astype(BF),
            mm_tn(grad_mid, gated_att.reshape(group, 2 * HEAD)).astype(BF),
        ],
        axis=1,
    )
    out_hidden, grad_in, small, *mlp_grads, attn_grads = leave(
        4, back_a, branch_m, after, grad_mid_own, hidden_own, attn_gain, mine(gates_a), routers, small_m,
        summed, [mm_tn(group_cot, h).astype(BF), attn_grads],
    )
    out_hidden = restore(out_hidden.reshape(seq, width), 1)
    grad_in = restore(grad_in.reshape(seq, width), 1).astype(F32)
    small = restore(small, 1)

    attn_grads = attn_grads.astype(F32).reshape(2, 4, rows, 6, HEAD).transpose(2, 0, 3, 1, 4)
    attn_grads = attn_grads.reshape(rows, 2, 6, 4 * HEAD)
    query_grad = attn_grads[:, :, :2].reshape(rows, EXPERTS, 4 * HEAD)
    kv_grad = attn_grads[:, 0, 2:4] + attn_grads[:, 1, 2:4]
    qkv_grad = jnp.concatenate([query_grad, kv_grad], axis=1)
    out_grad = attn_grads[:, :, 4:].reshape(rows, EXPERTS, 4 * HEAD)

    def placed_back(grad):
        grad = grad.reshape(2, EXPERTS, rows, part)
        return jnp.concatenate([grad[0], grad[1, ..., 2 * part - features :]], axis=-1).transpose(1, 0, 2)

    gate_grad, up_grad, down_grad = [placed_back(g) for g in mlp_grads]
    return (
        out_hidden,
        grad_in,
        small[1],
        small[8 : 8 + EXPERTS].T,
        qkv_grad,
        out_grad,
        small[0],
        small[8 + EXPERTS :].T,
        jnp.stack([gate_grad, up_grad], axis=2).astype(F32),
        down_grad.astype(F32),
    )


def solution(mesh):
    fine = Mesh(mesh.devices.reshape(2, 4, 4, 2, 2), ALL)
    dp, tensor = ("zl", "y", "x"), ("zh", "c")
    placed = (
        P(dp, None),
        P(dp, None),
        P(),
        P(),
        P(dp, None, tensor),
        P(dp, None, tensor),
        P(),
        P(),
        P(dp, None, None, tensor),
        P(dp, None, tensor),
        P(dp, None),
        P(dp, None),
        P(dp, None),
        P(dp, None),
    )
    return jax.shard_map(
        local,
        mesh=fine,
        in_specs=placed,
        out_specs=(
            P(dp, None),
            P(dp, None),
            P(),
            P(),
            P(dp, None, tensor),
            P(dp, None, tensor),
            P(),
            P(),
            P(dp, None, None, tensor),
            P(dp, None, tensor),
        ),
        check_vma=False,
    )
```

```python
import itertools

import jax
import jax.numpy as jnp
import numpy as np
from jax import lax
from jax.experimental import pallas as pl
from jax.experimental.pallas import tpu as pltpu
from jax.sharding import Mesh, PartitionSpec as P

HEAD = 128
LANE = 128
EPS = 1e-05
THETA = 10000.0
NEG = -1e30
EXPERTS = 4
GROUP = ("zl", "x")
TEAM = ("zl", "x", "zh", "c")
ALL = ("zl", "y", "x", "zh", "c")
SIZES = dict(zl=2, y=4, x=4, zh=2, c=2)
BF = jnp.bfloat16
F32 = jnp.float32
MESH = pl.DeviceIdType.MESH
ANY = pl.BlockSpec(memory_space=pl.ANY)
VMEM = pl.BlockSpec(memory_space=pltpu.VMEM)


def dot(a, b, dims):
    return lax.dot_general(a, b, (dims, ((), ())), preferred_element_type=F32)


def mm(a, b):
    return dot(a, b, ((1,), (0,)))


def mm_nt(a, b):
    return dot(a, b, ((1,), (1,)))


def mm_tn(a, b):
    return dot(a, b, ((0,), (0,)))


def rms_scale(values):
    return lax.rsqrt(jnp.mean(values * values, axis=-1, keepdims=True) + EPS)


def lanes(rows):
    return lax.broadcasted_iota(jnp.int32, (rows, LANE), 1)


def chosen(routes, first):
    lane = lanes(routes.shape[0])
    named = [pick(routes, first + c).astype(jnp.int32) + first for c in range(2)]
    return (lane == named[0]) | (lane == named[1])


def dense_gates(logits, mask):
    top = jnp.max(jnp.where(mask, logits, NEG), axis=1, keepdims=True)
    expon = jnp.where(mask, jnp.exp(jnp.where(mask, logits - top, 0.0)), 0.0)
    return expon / jnp.sum(expon, axis=1, keepdims=True)


def pick(values, lane):
    return jnp.sum(jnp.where(lanes(values.shape[0]) == lane, values, 0.0), axis=1, keepdims=True)


def gates_back(gates, dots):
    return gates * (dots - jnp.sum(gates * dots, axis=1, keepdims=True))


def rope_tables(count):
    frequency = THETA ** (-(np.arange(HEAD // 2).astype(np.float32) * 2.0 / HEAD))
    angles = np.arange(count).astype(np.float32)[:, None] * frequency[None, :].astype(np.float32)
    cosines, sines = np.cos(angles), np.sin(angles)
    return (
        jnp.asarray(np.concatenate([cosines, cosines], axis=1), F32),
        jnp.asarray(np.concatenate([-sines, sines], axis=1), F32),
    )


def rotate(values, cosines, sines):
    return values * cosines + pltpu.roll(values, HEAD // 2, 1) * sines


def norm_back(inputs, gain, grad_normed):
    scale = rms_scale(inputs)
    scaled = inputs * scale
    grad_scaled = grad_normed * gain
    grad_inputs = scale * (
        grad_scaled - scaled * jnp.mean(grad_scaled * scaled, axis=-1, keepdims=True)
    )
    return grad_inputs, jnp.sum(grad_normed * scaled, axis=0, keepdims=True)


def moves(*axes):
    return [dict(zip(axes, steps)) for steps in itertools.product(*[range(SIZES[a]) for a in axes])]


def place(move, sign=1):
    return {a: lax.rem(lax.axis_index(a) + sign * v + SIZES[a], SIZES[a]) for a, v in move.items()}


def number(coords):
    total = 0
    for axis, value in coords.items():
        total = total * SIZES[axis] + value
    return total


def meet(partners):
    barrier = pltpu.get_barrier_semaphore()
    for partner in partners:
        pl.semaphore_signal(barrier, inc=1, device_id=partner, device_id_type=MESH)
    pl.semaphore_wait(barrier, len(partners))


def push(src, dst, send, recv, to):
    return pltpu.make_async_remote_copy(
        src_ref=src, dst_ref=dst, send_sem=send, recv_sem=recv, device_id=to, device_id_type=MESH
    )


def settings(number, moved, vmem=32):
    return dict(
        compiler_params=pltpu.CompilerParams(
            collective_id=number, has_side_effects=True, vmem_limit_bytes=vmem << 20
        ),
        cost_estimate=pl.CostEstimate(flops=0, bytes_accessed=moved, transcendentals=0),
    )


GROUP_MOVES = moves("zl", "x")
TEAM_MOVES = moves("zl", "x", "zh")
X_MOVES = moves("x")
Y_MOVES = moves("y")
Z_MOVES = moves("zl", "zh")


def sibling():
    return {"c": 1 - lax.axis_index("c")}


class RingY:
    sems = [pltpu.SemaphoreType.DMA((5,)), pltpu.SemaphoreType.DMA((5,))]

    def __init__(self, src, out, sems):
        self.src, self.out = src, out
        self.send, self.recv = sems
        self.y = lax.axis_index("y")
        self.half = src.shape[0] // 2

    def line(self, step):
        return lax.rem(self.y + step, 4)

    def copy(self, k):
        y = self.y
        if k < 2:
            src, dst, to = self.src, self.out.at[y], self.line((1, 3)[k])
        else:
            half = pl.ds((k - 2) * self.half, self.half)
            src = dst = self.out.at[self.line((3, 1)[k - 2]), half]
            to = self.line((1, 3)[k - 2])
        return push(src, dst, self.send.at[k], self.recv.at[k], {"y": to})

    def start(self):
        self.stay = pltpu.make_async_copy(self.src, self.out.at[self.y], self.send.at[4])
        for k in range(2):
            self.copy(k).start()
        self.stay.start()

    def forward(self):
        for k in range(2):
            self.copy(k).wait_recv()
            self.copy(k + 2).start()

    def finish(self):
        for k in range(2):
            self.copy(k + 2).wait_recv()
        for k in range(4):
            self.copy(k).wait_send()
        self.stay.wait()


class Swap:
    sems = [pltpu.SemaphoreType.DMA((8,))] * 2

    def __init__(self, src, dst, sems):
        self.src, self.dst = src, dst
        self.send, self.recv = sems

    def start(self):
        me = number(place(GROUP_MOVES[0]))
        self.copies = [
            pltpu.make_async_copy(self.src.at[me], self.dst.at[me], self.send.at[0])
        ]
        for k, move in enumerate(GROUP_MOVES):
            if k:
                to = place(move)
                self.copies.append(
                    push(
                        self.src.at[number(to)],
                        self.dst.at[me],
                        self.send.at[k],
                        self.recv.at[k],
                        to,
                    )
                )
        for copy in self.copies:
            copy.start()

    def finish(self):
        for copy in self.copies:
            copy.wait()


class ColumnSwap(Swap):
    def start(self):
        zl, x = lax.axis_index("zl"), lax.axis_index("x")
        mine = self.dst.at[zl, :, :, pl.ds(pl.multiple_of(x * HEAD, HEAD), HEAD)]
        self.copies = [
            pltpu.make_async_copy(self.src.at[zl * 4 + x], mine, self.send.at[0])
        ]
        for k, move in enumerate(GROUP_MOVES):
            if k:
                to = place(move)
                block = self.src.at[number(to)]
                self.copies.append(push(block, mine, self.send.at[k], self.recv.at[k], to))
        for copy in self.copies:
            copy.start()


def enter(collective, attn_blocks, blocks, rows):
    own, width = rows.shape

    def kernel(a_ref, *refs):
        m_refs, row_ref, a_mid, a_out, m_outs, row_out, g_out, sems = (
            refs[:3], refs[3], refs[4], refs[5], refs[6:9], refs[9], refs[10], refs[11:],
        )
        meet([place(m) for m in TEAM_MOVES[1:] + [Y_MOVES[1], Y_MOVES[3]]] + [sibling()])
        first = Swap(a_ref, a_mid, sems[2:4])
        first.start()
        spread = TeamSpread(row_ref, row_out, sems[10:14])
        spread.start()
        first.finish()
        ring = RingY(a_mid, a_out, sems[0:2])
        ring.start()
        swaps = [Swap(m_refs[i], m_outs[i], sems[4 + 2 * i : 6 + 2 * i]) for i in range(3)]
        swaps[0].start()
        spread.middle()
        swaps[1].start()
        ring.forward()
        swaps[0].finish()
        second = RingY(m_outs[0], g_out, sems[14:16])
        second.start()
        swaps[2].start()
        spread.finish()
        swaps[1].finish()
        second.forward()
        swaps[2].finish()
        ring.finish()
        second.finish()

    like = jax.ShapeDtypeStruct(attn_blocks.shape, attn_blocks.dtype)
    return pl.pallas_call(
        kernel,
        out_shape=[like, jax.ShapeDtypeStruct((4,) + like.shape, like.dtype)]
        + [jax.ShapeDtypeStruct(b.shape, b.dtype) for b in blocks]
        + [jax.ShapeDtypeStruct((2, 4, 2, 2, own, width), rows.dtype)]
        + [jax.ShapeDtypeStruct((4,) + blocks[0].shape, blocks[0].dtype)],
        in_specs=[ANY] * 5,
        out_specs=[ANY] * 7,
        scratch_shapes=RingY.sems + Swap.sems * 4 + TeamSpread.sems + RingY.sems,
        name="enter",
        **settings(collective, 120 << 20),
    )(attn_blocks, *blocks, rows)[1:]


class RingSum:
    @staticmethod
    def scratch(rows, cols):
        return [
            pltpu.VMEM((2, rows // 2, cols), BF),
            pltpu.VMEM((2, rows // 2, cols), BF),
            pltpu.VMEM((2, rows, cols), BF),
            pltpu.SemaphoreType.DMA((6,)),
            pltpu.SemaphoreType.DMA((6,)),
        ]

    count = 5

    def __init__(self, part, scratch):
        self.part = part
        self.got, self.mix, self.sums, self.send, self.recv = scratch
        self.y = lax.axis_index("y")
        half = part.shape[1] // 2
        self.halves = [pl.ds(0, half), pl.ds(half, half)]

    def line(self, step):
        return lax.rem(self.y + step, 4)

    def copy(self, k):
        kind, way = k // 2, k % 2
        step = (1, 3)[way]
        top, low = self.halves[way], self.halves[1 - way]
        if kind == 0:
            src, dst = self.part.at[self.line(2), top], self.got.at[way]
        elif kind == 1:
            src, dst = self.part.at[self.line(step), low], self.sums.at[way, low]
        else:
            src, dst = self.mix.at[way], self.sums.at[way, top]
        return push(src, dst, self.send.at[k], self.recv.at[k], {"y": self.line(step)})

    def start(self):
        for k in range(4):
            self.copy(k).start()

    def middle(self):
        for way in range(2):
            self.copy(way).wait_recv()
            mine = self.part[self.line((1, 3)[way]), self.halves[way]].astype(F32)
            self.mix[way] = (mine + self.got[way].astype(F32)).astype(BF)
            self.copy(4 + way).start()

    def finish(self, out):
        for k in range(2, 6):
            self.copy(k).wait_recv()
        total = self.part[self.y].astype(F32) + self.sums[0].astype(F32) + self.sums[1].astype(F32)
        total = total.astype(BF)
        if len(out.shape) == 3:
            out[...] = total.reshape(out.shape)
        else:
            targets, count, rows, cols = out.shape
            for t in range(targets):
                for n in range(count):
                    out[t, n] = total[t * rows : (t + 1) * rows, n * cols : (n + 1) * cols]
        for k in range(6):
            self.copy(k).wait_send()


class TeamSum:
    @staticmethod
    def scratch(own, width):
        half = own // 2
        return [
            pltpu.VMEM((8, 2, own, width), BF),
            pltpu.VMEM((3, 2, 2, half, width), BF),
            pltpu.VMEM((3, 4, half, width), BF),
            pltpu.VMEM((6, half, width), BF),
            pltpu.SemaphoreType.DMA((8,)),
            pltpu.SemaphoreType.DMA((8,)),
            pltpu.SemaphoreType.DMA((6,)),
            pltpu.SemaphoreType.DMA((6,)),
            pltpu.SemaphoreType.DMA((6,)),
            pltpu.SemaphoreType.DMA((6,)),
        ]

    count = 10

    def __init__(self, part, scratch):
        self.part = part
        self.other, self.got_x, self.got_z, self.late = scratch[:4]
        self.ssem, self.rsem, self.send1, self.recv1, self.send2, self.recv2 = scratch[4:]
        self.zl, self.x, self.zh, self.c = (lax.axis_index(a) for a in TEAM)
        self.half = part.shape[4] // 2
        self.top, self.low = pl.ds(0, self.half), pl.ds(self.half, self.half)

    def swap(self, seq):
        return push(
            self.part.at[seq // 4, lax.rem(seq, 4), :, 1 - self.c],
            self.other.at[seq],
            self.ssem.at[seq],
            self.rsem.at[seq],
            sibling(),
        )

    def send_x(self, x):
        slot = lax.rem(x - self.x + 4, 4) - 1
        return push(
            self.part.at[:, x, :, self.c, self.top],
            self.got_x.at[slot],
            self.send1.at[slot],
            self.recv1.at[slot],
            {"x": x},
        )

    def send_z(self, zl, zh):
        slot = lax.rem(zl - self.zl + 2, 2) * 2 + lax.rem(zh - self.zh + 2, 2) - 1
        return push(
            self.part.at[zl, :, zh, self.c, self.low],
            self.got_z.at[slot],
            self.send1.at[3 + slot],
            self.recv1.at[3 + slot],
            {"zl": zl, "zh": zh},
        )

    def late_z(self, k):
        to = place(Z_MOVES[k])
        return push(
            self.part.at[to["zl"], self.x, to["zh"], self.c, self.top],
            self.late.at[k - 1],
            self.send2.at[k - 1],
            self.recv2.at[k - 1],
            to,
        )

    def late_x(self, k):
        to = place(X_MOVES[k])
        return push(
            self.part.at[self.zl, to["x"], self.zh, self.c, self.low],
            self.late.at[2 + k],
            self.send2.at[2 + k],
            self.recv2.at[2 + k],
            to,
        )

    def add(self, seq):
        self.swap(seq).wait_recv()
        zl, x = seq // 4, lax.rem(seq, 4)
        for zh in range(2):
            mine = self.part[zl, x, zh, self.c].astype(F32)
            self.part[zl, x, zh, self.c] = (mine + self.other[seq, zh].astype(F32)).astype(BF)

    def pair(self, step):
        back = 3 - step
        return lax.rem(self.zl + back // 2, 2) * 2 + lax.rem(self.x // 2 + back, 2)

    def add_pair(self, step):
        for j in range(2):
            self.add(self.pair(step) * 2 + j)

    def send_far_z(self):
        for zh in range(2):
            self.send_z(1 - self.zl, zh).start()

    def send_far_x(self):
        for j in range(2):
            self.send_x((1 - self.x // 2) * 2 + j).start()

    def last(self):
        self.add_pair(3)
        self.send_x(self.x + 1 - 2 * lax.rem(self.x, 2)).start()
        self.send_z(self.zl, 1 - self.zh).start()

    def got(self, ref, sem):
        pltpu.make_async_copy(ref, ref, sem).wait()

    def total(self, total_ref):
        self.total1(total_ref)
        self.total2(total_ref)

    def total1(self, total_ref):
        half, c = self.half, self.c
        for k in range(3):
            self.got(self.got_x.at[k], self.recv1.at[k])
        for k, move in reversed(list(enumerate(Z_MOVES))):
            at = place(move)
            rows = self.part[at["zl"], self.x, at["zh"], c, :half].astype(F32)
            for j in range(3):
                rows += self.got_x[j, at["zl"], at["zh"]].astype(F32)
            if k:
                self.part[at["zl"], self.x, at["zh"], c, :half] = rows.astype(BF)
                self.late_z(k).start()
            else:
                total_ref[:half] = rows
        for k in range(3):
            self.got(self.got_z.at[k], self.recv1.at[3 + k])
        for k, move in reversed(list(enumerate(X_MOVES))):
            at = place(move)
            rows = self.part[self.zl, at["x"], self.zh, c, half:].astype(F32)
            for j in range(3):
                rows += self.got_z[j, at["x"]].astype(F32)
            if k:
                self.part[self.zl, at["x"], self.zh, c, half:] = rows.astype(BF)
                self.late_x(k).start()
            else:
                total_ref[half:] = rows

    def total2(self, total_ref):
        half = self.half
        for k in range(3):
            self.got(self.late.at[k], self.recv2.at[k])
            total_ref[:half] += self.late[k].astype(F32)
        for k in range(3):
            self.got(self.late.at[3 + k], self.recv2.at[3 + k])
            total_ref[half:] += self.late[3 + k].astype(F32)

    def close(self):
        for seq in range(8):
            self.swap(seq).wait_send()
        for k in range(1, 4):
            x, z = place(X_MOVES[k])["x"], place(Z_MOVES[k])
            self.send_x(x).wait_send()
            self.send_z(z["zl"], z["zh"]).wait_send()
            self.late_z(k).wait_send()
            self.late_x(k).wait_send()

    def run(self):
        for step in range(4):
            for j in range(2):
                self.swap(self.pair(step) * 2 + j).start()
        self.add_pair(0)
        self.add_pair(1)
        self.send_far_z()
        self.add_pair(2)
        self.send_far_x()
        self.last()


class TeamSpread:
    sems = [pltpu.SemaphoreType.DMA((12,))] * 2 + [pltpu.SemaphoreType.DMA((9,))] * 2

    def __init__(self, rows, out, sems):
        self.rows, self.out = rows, out
        self.send, self.recv, self.fsend, self.frecv = sems
        self.zl, self.x, self.zh, self.c = (lax.axis_index(a) for a in TEAM)
        self.half = rows.shape[0] // 2
        self.top, self.low = pl.ds(0, self.half), pl.ds(self.half, self.half)

    def tops(self, zl, zh):
        return self.out.at[zl, :, zh, self.c, self.top]

    def lows(self, x):
        return self.out.at[:, x, :, self.c, self.low]

    def hop(self, k, src, dst, to):
        return push(src, dst, self.send.at[k], self.recv.at[k], to)

    def first(self, k):
        here = (self.zl, self.x, self.zh, self.c)
        if k < 3:
            return self.hop(k, self.rows.at[self.top], self.out.at[(*here, self.top)], place(X_MOVES[k + 1]))
        return self.hop(k, self.rows.at[self.low], self.out.at[(*here, self.low)], place(Z_MOVES[k - 2]))

    def second(self, k):
        if k < 3:
            block = self.tops(self.zl, self.zh)
            return self.hop(6 + k, block, block, place(Z_MOVES[k + 1]))
        block = self.lows(self.x)
        return self.hop(6 + k, block, block, place(X_MOVES[k - 2]))

    def forward(self, k, block):
        return push(block, block, self.fsend.at[k], self.frecv.at[k], sibling())

    def start(self):
        self.stay = pltpu.make_async_copy(
            self.rows, self.out.at[self.zl, self.x, self.zh, self.c], self.fsend.at[8]
        )
        for k in range(6):
            self.first(k).start()
        self.stay.start()

    def middle(self):
        self.stay.wait()
        for k in range(3):
            self.first(k).wait_recv()
        for k in range(3):
            self.second(k).start()
        self.forward(0, self.tops(self.zl, self.zh)).start()
        for k in range(3, 6):
            self.first(k).wait_recv()
        for k in range(3, 6):
            self.second(k).start()
        self.forward(1, self.lows(self.x)).start()

    def block(self, k):
        if k < 3:
            at = place(Z_MOVES[k + 1], -1)
            return self.tops(at["zl"], at["zh"])
        return self.lows(place(X_MOVES[k - 2], -1)["x"])

    def finish(self):
        for k in range(6):
            self.second(k).wait_recv()
            self.forward(2 + k, self.block(k)).start()
        blocks = [self.tops(self.zl, self.zh), self.lows(self.x)] + [self.block(k) for k in range(6)]
        for k in range(8):
            self.forward(k, blocks[k]).wait()
        for k in range(6):
            self.first(k).wait_send()
            self.second(k).wait_send()


def meet_team():
    meet([place(m) for m in TEAM_MOVES[1:]] + [sibling()])


def soft(scores, causal):
    scores = jnp.where(causal, scores, NEG)
    expon = jnp.exp(scores - jnp.max(scores, axis=-1, keepdims=True))
    return expon / jnp.sum(expon, axis=-1, keepdims=True)


def causal_mask(copies, seq):
    rows = lax.rem(lax.broadcasted_iota(jnp.int32, (copies * seq, seq), 0), seq)
    return lax.broadcasted_iota(jnp.int32, (copies * seq, seq), 1) <= rows


def attn_forward(
    collective, hidden, weights, gain, routers, cosines, sines, mlp_gain, hidden_own, cot_own, blocks
):
    own, width = hidden_own.shape
    seq = hidden.shape[1]
    scale = HEAD ** (-0.5)

    def kernel(
        hid_ref, weight_ref, gain_ref, router_ref, cos_ref, sin_ref, gain_m_ref, own_ref, cot_ref, b0, b1,
        normed_out, qkv_out, gated_out, gates_out, after_out, spread_out, cot_out, w0, w1,
        hid, w_ref, load, part, total, row, *rest,
    ):
        fetches = [
            pltpu.make_async_copy(hid_ref, hid, load.at[0]),
            pltpu.make_async_copy(weight_ref, w_ref, load.at[1]),
        ]
        for fetch in fetches:
            fetch.start()
        meet([place(m) for m in TEAM_MOVES[1:] + [Y_MOVES[1], Y_MOVES[3]]] + [sibling()])
        count = TeamSum.count
        team = TeamSum(part, rest[:count])
        cot = TeamSpread(cot_ref, cot_out, rest[count : count + 4])
        cot.start()
        rings = [
            RingY(b, w, rest[count + 8 + 2 * k : count + 10 + 2 * k])
            for k, (b, w) in enumerate(((b0, w0), (b1, w1)))
        ]
        for ring in rings:
            ring.start()
        for fetch in fetches:
            fetch.wait()
        first = 2 * team.zl
        causal = causal_mask(2, seq)

        def step(i, _):
            pair = team.pair(i)
            for j in range(2):
                values = hid[pair * 2 + j, :, :width].astype(F32)
                normed_out[pair * 2 + j] = (values * rms_scale(values) * gain_ref[...]).astype(BF)
            normed = normed_out[pl.ds(pair * 2, 2)].reshape(2 * seq, width)
            logits = mm(normed, router_ref[...])
            proj = mm(normed, w_ref[:, : 4 * HEAD])
            routes = hid[pl.ds(pair * 2, 2), :, width:].reshape(2 * seq, LANE).astype(F32)
            gates = dense_gates(logits, chosen(routes, 0))
            gates_out[pl.ds(pair * 2, 2)] = gates.reshape(2, seq, LANE)
            gated = []
            for j in range(2):
                rows = slice(j * seq, (j + 1) * seq)
                query = [
                    rotate(proj[rows, e * HEAD : (e + 1) * HEAD], cos_ref[...], sin_ref[...]).astype(BF)
                    for e in range(2)
                ]
                key = rotate(proj[rows, 2 * HEAD : 3 * HEAD], cos_ref[...], sin_ref[...]).astype(BF)
                value = proj[rows, 3 * HEAD :].astype(BF)
                probs = soft(mm_nt(jnp.concatenate(query, axis=0), key) * scale, causal)
                attended = mm(probs.astype(BF), value)
                out = [
                    (attended[e * seq : (e + 1) * seq] * pick(gates[rows], first + e)).astype(BF)
                    for e in range(2)
                ]
                qkv_out[pair * 2 + j] = jnp.concatenate(query + [key, value], axis=1)
                gated.append(jnp.concatenate(out, axis=1))
                gated_out[pair * 2 + j] = gated[-1]
            branch = mm_nt(jnp.concatenate(gated, axis=0), w_ref[:, 4 * HEAD :])
            part[pair // 2, pl.ds(lax.rem(pair, 2) * 2, 2)] = branch.astype(BF).reshape(
                2, 2, 2, own, width
            )
            for j in range(2):
                team.swap(pair * 2 + j).start()

            @pl.when(i == 0)
            def _():
                cot.middle()

            @pl.when(i > 0)
            def _():
                team.add_pair(i - 1)

            @pl.when(i == 2)
            def _():
                team.send_far_z()

            @pl.when(i == 3)
            def _():
                team.send_far_x()

            return 0

        lax.fori_loop(0, 4, step, 0)
        team.last()
        rings[0].forward()
        cot.finish()
        team.total(total)
        after = total[...] + own_ref[...].astype(F32)
        after_out[...] = after
        row[...] = (after * rms_scale(after) * gain_m_ref[...]).astype(BF)
        spread = TeamSpread(row, spread_out, rest[count + 4 : count + 8])
        spread.start()
        rings[1].forward()
        spread.middle()
        spread.finish()
        team.close()
        for ring in rings:
            ring.finish()

    return pl.pallas_call(
        kernel,
        out_shape=[
            jax.ShapeDtypeStruct((8, seq, width), BF),
            jax.ShapeDtypeStruct((8, seq, 4 * HEAD), BF),
            jax.ShapeDtypeStruct((8, seq, 2 * HEAD), BF),
            jax.ShapeDtypeStruct((8, seq, LANE), F32),
            jax.ShapeDtypeStruct((own, width), F32),
            jax.ShapeDtypeStruct((2, 4, 2, 2, own, width), BF),
            jax.ShapeDtypeStruct((2, 4, 2, 2, own, width), BF),
        ]
        + [jax.ShapeDtypeStruct((4,) + b.shape, b.dtype) for b in blocks],
        in_specs=[ANY] * 2 + [VMEM] * 6 + [ANY] * 3,
        out_specs=[VMEM] * 5 + [ANY] * 4,
        scratch_shapes=[
            pltpu.VMEM(hidden.shape, BF),
            pltpu.VMEM(weights.shape, BF),
            pltpu.SemaphoreType.DMA((2,)),
            pltpu.VMEM((2, 4, 2, 2, own, width), BF),
            pltpu.VMEM((own, width), F32),
            pltpu.VMEM((own, width), BF),
        ]
        + TeamSum.scratch(own, width)
        + TeamSpread.sems * 2
        + RingY.sems * 2,
        name="attn_forward",
        **settings(collective, 200 << 20, 48),
    )(hidden, weights, gain, routers, cosines, sines, mlp_gain, hidden_own, cot_own, *blocks)


def experts(normed, cotangent, entered, routers, weights, extra):
    rows, width = normed.shape
    part = weights[0].shape[1]
    tile = rows // 4

    def kernel(x_ref, cot_ref, route_ref, router_ref, wg, wu, wd, h_out, dg_out, du_out, branch_out, back_out, gates_out):
        lane = EXPERTS + lax.axis_index("x")
        skip = lax.axis_index("zl") * extra
        x = x_ref[...]
        logits = mm(x, router_ref[...])
        index = lanes(tile)
        gates = dense_gates(logits, chosen(route_ref[...].astype(F32), EXPERTS))
        gates_out[...] = gates
        valid = (lax.broadcasted_iota(jnp.int32, (1, part), 1) >= skip).astype(F32)
        gate = pick(gates, lane) * valid
        gate_part = mm(x, wg[...])
        up_part = mm(x, wu[...])
        sigma = 1.0 / (1.0 + jnp.exp(-gate_part))
        silu = gate_part * sigma
        activated = silu * up_part
        h = (activated * gate).astype(BF)
        h_out[...] = h
        branch_out[...] = mm_nt(h, wd[...]).astype(BF)
        cot_down = mm(cot_ref[...], wd[...])
        dots = jnp.sum(activated * valid * cot_down, axis=1, keepdims=True)
        grad_act = cot_down * gate
        grad_gate = (grad_act * up_part * sigma * (1.0 + gate_part * (1.0 - sigma))).astype(BF)
        grad_up = (grad_act * silu).astype(BF)
        dg_out[...] = grad_gate
        du_out[...] = grad_up
        back_out[:, :width] = (mm_nt(grad_gate, wg[...]) + mm_nt(grad_up, wu[...])).astype(BF)
        back_out[:, width:] = jnp.where(index == lane, dots, 0.0).astype(BF)

    def tiled(cols):
        return pl.BlockSpec((tile, cols), lambda i: (i, 0))

    def whole(array):
        return pl.BlockSpec(array.shape, lambda i: (0, 0), pipeline_mode=pl.Buffered(1))

    cols = [part, part, part, width, width + LANE]
    return pl.pallas_call(
        kernel,
        grid=(4,),
        out_shape=[jax.ShapeDtypeStruct((rows, c), BF) for c in cols]
        + [jax.ShapeDtypeStruct((rows, LANE), F32)],
        in_specs=[tiled(width), tiled(width)]
        + [pl.BlockSpec((tile, LANE), lambda i: (i, width // LANE)), whole(routers)]
        + [whole(w) for w in weights],
        out_specs=[tiled(c) for c in cols] + [tiled(LANE)],
        compiler_params=pltpu.CompilerParams(vmem_limit_bytes=48 << 20),
        cost_estimate=pl.CostEstimate(
            flops=12 * rows * width * part, bytes_accessed=40 << 20, transcendentals=rows * part
        ),
        name="experts",
    )(normed, cotangent, entered, routers, *weights)


def attn_backward(grad_mid, qkv, gates, weights, cosines, sines):
    rows, width = grad_mid.shape
    tile = rows // 4
    seq = tile // 2
    scale = HEAD ** (-0.5)

    def kernel(gm_ref, qkv_ref, gates_ref, w_ref, cos_ref, sin_ref, proj_out, back_out):
        first = 2 * lax.axis_index("zl")
        causal = causal_mask(2, seq)
        grads = mm(gm_ref[...], w_ref[:, 4 * HEAD :])
        gates = gates_ref[...]
        index = lanes(tile)
        dots = jnp.zeros((tile, LANE), F32)
        for j in range(2):
            here = slice(j * seq, (j + 1) * seq)
            query = jnp.concatenate(
                [qkv_ref[here, e * HEAD : (e + 1) * HEAD] for e in range(2)], axis=0
            )
            key = qkv_ref[here, 2 * HEAD : 3 * HEAD]
            value = qkv_ref[here, 3 * HEAD :]
            probs = soft(mm_nt(query, key) * scale, causal)
            probs_b = probs.astype(BF)
            attended = mm(probs_b, value)
            grad = jnp.concatenate(
                [grads[here, e * HEAD : (e + 1) * HEAD] for e in range(2)], axis=0
            )
            gate = jnp.concatenate([pick(gates[here], first + e) for e in range(2)], axis=0)
            each = jnp.sum(attended * grad, axis=1, keepdims=True)
            spread = jnp.where(lanes(seq) == first, each[:seq], 0.0)
            spread += jnp.where(lanes(seq) == first + 1, each[seq:], 0.0)
            grad = (grad * gate).astype(BF)
            grad_probs = mm_nt(grad, value)
            inner = jnp.sum(probs * grad_probs, axis=1, keepdims=True)
            grad_scores = (probs * (grad_probs - inner) * scale).astype(BF)
            grad_query = mm(grad_scores, key)
            grad_key = mm_tn(grad_scores, query)
            grad_value = mm_tn(probs_b, grad)
            proj_out[here, :HEAD] = rotate(grad_query[:seq], cos_ref[...], -sin_ref[...]).astype(BF)
            proj_out[here, HEAD : 2 * HEAD] = rotate(
                grad_query[seq:], cos_ref[...], -sin_ref[...]
            ).astype(BF)
            proj_out[here, 2 * HEAD : 3 * HEAD] = rotate(
                grad_key, cos_ref[...], -sin_ref[...]
            ).astype(BF)
            proj_out[here, 3 * HEAD :] = grad_value.astype(BF)
            back_out[here, width:] = spread.astype(BF)
        back_out[:, :width] = mm_nt(proj_out[...], w_ref[:, : 4 * HEAD]).astype(BF)

    def tiled(cols):
        return pl.BlockSpec((tile, cols), lambda i: (i, 0))

    def whole(array):
        return pl.BlockSpec(array.shape, lambda i: (0, 0), pipeline_mode=pl.Buffered(1))

    return pl.pallas_call(
        kernel,
        grid=(4,),
        out_shape=[
            jax.ShapeDtypeStruct((rows, 4 * HEAD), BF),
            jax.ShapeDtypeStruct((rows, width + LANE), BF),
        ],
        in_specs=[tiled(width), tiled(4 * HEAD), tiled(LANE)]
        + [whole(a) for a in (weights, cosines, sines)],
        out_specs=[tiled(4 * HEAD), tiled(width + LANE)],
        compiler_params=pltpu.CompilerParams(vmem_limit_bytes=48 << 20),
        cost_estimate=pl.CostEstimate(
            flops=2 * rows * width * 6 * HEAD, bytes_accessed=20 << 20, transcendentals=0
        ),
        name="attn_backward",
    )(grad_mid, qkv, gates, weights, cosines, sines)


def back_through_norm(total, inputs, gain, gates, normed, routers):
    width = inputs.shape[1]
    logits_back = gates_back(gates, total[:, width:])
    full = total[:, :width] + mm_nt(logits_back.astype(BF), routers)
    inner, gain_grad = norm_back(inputs, gain, full)
    return inner, gain_grad, mm_tn(logits_back.astype(BF), normed)[:8]


def middle(collective, back, after, gain, gates_own, routers, cot_own, grads):
    own, width = after.shape
    rows, cols = grads[0].shape[0] // 4, grads[0].shape[1]

    def kernel(
        part_ref, after_ref, gain_ref, gates_ref, router_ref, cot_ref, g0, g1,
        mid_out, small_out, spread_out, s0, s1,
        part, load, total, row, *rest,
    ):
        fetch = pltpu.make_async_copy(part_ref, part, load.at[0])
        fetch.start()
        meet([place(m) for m in TEAM_MOVES[1:] + [Y_MOVES[1], Y_MOVES[3]]] + [sibling()])
        count = TeamSum.count
        team = TeamSum(part, rest[:count])
        rings = [
            RingSum(g, rest[count + 4 + RingSum.count * k : count + 4 + RingSum.count * (k + 1)])
            for k, g in enumerate((g0, g1))
        ]
        for ring in rings:
            ring.start()
        fetch.wait()
        team.run()
        rings[0].middle()
        after = after_ref[...]
        normed = (after * rms_scale(after) * gain_ref[...]).astype(BF)
        team.total1(total)
        rings[1].middle()
        team.total2(total)
        inner, gain_grad, router_grad = back_through_norm(
            total[...], after, gain_ref[...], gates_ref[...], normed, router_ref[...]
        )
        grad_mid = cot_ref[...].astype(F32) + inner
        mid_out[...] = grad_mid
        row[...] = grad_mid.astype(BF)
        small_out[:8] = jnp.zeros((8, width), F32)
        small_out[0:1] = gain_grad
        small_out[8:] = router_grad
        spread = TeamSpread(row, spread_out, rest[count : count + 4])
        spread.start()
        spread.middle()
        spread.finish()
        rings[0].finish(s0)
        rings[1].finish(s1)
        team.close()

    return pl.pallas_call(
        kernel,
        out_shape=[
            jax.ShapeDtypeStruct((own, width), F32),
            jax.ShapeDtypeStruct((16, width), F32),
            jax.ShapeDtypeStruct((2, 4, 2, 2, own, width), BF),
        ]
        + [jax.ShapeDtypeStruct((8, rows // 8, cols), BF)] * 2,
        in_specs=[ANY] + [VMEM] * 7,
        out_specs=[VMEM] * 2 + [ANY] + [VMEM] * 2,
        scratch_shapes=[
            pltpu.VMEM((2, 4, 2, 2, own, width + LANE), BF),
            pltpu.SemaphoreType.DMA((1,)),
            pltpu.VMEM((own, width + LANE), F32),
            pltpu.VMEM((own, width), BF),
        ]
        + TeamSum.scratch(own, width + LANE)
        + TeamSpread.sems
        + RingSum.scratch(rows, cols) * 2,
        name="middle",
        **settings(collective, 160 << 20, 48),
    )(back.reshape(2, 4, 2, 2, own, width + LANE), after, gain, gates_own, routers, cot_own, *[
        g.reshape(4, rows, cols) for g in grads
    ])


def in_order(values):
    block = values.shape[1] // 8
    order = [(b % 4) * 2 + b // 4 for b in range(8)]
    return jnp.concatenate([values[:, k * block : (k + 1) * block] for k in order], axis=1)


def leave(
    collective, back, branch, after, grad_mid, inputs, gain, gates_own, routers, small, summed, grads, attn_grads
):
    own, width = after.shape
    rows, cols = grads.shape[0] // 4, grads.shape[1]
    shard = rows // 8
    cuts = [a.shape[1] for a in attn_grads]
    stages = [X_MOVES, Y_MOVES, Z_MOVES]

    def kernel(
        back_ref, branch_ref, after_ref, mid_ref, in_ref, gain_ref, gates_ref, router_ref, small_ref,
        y0, y1, g2, a0, a1, out_all, grad_all, small_out, s0, s1, s2, s3,
        y2, y3, g3, part_a, part_b, load, total_a, total_b, row_a, row_b,
        acc, got, other, rest_rows, csem, send, recv, ssend, srecv, *rest,
    ):
        loads = [
            (a0, g3.at[:, :, : cuts[0]]), (a1, g3.at[:, :, cuts[0] :]), (back_ref, part_a), (branch_ref, part_b)
        ]
        fetches = [pltpu.make_async_copy(a, b, load.at[k]) for k, (a, b) in enumerate(loads)]
        for fetch in fetches:
            fetch.start()
        meet([place(m) for m in TEAM_MOVES[1:] + Y_MOVES[1:]] + [sibling()])
        count = TeamSum.count
        team_a, team_b = TeamSum(part_a, rest[:count]), TeamSum(part_b, rest[count : 2 * count])
        count = 2 * count
        swaps_back = [
            Swap(y, s, rest[count + 2 * k : count + 2 * k + 2])
            for k, (y, s) in enumerate(((y0, s0), (y1, s1), (y2, s2)))
        ]
        last_swap = ColumnSwap(y3, s3, rest[count + 6 : count + 8])
        count += 8
        rings = [
            RingSum(g, rest[count + RingSum.count * k : count + RingSum.count * (k + 1)])
            for k, g in enumerate((g2, g3))
        ]
        rings[0].start()
        fetches[0].wait()
        fetches[1].wait()
        rings[1].start()
        fetches[2].wait()
        team_a.run()
        fetches[3].wait()
        team_b.run()
        rings[0].middle()
        swaps_back[0].start()
        swaps_back[1].start()
        inputs = in_ref[...].astype(F32)
        normed = (inputs * rms_scale(inputs) * gain_ref[...]).astype(BF)
        team_a.total1(total_a)
        rings[1].middle()
        team_a.total2(total_a)
        inner, gain_grad, router_grad = back_through_norm(
            total_a[...], inputs, gain_ref[...], gates_ref[...], normed, router_ref[...]
        )
        row_a[...] = in_order((mid_ref[...] + inner).astype(BF))
        acc[...] = small_ref[...]
        acc[1:2] = gain_grad
        acc[8:] += router_grad
        zh, c = lax.axis_index("zh"), lax.axis_index("c")

        def spread(i, src, dst):
            mine, far = dst.at[zh, c], dst.at[1 - zh, c]
            copies = [
                pltpu.make_async_copy(src, mine, send.at[i, 0]),
                push(src, mine, send.at[i, 1], recv.at[i, 1], {"zh": 1 - zh}),
                push(src, mine, send.at[i, 2], recv.at[i, 2], sibling()),
                push(far, far, send.at[i, 3], recv.at[i, 3], sibling()),
            ]
            for copy in copies[:3]:
                copy.start()
            return copies

        def settle(copies):
            copies[1].wait_recv()
            copies[3].start()
            copies[0].wait()
            copies[1].wait_send()
            copies[2].wait()
            copies[3].wait()

        first = spread(0, row_a, grad_all)
        half = pl.ds(pl.multiple_of(c * 8, 8), 8)
        rest_half = pl.ds(pl.multiple_of((1 - c) * 8, 8), 8)
        over = push(acc.at[rest_half], other, csem.at[0], csem.at[1], sibling())
        over.start()
        team_b.total(total_b)
        row_b[...] = in_order((after_ref[...] + total_b[...]).astype(BF))
        second = spread(1, row_b, out_all)
        over.wait()
        acc[half] = acc[half] + other[...]
        for s, stage in enumerate(stages):
            swaps = [
                push(acc.at[half], got.at[s, k - 1], ssend.at[s, k], srecv.at[s, k], place(stage[k]))
                for k in range(1, 4)
            ]
            for swap in swaps:
                swap.start()
            if s == 0:
                rings[0].finish(y2)
                swaps_back[2].start()
            if s == 1:
                rings[1].finish(y3)
                last_swap.start()
            for swap in swaps:
                swap.wait()
            acc[half] = acc[half] + got[s, 0] + got[s, 1] + got[s, 2]
        back_over = push(acc.at[half], rest_rows, csem.at[2], csem.at[3], sibling())
        back_over.start()
        small_out[half] = in_order(acc[half])
        settle(first)
        settle(second)
        back_over.wait()
        small_out[rest_half] = in_order(rest_rows[...])
        for swap in swaps_back + [last_swap]:
            swap.finish()
        team_a.close()
        team_b.close()

    block = jax.ShapeDtypeStruct((8, shard, cols), BF)
    count = cols // HEAD
    return pl.pallas_call(
        kernel,
        out_shape=[jax.ShapeDtypeStruct((2, 2, own, width), BF)] * 2
        + [jax.ShapeDtypeStruct((16, width), F32)]
        + [block] * 3
        + [jax.ShapeDtypeStruct((2, count, shard, 4 * HEAD), BF)],
        in_specs=[ANY, ANY] + [VMEM] * 7 + [ANY] * 2 + [VMEM] + [ANY] * 2,
        out_specs=[ANY, ANY, VMEM] + [ANY] * 4,
        scratch_shapes=[
            pltpu.VMEM((8, shard, cols), BF),
            pltpu.VMEM((8, count, shard, HEAD), BF),
            pltpu.VMEM((4, rows, cols), BF),
            pltpu.VMEM((2, 4, 2, 2, own, width + LANE), BF),
            pltpu.VMEM((2, 4, 2, 2, own, width), BF),
            pltpu.SemaphoreType.DMA((4,)),
            pltpu.VMEM((own, width + LANE), F32),
            pltpu.VMEM((own, width), F32),
            pltpu.VMEM((own, width), BF),
            pltpu.VMEM((own, width), BF),
            pltpu.VMEM((16, width), F32),
            pltpu.VMEM((3, 3, 8, width), F32),
            pltpu.VMEM((8, width), F32),
            pltpu.VMEM((8, width), F32),
            pltpu.SemaphoreType.DMA((4,)),
        ]
        + [pltpu.SemaphoreType.DMA((2, 4))] * 2
        + [pltpu.SemaphoreType.DMA((4, 4))] * 2
        + TeamSum.scratch(own, width + LANE)
        + TeamSum.scratch(own, width)
        + Swap.sems * 4
        + RingSum.scratch(rows, cols) * 2,
        name="leave",
        **settings(collective, 200 << 20, 56),
    )(
        back.reshape(2, 4, 2, 2, own, width + LANE),
        branch.reshape(2, 4, 2, 2, own, width),
        after, grad_mid, inputs, gain, gates_own, routers, small, *summed,
        grads.reshape(4, rows, cols), *[a.reshape(4, rows, a.shape[1]) for a in attn_grads],
    )


def reorder(array, axis):
    shape = array.shape
    split = shape[:axis] + (2, 4, shape[axis] // 8) + shape[axis + 1 :]
    return jnp.swapaxes(array.reshape(split), axis, axis + 1).reshape(shape)


def local(
    hidden,
    cotangent,
    attn_gain,
    attn_router,
    qkv_weight,
    out_weight,
    mlp_gain,
    mlp_router,
    gate_up_weight,
    down_weight,
    attn_route,
    attn_slot,
    mlp_route,
    mlp_slot,
):
    seq, width = hidden.shape
    rows = qkv_weight.shape[0]
    features = down_weight.shape[2]
    part = (features // LANE + 1) // 2 * LANE
    low = features - part
    zl, x = lax.axis_index("zl"), lax.axis_index("x")
    quarter = lax.axis_index("zh") * 2 + lax.axis_index("c")
    own = seq // 4
    group = 8 * seq
    cosines, sines = rope_tables(seq)

    query_blocks = qkv_weight[:, :EXPERTS].reshape(rows, 2, 2, 4, HEAD).transpose(1, 3, 0, 2, 4)
    kv_blocks = qkv_weight[:, EXPERTS:].reshape(rows, 2, 4, HEAD).transpose(2, 0, 1, 3)
    kv_blocks = jnp.broadcast_to(kv_blocks[None], (2,) + kv_blocks.shape)
    out_blocks = out_weight.reshape(rows, 2, 2, 4, HEAD).transpose(1, 3, 0, 2, 4)
    attn_blocks = jnp.concatenate([query_blocks, kv_blocks, out_blocks], axis=3)
    attn_blocks = attn_blocks.reshape(8, rows, 6 * HEAD)

    def by_target(weight):
        weight = weight.transpose(1, 0, 2)
        return jnp.stack([weight[..., :part], weight[..., low:]], axis=0).reshape(8, rows, part)

    mlp_blocks = [
        by_target(w) for w in (gate_up_weight[:, :, 0], gate_up_weight[:, :, 1], down_weight)
    ]

    attn_gain, mlp_gain = reorder(attn_gain, 0)[None], reorder(mlp_gain, 0)[None]
    routers = reorder(jnp.concatenate([attn_router, mlp_router], axis=1), 0)
    routers = jnp.pad(routers, ((0, 0), (0, LANE - 2 * EXPERTS)))

    def quarter_of(array):
        return lax.dynamic_slice_in_dim(array, quarter * own, own, axis=0)

    hidden_own = reorder(quarter_of(hidden), 1)
    cot_own = reorder(quarter_of(cotangent), 1)
    start = (zl * 4 + x) * seq + quarter * own

    def mine(array):
        return lax.dynamic_slice_in_dim(array, start, own, axis=0)

    no_routes = jnp.zeros((own, 2), jnp.int32)
    routes = [quarter_of(attn_route), no_routes, quarter_of(mlp_route)]
    routes = jnp.pad(jnp.concatenate(routes, axis=1), ((0, 0), (0, LANE - 6)))
    entering = jnp.concatenate([hidden_own, routes.astype(BF)], axis=1)
    attn_w, _, *mlp_rows, group_in, gate_w = enter(1, attn_blocks, mlp_blocks, entering)
    attn_w = attn_w.reshape(width, 6 * HEAD)
    group_in = group_in.reshape(8, seq, width + LANE)

    normed_a, qkv, gated_att, gates_a, after, normed_m, group_cot, *mlp_w = attn_forward(
        2, group_in, attn_w, attn_gain, routers, cosines, sines, mlp_gain, hidden_own, cot_own, mlp_rows
    )
    mlp_w = [w.reshape(width, part) for w in [gate_w] + mlp_w]
    group_cot = group_cot.reshape(group, width)
    normed_a = normed_a.reshape(group, width)
    normed_m = normed_m.reshape(group, width)
    gates_a = gates_a.reshape(group, LANE)

    h, grad_gate, grad_up, branch_m, back_m, gates_m = experts(
        normed_m, group_cot, group_in.reshape(group, width + LANE), routers, mlp_w, 2 * part - features
    )
    grad_mid_own, small_m, grad_mid, *summed = middle(
        3, back_m, after, mlp_gain, mine(gates_m), routers, cot_own,
        [mm_tn(normed_m, grad_gate).astype(BF), mm_tn(normed_m, grad_up).astype(BF)],
    )
    grad_mid = grad_mid.reshape(group, width)
    grad_proj, back_a = attn_backward(
        grad_mid, qkv.reshape(group, 4 * HEAD), gates_a, attn_w, cosines, sines
    )
    attn_grads = [
        mm_tn(normed_a, grad_proj).astype(BF),
        mm_tn(grad_mid, gated_att.reshape(group, 2 * HEAD)).astype(BF),
    ]
    out_hidden, grad_in, small, *mlp_grads, attn_grads = leave(
        4, back_a, branch_m, after, grad_mid_own, hidden_own, attn_gain, mine(gates_a), routers, small_m,
        summed, mm_tn(group_cot, h).astype(BF), attn_grads,
    )
    out_hidden = out_hidden.reshape(seq, width)
    grad_in = grad_in.reshape(seq, width).astype(F32)

    attn_grads = attn_grads.astype(F32)
    query_grad = attn_grads[:, :2].reshape(EXPERTS, rows, 4 * HEAD)
    kv_grad = attn_grads[0, 2:4] + attn_grads[1, 2:4]
    qkv_grad = jnp.concatenate([query_grad, kv_grad], axis=0).transpose(1, 0, 2)
    out_grad = attn_grads[:, 4:].reshape(EXPERTS, rows, 4 * HEAD).transpose(1, 0, 2)

    def placed_back(grad):
        grad = grad.reshape(2, EXPERTS, rows, part)
        return jnp.concatenate([grad[0], grad[1, ..., 2 * part - features :]], axis=-1).transpose(1, 0, 2)

    gate_grad, up_grad, down_grad = [placed_back(g) for g in mlp_grads]
    return (
        out_hidden,
        grad_in,
        small[1],
        small[8 : 8 + EXPERTS].T,
        qkv_grad,
        out_grad,
        small[0],
        small[8 + EXPERTS :].T,
        jnp.stack([gate_grad, up_grad], axis=2).astype(F32),
        down_grad.astype(F32),
    )


def solution(mesh):
    fine = Mesh(mesh.devices.reshape(2, 4, 4, 2, 2), ALL)
    dp, tensor = ("zl", "y", "x"), ("zh", "c")
    placed = (
        P(dp, None),
        P(dp, None),
        P(),
        P(),
        P(dp, None, tensor),
        P(dp, None, tensor),
        P(),
        P(),
        P(dp, None, None, tensor),
        P(dp, None, tensor),
        P(dp, None),
        P(dp, None),
        P(dp, None),
        P(dp, None),
    )
    return jax.shard_map(
        local,
        mesh=fine,
        in_specs=placed,
        out_specs=(
            P(dp, None),
            P(dp, None),
            P(),
            P(),
            P(dp, None, tensor),
            P(dp, None, tensor),
            P(),
            P(),
            P(dp, None, None, tensor),
            P(dp, None, tensor),
        ),
        check_vma=False,
    )
```

```python
import itertools

import jax
import jax.numpy as jnp
import numpy as np
from jax import lax
from jax.experimental import pallas as pl
from jax.experimental.pallas import tpu as pltpu
from jax.sharding import Mesh, PartitionSpec as P

HEAD = 128
LANE = 128
EPS = 1e-05
THETA = 10000.0
NEG = -1e30
EXPERTS = 4
GROUP = ("zl", "x")
TEAM = ("zl", "x", "zh", "c")
ALL = ("zl", "y", "x", "zh", "c")
SIZES = dict(zl=2, y=4, x=4, zh=2, c=2)
BF = jnp.bfloat16
F32 = jnp.float32
MESH = pl.DeviceIdType.MESH
ANY = pl.BlockSpec(memory_space=pl.ANY)
VMEM = pl.BlockSpec(memory_space=pltpu.VMEM)


def dot(a, b, dims):
    return lax.dot_general(a, b, (dims, ((), ())), preferred_element_type=F32)


def mm(a, b):
    return dot(a, b, ((1,), (0,)))


def mm_nt(a, b):
    return dot(a, b, ((1,), (1,)))


def mm_tn(a, b):
    return dot(a, b, ((0,), (0,)))


def rms_scale(values):
    return lax.rsqrt(jnp.mean(values * values, axis=-1, keepdims=True) + EPS)


def lanes(rows):
    return lax.broadcasted_iota(jnp.int32, (rows, LANE), 1)


def chosen(routes, first):
    lane = lanes(routes.shape[0])
    named = [pick(routes, first + c).astype(jnp.int32) + first for c in range(2)]
    return (lane == named[0]) | (lane == named[1])


def dense_gates(logits, mask):
    top = jnp.max(jnp.where(mask, logits, NEG), axis=1, keepdims=True)
    expon = jnp.where(mask, jnp.exp(jnp.where(mask, logits - top, 0.0)), 0.0)
    return expon / jnp.sum(expon, axis=1, keepdims=True)


def pick(values, lane):
    return jnp.sum(jnp.where(lanes(values.shape[0]) == lane, values, 0.0), axis=1, keepdims=True)


def gates_back(gates, dots):
    return gates * (dots - jnp.sum(gates * dots, axis=1, keepdims=True))


def rope_tables(count):
    frequency = THETA ** (-(np.arange(HEAD // 2).astype(np.float32) * 2.0 / HEAD))
    angles = np.arange(count).astype(np.float32)[:, None] * frequency[None, :].astype(np.float32)
    cosines, sines = np.cos(angles), np.sin(angles)
    return (
        jnp.asarray(np.concatenate([cosines, cosines], axis=1), F32),
        jnp.asarray(np.concatenate([-sines, sines], axis=1), F32),
    )


def rotate(values, cosines, sines):
    return values * cosines + pltpu.roll(values, HEAD // 2, 1) * sines


def norm_back(inputs, gain, grad_normed):
    scale = rms_scale(inputs)
    scaled = inputs * scale
    grad_scaled = grad_normed * gain
    grad_inputs = scale * (
        grad_scaled - scaled * jnp.mean(grad_scaled * scaled, axis=-1, keepdims=True)
    )
    return grad_inputs, jnp.sum(grad_normed * scaled, axis=0, keepdims=True)


def moves(*axes):
    return [dict(zip(axes, steps)) for steps in itertools.product(*[range(SIZES[a]) for a in axes])]


def place(move, sign=1):
    return {a: lax.rem(lax.axis_index(a) + sign * v + SIZES[a], SIZES[a]) for a, v in move.items()}


def number(coords):
    total = 0
    for axis, value in coords.items():
        total = total * SIZES[axis] + value
    return total


def meet(partners):
    barrier = pltpu.get_barrier_semaphore()
    for partner in partners:
        pl.semaphore_signal(barrier, inc=1, device_id=partner, device_id_type=MESH)
    pl.semaphore_wait(barrier, len(partners))


def push(src, dst, send, recv, to):
    return pltpu.make_async_remote_copy(
        src_ref=src, dst_ref=dst, send_sem=send, recv_sem=recv, device_id=to, device_id_type=MESH
    )


def settings(number, moved, vmem=32):
    return dict(
        compiler_params=pltpu.CompilerParams(
            collective_id=number, has_side_effects=True, vmem_limit_bytes=vmem << 20
        ),
        cost_estimate=pl.CostEstimate(flops=0, bytes_accessed=moved, transcendentals=0),
    )


GROUP_MOVES = moves("zl", "x")
TEAM_MOVES = moves("zl", "x", "zh")
X_MOVES = moves("x")
Y_MOVES = moves("y")
Z_MOVES = moves("zl", "zh")


def sibling():
    return {"c": 1 - lax.axis_index("c")}


class RingY:
    sems = [pltpu.SemaphoreType.DMA((5,)), pltpu.SemaphoreType.DMA((5,))]

    def __init__(self, src, out, sems):
        self.src, self.out = src, out
        self.send, self.recv = sems
        self.y = lax.axis_index("y")
        self.half = src.shape[0] // 2

    def line(self, step):
        return lax.rem(self.y + step, 4)

    def copy(self, k):
        y = self.y
        if k < 2:
            src, dst, to = self.src, self.out.at[y], self.line((1, 3)[k])
        else:
            half = pl.ds((k - 2) * self.half, self.half)
            src = dst = self.out.at[self.line((3, 1)[k - 2]), half]
            to = self.line((1, 3)[k - 2])
        return push(src, dst, self.send.at[k], self.recv.at[k], {"y": to})

    def start(self):
        self.stay = pltpu.make_async_copy(self.src, self.out.at[self.y], self.send.at[4])
        for k in range(2):
            self.copy(k).start()
        self.stay.start()

    def forward(self):
        for k in range(2):
            self.copy(k).wait_recv()
            self.copy(k + 2).start()

    def finish(self):
        for k in range(2):
            self.copy(k + 2).wait_recv()
        for k in range(4):
            self.copy(k).wait_send()
        self.stay.wait()


class Swap:
    sems = [pltpu.SemaphoreType.DMA((8,))] * 2

    def __init__(self, src, dst, sems):
        self.src, self.dst = src, dst
        self.send, self.recv = sems

    def start(self):
        me = number(place(GROUP_MOVES[0]))
        self.copies = [
            pltpu.make_async_copy(self.src.at[me], self.dst.at[me], self.send.at[0])
        ]
        for k, move in enumerate(GROUP_MOVES):
            if k:
                to = place(move)
                self.copies.append(
                    push(
                        self.src.at[number(to)],
                        self.dst.at[me],
                        self.send.at[k],
                        self.recv.at[k],
                        to,
                    )
                )
        for copy in self.copies:
            copy.start()

    def finish(self):
        for copy in self.copies:
            copy.wait()


class ColumnSwap(Swap):
    def start(self):
        zl, x = lax.axis_index("zl"), lax.axis_index("x")
        mine = self.dst.at[zl, :, :, pl.ds(pl.multiple_of(x * HEAD, HEAD), HEAD)]
        self.copies = [
            pltpu.make_async_copy(self.src.at[zl * 4 + x], mine, self.send.at[0])
        ]
        for k, move in enumerate(GROUP_MOVES):
            if k:
                to = place(move)
                block = self.src.at[number(to)]
                self.copies.append(push(block, mine, self.send.at[k], self.recv.at[k], to))
        for copy in self.copies:
            copy.start()


def enter(collective, attn_blocks, blocks, rows):
    own, width = rows.shape

    def kernel(a_ref, *refs):
        m_refs, row_ref, a_mid, a_out, m_outs, row_out, g_out, sems = (
            refs[:3], refs[3], refs[4], refs[5], refs[6:9], refs[9], refs[10], refs[11:],
        )
        meet([place(m) for m in TEAM_MOVES[1:] + [Y_MOVES[1], Y_MOVES[3]]] + [sibling()])
        first = Swap(a_ref, a_mid, sems[2:4])
        first.start()
        spread = TeamSpread(row_ref, row_out, sems[10:14])
        spread.start()
        first.finish()
        ring = RingY(a_mid, a_out, sems[0:2])
        ring.start()
        swaps = [Swap(m_refs[i], m_outs[i], sems[4 + 2 * i : 6 + 2 * i]) for i in range(3)]
        swaps[0].start()
        spread.middle()
        swaps[1].start()
        ring.forward()
        swaps[0].finish()
        second = RingY(m_outs[0], g_out, sems[14:16])
        second.start()
        swaps[2].start()
        spread.finish()
        swaps[1].finish()
        second.forward()
        swaps[2].finish()
        ring.finish()
        second.finish()

    like = jax.ShapeDtypeStruct(attn_blocks.shape, attn_blocks.dtype)
    return pl.pallas_call(
        kernel,
        out_shape=[like, jax.ShapeDtypeStruct((4,) + like.shape, like.dtype)]
        + [jax.ShapeDtypeStruct(b.shape, b.dtype) for b in blocks]
        + [jax.ShapeDtypeStruct((2, 4, 2, 2, own, width), rows.dtype)]
        + [jax.ShapeDtypeStruct((4,) + blocks[0].shape, blocks[0].dtype)],
        in_specs=[ANY] * 5,
        out_specs=[ANY] * 7,
        scratch_shapes=RingY.sems + Swap.sems * 4 + TeamSpread.sems + RingY.sems,
        name="enter",
        **settings(collective, 120 << 20),
    )(attn_blocks, *blocks, rows)[1:]


class RingSum:
    @staticmethod
    def scratch(rows, cols):
        return [
            pltpu.VMEM((2, rows // 2, cols), BF),
            pltpu.VMEM((2, rows // 2, cols), BF),
            pltpu.VMEM((2, rows, cols), BF),
            pltpu.SemaphoreType.DMA((6,)),
            pltpu.SemaphoreType.DMA((6,)),
        ]

    count = 5

    def __init__(self, part, scratch):
        self.part = part
        self.got, self.mix, self.sums, self.send, self.recv = scratch
        self.y = lax.axis_index("y")
        half = part.shape[1] // 2
        self.halves = [pl.ds(0, half), pl.ds(half, half)]

    def line(self, step):
        return lax.rem(self.y + step, 4)

    def copy(self, k):
        kind, way = k // 2, k % 2
        step = (1, 3)[way]
        top, low = self.halves[way], self.halves[1 - way]
        if kind == 0:
            src, dst = self.part.at[self.line(2), top], self.got.at[way]
        elif kind == 1:
            src, dst = self.part.at[self.line(step), low], self.sums.at[way, low]
        else:
            src, dst = self.mix.at[way], self.sums.at[way, top]
        return push(src, dst, self.send.at[k], self.recv.at[k], {"y": self.line(step)})

    def start(self):
        for k in range(4):
            self.copy(k).start()

    def start_with(self, product):
        product(self.line(2))
        self.copy(0).start()
        self.copy(1).start()
        product(self.line(1))
        self.copy(2).start()
        product(self.line(3))
        self.copy(3).start()
        product(self.y)

    def middle(self):
        for way in range(2):
            self.copy(way).wait_recv()
            mine = self.part[self.line((1, 3)[way]), self.halves[way]].astype(F32)
            self.mix[way] = (mine + self.got[way].astype(F32)).astype(BF)
            self.copy(4 + way).start()

    def finish(self, out):
        for k in range(2, 6):
            self.copy(k).wait_recv()
        total = self.part[self.y].astype(F32) + self.sums[0].astype(F32) + self.sums[1].astype(F32)
        total = total.astype(BF)
        if len(out.shape) == 3:
            out[...] = total.reshape(out.shape)
        else:
            targets, count, rows, cols = out.shape
            for t in range(targets):
                for n in range(count):
                    out[t, n] = total[t * rows : (t + 1) * rows, n * cols : (n + 1) * cols]
        for k in range(6):
            self.copy(k).wait_send()


class TeamSum:
    @staticmethod
    def scratch(own, width):
        half = own // 2
        return [
            pltpu.VMEM((8, 2, own, width), BF),
            pltpu.VMEM((3, 2, 2, half, width), BF),
            pltpu.VMEM((3, 4, half, width), BF),
            pltpu.VMEM((6, half, width), BF),
            pltpu.SemaphoreType.DMA((8,)),
            pltpu.SemaphoreType.DMA((8,)),
            pltpu.SemaphoreType.DMA((6,)),
            pltpu.SemaphoreType.DMA((6,)),
            pltpu.SemaphoreType.DMA((6,)),
            pltpu.SemaphoreType.DMA((6,)),
        ]

    count = 10

    def __init__(self, part, scratch):
        self.part = part
        self.other, self.got_x, self.got_z, self.late = scratch[:4]
        self.ssem, self.rsem, self.send1, self.recv1, self.send2, self.recv2 = scratch[4:]
        self.zl, self.x, self.zh, self.c = (lax.axis_index(a) for a in TEAM)
        self.half = part.shape[4] // 2
        self.top, self.low = pl.ds(0, self.half), pl.ds(self.half, self.half)

    def swap(self, seq):
        return push(
            self.part.at[seq // 4, lax.rem(seq, 4), :, 1 - self.c],
            self.other.at[seq],
            self.ssem.at[seq],
            self.rsem.at[seq],
            sibling(),
        )

    def send_x(self, x):
        slot = lax.rem(x - self.x + 4, 4) - 1
        return push(
            self.part.at[:, x, :, self.c, self.top],
            self.got_x.at[slot],
            self.send1.at[slot],
            self.recv1.at[slot],
            {"x": x},
        )

    def send_z(self, zl, zh):
        slot = lax.rem(zl - self.zl + 2, 2) * 2 + lax.rem(zh - self.zh + 2, 2) - 1
        return push(
            self.part.at[zl, :, zh, self.c, self.low],
            self.got_z.at[slot],
            self.send1.at[3 + slot],
            self.recv1.at[3 + slot],
            {"zl": zl, "zh": zh},
        )

    def late_z(self, k):
        to = place(Z_MOVES[k])
        return push(
            self.part.at[to["zl"], self.x, to["zh"], self.c, self.top],
            self.late.at[k - 1],
            self.send2.at[k - 1],
            self.recv2.at[k - 1],
            to,
        )

    def late_x(self, k):
        to = place(X_MOVES[k])
        return push(
            self.part.at[self.zl, to["x"], self.zh, self.c, self.low],
            self.late.at[2 + k],
            self.send2.at[2 + k],
            self.recv2.at[2 + k],
            to,
        )

    def add(self, seq):
        self.swap(seq).wait_recv()
        zl, x = seq // 4, lax.rem(seq, 4)
        for zh in range(2):
            mine = self.part[zl, x, zh, self.c].astype(F32)
            self.part[zl, x, zh, self.c] = (mine + self.other[seq, zh].astype(F32)).astype(BF)

    def pair(self, step):
        back = 3 - step
        return lax.rem(self.zl + back // 2, 2) * 2 + lax.rem(self.x // 2 + back, 2)

    def add_pair(self, step):
        for j in range(2):
            self.add(self.pair(step) * 2 + j)

    def send_far_z(self):
        for zh in range(2):
            self.send_z(1 - self.zl, zh).start()

    def send_far_x(self):
        for j in range(2):
            self.send_x((1 - self.x // 2) * 2 + j).start()

    def last(self):
        self.add_pair(3)
        self.send_x(self.x + 1 - 2 * lax.rem(self.x, 2)).start()
        self.send_z(self.zl, 1 - self.zh).start()

    def got(self, ref, sem):
        pltpu.make_async_copy(ref, ref, sem).wait()

    def total(self, total_ref):
        self.total1(total_ref)
        self.total2(total_ref)

    def total1(self, total_ref):
        half, c = self.half, self.c
        for k in range(3):
            self.got(self.got_x.at[k], self.recv1.at[k])
        for k, move in reversed(list(enumerate(Z_MOVES))):
            at = place(move)
            rows = self.part[at["zl"], self.x, at["zh"], c, :half].astype(F32)
            for j in range(3):
                rows += self.got_x[j, at["zl"], at["zh"]].astype(F32)
            if k:
                self.part[at["zl"], self.x, at["zh"], c, :half] = rows.astype(BF)
                self.late_z(k).start()
            else:
                total_ref[:half] = rows
        for k in range(3):
            self.got(self.got_z.at[k], self.recv1.at[3 + k])
        for k, move in reversed(list(enumerate(X_MOVES))):
            at = place(move)
            rows = self.part[self.zl, at["x"], self.zh, c, half:].astype(F32)
            for j in range(3):
                rows += self.got_z[j, at["x"]].astype(F32)
            if k:
                self.part[self.zl, at["x"], self.zh, c, half:] = rows.astype(BF)
                self.late_x(k).start()
            else:
                total_ref[half:] = rows

    def total2(self, total_ref):
        half = self.half
        for k in range(3):
            self.got(self.late.at[k], self.recv2.at[k])
            total_ref[:half] += self.late[k].astype(F32)
        for k in range(3):
            self.got(self.late.at[3 + k], self.recv2.at[3 + k])
            total_ref[half:] += self.late[3 + k].astype(F32)

    def close(self):
        for seq in range(8):
            self.swap(seq).wait_send()
        for k in range(1, 4):
            x, z = place(X_MOVES[k])["x"], place(Z_MOVES[k])
            self.send_x(x).wait_send()
            self.send_z(z["zl"], z["zh"]).wait_send()
            self.late_z(k).wait_send()
            self.late_x(k).wait_send()

    def swap_all(self):
        for step in range(4):
            for j in range(2):
                self.swap(self.pair(step) * 2 + j).start()

    def add_all(self):
        self.add_pair(0)
        self.add_pair(1)
        self.send_far_z()
        self.add_pair(2)
        self.send_far_x()
        self.last()


class TeamSpread:
    sems = [pltpu.SemaphoreType.DMA((12,))] * 2 + [pltpu.SemaphoreType.DMA((9,))] * 2

    def __init__(self, rows, out, sems):
        self.rows, self.out = rows, out
        self.send, self.recv, self.fsend, self.frecv = sems
        self.zl, self.x, self.zh, self.c = (lax.axis_index(a) for a in TEAM)
        self.half = rows.shape[0] // 2
        self.top, self.low = pl.ds(0, self.half), pl.ds(self.half, self.half)

    def tops(self, zl, zh):
        return self.out.at[zl, :, zh, self.c, self.top]

    def lows(self, x):
        return self.out.at[:, x, :, self.c, self.low]

    def hop(self, k, src, dst, to):
        return push(src, dst, self.send.at[k], self.recv.at[k], to)

    def first(self, k):
        here = (self.zl, self.x, self.zh, self.c)
        if k < 3:
            return self.hop(k, self.rows.at[self.top], self.out.at[(*here, self.top)], place(X_MOVES[k + 1]))
        return self.hop(k, self.rows.at[self.low], self.out.at[(*here, self.low)], place(Z_MOVES[k - 2]))

    def second(self, k):
        if k < 3:
            block = self.tops(self.zl, self.zh)
            return self.hop(6 + k, block, block, place(Z_MOVES[k + 1]))
        block = self.lows(self.x)
        return self.hop(6 + k, block, block, place(X_MOVES[k - 2]))

    def forward(self, k, block):
        return push(block, block, self.fsend.at[k], self.frecv.at[k], sibling())

    def start(self):
        self.stay = pltpu.make_async_copy(
            self.rows, self.out.at[self.zl, self.x, self.zh, self.c], self.fsend.at[8]
        )
        for k in range(6):
            self.first(k).start()
        self.stay.start()

    def middle(self):
        self.stay.wait()
        for k in range(3):
            self.first(k).wait_recv()
        for k in range(3):
            self.second(k).start()
        self.forward(0, self.tops(self.zl, self.zh)).start()
        for k in range(3, 6):
            self.first(k).wait_recv()
        for k in range(3, 6):
            self.second(k).start()
        self.forward(1, self.lows(self.x)).start()

    def block(self, k):
        if k < 3:
            at = place(Z_MOVES[k + 1], -1)
            return self.tops(at["zl"], at["zh"])
        return self.lows(place(X_MOVES[k - 2], -1)["x"])

    def finish(self):
        for k in range(6):
            self.second(k).wait_recv()
            self.forward(2 + k, self.block(k)).start()
        blocks = [self.tops(self.zl, self.zh), self.lows(self.x)] + [self.block(k) for k in range(6)]
        for k in range(8):
            self.forward(k, blocks[k]).wait()
        for k in range(6):
            self.first(k).wait_send()
            self.second(k).wait_send()


def meet_team():
    meet([place(m) for m in TEAM_MOVES[1:]] + [sibling()])


def soft(scores, causal):
    scores = jnp.where(causal, scores, NEG)
    expon = jnp.exp(scores - jnp.max(scores, axis=-1, keepdims=True))
    return expon / jnp.sum(expon, axis=-1, keepdims=True)


def causal_mask(copies, seq):
    rows = lax.rem(lax.broadcasted_iota(jnp.int32, (copies * seq, seq), 0), seq)
    return lax.broadcasted_iota(jnp.int32, (copies * seq, seq), 1) <= rows


def attn_forward(
    collective, hidden, weights, gain, routers, cosines, sines, mlp_gain, hidden_own, cot_own, blocks
):
    own, width = hidden_own.shape
    seq = hidden.shape[1]
    scale = HEAD ** (-0.5)

    def kernel(
        hid_ref, weight_ref, gain_ref, router_ref, cos_ref, sin_ref, gain_m_ref, own_ref, cot_ref, b0, b1,
        normed_out, qkv_out, gated_out, gates_out, after_out, spread_out, cot_out, w0, w1,
        hid, w_ref, load, part, total, row, *rest,
    ):
        fetches = [
            pltpu.make_async_copy(hid_ref, hid, load.at[0]),
            pltpu.make_async_copy(weight_ref, w_ref, load.at[1]),
        ]
        for fetch in fetches:
            fetch.start()
        meet([place(m) for m in TEAM_MOVES[1:] + [Y_MOVES[1], Y_MOVES[3]]] + [sibling()])
        count = TeamSum.count
        team = TeamSum(part, rest[:count])
        cot = TeamSpread(cot_ref, cot_out, rest[count : count + 4])
        cot.start()
        rings = [
            RingY(b, w, rest[count + 8 + 2 * k : count + 10 + 2 * k])
            for k, (b, w) in enumerate(((b0, w0), (b1, w1)))
        ]
        for ring in rings:
            ring.start()
        for fetch in fetches:
            fetch.wait()
        first = 2 * team.zl
        causal = causal_mask(2, seq)

        def step(i, _):
            pair = team.pair(i)
            for j in range(2):
                values = hid[pair * 2 + j, :, :width].astype(F32)
                normed_out[pair * 2 + j] = (values * rms_scale(values) * gain_ref[...]).astype(BF)
            normed = normed_out[pl.ds(pair * 2, 2)].reshape(2 * seq, width)
            logits = mm(normed, router_ref[...])
            proj = mm(normed, w_ref[:, : 4 * HEAD])
            routes = hid[pl.ds(pair * 2, 2), :, width:].reshape(2 * seq, LANE).astype(F32)
            gates = dense_gates(logits, chosen(routes, 0))
            gates_out[pl.ds(pair * 2, 2)] = gates.reshape(2, seq, LANE)
            gated = []
            for j in range(2):
                rows = slice(j * seq, (j + 1) * seq)
                query = [
                    rotate(proj[rows, e * HEAD : (e + 1) * HEAD], cos_ref[...], sin_ref[...]).astype(BF)
                    for e in range(2)
                ]
                key = rotate(proj[rows, 2 * HEAD : 3 * HEAD], cos_ref[...], sin_ref[...]).astype(BF)
                value = proj[rows, 3 * HEAD :].astype(BF)
                probs = soft(mm_nt(jnp.concatenate(query, axis=0), key) * scale, causal)
                attended = mm(probs.astype(BF), value)
                out = [
                    (attended[e * seq : (e + 1) * seq] * pick(gates[rows], first + e)).astype(BF)
                    for e in range(2)
                ]
                qkv_out[pair * 2 + j] = jnp.concatenate(query + [key, value], axis=1)
                gated.append(jnp.concatenate(out, axis=1))
                gated_out[pair * 2 + j] = gated[-1]
            branch = mm_nt(jnp.concatenate(gated, axis=0), w_ref[:, 4 * HEAD :])
            part[pair // 2, pl.ds(lax.rem(pair, 2) * 2, 2)] = branch.astype(BF).reshape(
                2, 2, 2, own, width
            )
            for j in range(2):
                team.swap(pair * 2 + j).start()

            @pl.when(i == 0)
            def _():
                cot.middle()

            @pl.when(i > 0)
            def _():
                team.add_pair(i - 1)

            @pl.when(i == 2)
            def _():
                team.send_far_z()

            @pl.when(i == 3)
            def _():
                team.send_far_x()

            return 0

        lax.fori_loop(0, 4, step, 0)
        team.last()
        rings[0].forward()
        cot.finish()
        team.total(total)
        after = total[...] + own_ref[...].astype(F32)
        after_out[...] = after
        row[...] = (after * rms_scale(after) * gain_m_ref[...]).astype(BF)
        spread = TeamSpread(row, spread_out, rest[count + 4 : count + 8])
        spread.start()
        rings[1].forward()
        spread.middle()
        spread.finish()
        team.close()
        for ring in rings:
            ring.finish()

    return pl.pallas_call(
        kernel,
        out_shape=[
            jax.ShapeDtypeStruct((8, seq, width), BF),
            jax.ShapeDtypeStruct((8, seq, 4 * HEAD), BF),
            jax.ShapeDtypeStruct((8, seq, 2 * HEAD), BF),
            jax.ShapeDtypeStruct((8, seq, LANE), F32),
            jax.ShapeDtypeStruct((own, width), F32),
            jax.ShapeDtypeStruct((2, 4, 2, 2, own, width), BF),
            jax.ShapeDtypeStruct((2, 4, 2, 2, own, width), BF),
        ]
        + [jax.ShapeDtypeStruct((4,) + b.shape, b.dtype) for b in blocks],
        in_specs=[ANY] * 2 + [VMEM] * 6 + [ANY] * 3,
        out_specs=[VMEM] * 5 + [ANY] * 4,
        scratch_shapes=[
            pltpu.VMEM(hidden.shape, BF),
            pltpu.VMEM(weights.shape, BF),
            pltpu.SemaphoreType.DMA((2,)),
            pltpu.VMEM((2, 4, 2, 2, own, width), BF),
            pltpu.VMEM((own, width), F32),
            pltpu.VMEM((own, width), BF),
        ]
        + TeamSum.scratch(own, width)
        + TeamSpread.sems * 2
        + RingY.sems * 2,
        name="attn_forward",
        **settings(collective, 200 << 20, 48),
    )(hidden, weights, gain, routers, cosines, sines, mlp_gain, hidden_own, cot_own, *blocks)


def experts(normed, cotangent, entered, routers, weights, extra):
    rows, width = normed.shape
    part = weights[0].shape[1]
    tile = rows // 4

    def kernel(x_ref, cot_ref, route_ref, router_ref, wg, wu, wd, h_out, dg_out, du_out, branch_out, back_out, gates_out):
        lane = EXPERTS + lax.axis_index("x")
        skip = lax.axis_index("zl") * extra
        x = x_ref[...]
        logits = mm(x, router_ref[...])
        index = lanes(tile)
        gates = dense_gates(logits, chosen(route_ref[...].astype(F32), EXPERTS))
        gates_out[...] = gates
        valid = (lax.broadcasted_iota(jnp.int32, (1, part), 1) >= skip).astype(F32)
        gate = pick(gates, lane) * valid
        gate_part = mm(x, wg[...])
        up_part = mm(x, wu[...])
        sigma = 1.0 / (1.0 + jnp.exp(-gate_part))
        silu = gate_part * sigma
        activated = silu * up_part
        h = (activated * gate).astype(BF)
        h_out[...] = h
        branch_out[...] = mm_nt(h, wd[...]).astype(BF)
        cot_down = mm(cot_ref[...], wd[...])
        dots = jnp.sum(activated * valid * cot_down, axis=1, keepdims=True)
        grad_act = cot_down * gate
        grad_gate = (grad_act * up_part * sigma * (1.0 + gate_part * (1.0 - sigma))).astype(BF)
        grad_up = (grad_act * silu).astype(BF)
        dg_out[...] = grad_gate
        du_out[...] = grad_up
        back_out[:, :width] = (mm_nt(grad_gate, wg[...]) + mm_nt(grad_up, wu[...])).astype(BF)
        back_out[:, width:] = jnp.where(index == lane, dots, 0.0).astype(BF)

    def tiled(cols):
        return pl.BlockSpec((tile, cols), lambda i: (i, 0))

    def whole(array):
        return pl.BlockSpec(array.shape, lambda i: (0, 0), pipeline_mode=pl.Buffered(1))

    cols = [part, part, part, width, width + LANE]
    return pl.pallas_call(
        kernel,
        grid=(4,),
        out_shape=[jax.ShapeDtypeStruct((rows, c), BF) for c in cols]
        + [jax.ShapeDtypeStruct((rows, LANE), F32)],
        in_specs=[tiled(width), tiled(width)]
        + [pl.BlockSpec((tile, LANE), lambda i: (i, width // LANE)), whole(routers)]
        + [whole(w) for w in weights],
        out_specs=[tiled(c) for c in cols] + [tiled(LANE)],
        compiler_params=pltpu.CompilerParams(vmem_limit_bytes=48 << 20),
        cost_estimate=pl.CostEstimate(
            flops=12 * rows * width * part, bytes_accessed=40 << 20, transcendentals=rows * part
        ),
        name="experts",
    )(normed, cotangent, entered, routers, *weights)


def back_through_norm(total, inputs, gain, gates, normed, routers):
    width = inputs.shape[1]
    logits_back = gates_back(gates, total[:, width:])
    full = total[:, :width] + mm_nt(logits_back.astype(BF), routers)
    inner, gain_grad = norm_back(inputs, gain, full)
    return inner, gain_grad, mm_tn(logits_back.astype(BF), normed)[:8]


def row_block(array, block, count):
    cols = array.shape[-1] // 4
    part = array[..., pl.ds(pl.multiple_of(block * cols, cols), cols)]
    return part.reshape(count, cols)


class Pass:
    sems = [pltpu.SemaphoreType.DMA((4,))] * 2

    def __init__(self, src, dst, sems):
        send, recv = sems
        zh, c = lax.axis_index("zh"), lax.axis_index("c")
        mine, far = dst.at[zh, c], dst.at[1 - zh, c]
        self.copies = [
            pltpu.make_async_copy(src, mine, send.at[0]),
            push(src, mine, send.at[1], recv.at[1], {"zh": 1 - zh}),
            push(src, mine, send.at[2], recv.at[2], sibling()),
            push(far, far, send.at[3], recv.at[3], sibling()),
        ]

    def start(self):
        for copy in self.copies[:3]:
            copy.start()

    def finish(self):
        self.copies[1].wait_recv()
        self.copies[3].start()
        self.copies[0].wait()
        self.copies[1].wait_send()
        self.copies[2].wait()
        self.copies[3].wait()


def own_tile():
    zl, x, zh, c = (lax.axis_index(a) for a in TEAM)
    return zl * 4 + x, zh * 2 + c


def middle(collective, back, branch, normed, cotangent, grads, after, gain, gates, routers, cot_own):
    own, width = after.shape
    count, cols = grads[0].shape
    rows = width // 4

    def kernel(
        part_ref, branch_ref, x_ref, cot_ref, d0_ref, d1_ref, d2_ref,
        after_ref, gain_ref, gates_ref, router_ref, own_ref,
        mid_out, small_out, spread_out, s0, s1, g2, out_all,
        x, cot, d0, d1, d2, g0, g1, part_a, part_b, load, total_a, total_b, row_a, row_b, *rest,
    ):
        loads = [
            (part_ref, part_a), (x_ref, x), (d0_ref, d0), (d1_ref, d1), (cot_ref, cot), (d2_ref, d2), (branch_ref, part_b)
        ]
        fetches = [pltpu.make_async_copy(a, b, load.at[k]) for k, (a, b) in enumerate(loads)]
        for fetch in fetches:
            fetch.start()
        meet([place(m) for m in TEAM_MOVES[1:] + [Y_MOVES[1], Y_MOVES[3]]] + [sibling()])
        n = TeamSum.count
        team_a, team_b = TeamSum(part_a, rest[:n]), TeamSum(part_b, rest[n : 2 * n])
        rest = rest[2 * n :]
        n = RingSum.count
        rings = [RingSum(g0, rest[:n]), RingSum(g1, rest[n : 2 * n])]
        rest = rest[2 * n :]
        spread = TeamSpread(row_a, spread_out, rest[:4])
        out = Pass(row_b, out_all, rest[4:6])

        def product(left, right, dst):
            def one(block):
                dst[block] = mm_tn(row_block(left, block, count), right[...]).astype(BF)

            return one

        fetches[0].wait()
        team_a.swap_all()
        fetches[1].wait()
        fetches[2].wait()
        team_a.add_all()
        rings[0].start_with(product(x, d0, g0))
        fetches[3].wait()
        rings[0].middle()
        rings[1].start_with(product(x, d1, g1))
        team_a.total1(total_a)
        rings[1].middle()
        after = after_ref[...]
        normed_own = (after * rms_scale(after) * gain_ref[...]).astype(BF)
        seq, quarter = own_tile()
        team_a.total2(total_a)
        inner, gain_grad, router_grad = back_through_norm(
            total_a[...], after, gain_ref[...], gates_ref[seq * 4 + quarter], normed_own, router_ref[...]
        )
        grad_mid = own_ref[...].astype(F32) + inner
        mid_out[...] = grad_mid
        row_a[...] = grad_mid.astype(BF)
        spread.start()
        small_out[:8] = jnp.zeros((8, width), F32)
        small_out[0:1] = gain_grad
        small_out[8:] = router_grad
        fetches[6].wait()
        team_b.swap_all()
        spread.middle()
        team_b.add_all()
        fetches[4].wait()
        fetches[5].wait()

        def down(block, _):
            product(cot, d2, g2)(block)
            return 0

        lax.fori_loop(0, 4, down, 0)
        spread.finish()
        team_b.total(total_b)
        row_b[...] = in_order((after + total_b[...]).astype(BF))
        out.start()
        rings[0].finish(s0)
        rings[1].finish(s1)
        out.finish()
        team_a.close()
        team_b.close()

    return pl.pallas_call(
        kernel,
        out_shape=[
            jax.ShapeDtypeStruct((own, width), F32),
            jax.ShapeDtypeStruct((16, width), F32),
            jax.ShapeDtypeStruct((2, 4, 2, 2, own, width), BF),
            jax.ShapeDtypeStruct((8, rows // 8, cols), BF),
            jax.ShapeDtypeStruct((8, rows // 8, cols), BF),
            jax.ShapeDtypeStruct((4, rows, cols), BF),
            jax.ShapeDtypeStruct((2, 2, own, width), BF),
        ],
        in_specs=[ANY] * 7 + [VMEM] * 5,
        out_specs=[VMEM] * 2 + [ANY] + [VMEM] * 3 + [ANY],
        scratch_shapes=[
            pltpu.VMEM((count, width), BF),
            pltpu.VMEM((count, width), BF),
            pltpu.VMEM((count, cols), BF),
            pltpu.VMEM((count, cols), BF),
            pltpu.VMEM((count, cols), BF),
            pltpu.VMEM((4, rows, cols), BF),
            pltpu.VMEM((4, rows, cols), BF),
            pltpu.VMEM((2, 4, 2, 2, own, width + LANE), BF),
            pltpu.VMEM((2, 4, 2, 2, own, width), BF),
            pltpu.SemaphoreType.DMA((7,)),
            pltpu.VMEM((own, width + LANE), F32),
            pltpu.VMEM((own, width), F32),
            pltpu.VMEM((own, width), BF),
            pltpu.VMEM((own, width), BF),
        ]
        + TeamSum.scratch(own, width + LANE)
        + TeamSum.scratch(own, width)
        + RingSum.scratch(rows, cols) * 2
        + TeamSpread.sems
        + Pass.sems,
        name="middle",
        **settings(collective, 200 << 20, 58),
    )(
        back.reshape(2, 4, 2, 2, own, width + LANE), branch.reshape(2, 4, 2, 2, own, width),
        normed, cotangent, *grads, after, gain, gates.reshape(-1, own, LANE), routers, cot_own,
    )


def in_order(values):
    block = values.shape[1] // 8
    order = [(b % 4) * 2 + b // 4 for b in range(8)]
    return jnp.concatenate([values[:, k * block : (k + 1) * block] for k in order], axis=1)


def attn_backward(
    collective, grad_mid, qkv, gated, normed, gates, weights, cosines, sines, mid_own, inputs, gain, routers, small, summed, grads
):
    own, width = inputs.shape
    seq = qkv.shape[1]
    rows, cols = grads.shape[1:]
    shard = rows // 8
    scale = HEAD ** (-0.5)
    stages = [X_MOVES, Y_MOVES, Z_MOVES]

    def kernel(
        gm_ref, w_ref, x_ref, g2_ref, y0, y1, qkv_ref, gated_ref, gates_ref, cos_ref, sin_ref,
        mid_ref, in_ref, gain_ref, router_ref, small_ref,
        grad_all, small_out, s0, s1, s2, s3,
        gm, w, x, g2, g3, y2, y3, proj, part, load, total, row,
        acc, got, other, rest_rows, csem, ssend, srecv, *rest,
    ):
        loads = [(gm_ref, gm), (w_ref, w), (g2_ref, g2), (x_ref, x)]
        fetches = [pltpu.make_async_copy(a, b, load.at[k]) for k, (a, b) in enumerate(loads)]
        for fetch in fetches:
            fetch.start()
        meet([place(m) for m in TEAM_MOVES[1:] + Y_MOVES[1:]] + [sibling()])
        n = TeamSum.count
        team, rest = TeamSum(part, rest[:n]), rest[n:]
        n = RingSum.count
        rings, rest = [RingSum(g2, rest[:n]), RingSum(g3, rest[n : 2 * n])], rest[2 * n :]
        swaps_back = [
            Swap(y, s, rest[2 * k : 2 * k + 2]) for k, (y, s) in enumerate(((y0, s0), (y1, s1), (y2, s2)))
        ]
        last_swap = ColumnSwap(y3, s3, rest[6:8])
        out = Pass(row, grad_all, rest[8:10])
        first = 2 * team.zl
        causal = causal_mask(2, seq)
        swaps_back[0].start()
        swaps_back[1].start()
        fetches[0].wait()
        fetches[1].wait()

        def step(i, _):
            pair = team.pair(i)
            grads = mm(gm[pl.ds(pair * 2, 2)].reshape(2 * seq, width), w[:, 4 * HEAD :])
            both = []
            for j in range(2):
                at = pair * 2 + j
                here = slice(j * seq, (j + 1) * seq)
                query = jnp.concatenate(
                    [qkv_ref[at, :, e * HEAD : (e + 1) * HEAD] for e in range(2)], axis=0
                )
                key = qkv_ref[at, :, 2 * HEAD : 3 * HEAD]
                value = qkv_ref[at, :, 3 * HEAD :]
                probs = soft(mm_nt(query, key) * scale, causal)
                probs_b = probs.astype(BF)
                attended = mm(probs_b, value)
                grad = jnp.concatenate(
                    [grads[here, e * HEAD : (e + 1) * HEAD] for e in range(2)], axis=0
                )
                gates = gates_ref[at]
                gate = jnp.concatenate([pick(gates, first + e) for e in range(2)], axis=0)
                each = jnp.sum(attended * grad, axis=1, keepdims=True)
                dots = jnp.where(lanes(seq) == first, each[:seq], 0.0)
                dots += jnp.where(lanes(seq) == first + 1, each[seq:], 0.0)
                grad = (grad * gate).astype(BF)
                grad_probs = mm_nt(grad, value)
                inner = jnp.sum(probs * grad_probs, axis=1, keepdims=True)
                grad_scores = (probs * (grad_probs - inner) * scale).astype(BF)
                turned = [mm(grad_scores, key), mm_tn(grad_scores, query)]
                turned = [turned[0][:seq], turned[0][seq:], turned[1]]
                turned = [rotate(t, cos_ref[...], -sin_ref[...]).astype(BF) for t in turned]
                grad_value = mm_tn(probs_b, grad).astype(BF)
                both.append(jnp.concatenate(turned + [grad_value], axis=1))
                proj[at] = both[-1]
                part[pair // 2, lax.rem(pair, 2) * 2 + j, :, :, :, width:] = dots.astype(BF).reshape(
                    2, 2, own, LANE
                )
            back = mm_nt(jnp.concatenate(both, axis=0), w[:, : 4 * HEAD])
            part[pair // 2, pl.ds(lax.rem(pair, 2) * 2, 2), :, :, :, :width] = back.astype(BF).reshape(
                2, 2, 2, own, width
            )
            for j in range(2):
                team.swap(pair * 2 + j).start()

            @pl.when(i == 0)
            def _():
                fetches[2].wait()
                rings[0].start()

            @pl.when(i > 0)
            def _():
                team.add_pair(i - 1)

            @pl.when(i == 2)
            def _():
                team.send_far_z()

            @pl.when(i == 3)
            def _():
                team.send_far_x()

            return 0

        lax.fori_loop(0, 4, step, 0)
        team.last()
        fetches[3].wait()

        def product(block):
            g3[block, :, : 4 * HEAD] = mm_tn(
                row_block(x, block, 8 * seq), proj[...].reshape(8 * seq, 4 * HEAD)
            ).astype(BF)
            g3[block, :, 4 * HEAD :] = mm_tn(
                row_block(gm, block, 8 * seq), gated_ref[...].reshape(8 * seq, 2 * HEAD)
            ).astype(BF)

        rings[1].start_with(product)
        rings[0].middle()
        inputs = in_ref[...].astype(F32)
        normed_own = (inputs * rms_scale(inputs) * gain_ref[...]).astype(BF)
        own_seq, quarter = own_tile()
        gates_own = gates_ref[own_seq, pl.ds(pl.multiple_of(quarter * own, own), own)]
        team.total1(total)
        rings[1].middle()
        team.total2(total)
        inner, gain_grad, router_grad = back_through_norm(
            total[...], inputs, gain_ref[...], gates_own, normed_own, router_ref[...]
        )
        row[...] = in_order((mid_ref[...] + inner).astype(BF))
        out.start()
        acc[...] = small_ref[...]
        acc[1:2] = gain_grad
        acc[8:] += router_grad
        c = lax.axis_index("c")
        half = pl.ds(pl.multiple_of(c * 8, 8), 8)
        rest_half = pl.ds(pl.multiple_of((1 - c) * 8, 8), 8)
        over = push(acc.at[rest_half], other, csem.at[0], csem.at[1], sibling())
        over.start()
        over.wait()
        acc[half] = acc[half] + other[...]
        for s, stage in enumerate(stages):
            swaps = [
                push(acc.at[half], got.at[s, k - 1], ssend.at[s, k], srecv.at[s, k], place(stage[k]))
                for k in range(1, 4)
            ]
            for swap in swaps:
                swap.start()
            if s == 0:
                rings[0].finish(y2)
                swaps_back[2].start()
            for swap in swaps:
                swap.wait()
            acc[half] = acc[half] + got[s, 0] + got[s, 1] + got[s, 2]
        back_over = push(acc.at[half], rest_rows, csem.at[2], csem.at[3], sibling())
        back_over.start()
        small_out[half] = in_order(acc[half])
        rings[1].finish(y3)
        last_swap.start()
        out.finish()
        back_over.wait()
        small_out[rest_half] = in_order(rest_rows[...])
        for swap in swaps_back + [last_swap]:
            swap.finish()
        team.close()

    block = jax.ShapeDtypeStruct((8, shard, cols), BF)
    heads = cols // HEAD
    return pl.pallas_call(
        kernel,
        out_shape=[
            jax.ShapeDtypeStruct((2, 2, own, width), BF),
            jax.ShapeDtypeStruct((16, width), F32),
            block, block, block,
            jax.ShapeDtypeStruct((2, heads, shard, 4 * HEAD), BF),
        ],
        in_specs=[ANY] * 6 + [VMEM] * 10,
        out_specs=[ANY, VMEM] + [ANY] * 4,
        scratch_shapes=[
            pltpu.VMEM((8, seq, width), BF),
            pltpu.VMEM(weights.shape, BF),
            pltpu.VMEM((8, seq, width), BF),
            pltpu.VMEM((4, rows, cols), BF),
            pltpu.VMEM((4, rows, cols), BF),
            pltpu.VMEM((8, shard, cols), BF),
            pltpu.VMEM((8, heads, shard, HEAD), BF),
            pltpu.VMEM((8, seq, 4 * HEAD), BF),
            pltpu.VMEM((2, 4, 2, 2, own, width + LANE), BF),
            pltpu.SemaphoreType.DMA((4,)),
            pltpu.VMEM((own, width + LANE), F32),
            pltpu.VMEM((own, width), BF),
            pltpu.VMEM((16, width), F32),
            pltpu.VMEM((3, 3, 8, width), F32),
            pltpu.VMEM((8, width), F32),
            pltpu.VMEM((8, width), F32),
            pltpu.SemaphoreType.DMA((4,)),
        ]
        + [pltpu.SemaphoreType.DMA((4, 4))] * 2
        + TeamSum.scratch(own, width + LANE)
        + RingSum.scratch(rows, cols) * 2
        + Swap.sems * 4
        + Pass.sems,
        name="attn_backward",
        **settings(collective, 200 << 20, 58),
    )(
        grad_mid.reshape(8, seq, width), weights, normed, grads, *summed, qkv, gated, gates, cosines, sines,
        mid_own, inputs, gain, routers, small,
    )


def reorder(array, axis):
    shape = array.shape
    split = shape[:axis] + (2, 4, shape[axis] // 8) + shape[axis + 1 :]
    return jnp.swapaxes(array.reshape(split), axis, axis + 1).reshape(shape)


def local(
    hidden,
    cotangent,
    attn_gain,
    attn_router,
    qkv_weight,
    out_weight,
    mlp_gain,
    mlp_router,
    gate_up_weight,
    down_weight,
    attn_route,
    attn_slot,
    mlp_route,
    mlp_slot,
):
    seq, width = hidden.shape
    rows = qkv_weight.shape[0]
    features = down_weight.shape[2]
    part = (features // LANE + 1) // 2 * LANE
    low = features - part
    quarter = lax.axis_index("zh") * 2 + lax.axis_index("c")
    own = seq // 4
    group = 8 * seq
    cosines, sines = rope_tables(seq)

    query_blocks = qkv_weight[:, :EXPERTS].reshape(rows, 2, 2, 4, HEAD).transpose(1, 3, 0, 2, 4)
    kv_blocks = qkv_weight[:, EXPERTS:].reshape(rows, 2, 4, HEAD).transpose(2, 0, 1, 3)
    kv_blocks = jnp.broadcast_to(kv_blocks[None], (2,) + kv_blocks.shape)
    out_blocks = out_weight.reshape(rows, 2, 2, 4, HEAD).transpose(1, 3, 0, 2, 4)
    attn_blocks = jnp.concatenate([query_blocks, kv_blocks, out_blocks], axis=3)
    attn_blocks = attn_blocks.reshape(8, rows, 6 * HEAD)

    def by_target(weight):
        weight = weight.transpose(1, 0, 2)
        return jnp.stack([weight[..., :part], weight[..., low:]], axis=0).reshape(8, rows, part)

    mlp_blocks = [
        by_target(w) for w in (gate_up_weight[:, :, 0], gate_up_weight[:, :, 1], down_weight)
    ]

    attn_gain, mlp_gain = reorder(attn_gain, 0)[None], reorder(mlp_gain, 0)[None]
    routers = reorder(jnp.concatenate([attn_router, mlp_router], axis=1), 0)
    routers = jnp.pad(routers, ((0, 0), (0, LANE - 2 * EXPERTS)))

    def quarter_of(array):
        return lax.dynamic_slice_in_dim(array, quarter * own, own, axis=0)

    hidden_own = reorder(quarter_of(hidden), 1)
    cot_own = reorder(quarter_of(cotangent), 1)
    no_routes = jnp.zeros((own, 2), jnp.int32)
    routes = [quarter_of(attn_route), no_routes, quarter_of(mlp_route)]
    routes = jnp.pad(jnp.concatenate(routes, axis=1), ((0, 0), (0, LANE - 6)))
    entering = jnp.concatenate([hidden_own, routes.astype(BF)], axis=1)
    attn_w, _, *mlp_rows, group_in, gate_w = enter(1, attn_blocks, mlp_blocks, entering)
    attn_w = attn_w.reshape(width, 6 * HEAD)
    group_in = group_in.reshape(8, seq, width + LANE)

    normed_a, qkv, gated_att, gates_a, after, normed_m, group_cot, *mlp_w = attn_forward(
        2, group_in, attn_w, attn_gain, routers, cosines, sines, mlp_gain, hidden_own, cot_own, mlp_rows
    )
    mlp_w = [w.reshape(width, part) for w in [gate_w] + mlp_w]
    group_cot = group_cot.reshape(group, width)
    normed_m = normed_m.reshape(group, width)

    h, grad_gate, grad_up, branch_m, back_m, gates_m = experts(
        normed_m, group_cot, group_in.reshape(group, width + LANE), routers, mlp_w, 2 * part - features
    )
    grad_mid_own, small_m, grad_mid, gate_sum, up_sum, down_part, out_hidden = middle(
        3, back_m, branch_m, normed_m, group_cot, [grad_gate, grad_up, h], after, mlp_gain, gates_m, routers, cot_own
    )
    grad_in, small, *mlp_grads, attn_grads = attn_backward(
        4, grad_mid, qkv, gated_att, normed_a, gates_a, attn_w, cosines, sines, grad_mid_own, hidden_own, attn_gain,
        routers, small_m, [gate_sum, up_sum], down_part,
    )
    out_hidden = out_hidden.reshape(seq, width)
    grad_in = grad_in.reshape(seq, width).astype(F32)

    attn_grads = attn_grads.astype(F32)
    query_grad = attn_grads[:, :2].reshape(EXPERTS, rows, 4 * HEAD)
    kv_grad = attn_grads[0, 2:4] + attn_grads[1, 2:4]
    qkv_grad = jnp.concatenate([query_grad, kv_grad], axis=0).transpose(1, 0, 2)
    out_grad = attn_grads[:, 4:].reshape(EXPERTS, rows, 4 * HEAD).transpose(1, 0, 2)

    def placed_back(grad):
        grad = grad.reshape(2, EXPERTS, rows, part)
        return jnp.concatenate([grad[0], grad[1, ..., 2 * part - features :]], axis=-1).transpose(1, 0, 2)

    gate_grad, up_grad, down_grad = [placed_back(g) for g in mlp_grads]
    return (
        out_hidden,
        grad_in,
        small[1],
        small[8 : 8 + EXPERTS].T,
        qkv_grad,
        out_grad,
        small[0],
        small[8 + EXPERTS :].T,
        jnp.stack([gate_grad, up_grad], axis=2).astype(F32),
        down_grad.astype(F32),
    )


def solution(mesh):
    fine = Mesh(mesh.devices.reshape(2, 4, 4, 2, 2), ALL)
    dp, tensor = ("zl", "y", "x"), ("zh", "c")
    placed = (
        P(dp, None),
        P(dp, None),
        P(),
        P(),
        P(dp, None, tensor),
        P(dp, None, tensor),
        P(),
        P(),
        P(dp, None, None, tensor),
        P(dp, None, tensor),
        P(dp, None),
        P(dp, None),
        P(dp, None),
        P(dp, None),
    )
    return jax.shard_map(
        local,
        mesh=fine,
        in_specs=placed,
        out_specs=(
            P(dp, None),
            P(dp, None),
            P(),
            P(),
            P(dp, None, tensor),
            P(dp, None, tensor),
            P(),
            P(),
            P(dp, None, None, tensor),
            P(dp, None, tensor),
        ),
        check_vma=False,
    )
```

```python
import itertools

import jax
import jax.numpy as jnp
import numpy as np
from jax import lax
from jax.experimental import pallas as pl
from jax.experimental.pallas import tpu as pltpu
from jax.sharding import Mesh, PartitionSpec as P

HEAD = 128
LANE = 128
EPS = 1e-05
THETA = 10000.0
NEG = -1e30
EXPERTS = 4
GROUP = ("zl", "x")
TEAM = ("zl", "x", "zh", "c")
ALL = ("zl", "y", "x", "zh", "c")
SIZES = dict(zl=2, y=4, x=4, zh=2, c=2)
BF = jnp.bfloat16
F32 = jnp.float32
MESH = pl.DeviceIdType.MESH
ANY = pl.BlockSpec(memory_space=pl.ANY)
VMEM = pl.BlockSpec(memory_space=pltpu.VMEM)


def dot(a, b, dims):
    return lax.dot_general(a, b, (dims, ((), ())), preferred_element_type=F32)


def mm(a, b):
    return dot(a, b, ((1,), (0,)))


def mm_nt(a, b):
    return dot(a, b, ((1,), (1,)))


def mm_tn(a, b):
    return dot(a, b, ((0,), (0,)))


def rms_scale(values):
    return lax.rsqrt(jnp.mean(values * values, axis=-1, keepdims=True) + EPS)


def lanes(rows):
    return lax.broadcasted_iota(jnp.int32, (rows, LANE), 1)


def chosen(routes, first):
    lane = lanes(routes.shape[0])
    named = [pick(routes, first + c).astype(jnp.int32) + first for c in range(2)]
    return (lane == named[0]) | (lane == named[1])


def dense_gates(logits, mask):
    top = jnp.max(jnp.where(mask, logits, NEG), axis=1, keepdims=True)
    expon = jnp.where(mask, jnp.exp(jnp.where(mask, logits - top, 0.0)), 0.0)
    return expon / jnp.sum(expon, axis=1, keepdims=True)


def pick(values, lane):
    return jnp.sum(jnp.where(lanes(values.shape[0]) == lane, values, 0.0), axis=1, keepdims=True)


def gates_back(gates, dots):
    return gates * (dots - jnp.sum(gates * dots, axis=1, keepdims=True))


def rope_tables(count):
    frequency = THETA ** (-(np.arange(HEAD // 2).astype(np.float32) * 2.0 / HEAD))
    angles = np.arange(count).astype(np.float32)[:, None] * frequency[None, :].astype(np.float32)
    cosines, sines = np.cos(angles), np.sin(angles)
    return (
        jnp.asarray(np.concatenate([cosines, cosines], axis=1), F32),
        jnp.asarray(np.concatenate([-sines, sines], axis=1), F32),
    )


def rotate(values, cosines, sines):
    return values * cosines + pltpu.roll(values, HEAD // 2, 1) * sines


def norm_back(inputs, gain, grad_normed):
    scale = rms_scale(inputs)
    scaled = inputs * scale
    grad_scaled = grad_normed * gain
    grad_inputs = scale * (
        grad_scaled - scaled * jnp.mean(grad_scaled * scaled, axis=-1, keepdims=True)
    )
    return grad_inputs, jnp.sum(grad_normed * scaled, axis=0, keepdims=True)


def moves(*axes):
    return [dict(zip(axes, steps)) for steps in itertools.product(*[range(SIZES[a]) for a in axes])]


def place(move, sign=1):
    return {a: lax.rem(lax.axis_index(a) + sign * v + SIZES[a], SIZES[a]) for a, v in move.items()}


def number(coords):
    total = 0
    for axis, value in coords.items():
        total = total * SIZES[axis] + value
    return total


def meet(partners):
    barrier = pltpu.get_barrier_semaphore()
    for partner in partners:
        pl.semaphore_signal(barrier, inc=1, device_id=partner, device_id_type=MESH)
    pl.semaphore_wait(barrier, len(partners))


def push(src, dst, send, recv, to):
    return pltpu.make_async_remote_copy(
        src_ref=src, dst_ref=dst, send_sem=send, recv_sem=recv, device_id=to, device_id_type=MESH
    )


def settings(number, moved, vmem=32):
    return dict(
        compiler_params=pltpu.CompilerParams(
            collective_id=number, has_side_effects=True, vmem_limit_bytes=vmem << 20
        ),
        cost_estimate=pl.CostEstimate(flops=0, bytes_accessed=moved, transcendentals=0),
    )


GROUP_MOVES = moves("zl", "x")
TEAM_MOVES = moves("zl", "x", "zh")
X_MOVES = moves("x")
Y_MOVES = moves("y")
Z_MOVES = moves("zl", "zh")


def sibling():
    return {"c": 1 - lax.axis_index("c")}


class RingY:
    sems = [pltpu.SemaphoreType.DMA((5,)), pltpu.SemaphoreType.DMA((5,))]

    def __init__(self, src, out, sems):
        self.src, self.out = src, out
        self.send, self.recv = sems
        self.y = lax.axis_index("y")
        self.half = src.shape[0] // 2

    def line(self, step):
        return lax.rem(self.y + step, 4)

    def copy(self, k):
        y = self.y
        if k < 2:
            src, dst, to = self.src, self.out.at[y], self.line((1, 3)[k])
        else:
            half = pl.ds((k - 2) * self.half, self.half)
            src = dst = self.out.at[self.line((3, 1)[k - 2]), half]
            to = self.line((1, 3)[k - 2])
        return push(src, dst, self.send.at[k], self.recv.at[k], {"y": to})

    def start(self):
        self.stay = pltpu.make_async_copy(self.src, self.out.at[self.y], self.send.at[4])
        for k in range(2):
            self.copy(k).start()
        self.stay.start()

    def forward(self):
        for k in range(2):
            self.copy(k).wait_recv()
            self.copy(k + 2).start()

    def finish(self):
        for k in range(2):
            self.copy(k + 2).wait_recv()
        for k in range(4):
            self.copy(k).wait_send()
        self.stay.wait()


class Swap:
    sems = [pltpu.SemaphoreType.DMA((8,))] * 2

    def __init__(self, src, dst, sems):
        self.src, self.dst = src, dst
        self.send, self.recv = sems

    def start(self):
        me = number(place(GROUP_MOVES[0]))
        self.copies = [
            pltpu.make_async_copy(self.src.at[me], self.dst.at[me], self.send.at[0])
        ]
        for k, move in enumerate(GROUP_MOVES):
            if k:
                to = place(move)
                self.copies.append(
                    push(
                        self.src.at[number(to)],
                        self.dst.at[me],
                        self.send.at[k],
                        self.recv.at[k],
                        to,
                    )
                )
        for copy in self.copies:
            copy.start()

    def finish(self):
        for copy in self.copies:
            copy.wait()


class ColumnSwap(Swap):
    def start(self):
        zl, x = lax.axis_index("zl"), lax.axis_index("x")
        mine = self.dst.at[zl, :, :, pl.ds(pl.multiple_of(x * HEAD, HEAD), HEAD)]
        self.copies = [
            pltpu.make_async_copy(self.src.at[zl * 4 + x], mine, self.send.at[0])
        ]
        for k, move in enumerate(GROUP_MOVES):
            if k:
                to = place(move)
                block = self.src.at[number(to)]
                self.copies.append(push(block, mine, self.send.at[k], self.recv.at[k], to))
        for copy in self.copies:
            copy.start()


class RingSum:
    @staticmethod
    def scratch(rows, cols):
        return [
            pltpu.VMEM((2, rows // 2, cols), BF),
            pltpu.VMEM((2, rows // 2, cols), BF),
            pltpu.VMEM((2, rows, cols), BF),
            pltpu.SemaphoreType.DMA((6,)),
            pltpu.SemaphoreType.DMA((6,)),
        ]

    count = 5

    def __init__(self, part, scratch):
        self.part = part
        self.got, self.mix, self.sums, self.send, self.recv = scratch
        self.y = lax.axis_index("y")
        half = part.shape[1] // 2
        self.halves = [pl.ds(0, half), pl.ds(half, half)]

    def line(self, step):
        return lax.rem(self.y + step, 4)

    def copy(self, k):
        kind, way = k // 2, k % 2
        step = (1, 3)[way]
        top, low = self.halves[way], self.halves[1 - way]
        if kind == 0:
            src, dst = self.part.at[self.line(2), top], self.got.at[way]
        elif kind == 1:
            src, dst = self.part.at[self.line(step), low], self.sums.at[way, low]
        else:
            src, dst = self.mix.at[way], self.sums.at[way, top]
        return push(src, dst, self.send.at[k], self.recv.at[k], {"y": self.line(step)})

    def start(self):
        for k in range(4):
            self.copy(k).start()

    def start_with(self, product):
        product(self.line(2))
        self.copy(0).start()
        self.copy(1).start()
        product(self.line(1))
        self.copy(2).start()
        product(self.line(3))
        self.copy(3).start()
        product(self.y)

    def middle(self):
        for way in range(2):
            self.copy(way).wait_recv()
            mine = self.part[self.line((1, 3)[way]), self.halves[way]].astype(F32)
            self.mix[way] = (mine + self.got[way].astype(F32)).astype(BF)
            self.copy(4 + way).start()

    def finish(self, out):
        for k in range(2, 6):
            self.copy(k).wait_recv()
        total = self.part[self.y].astype(F32) + self.sums[0].astype(F32) + self.sums[1].astype(F32)
        total = total.astype(BF)
        if len(out.shape) == 3:
            out[...] = total.reshape(out.shape)
        else:
            targets, count, rows, cols = out.shape
            for t in range(targets):
                for n in range(count):
                    out[t, n] = total[t * rows : (t + 1) * rows, n * cols : (n + 1) * cols]
        for k in range(6):
            self.copy(k).wait_send()


class TeamSum:
    @staticmethod
    def scratch(own, width):
        half = own // 2
        return [
            pltpu.VMEM((8, 2, own, width), BF),
            pltpu.VMEM((3, 2, 2, half, width), BF),
            pltpu.VMEM((3, 4, half, width), BF),
            pltpu.VMEM((6, half, width), BF),
            pltpu.SemaphoreType.DMA((8,)),
            pltpu.SemaphoreType.DMA((8,)),
            pltpu.SemaphoreType.DMA((6,)),
            pltpu.SemaphoreType.DMA((6,)),
            pltpu.SemaphoreType.DMA((6,)),
            pltpu.SemaphoreType.DMA((6,)),
        ]

    count = 10

    def __init__(self, part, scratch):
        self.part = part
        self.other, self.got_x, self.got_z, self.late = scratch[:4]
        self.ssem, self.rsem, self.send1, self.recv1, self.send2, self.recv2 = scratch[4:]
        self.zl, self.x, self.zh, self.c = (lax.axis_index(a) for a in TEAM)
        self.half = part.shape[4] // 2
        self.top, self.low = pl.ds(0, self.half), pl.ds(self.half, self.half)

    def swap(self, seq):
        return push(
            self.part.at[seq // 4, lax.rem(seq, 4), :, 1 - self.c],
            self.other.at[seq],
            self.ssem.at[seq],
            self.rsem.at[seq],
            sibling(),
        )

    def send_x(self, x):
        slot = lax.rem(x - self.x + 4, 4) - 1
        return push(
            self.part.at[:, x, :, self.c, self.top],
            self.got_x.at[slot],
            self.send1.at[slot],
            self.recv1.at[slot],
            {"x": x},
        )

    def send_z(self, zl, zh):
        slot = lax.rem(zl - self.zl + 2, 2) * 2 + lax.rem(zh - self.zh + 2, 2) - 1
        return push(
            self.part.at[zl, :, zh, self.c, self.low],
            self.got_z.at[slot],
            self.send1.at[3 + slot],
            self.recv1.at[3 + slot],
            {"zl": zl, "zh": zh},
        )

    def late_z(self, k):
        to = place(Z_MOVES[k])
        return push(
            self.part.at[to["zl"], self.x, to["zh"], self.c, self.top],
            self.late.at[k - 1],
            self.send2.at[k - 1],
            self.recv2.at[k - 1],
            to,
        )

    def late_x(self, k):
        to = place(X_MOVES[k])
        return push(
            self.part.at[self.zl, to["x"], self.zh, self.c, self.low],
            self.late.at[2 + k],
            self.send2.at[2 + k],
            self.recv2.at[2 + k],
            to,
        )

    def add(self, seq):
        self.swap(seq).wait_recv()
        zl, x = seq // 4, lax.rem(seq, 4)
        for zh in range(2):
            mine = self.part[zl, x, zh, self.c].astype(F32)
            self.part[zl, x, zh, self.c] = (mine + self.other[seq, zh].astype(F32)).astype(BF)

    def pair(self, step):
        back = 3 - step
        return lax.rem(self.zl + back // 2, 2) * 2 + lax.rem(self.x // 2 + back, 2)

    def add_pair(self, step):
        for j in range(2):
            self.add(self.pair(step) * 2 + j)

    def send_far_z(self):
        for zh in range(2):
            self.send_z(1 - self.zl, zh).start()

    def send_far_x(self):
        for j in range(2):
            self.send_x((1 - self.x // 2) * 2 + j).start()

    def last(self):
        self.add_pair(3)
        self.send_x(self.x + 1 - 2 * lax.rem(self.x, 2)).start()
        self.send_z(self.zl, 1 - self.zh).start()

    def got(self, ref, sem):
        pltpu.make_async_copy(ref, ref, sem).wait()

    def total(self, total_ref):
        self.total1(total_ref)
        self.total2(total_ref)

    def total1(self, total_ref):
        half, c = self.half, self.c
        for k in range(3):
            self.got(self.got_x.at[k], self.recv1.at[k])
        for k, move in reversed(list(enumerate(Z_MOVES))):
            at = place(move)
            rows = self.part[at["zl"], self.x, at["zh"], c, :half].astype(F32)
            for j in range(3):
                rows += self.got_x[j, at["zl"], at["zh"]].astype(F32)
            if k:
                self.part[at["zl"], self.x, at["zh"], c, :half] = rows.astype(BF)
                self.late_z(k).start()
            else:
                total_ref[:half] = rows
        for k in range(3):
            self.got(self.got_z.at[k], self.recv1.at[3 + k])
        for k, move in reversed(list(enumerate(X_MOVES))):
            at = place(move)
            rows = self.part[self.zl, at["x"], self.zh, c, half:].astype(F32)
            for j in range(3):
                rows += self.got_z[j, at["x"]].astype(F32)
            if k:
                self.part[self.zl, at["x"], self.zh, c, half:] = rows.astype(BF)
                self.late_x(k).start()
            else:
                total_ref[half:] = rows

    def total2(self, total_ref):
        half = self.half
        for k in range(3):
            self.got(self.late.at[k], self.recv2.at[k])
            total_ref[:half] += self.late[k].astype(F32)
        for k in range(3):
            self.got(self.late.at[3 + k], self.recv2.at[3 + k])
            total_ref[half:] += self.late[3 + k].astype(F32)

    def close(self):
        for seq in range(8):
            self.swap(seq).wait_send()
        for k in range(1, 4):
            x, z = place(X_MOVES[k])["x"], place(Z_MOVES[k])
            self.send_x(x).wait_send()
            self.send_z(z["zl"], z["zh"]).wait_send()
            self.late_z(k).wait_send()
            self.late_x(k).wait_send()

    def swap_all(self):
        for step in range(4):
            for j in range(2):
                self.swap(self.pair(step) * 2 + j).start()

    def add_all(self):
        self.add_pair(0)
        self.add_pair(1)
        self.send_far_z()
        self.add_pair(2)
        self.send_far_x()
        self.last()


class TeamSpread:
    sems = [pltpu.SemaphoreType.DMA((12,))] * 2 + [pltpu.SemaphoreType.DMA((9,))] * 2

    def __init__(self, rows, out, sems):
        self.rows, self.out = rows, out
        self.send, self.recv, self.fsend, self.frecv = sems
        self.zl, self.x, self.zh, self.c = (lax.axis_index(a) for a in TEAM)
        self.half = rows.shape[0] // 2
        self.top, self.low = pl.ds(0, self.half), pl.ds(self.half, self.half)

    def tops(self, zl, zh):
        return self.out.at[zl, :, zh, self.c, self.top]

    def lows(self, x):
        return self.out.at[:, x, :, self.c, self.low]

    def hop(self, k, src, dst, to):
        return push(src, dst, self.send.at[k], self.recv.at[k], to)

    def first(self, k):
        here = (self.zl, self.x, self.zh, self.c)
        if k < 3:
            return self.hop(k, self.rows.at[self.top], self.out.at[(*here, self.top)], place(X_MOVES[k + 1]))
        return self.hop(k, self.rows.at[self.low], self.out.at[(*here, self.low)], place(Z_MOVES[k - 2]))

    def second(self, k):
        if k < 3:
            block = self.tops(self.zl, self.zh)
            return self.hop(6 + k, block, block, place(Z_MOVES[k + 1]))
        block = self.lows(self.x)
        return self.hop(6 + k, block, block, place(X_MOVES[k - 2]))

    def forward(self, k, block):
        return push(block, block, self.fsend.at[k], self.frecv.at[k], sibling())

    def start(self):
        self.stay = pltpu.make_async_copy(
            self.rows, self.out.at[self.zl, self.x, self.zh, self.c], self.fsend.at[8]
        )
        for k in range(6):
            self.first(k).start()
        self.stay.start()

    def middle(self):
        self.stay.wait()
        for k in range(3):
            self.first(k).wait_recv()
        for k in range(3):
            self.second(k).start()
        self.forward(0, self.tops(self.zl, self.zh)).start()
        for k in range(3, 6):
            self.first(k).wait_recv()
        for k in range(3, 6):
            self.second(k).start()
        self.forward(1, self.lows(self.x)).start()

    def block(self, k):
        if k < 3:
            at = place(Z_MOVES[k + 1], -1)
            return self.tops(at["zl"], at["zh"])
        return self.lows(place(X_MOVES[k - 2], -1)["x"])

    def finish(self):
        for k in range(6):
            self.second(k).wait_recv()
            self.forward(2 + k, self.block(k)).start()
        blocks = [self.tops(self.zl, self.zh), self.lows(self.x)] + [self.block(k) for k in range(6)]
        for k in range(8):
            self.forward(k, blocks[k]).wait()
        for k in range(6):
            self.first(k).wait_send()
            self.second(k).wait_send()


def soft(scores, causal):
    scores = jnp.where(causal, scores, NEG)
    expon = jnp.exp(scores - jnp.max(scores, axis=-1, keepdims=True))
    return expon / jnp.sum(expon, axis=-1, keepdims=True)


def causal_mask(copies, seq):
    rows = lax.rem(lax.broadcasted_iota(jnp.int32, (copies * seq, seq), 0), seq)
    return lax.broadcasted_iota(jnp.int32, (copies * seq, seq), 1) <= rows


def attn_forward(
    collective, attn_blocks, blocks, entering, cot_own, gain, routers, cosines, sines, mlp_gain, hidden_own
):
    own, width = hidden_own.shape
    seq = 4 * own
    scale = HEAD ** (-0.5)

    def kernel(
        a_ref, b0, b1, b2, enter_ref, cot_ref, gain_ref, router_ref, cos_ref, sin_ref, gain_m_ref, own_ref,
        w_out, normed_out, qkv_out, gated_out, gates_out, routes_out, after_out,
        spread_out, cot_out, w0, w1, w2, a_mid, m0, m1, m2,
        hid, part, total, row, *rest,
    ):
        meet([place(m) for m in TEAM_MOVES[1:] + [Y_MOVES[1], Y_MOVES[3]]] + [sibling()])
        n = TeamSum.count
        team, rest = TeamSum(part, rest[:n]), rest[n:]
        enters = TeamSpread(enter_ref, hid, rest[:4])
        cot = TeamSpread(cot_ref, cot_out, rest[4:8])
        spread = TeamSpread(row, spread_out, rest[8:12])
        rest = rest[12:]
        swaps = [
            Swap(b, m, rest[2 * k : 2 * k + 2])
            for k, (b, m) in enumerate(((a_ref, a_mid), (b0, m0), (b1, m1), (b2, m2)))
        ]
        rings = [
            RingY(m, w, rest[8 + 2 * k : 10 + 2 * k])
            for k, (m, w) in enumerate(((a_mid, w_out), (m0, w0), (m1, w1), (m2, w2)))
        ]
        swaps[0].start()
        enters.start()
        swaps[0].finish()
        rings[0].start()
        swaps[1].start()
        enters.middle()
        swaps[2].start()
        rings[0].forward()
        swaps[1].finish()
        rings[1].start()
        swaps[3].start()
        enters.finish()
        rings[0].finish()
        first = 2 * team.zl
        causal = causal_mask(2, seq)

        def step(i, _):
            pair = team.pair(i)
            zl, x = pair // 2, lax.rem(pair, 2) * 2
            routes = []
            for j in range(2):
                entered = hid[zl, x + j].reshape(seq, width + LANE)
                values = entered[:, :width].astype(F32)
                normed_out[pair * 2 + j] = (values * rms_scale(values) * gain_ref[...]).astype(BF)
                routes.append(entered[:, width:])
                routes_out[pair * 2 + j] = routes[j]
            normed = normed_out[pl.ds(pair * 2, 2)].reshape(2 * seq, width)
            weights = w_out.reshape(width, 6 * HEAD)
            logits = mm(normed, router_ref[...])
            proj = mm(normed, weights[:, : 4 * HEAD])
            gates = dense_gates(logits, chosen(jnp.concatenate(routes, axis=0).astype(F32), 0))
            gates_out[pl.ds(pair * 2, 2)] = gates.reshape(2, seq, LANE)
            gated = []
            for j in range(2):
                rows = slice(j * seq, (j + 1) * seq)
                query = [
                    rotate(proj[rows, e * HEAD : (e + 1) * HEAD], cos_ref[...], sin_ref[...]).astype(BF)
                    for e in range(2)
                ]
                key = rotate(proj[rows, 2 * HEAD : 3 * HEAD], cos_ref[...], sin_ref[...]).astype(BF)
                value = proj[rows, 3 * HEAD :].astype(BF)
                probs = soft(mm_nt(jnp.concatenate(query, axis=0), key) * scale, causal)
                attended = mm(probs.astype(BF), value)
                out = [
                    (attended[e * seq : (e + 1) * seq] * pick(gates[rows], first + e)).astype(BF)
                    for e in range(2)
                ]
                qkv_out[pair * 2 + j] = jnp.concatenate(query + [key, value], axis=1)
                gated.append(jnp.concatenate(out, axis=1))
                gated_out[pair * 2 + j] = gated[-1]
            branch = mm_nt(jnp.concatenate(gated, axis=0), weights[:, 4 * HEAD :])
            part[zl, pl.ds(x, 2)] = branch.astype(BF).reshape(2, 2, 2, own, width)
            for j in range(2):
                team.swap(pair * 2 + j).start()

            @pl.when(i > 0)
            def _():
                team.add_pair(i - 1)

            @pl.when(i == 2)
            def _():
                team.send_far_z()

            @pl.when(i == 3)
            def _():
                team.send_far_x()

            return 0

        lax.fori_loop(0, 4, step, 0)
        team.last()
        swaps[2].finish()
        rings[2].start()
        swaps[3].finish()
        rings[3].start()
        cot.start()
        rings[1].forward()
        team.total1(total)
        cot.middle()
        team.total2(total)
        after = total[...] + own_ref[...].astype(F32)
        after_out[...] = after
        row[...] = (after * rms_scale(after) * gain_m_ref[...]).astype(BF)
        spread.start()
        spread.middle()
        rings[2].forward()
        cot.finish()
        spread.finish()
        rings[3].forward()
        team.close()
        for ring in rings[1:]:
            ring.finish()

    block = jax.ShapeDtypeStruct(attn_blocks.shape, BF)
    four = jax.ShapeDtypeStruct((4,) + attn_blocks.shape, BF)
    rows = jax.ShapeDtypeStruct((2, 4, 2, 2, own, width), BF)
    return pl.pallas_call(
        kernel,
        out_shape=[
            four,
            jax.ShapeDtypeStruct((8, seq, width), BF),
            jax.ShapeDtypeStruct((8, seq, 4 * HEAD), BF),
            jax.ShapeDtypeStruct((8, seq, 2 * HEAD), BF),
            jax.ShapeDtypeStruct((8, seq, LANE), F32),
            jax.ShapeDtypeStruct((8, seq, LANE), BF),
            jax.ShapeDtypeStruct((own, width), F32),
            rows, rows, four, four, four, block, block, block, block,
        ],
        in_specs=[ANY] * 6 + [VMEM] * 6,
        out_specs=[VMEM] * 7 + [ANY] * 9,
        scratch_shapes=[
            pltpu.VMEM((2, 4, 2, 2, own, width + LANE), BF),
            pltpu.VMEM((2, 4, 2, 2, own, width), BF),
            pltpu.VMEM((own, width), F32),
            pltpu.VMEM((own, width), BF),
        ]
        + TeamSum.scratch(own, width)
        + TeamSpread.sems * 3
        + Swap.sems * 4
        + RingY.sems * 4,
        name="attn_forward",
        **settings(collective, 200 << 20, 56),
    )(attn_blocks, *blocks, entering, cot_own, gain, routers, cosines, sines, mlp_gain, hidden_own)[:12]


def experts(normed, cotangent, routes, routers, weights, extra):
    rows, width = normed.shape
    part = weights[0].shape[1]
    tile = rows // 4

    def kernel(x_ref, cot_ref, route_ref, router_ref, wg, wu, wd, h_out, dg_out, du_out, branch_out, back_out, gates_out):
        lane = EXPERTS + lax.axis_index("x")
        skip = lax.axis_index("zl") * extra
        x = x_ref[...]
        logits = mm(x, router_ref[...])
        index = lanes(tile)
        gates = dense_gates(logits, chosen(route_ref[...].astype(F32), EXPERTS))
        gates_out[...] = gates
        valid = (lax.broadcasted_iota(jnp.int32, (1, part), 1) >= skip).astype(F32)
        gate = pick(gates, lane) * valid
        gate_part = mm(x, wg[...])
        up_part = mm(x, wu[...])
        sigma = 1.0 / (1.0 + jnp.exp(-gate_part))
        silu = gate_part * sigma
        activated = silu * up_part
        h = (activated * gate).astype(BF)
        h_out[...] = h
        branch_out[...] = mm_nt(h, wd[...]).astype(BF)
        cot_down = mm(cot_ref[...], wd[...])
        dots = jnp.sum(activated * valid * cot_down, axis=1, keepdims=True)
        grad_act = cot_down * gate
        grad_gate = (grad_act * up_part * sigma * (1.0 + gate_part * (1.0 - sigma))).astype(BF)
        grad_up = (grad_act * silu).astype(BF)
        dg_out[...] = grad_gate
        du_out[...] = grad_up
        back_out[:, :width] = (mm_nt(grad_gate, wg[...]) + mm_nt(grad_up, wu[...])).astype(BF)
        back_out[:, width:] = jnp.where(index == lane, dots, 0.0).astype(BF)

    def tiled(cols):
        return pl.BlockSpec((tile, cols), lambda i: (i, 0))

    def whole(array):
        return pl.BlockSpec(array.shape, lambda i: (0, 0), pipeline_mode=pl.Buffered(1))

    cols = [part, part, part, width, width + LANE]
    return pl.pallas_call(
        kernel,
        grid=(4,),
        out_shape=[jax.ShapeDtypeStruct((rows, c), BF) for c in cols]
        + [jax.ShapeDtypeStruct((rows, LANE), F32)],
        in_specs=[tiled(width), tiled(width)]
        + [tiled(LANE), whole(routers)]
        + [whole(w) for w in weights],
        out_specs=[tiled(c) for c in cols] + [tiled(LANE)],
        compiler_params=pltpu.CompilerParams(vmem_limit_bytes=48 << 20),
        cost_estimate=pl.CostEstimate(
            flops=12 * rows * width * part, bytes_accessed=40 << 20, transcendentals=rows * part
        ),
        name="experts",
    )(normed, cotangent, routes, routers, *weights)


def back_through_norm(total, inputs, gain, gates, normed, routers):
    width = inputs.shape[1]
    logits_back = gates_back(gates, total[:, width:])
    full = total[:, :width] + mm_nt(logits_back.astype(BF), routers)
    inner, gain_grad = norm_back(inputs, gain, full)
    return inner, gain_grad, mm_tn(logits_back.astype(BF), normed)[:8]


def row_block(array, block, count):
    cols = array.shape[-1] // 4
    part = array[..., pl.ds(pl.multiple_of(block * cols, cols), cols)]
    return part.reshape(count, cols)


class Pass:
    sems = [pltpu.SemaphoreType.DMA((4,))] * 2

    def __init__(self, src, dst, sems):
        send, recv = sems
        zh, c = lax.axis_index("zh"), lax.axis_index("c")
        mine, far = dst.at[zh, c], dst.at[1 - zh, c]
        self.copies = [
            pltpu.make_async_copy(src, mine, send.at[0]),
            push(src, mine, send.at[1], recv.at[1], {"zh": 1 - zh}),
            push(src, mine, send.at[2], recv.at[2], sibling()),
            push(far, far, send.at[3], recv.at[3], sibling()),
        ]

    def start(self):
        for copy in self.copies[:3]:
            copy.start()

    def finish(self):
        self.copies[1].wait_recv()
        self.copies[3].start()
        self.copies[0].wait()
        self.copies[1].wait_send()
        self.copies[2].wait()
        self.copies[3].wait()


def own_tile():
    zl, x, zh, c = (lax.axis_index(a) for a in TEAM)
    return zl * 4 + x, zh * 2 + c


def middle(collective, back, branch, normed, cotangent, grads, after, gain, gates, routers, cot_own):
    own, width = after.shape
    count, cols = grads[0].shape
    rows = width // 4

    def kernel(
        part_ref, branch_ref, x_ref, cot_ref, d0_ref, d1_ref, d2_ref,
        after_ref, gain_ref, gates_ref, router_ref, own_ref,
        mid_out, small_out, spread_out, s0, s1, g2, out_all,
        x, cot, d0, d1, d2, g0, g1, part_a, part_b, load, total_a, total_b, row_a, row_b, *rest,
    ):
        loads = [
            (x_ref, x), (d0_ref, d0), (part_ref, part_a), (branch_ref, part_b), (d1_ref, d1), (cot_ref, cot), (d2_ref, d2)
        ]
        fetches = [pltpu.make_async_copy(a, b, load.at[k]) for k, (a, b) in enumerate(loads)]
        for fetch in fetches:
            fetch.start()
        meet([place(m) for m in TEAM_MOVES[1:] + [Y_MOVES[1], Y_MOVES[3]]] + [sibling()])
        n = TeamSum.count
        team_a, team_b = TeamSum(part_a, rest[:n]), TeamSum(part_b, rest[n : 2 * n])
        rest = rest[2 * n :]
        n = RingSum.count
        rings = [RingSum(g0, rest[:n]), RingSum(g1, rest[n : 2 * n])]
        rest = rest[2 * n :]
        spread = TeamSpread(row_a, spread_out, rest[:4])
        out = Pass(row_b, out_all, rest[4:6])

        def product(left, right, dst):
            def one(block):
                dst[block] = mm_tn(row_block(left, block, count), right[...]).astype(BF)

            return one

        fetches[0].wait()
        fetches[1].wait()
        rings[0].start_with(product(x, d0, g0))
        fetches[2].wait()
        team_a.swap_all()
        fetches[3].wait()
        team_b.swap_all()
        team_a.add_all()
        fetches[4].wait()
        rings[1].start_with(product(x, d1, g1))
        rings[0].middle()
        team_a.total1(total_a)
        team_b.add_all()
        after = after_ref[...]
        normed_own = (after * rms_scale(after) * gain_ref[...]).astype(BF)
        seq, quarter = own_tile()
        team_a.total2(total_a)
        inner, gain_grad, router_grad = back_through_norm(
            total_a[...], after, gain_ref[...], gates_ref[seq * 4 + quarter], normed_own, router_ref[...]
        )
        grad_mid = own_ref[...].astype(F32) + inner
        mid_out[...] = grad_mid
        row_a[...] = grad_mid.astype(BF)
        spread.start()
        rings[1].middle()
        small_out[:8] = jnp.zeros((8, width), F32)
        small_out[0:1] = gain_grad
        small_out[8:] = router_grad
        fetches[5].wait()
        fetches[6].wait()

        def down(block, _):
            product(cot, d2, g2)(block)
            return 0

        lax.fori_loop(0, 4, down, 0)
        spread.middle()
        team_b.total1(total_b)
        spread.finish()
        team_b.total2(total_b)
        row_b[...] = in_order((after + total_b[...]).astype(BF))
        out.start()
        rings[0].finish(s0)
        rings[1].finish(s1)
        out.finish()
        team_a.close()
        team_b.close()

    return pl.pallas_call(
        kernel,
        out_shape=[
            jax.ShapeDtypeStruct((own, width), F32),
            jax.ShapeDtypeStruct((16, width), F32),
            jax.ShapeDtypeStruct((2, 4, 2, 2, own, width), BF),
            jax.ShapeDtypeStruct((8, rows // 8, cols), BF),
            jax.ShapeDtypeStruct((8, rows // 8, cols), BF),
            jax.ShapeDtypeStruct((4, rows, cols), BF),
            jax.ShapeDtypeStruct((2, 2, own, width), BF),
        ],
        in_specs=[ANY] * 7 + [VMEM] * 5,
        out_specs=[VMEM] * 2 + [ANY] + [VMEM] * 3 + [ANY],
        scratch_shapes=[
            pltpu.VMEM((count, width), BF),
            pltpu.VMEM((count, width), BF),
            pltpu.VMEM((count, cols), BF),
            pltpu.VMEM((count, cols), BF),
            pltpu.VMEM((count, cols), BF),
            pltpu.VMEM((4, rows, cols), BF),
            pltpu.VMEM((4, rows, cols), BF),
            pltpu.VMEM((2, 4, 2, 2, own, width + LANE), BF),
            pltpu.VMEM((2, 4, 2, 2, own, width), BF),
            pltpu.SemaphoreType.DMA((7,)),
            pltpu.VMEM((own, width + LANE), F32),
            pltpu.VMEM((own, width), F32),
            pltpu.VMEM((own, width), BF),
            pltpu.VMEM((own, width), BF),
        ]
        + TeamSum.scratch(own, width + LANE)
        + TeamSum.scratch(own, width)
        + RingSum.scratch(rows, cols) * 2
        + TeamSpread.sems
        + Pass.sems,
        name="middle",
        **settings(collective, 200 << 20, 58),
    )(
        back.reshape(2, 4, 2, 2, own, width + LANE), branch.reshape(2, 4, 2, 2, own, width),
        normed, cotangent, *grads, after, gain, gates.reshape(-1, own, LANE), routers, cot_own,
    )


def in_order(values):
    block = values.shape[1] // 8
    order = [(b % 4) * 2 + b // 4 for b in range(8)]
    return jnp.concatenate([values[:, k * block : (k + 1) * block] for k in order], axis=1)


def attn_backward(
    collective, grad_mid, qkv, gated, normed, gates, weights, cosines, sines, mid_own, inputs, gain, routers, small, summed, grads
):
    own, width = inputs.shape
    seq = qkv.shape[1]
    rows, cols = grads.shape[1:]
    shard = rows // 8
    scale = HEAD ** (-0.5)
    stages = [X_MOVES, Y_MOVES, Z_MOVES]

    def kernel(
        gm_ref, w_ref, x_ref, g2_ref, y0, y1, qkv_ref, gated_ref, gates_ref, cos_ref, sin_ref,
        mid_ref, in_ref, gain_ref, router_ref, small_ref,
        grad_all, small_out, s0, s1, s2, s3,
        gm, w, x, g2, g3, y2, y3, proj, part, load, total, row,
        acc, got, other, rest_rows, csem, ssend, srecv, *rest,
    ):
        loads = [(gm_ref, gm), (w_ref, w), (g2_ref, g2), (x_ref, x)]
        fetches = [pltpu.make_async_copy(a, b, load.at[k]) for k, (a, b) in enumerate(loads)]
        for fetch in fetches:
            fetch.start()
        meet([place(m) for m in TEAM_MOVES[1:] + Y_MOVES[1:]] + [sibling()])
        n = TeamSum.count
        team, rest = TeamSum(part, rest[:n]), rest[n:]
        n = RingSum.count
        rings, rest = [RingSum(g2, rest[:n]), RingSum(g3, rest[n : 2 * n])], rest[2 * n :]
        swaps_back = [
            Swap(y, s, rest[2 * k : 2 * k + 2]) for k, (y, s) in enumerate(((y0, s0), (y1, s1), (y2, s2)))
        ]
        last_swap = ColumnSwap(y3, s3, rest[6:8])
        out = Pass(row, grad_all, rest[8:10])
        first = 2 * team.zl
        causal = causal_mask(2, seq)
        swaps_back[0].start()
        swaps_back[1].start()
        fetches[0].wait()
        fetches[1].wait()

        def step(i, _):
            pair = team.pair(i)
            grads = mm(gm[pl.ds(pair * 2, 2)].reshape(2 * seq, width), w[:, 4 * HEAD :])
            both = []
            for j in range(2):
                at = pair * 2 + j
                here = slice(j * seq, (j + 1) * seq)
                query = jnp.concatenate(
                    [qkv_ref[at, :, e * HEAD : (e + 1) * HEAD] for e in range(2)], axis=0
                )
                key = qkv_ref[at, :, 2 * HEAD : 3 * HEAD]
                value = qkv_ref[at, :, 3 * HEAD :]
                probs = soft(mm_nt(query, key) * scale, causal)
                probs_b = probs.astype(BF)
                attended = mm(probs_b, value)
                grad = jnp.concatenate(
                    [grads[here, e * HEAD : (e + 1) * HEAD] for e in range(2)], axis=0
                )
                gates = gates_ref[at]
                gate = jnp.concatenate([pick(gates, first + e) for e in range(2)], axis=0)
                each = jnp.sum(attended * grad, axis=1, keepdims=True)
                dots = jnp.where(lanes(seq) == first, each[:seq], 0.0)
                dots += jnp.where(lanes(seq) == first + 1, each[seq:], 0.0)
                grad = (grad * gate).astype(BF)
                grad_probs = mm_nt(grad, value)
                inner = jnp.sum(probs * grad_probs, axis=1, keepdims=True)
                grad_scores = (probs * (grad_probs - inner) * scale).astype(BF)
                turned = [mm(grad_scores, key), mm_tn(grad_scores, query)]
                turned = [turned[0][:seq], turned[0][seq:], turned[1]]
                turned = [rotate(t, cos_ref[...], -sin_ref[...]).astype(BF) for t in turned]
                grad_value = mm_tn(probs_b, grad).astype(BF)
                both.append(jnp.concatenate(turned + [grad_value], axis=1))
                proj[at] = both[-1]
                part[pair // 2, lax.rem(pair, 2) * 2 + j, :, :, :, width:] = dots.astype(BF).reshape(
                    2, 2, own, LANE
                )
            back = mm_nt(jnp.concatenate(both, axis=0), w[:, : 4 * HEAD])
            part[pair // 2, pl.ds(lax.rem(pair, 2) * 2, 2), :, :, :, :width] = back.astype(BF).reshape(
                2, 2, 2, own, width
            )
            for j in range(2):
                team.swap(pair * 2 + j).start()

            @pl.when(i == 0)
            def _():
                fetches[2].wait()
                rings[0].start()

            @pl.when(i > 0)
            def _():
                team.add_pair(i - 1)

            @pl.when(i == 2)
            def _():
                team.send_far_z()

            @pl.when(i == 3)
            def _():
                team.send_far_x()

            return 0

        lax.fori_loop(0, 4, step, 0)
        team.last()
        fetches[3].wait()

        def product(block):
            g3[block, :, : 4 * HEAD] = mm_tn(
                row_block(x, block, 8 * seq), proj[...].reshape(8 * seq, 4 * HEAD)
            ).astype(BF)
            g3[block, :, 4 * HEAD :] = mm_tn(
                row_block(gm, block, 8 * seq), gated_ref[...].reshape(8 * seq, 2 * HEAD)
            ).astype(BF)

        rings[1].start_with(product)
        rings[0].middle()
        inputs = in_ref[...].astype(F32)
        normed_own = (inputs * rms_scale(inputs) * gain_ref[...]).astype(BF)
        own_seq, quarter = own_tile()
        gates_own = gates_ref[own_seq, pl.ds(pl.multiple_of(quarter * own, own), own)]
        team.total1(total)
        rings[1].middle()
        team.total2(total)
        inner, gain_grad, router_grad = back_through_norm(
            total[...], inputs, gain_ref[...], gates_own, normed_own, router_ref[...]
        )
        row[...] = in_order((mid_ref[...] + inner).astype(BF))
        out.start()
        acc[...] = small_ref[...]
        acc[1:2] = gain_grad
        acc[8:] += router_grad
        c = lax.axis_index("c")
        half = pl.ds(pl.multiple_of(c * 8, 8), 8)
        rest_half = pl.ds(pl.multiple_of((1 - c) * 8, 8), 8)
        over = push(acc.at[rest_half], other, csem.at[0], csem.at[1], sibling())
        over.start()
        over.wait()
        acc[half] = acc[half] + other[...]
        for s, stage in enumerate(stages):
            swaps = [
                push(acc.at[half], got.at[s, k - 1], ssend.at[s, k], srecv.at[s, k], place(stage[k]))
                for k in range(1, 4)
            ]
            for swap in swaps:
                swap.start()
            if s == 0:
                rings[0].finish(y2)
                swaps_back[2].start()
            for swap in swaps:
                swap.wait()
            acc[half] = acc[half] + got[s, 0] + got[s, 1] + got[s, 2]
        back_over = push(acc.at[half], rest_rows, csem.at[2], csem.at[3], sibling())
        back_over.start()
        small_out[half] = in_order(acc[half])
        rings[1].finish(y3)
        last_swap.start()
        out.finish()
        back_over.wait()
        small_out[rest_half] = in_order(rest_rows[...])
        for swap in swaps_back + [last_swap]:
            swap.finish()
        team.close()

    block = jax.ShapeDtypeStruct((8, shard, cols), BF)
    heads = cols // HEAD
    return pl.pallas_call(
        kernel,
        out_shape=[
            jax.ShapeDtypeStruct((2, 2, own, width), BF),
            jax.ShapeDtypeStruct((16, width), F32),
            block, block, block,
            jax.ShapeDtypeStruct((2, heads, shard, 4 * HEAD), BF),
        ],
        in_specs=[ANY] * 6 + [VMEM] * 10,
        out_specs=[ANY, VMEM] + [ANY] * 4,
        scratch_shapes=[
            pltpu.VMEM((8, seq, width), BF),
            pltpu.VMEM(weights.shape, BF),
            pltpu.VMEM((8, seq, width), BF),
            pltpu.VMEM((4, rows, cols), BF),
            pltpu.VMEM((4, rows, cols), BF),
            pltpu.VMEM((8, shard, cols), BF),
            pltpu.VMEM((8, heads, shard, HEAD), BF),
            pltpu.VMEM((8, seq, 4 * HEAD), BF),
            pltpu.VMEM((2, 4, 2, 2, own, width + LANE), BF),
            pltpu.SemaphoreType.DMA((4,)),
            pltpu.VMEM((own, width + LANE), F32),
            pltpu.VMEM((own, width), BF),
            pltpu.VMEM((16, width), F32),
            pltpu.VMEM((3, 3, 8, width), F32),
            pltpu.VMEM((8, width), F32),
            pltpu.VMEM((8, width), F32),
            pltpu.SemaphoreType.DMA((4,)),
        ]
        + [pltpu.SemaphoreType.DMA((4, 4))] * 2
        + TeamSum.scratch(own, width + LANE)
        + RingSum.scratch(rows, cols) * 2
        + Swap.sems * 4
        + Pass.sems,
        name="attn_backward",
        **settings(collective, 200 << 20, 58),
    )(
        grad_mid.reshape(8, seq, width), weights, normed, grads, *summed, qkv, gated, gates, cosines, sines,
        mid_own, inputs, gain, routers, small,
    )


def reorder(array, axis):
    shape = array.shape
    split = shape[:axis] + (2, 4, shape[axis] // 8) + shape[axis + 1 :]
    return jnp.swapaxes(array.reshape(split), axis, axis + 1).reshape(shape)


def local(
    hidden,
    cotangent,
    attn_gain,
    attn_router,
    qkv_weight,
    out_weight,
    mlp_gain,
    mlp_router,
    gate_up_weight,
    down_weight,
    attn_route,
    attn_slot,
    mlp_route,
    mlp_slot,
):
    seq, width = hidden.shape
    rows = qkv_weight.shape[0]
    features = down_weight.shape[2]
    part = (features // LANE + 1) // 2 * LANE
    low = features - part
    quarter = lax.axis_index("zh") * 2 + lax.axis_index("c")
    own = seq // 4
    group = 8 * seq
    cosines, sines = rope_tables(seq)

    query_blocks = qkv_weight[:, :EXPERTS].reshape(rows, 2, 2, 4, HEAD).transpose(1, 3, 0, 2, 4)
    kv_blocks = qkv_weight[:, EXPERTS:].reshape(rows, 2, 4, HEAD).transpose(2, 0, 1, 3)
    kv_blocks = jnp.broadcast_to(kv_blocks[None], (2,) + kv_blocks.shape)
    out_blocks = out_weight.reshape(rows, 2, 2, 4, HEAD).transpose(1, 3, 0, 2, 4)
    attn_blocks = jnp.concatenate([query_blocks, kv_blocks, out_blocks], axis=3)
    attn_blocks = attn_blocks.reshape(8, rows, 6 * HEAD)

    def by_target(weight):
        weight = weight.transpose(1, 0, 2)
        return jnp.stack([weight[..., :part], weight[..., low:]], axis=0).reshape(8, rows, part)

    mlp_blocks = [
        by_target(w) for w in (gate_up_weight[:, :, 0], gate_up_weight[:, :, 1], down_weight)
    ]

    attn_gain, mlp_gain = reorder(attn_gain, 0)[None], reorder(mlp_gain, 0)[None]
    routers = reorder(jnp.concatenate([attn_router, mlp_router], axis=1), 0)
    routers = jnp.pad(routers, ((0, 0), (0, LANE - 2 * EXPERTS)))

    def quarter_of(array):
        return lax.dynamic_slice_in_dim(array, quarter * own, own, axis=0)

    hidden_own = reorder(quarter_of(hidden), 1)
    cot_own = reorder(quarter_of(cotangent), 1)
    no_routes = jnp.zeros((own, 2), jnp.int32)
    routes = [quarter_of(attn_route), no_routes, quarter_of(mlp_route)]
    routes = jnp.pad(jnp.concatenate(routes, axis=1), ((0, 0), (0, LANE - 6)))
    entering = jnp.concatenate([hidden_own, routes.astype(BF)], axis=1)
    attn_w, normed_a, qkv, gated_att, gates_a, group_routes, after, normed_m, group_cot, *mlp_w = attn_forward(
        1, attn_blocks, mlp_blocks, entering, cot_own, attn_gain, routers, cosines, sines, mlp_gain, hidden_own
    )
    attn_w = attn_w.reshape(width, 6 * HEAD)
    mlp_w = [w.reshape(width, part) for w in mlp_w]
    group_cot = group_cot.reshape(group, width)
    normed_m = normed_m.reshape(group, width)

    h, grad_gate, grad_up, branch_m, back_m, gates_m = experts(
        normed_m, group_cot, group_routes.reshape(group, LANE), routers, mlp_w, 2 * part - features
    )
    grad_mid_own, small_m, grad_mid, gate_sum, up_sum, down_part, out_hidden = middle(
        2, back_m, branch_m, normed_m, group_cot, [grad_gate, grad_up, h], after, mlp_gain, gates_m, routers, cot_own
    )
    grad_in, small, *mlp_grads, attn_grads = attn_backward(
        3, grad_mid, qkv, gated_att, normed_a, gates_a, attn_w, cosines, sines, grad_mid_own, hidden_own, attn_gain,
        routers, small_m, [gate_sum, up_sum], down_part,
    )
    out_hidden = out_hidden.reshape(seq, width)
    grad_in = grad_in.reshape(seq, width).astype(F32)

    attn_grads = attn_grads.astype(F32)
    query_grad = attn_grads[:, :2].reshape(EXPERTS, rows, 4 * HEAD)
    kv_grad = attn_grads[0, 2:4] + attn_grads[1, 2:4]
    qkv_grad = jnp.concatenate([query_grad, kv_grad], axis=0).transpose(1, 0, 2)
    out_grad = attn_grads[:, 4:].reshape(EXPERTS, rows, 4 * HEAD).transpose(1, 0, 2)

    def placed_back(grad):
        grad = grad.reshape(2, EXPERTS, rows, part)
        return jnp.concatenate([grad[0], grad[1, ..., 2 * part - features :]], axis=-1).transpose(1, 0, 2)

    gate_grad, up_grad, down_grad = [placed_back(g) for g in mlp_grads]
    return (
        out_hidden,
        grad_in,
        small[1],
        small[8 : 8 + EXPERTS].T,
        qkv_grad,
        out_grad,
        small[0],
        small[8 + EXPERTS :].T,
        jnp.stack([gate_grad, up_grad], axis=2).astype(F32),
        down_grad.astype(F32),
    )


def solution(mesh):
    fine = Mesh(mesh.devices.reshape(2, 4, 4, 2, 2), ALL)
    dp, tensor = ("zl", "y", "x"), ("zh", "c")
    placed = (
        P(dp, None),
        P(dp, None),
        P(),
        P(),
        P(dp, None, tensor),
        P(dp, None, tensor),
        P(),
        P(),
        P(dp, None, None, tensor),
        P(dp, None, tensor),
        P(dp, None),
        P(dp, None),
        P(dp, None),
        P(dp, None),
    )
    return jax.shard_map(
        local,
        mesh=fine,
        in_specs=placed,
        out_specs=(
            P(dp, None),
            P(dp, None),
            P(),
            P(),
            P(dp, None, tensor),
            P(dp, None, tensor),
            P(),
            P(),
            P(dp, None, None, tensor),
            P(dp, None, tensor),
        ),
        check_vma=False,
    )
```

```python
import itertools

import jax
import jax.numpy as jnp
import numpy as np
from jax import lax
from jax.experimental import pallas as pl
from jax.experimental.pallas import tpu as pltpu
from jax.sharding import Mesh, PartitionSpec as P

HEAD = 128
LANE = 128
EPS = 1e-05
THETA = 10000.0
NEG = -1e30
EXPERTS = 4
GROUP = ("zl", "x")
TEAM = ("zl", "x", "zh", "c")
ALL = ("zl", "y", "x", "zh", "c")
SIZES = dict(zl=2, y=4, x=4, zh=2, c=2)
BF = jnp.bfloat16
F32 = jnp.float32
MESH = pl.DeviceIdType.MESH
ANY = pl.BlockSpec(memory_space=pl.ANY)
VMEM = pl.BlockSpec(memory_space=pltpu.VMEM)


def dot(a, b, dims):
    return lax.dot_general(a, b, (dims, ((), ())), preferred_element_type=F32)


def mm(a, b):
    return dot(a, b, ((1,), (0,)))


def mm_nt(a, b):
    return dot(a, b, ((1,), (1,)))


def mm_tn(a, b):
    return dot(a, b, ((0,), (0,)))


def rms_scale(values):
    return lax.rsqrt(jnp.mean(values * values, axis=-1, keepdims=True) + EPS)


def lanes(rows):
    return lax.broadcasted_iota(jnp.int32, (rows, LANE), 1)


def chosen(routes, first):
    lane = lanes(routes.shape[0])
    named = [pick(routes, first + c).astype(jnp.int32) + first for c in range(2)]
    return (lane == named[0]) | (lane == named[1])


def dense_gates(logits, mask):
    top = jnp.max(jnp.where(mask, logits, NEG), axis=1, keepdims=True)
    expon = jnp.where(mask, jnp.exp(jnp.where(mask, logits - top, 0.0)), 0.0)
    return expon / jnp.sum(expon, axis=1, keepdims=True)


def pick(values, lane):
    return jnp.sum(jnp.where(lanes(values.shape[0]) == lane, values, 0.0), axis=1, keepdims=True)


def gates_back(gates, dots):
    return gates * (dots - jnp.sum(gates * dots, axis=1, keepdims=True))


def rope_tables(count):
    frequency = THETA ** (-(np.arange(HEAD // 2).astype(np.float32) * 2.0 / HEAD))
    angles = np.arange(count).astype(np.float32)[:, None] * frequency[None, :].astype(np.float32)
    cosines, sines = np.cos(angles), np.sin(angles)
    return (
        jnp.asarray(np.concatenate([cosines, cosines], axis=1), F32),
        jnp.asarray(np.concatenate([-sines, sines], axis=1), F32),
    )


def rotate(values, cosines, sines):
    return values * cosines + pltpu.roll(values, HEAD // 2, 1) * sines


def norm_back(inputs, gain, grad_normed):
    scale = rms_scale(inputs)
    scaled = inputs * scale
    grad_scaled = grad_normed * gain
    grad_inputs = scale * (
        grad_scaled - scaled * jnp.mean(grad_scaled * scaled, axis=-1, keepdims=True)
    )
    return grad_inputs, jnp.sum(grad_normed * scaled, axis=0, keepdims=True)


def moves(*axes):
    return [dict(zip(axes, steps)) for steps in itertools.product(*[range(SIZES[a]) for a in axes])]


def place(move, sign=1):
    return {a: lax.rem(lax.axis_index(a) + sign * v + SIZES[a], SIZES[a]) for a, v in move.items()}


def number(coords):
    total = 0
    for axis, value in coords.items():
        total = total * SIZES[axis] + value
    return total


def meet(partners):
    barrier = pltpu.get_barrier_semaphore()
    for partner in partners:
        pl.semaphore_signal(barrier, inc=1, device_id=partner, device_id_type=MESH)
    pl.semaphore_wait(barrier, len(partners))


def push(src, dst, send, recv, to):
    return pltpu.make_async_remote_copy(
        src_ref=src, dst_ref=dst, send_sem=send, recv_sem=recv, device_id=to, device_id_type=MESH
    )


def settings(number, moved, vmem=32):
    return dict(
        compiler_params=pltpu.CompilerParams(
            collective_id=number, has_side_effects=True, vmem_limit_bytes=vmem << 20
        ),
        cost_estimate=pl.CostEstimate(flops=0, bytes_accessed=moved, transcendentals=0),
    )


GROUP_MOVES = moves("zl", "x")
TEAM_MOVES = moves("zl", "x", "zh")
X_MOVES = moves("x")
Y_MOVES = moves("y")
Z_MOVES = moves("zl", "zh")


def sibling():
    return {"c": 1 - lax.axis_index("c")}


class RingY:
    sems = [pltpu.SemaphoreType.DMA((5,)), pltpu.SemaphoreType.DMA((5,))]

    def __init__(self, src, out, sems):
        self.src, self.out = src, out
        self.send, self.recv = sems
        self.y = lax.axis_index("y")
        self.half = src.shape[0] // 2

    def line(self, step):
        return lax.rem(self.y + step, 4)

    def copy(self, k):
        y = self.y
        if k < 2:
            src, dst, to = self.src, self.out.at[y], self.line((1, 3)[k])
        else:
            half = pl.ds((k - 2) * self.half, self.half)
            src = dst = self.out.at[self.line((3, 1)[k - 2]), half]
            to = self.line((1, 3)[k - 2])
        return push(src, dst, self.send.at[k], self.recv.at[k], {"y": to})

    def start(self):
        self.stay = pltpu.make_async_copy(self.src, self.out.at[self.y], self.send.at[4])
        for k in range(2):
            self.copy(k).start()
        self.stay.start()

    def forward(self):
        for k in range(2):
            self.copy(k).wait_recv()
            self.copy(k + 2).start()

    def finish(self):
        for k in range(2):
            self.copy(k + 2).wait_recv()
        for k in range(4):
            self.copy(k).wait_send()
        self.stay.wait()


class Swap:
    sems = [pltpu.SemaphoreType.DMA((8,))] * 2

    def __init__(self, src, dst, sems):
        self.src, self.dst = src, dst
        self.send, self.recv = sems

    def start(self):
        me = number(place(GROUP_MOVES[0]))
        self.copies = [
            pltpu.make_async_copy(self.src.at[me], self.dst.at[me], self.send.at[0])
        ]
        for k, move in enumerate(GROUP_MOVES):
            if k:
                to = place(move)
                self.copies.append(
                    push(
                        self.src.at[number(to)],
                        self.dst.at[me],
                        self.send.at[k],
                        self.recv.at[k],
                        to,
                    )
                )
        for copy in self.copies:
            copy.start()

    def finish(self):
        for copy in self.copies:
            copy.wait()


class ColumnSwap(Swap):
    def start(self):
        zl, x = lax.axis_index("zl"), lax.axis_index("x")
        mine = self.dst.at[zl, :, :, pl.ds(pl.multiple_of(x * HEAD, HEAD), HEAD)]
        self.copies = [
            pltpu.make_async_copy(self.src.at[zl * 4 + x], mine, self.send.at[0])
        ]
        for k, move in enumerate(GROUP_MOVES):
            if k:
                to = place(move)
                block = self.src.at[number(to)]
                self.copies.append(push(block, mine, self.send.at[k], self.recv.at[k], to))
        for copy in self.copies:
            copy.start()


class RingSum:
    @staticmethod
    def scratch(rows, cols):
        return [
            pltpu.VMEM((2, rows // 2, cols), BF),
            pltpu.VMEM((2, rows // 2, cols), BF),
            pltpu.VMEM((2, rows, cols), BF),
            pltpu.SemaphoreType.DMA((6,)),
            pltpu.SemaphoreType.DMA((6,)),
        ]

    count = 5

    def __init__(self, part, scratch):
        self.part = part
        self.got, self.mix, self.sums, self.send, self.recv = scratch
        self.y = lax.axis_index("y")
        half = part.shape[1] // 2
        self.halves = [pl.ds(0, half), pl.ds(half, half)]

    def line(self, step):
        return lax.rem(self.y + step, 4)

    def copy(self, k):
        kind, way = k // 2, k % 2
        step = (1, 3)[way]
        top, low = self.halves[way], self.halves[1 - way]
        if kind == 0:
            src, dst = self.part.at[self.line(2), top], self.got.at[way]
        elif kind == 1:
            src, dst = self.part.at[self.line(step), low], self.sums.at[way, low]
        else:
            src, dst = self.mix.at[way], self.sums.at[way, top]
        return push(src, dst, self.send.at[k], self.recv.at[k], {"y": self.line(step)})

    def start(self):
        for k in range(4):
            self.copy(k).start()

    def start_with(self, product):
        product(self.line(2))
        self.copy(0).start()
        self.copy(1).start()
        product(self.line(1))
        self.copy(2).start()
        product(self.line(3))
        self.copy(3).start()
        product(self.y)

    def middle(self):
        for way in range(2):
            self.copy(way).wait_recv()
            mine = self.part[self.line((1, 3)[way]), self.halves[way]].astype(F32)
            self.mix[way] = (mine + self.got[way].astype(F32)).astype(BF)
            self.copy(4 + way).start()

    def finish(self, out):
        for k in range(2, 6):
            self.copy(k).wait_recv()
        total = self.part[self.y].astype(F32) + self.sums[0].astype(F32) + self.sums[1].astype(F32)
        total = total.astype(BF)
        if len(out.shape) == 3:
            out[...] = total.reshape(out.shape)
        else:
            targets, count, rows, cols = out.shape
            for t in range(targets):
                for n in range(count):
                    out[t, n] = total[t * rows : (t + 1) * rows, n * cols : (n + 1) * cols]
        for k in range(6):
            self.copy(k).wait_send()


class TeamSum:
    @staticmethod
    def scratch(own, width):
        half = own // 2
        return [
            pltpu.VMEM((8, 2, own, width), BF),
            pltpu.VMEM((3, 2, 2, half, width), BF),
            pltpu.VMEM((3, 4, half, width), BF),
            pltpu.VMEM((6, half, width), BF),
            pltpu.SemaphoreType.DMA((8,)),
            pltpu.SemaphoreType.DMA((8,)),
            pltpu.SemaphoreType.DMA((6,)),
            pltpu.SemaphoreType.DMA((6,)),
            pltpu.SemaphoreType.DMA((6,)),
            pltpu.SemaphoreType.DMA((6,)),
        ]

    count = 10

    def __init__(self, part, scratch):
        self.part = part
        self.other, self.got_x, self.got_z, self.late = scratch[:4]
        self.ssem, self.rsem, self.send1, self.recv1, self.send2, self.recv2 = scratch[4:]
        self.zl, self.x, self.zh, self.c = (lax.axis_index(a) for a in TEAM)
        self.half = part.shape[4] // 2
        self.top, self.low = pl.ds(0, self.half), pl.ds(self.half, self.half)

    def swap(self, seq):
        return push(
            self.part.at[seq // 4, lax.rem(seq, 4), :, 1 - self.c],
            self.other.at[seq],
            self.ssem.at[seq],
            self.rsem.at[seq],
            sibling(),
        )

    def send_x(self, x):
        slot = lax.rem(x - self.x + 4, 4) - 1
        return push(
            self.part.at[:, x, :, self.c, self.top],
            self.got_x.at[slot],
            self.send1.at[slot],
            self.recv1.at[slot],
            {"x": x},
        )

    def send_z(self, zl, zh):
        slot = lax.rem(zl - self.zl + 2, 2) * 2 + lax.rem(zh - self.zh + 2, 2) - 1
        return push(
            self.part.at[zl, :, zh, self.c, self.low],
            self.got_z.at[slot],
            self.send1.at[3 + slot],
            self.recv1.at[3 + slot],
            {"zl": zl, "zh": zh},
        )

    def late_z(self, k):
        to = place(Z_MOVES[k])
        return push(
            self.part.at[to["zl"], self.x, to["zh"], self.c, self.top],
            self.late.at[k - 1],
            self.send2.at[k - 1],
            self.recv2.at[k - 1],
            to,
        )

    def late_x(self, k):
        to = place(X_MOVES[k])
        return push(
            self.part.at[self.zl, to["x"], self.zh, self.c, self.low],
            self.late.at[2 + k],
            self.send2.at[2 + k],
            self.recv2.at[2 + k],
            to,
        )

    def add(self, seq):
        self.swap(seq).wait_recv()
        zl, x = seq // 4, lax.rem(seq, 4)
        for zh in range(2):
            mine = self.part[zl, x, zh, self.c].astype(F32)
            self.part[zl, x, zh, self.c] = (mine + self.other[seq, zh].astype(F32)).astype(BF)

    def pair(self, step):
        back = 3 - step
        return lax.rem(self.zl + back // 2, 2) * 2 + lax.rem(self.x // 2 + back, 2)

    def add_pair(self, step):
        for j in range(2):
            self.add(self.pair(step) * 2 + j)

    def send_far_z(self):
        for zh in range(2):
            self.send_z(1 - self.zl, zh).start()

    def send_far_x(self):
        for j in range(2):
            self.send_x((1 - self.x // 2) * 2 + j).start()

    def last(self):
        self.add_pair(3)
        self.send_x(self.x + 1 - 2 * lax.rem(self.x, 2)).start()
        self.send_z(self.zl, 1 - self.zh).start()

    def got(self, ref, sem):
        pltpu.make_async_copy(ref, ref, sem).wait()

    def total(self, total_ref):
        self.total1(total_ref)
        self.total2(total_ref)

    def total1(self, total_ref):
        half, c = self.half, self.c
        for k in range(3):
            self.got(self.got_x.at[k], self.recv1.at[k])
        for k, move in reversed(list(enumerate(Z_MOVES))):
            at = place(move)
            rows = self.part[at["zl"], self.x, at["zh"], c, :half].astype(F32)
            for j in range(3):
                rows += self.got_x[j, at["zl"], at["zh"]].astype(F32)
            if k:
                self.part[at["zl"], self.x, at["zh"], c, :half] = rows.astype(BF)
                self.late_z(k).start()
            else:
                total_ref[:half] = rows
        for k in range(3):
            self.got(self.got_z.at[k], self.recv1.at[3 + k])
        for k, move in reversed(list(enumerate(X_MOVES))):
            at = place(move)
            rows = self.part[self.zl, at["x"], self.zh, c, half:].astype(F32)
            for j in range(3):
                rows += self.got_z[j, at["x"]].astype(F32)
            if k:
                self.part[self.zl, at["x"], self.zh, c, half:] = rows.astype(BF)
                self.late_x(k).start()
            else:
                total_ref[half:] = rows

    def total2(self, total_ref):
        half = self.half
        for k in range(3):
            self.got(self.late.at[k], self.recv2.at[k])
            total_ref[:half] += self.late[k].astype(F32)
        for k in range(3):
            self.got(self.late.at[3 + k], self.recv2.at[3 + k])
            total_ref[half:] += self.late[3 + k].astype(F32)

    def close(self):
        for seq in range(8):
            self.swap(seq).wait_send()
        for k in range(1, 4):
            x, z = place(X_MOVES[k])["x"], place(Z_MOVES[k])
            self.send_x(x).wait_send()
            self.send_z(z["zl"], z["zh"]).wait_send()
            self.late_z(k).wait_send()
            self.late_x(k).wait_send()

    def swap_all(self):
        for step in range(4):
            for j in range(2):
                self.swap(self.pair(step) * 2 + j).start()

    def add_all(self):
        self.add_pair(0)
        self.add_pair(1)
        self.send_far_z()
        self.add_pair(2)
        self.send_far_x()
        self.last()


class TeamSpread:
    sems = [pltpu.SemaphoreType.DMA((12,))] * 2 + [pltpu.SemaphoreType.DMA((9,))] * 2

    def __init__(self, rows, out, sems):
        self.rows, self.out = rows, out
        self.send, self.recv, self.fsend, self.frecv = sems
        self.zl, self.x, self.zh, self.c = (lax.axis_index(a) for a in TEAM)
        self.half = rows.shape[0] // 2
        self.top, self.low = pl.ds(0, self.half), pl.ds(self.half, self.half)

    def tops(self, zl, zh):
        return self.out.at[zl, :, zh, self.c, self.top]

    def lows(self, x):
        return self.out.at[:, x, :, self.c, self.low]

    def hop(self, k, src, dst, to):
        return push(src, dst, self.send.at[k], self.recv.at[k], to)

    def first(self, k):
        here = (self.zl, self.x, self.zh, self.c)
        if k < 3:
            return self.hop(k, self.rows.at[self.top], self.out.at[(*here, self.top)], place(X_MOVES[k + 1]))
        return self.hop(k, self.rows.at[self.low], self.out.at[(*here, self.low)], place(Z_MOVES[k - 2]))

    def second(self, k):
        if k < 3:
            block = self.tops(self.zl, self.zh)
            return self.hop(6 + k, block, block, place(Z_MOVES[k + 1]))
        block = self.lows(self.x)
        return self.hop(6 + k, block, block, place(X_MOVES[k - 2]))

    def forward(self, k, block):
        return push(block, block, self.fsend.at[k], self.frecv.at[k], sibling())

    def start(self):
        self.stay = pltpu.make_async_copy(
            self.rows, self.out.at[self.zl, self.x, self.zh, self.c], self.fsend.at[8]
        )
        for k in range(6):
            self.first(k).start()
        self.stay.start()

    def middle(self):
        self.stay.wait()
        for k in range(3):
            self.first(k).wait_recv()
        for k in range(3):
            self.second(k).start()
        self.forward(0, self.tops(self.zl, self.zh)).start()
        for k in range(3, 6):
            self.first(k).wait_recv()
        for k in range(3, 6):
            self.second(k).start()
        self.forward(1, self.lows(self.x)).start()

    def block(self, k):
        if k < 3:
            at = place(Z_MOVES[k + 1], -1)
            return self.tops(at["zl"], at["zh"])
        return self.lows(place(X_MOVES[k - 2], -1)["x"])

    def finish(self):
        for k in range(6):
            self.second(k).wait_recv()
            self.forward(2 + k, self.block(k)).start()
        blocks = [self.tops(self.zl, self.zh), self.lows(self.x)] + [self.block(k) for k in range(6)]
        for k in range(8):
            self.forward(k, blocks[k]).wait()
        for k in range(6):
            self.first(k).wait_send()
            self.second(k).wait_send()


def soft(scores, causal):
    scores = jnp.where(causal, scores, NEG)
    expon = jnp.exp(scores - jnp.max(scores, axis=-1, keepdims=True))
    return expon / jnp.sum(expon, axis=-1, keepdims=True)


def causal_mask(copies, seq):
    rows = lax.rem(lax.broadcasted_iota(jnp.int32, (copies * seq, seq), 0), seq)
    return lax.broadcasted_iota(jnp.int32, (copies * seq, seq), 1) <= rows


def attn_forward(
    collective, attn_blocks, blocks, hidden, cotangent, routes, small, cosines, sines
):
    seq, width = hidden.shape
    own = seq // 4
    piece = width // 8
    scale = HEAD ** (-0.5)

    def kernel(
        a_ref, b0, b1, b2, hidden_ref, cotangent_ref, route_ref, small_ref, cos_ref, sin_ref,
        w_out, normed_out, qkv_out, gated_out, gates_out, routes_out, after_out, enter_row, cot_row, router_ref,
        spread_out, cot_out, w0, w1, w2, a_mid, m0, m1, m2,
        load, hid, part, total, row, *rest,
    ):
        mine = pl.ds(pl.multiple_of((lax.axis_index("zh") * 2 + lax.axis_index("c")) * own, own), own)
        loads = []
        for b in range(8):
            here, there = pl.ds(b * piece, piece), pl.ds(((b % 4) * 2 + b // 4) * piece, piece)
            loads.append((hidden_ref.at[mine, here], enter_row.at[:, there]))
            loads.append((cotangent_ref.at[mine, here], cot_row.at[:, there]))
        loads.append((route_ref.at[mine], enter_row.at[:, pl.ds(width, LANE)]))
        fetches = [pltpu.make_async_copy(a, b, load.at[k]) for k, (a, b) in enumerate(loads)]
        for fetch in fetches:
            fetch.start()
        meet([place(m) for m in TEAM_MOVES[1:] + [Y_MOVES[1], Y_MOVES[3]]] + [sibling()])
        n = TeamSum.count
        team, rest = TeamSum(part, rest[:n]), rest[n:]
        enters = TeamSpread(enter_row, hid, rest[:4])
        cot = TeamSpread(cot_row, cot_out, rest[4:8])
        spread = TeamSpread(row, spread_out, rest[8:12])
        rest = rest[12:]
        swaps = [
            Swap(b, m, rest[2 * k : 2 * k + 2])
            for k, (b, m) in enumerate(((a_ref, a_mid), (b0, m0), (b1, m1), (b2, m2)))
        ]
        rings = [
            RingY(m, w, rest[8 + 2 * k : 10 + 2 * k])
            for k, (m, w) in enumerate(((a_mid, w_out), (m0, w0), (m1, w1), (m2, w2)))
        ]
        swaps[0].start()
        for fetch in fetches:
            fetch.wait()
        enters.start()
        router_ref[...] = jnp.zeros_like(router_ref)
        router_ref[:8] = small_ref[8:].astype(BF)
        swaps[0].finish()
        rings[0].start()
        swaps[1].start()
        enters.middle()
        swaps[2].start()
        rings[0].forward()
        swaps[1].finish()
        rings[1].start()
        swaps[3].start()
        enters.finish()
        rings[0].finish()
        first = 2 * team.zl
        causal = causal_mask(2, seq)

        def step(i, _):
            pair = team.pair(i)
            zl, x = pair // 2, lax.rem(pair, 2) * 2
            routes = []
            for j in range(2):
                entered = hid[zl, x + j].reshape(seq, width + LANE)
                values = entered[:, :width].astype(F32)
                normed_out[pair * 2 + j] = (values * rms_scale(values) * small_ref[0:1]).astype(BF)
                routes.append(entered[:, width:])
                routes_out[pair * 2 + j] = routes[j]
            normed = normed_out[pl.ds(pair * 2, 2)].reshape(2 * seq, width)
            weights = w_out.reshape(width, 6 * HEAD)
            logits = mm_nt(normed, router_ref[...])
            proj = mm(normed, weights[:, : 4 * HEAD])
            gates = dense_gates(logits, chosen(jnp.concatenate(routes, axis=0).astype(F32), 0))
            gates_out[pl.ds(pair * 2, 2)] = gates.reshape(2, seq, LANE)
            gated = []
            for j in range(2):
                rows = slice(j * seq, (j + 1) * seq)
                query = [
                    rotate(proj[rows, e * HEAD : (e + 1) * HEAD], cos_ref[...], sin_ref[...]).astype(BF)
                    for e in range(2)
                ]
                key = rotate(proj[rows, 2 * HEAD : 3 * HEAD], cos_ref[...], sin_ref[...]).astype(BF)
                value = proj[rows, 3 * HEAD :].astype(BF)
                probs = soft(mm_nt(jnp.concatenate(query, axis=0), key) * scale, causal)
                attended = mm(probs.astype(BF), value)
                out = [
                    (attended[e * seq : (e + 1) * seq] * pick(gates[rows], first + e)).astype(BF)
                    for e in range(2)
                ]
                qkv_out[pair * 2 + j] = jnp.concatenate(query + [key, value], axis=1)
                gated.append(jnp.concatenate(out, axis=1))
                gated_out[pair * 2 + j] = gated[-1]
            branch = mm_nt(jnp.concatenate(gated, axis=0), weights[:, 4 * HEAD :])
            part[zl, pl.ds(x, 2)] = branch.astype(BF).reshape(2, 2, 2, own, width)
            for j in range(2):
                team.swap(pair * 2 + j).start()

            @pl.when(i > 0)
            def _():
                team.add_pair(i - 1)

            @pl.when(i == 2)
            def _():
                team.send_far_z()

            @pl.when(i == 3)
            def _():
                team.send_far_x()

            return 0

        lax.fori_loop(0, 4, step, 0)
        team.last()
        swaps[2].finish()
        cot.start()
        rings[1].forward()
        rings[2].start()
        swaps[3].finish()
        team.total1(total)
        cot.middle()
        team.total2(total)
        after = total[...] + enter_row[:, :width].astype(F32)
        after_out[...] = after
        row[...] = (after * rms_scale(after) * small_ref[1:2]).astype(BF)
        spread.start()
        rings[2].forward()
        rings[3].start()
        spread.middle()
        cot.finish()
        spread.finish()
        rings[3].forward()
        team.close()
        for ring in rings[1:]:
            ring.finish()

    block = jax.ShapeDtypeStruct(attn_blocks.shape, BF)
    four = jax.ShapeDtypeStruct((4,) + attn_blocks.shape, BF)
    rows = jax.ShapeDtypeStruct((2, 4, 2, 2, own, width), BF)
    return pl.pallas_call(
        kernel,
        out_shape=[
            four,
            jax.ShapeDtypeStruct((8, seq, width), BF),
            jax.ShapeDtypeStruct((8, seq, 4 * HEAD), BF),
            jax.ShapeDtypeStruct((8, seq, 2 * HEAD), BF),
            jax.ShapeDtypeStruct((8, seq, LANE), F32),
            jax.ShapeDtypeStruct((8, seq, LANE), BF),
            jax.ShapeDtypeStruct((own, width), F32),
            jax.ShapeDtypeStruct((own, width + LANE), BF),
            jax.ShapeDtypeStruct((own, width), BF),
            jax.ShapeDtypeStruct((LANE, width), BF),
            rows, rows, four, four, four, block, block, block, block,
        ],
        in_specs=[ANY] * 7 + [VMEM] * 3,
        out_specs=[VMEM] * 10 + [ANY] * 9,
        scratch_shapes=[
            pltpu.SemaphoreType.DMA((17,)),
            pltpu.VMEM((2, 4, 2, 2, own, width + LANE), BF),
            pltpu.VMEM((2, 4, 2, 2, own, width), BF),
            pltpu.VMEM((own, width), F32),
            pltpu.VMEM((own, width), BF),
        ]
        + TeamSum.scratch(own, width)
        + TeamSpread.sems * 3
        + Swap.sems * 4
        + RingY.sems * 4,
        name="attn_forward",
        **settings(collective, 200 << 20, 56),
    )(attn_blocks, *blocks, hidden, cotangent, routes, small, cosines, sines)[:15]


def experts(normed, cotangent, routes, routers, weights, extra):
    rows, width = normed.shape
    part = weights[0].shape[1]
    tile = rows // 4

    def kernel(x_ref, cot_ref, route_ref, router_ref, wg, wu, wd, h_out, dg_out, du_out, branch_out, back_out, gates_out):
        lane = EXPERTS + lax.axis_index("x")
        skip = lax.axis_index("zl") * extra
        x = x_ref[...]
        logits = mm_nt(x, router_ref[...])
        index = lanes(tile)
        gates = dense_gates(logits, chosen(route_ref[...].astype(F32), EXPERTS))
        gates_out[...] = gates
        valid = (lax.broadcasted_iota(jnp.int32, (1, part), 1) >= skip).astype(F32)
        gate = pick(gates, lane) * valid
        gate_part = mm(x, wg[...])
        up_part = mm(x, wu[...])
        sigma = 1.0 / (1.0 + jnp.exp(-gate_part))
        silu = gate_part * sigma
        activated = silu * up_part
        h = (activated * gate).astype(BF)
        h_out[...] = h
        branch_out[...] = mm_nt(h, wd[...]).astype(BF)
        cot_down = mm(cot_ref[...], wd[...])
        dots = jnp.sum(activated * valid * cot_down, axis=1, keepdims=True)
        grad_act = cot_down * gate
        grad_gate = (grad_act * up_part * sigma * (1.0 + gate_part * (1.0 - sigma))).astype(BF)
        grad_up = (grad_act * silu).astype(BF)
        dg_out[...] = grad_gate
        du_out[...] = grad_up
        back_out[:, :width] = (mm_nt(grad_gate, wg[...]) + mm_nt(grad_up, wu[...])).astype(BF)
        back_out[:, width:] = jnp.where(index == lane, dots, 0.0).astype(BF)

    def tiled(cols):
        return pl.BlockSpec((tile, cols), lambda i: (i, 0))

    def whole(array):
        return pl.BlockSpec(array.shape, lambda i: (0, 0), pipeline_mode=pl.Buffered(1))

    cols = [part, part, part, width, width + LANE]
    return pl.pallas_call(
        kernel,
        grid=(4,),
        out_shape=[jax.ShapeDtypeStruct((rows, c), BF) for c in cols]
        + [jax.ShapeDtypeStruct((rows, LANE), F32)],
        in_specs=[tiled(width), tiled(width)]
        + [tiled(LANE), whole(routers)]
        + [whole(w) for w in weights],
        out_specs=[tiled(c) for c in cols] + [tiled(LANE)],
        compiler_params=pltpu.CompilerParams(vmem_limit_bytes=48 << 20),
        cost_estimate=pl.CostEstimate(
            flops=12 * rows * width * part, bytes_accessed=40 << 20, transcendentals=rows * part
        ),
        name="experts",
    )(normed, cotangent, routes, routers, *weights)


def back_through_norm(total, inputs, gain, gates, normed, routers):
    width = inputs.shape[1]
    logits_back = gates_back(gates, total[:, width:])
    full = total[:, :width] + mm(logits_back.astype(BF), routers)
    inner, gain_grad = norm_back(inputs, gain, full)
    return inner, gain_grad, mm_tn(logits_back.astype(BF), normed)[:8]


def row_block(array, block, count):
    cols = array.shape[-1] // 4
    part = array[..., pl.ds(pl.multiple_of(block * cols, cols), cols)]
    return part.reshape(count, cols)


class Pass:
    sems = [pltpu.SemaphoreType.DMA((4,))] * 2

    def __init__(self, src, dst, sems):
        send, recv = sems
        zh, c = lax.axis_index("zh"), lax.axis_index("c")
        mine, far = dst.at[zh, c], dst.at[1 - zh, c]
        self.copies = [
            pltpu.make_async_copy(src, mine, send.at[0]),
            push(src, mine, send.at[1], recv.at[1], {"zh": 1 - zh}),
            push(src, mine, send.at[2], recv.at[2], sibling()),
            push(far, far, send.at[3], recv.at[3], sibling()),
        ]

    def start(self):
        for copy in self.copies[:3]:
            copy.start()

    def finish(self):
        self.copies[1].wait_recv()
        self.copies[3].start()
        self.copies[0].wait()
        self.copies[1].wait_send()
        self.copies[2].wait()
        self.copies[3].wait()


def own_tile():
    zl, x, zh, c = (lax.axis_index(a) for a in TEAM)
    return zl * 4 + x, zh * 2 + c


def middle(collective, back, branch, normed, cotangent, grads, after, small, gates, routers, cot_own):
    own, width = after.shape
    count, cols = grads[0].shape
    rows = width // 4

    def kernel(
        part_ref, branch_ref, x_ref, cot_ref, d0_ref, d1_ref, d2_ref,
        after_ref, small_ref, gates_ref, router_ref, own_ref,
        mid_out, small_out, spread_out, s0, s1, g2, out_all,
        x, cot, d0, d1, d2, g0, g1, part_a, part_b, load, total_a, total_b, row_a, row_b, *rest,
    ):
        loads = [
            (x_ref, x), (d0_ref, d0), (part_ref, part_a), (branch_ref, part_b), (d1_ref, d1), (cot_ref, cot), (d2_ref, d2)
        ]
        fetches = [pltpu.make_async_copy(a, b, load.at[k]) for k, (a, b) in enumerate(loads)]
        for fetch in fetches:
            fetch.start()
        meet([place(m) for m in TEAM_MOVES[1:] + [Y_MOVES[1], Y_MOVES[3]]] + [sibling()])
        n = TeamSum.count
        team_a, team_b = TeamSum(part_a, rest[:n]), TeamSum(part_b, rest[n : 2 * n])
        rest = rest[2 * n :]
        n = RingSum.count
        rings = [RingSum(g0, rest[:n]), RingSum(g1, rest[n : 2 * n])]
        rest = rest[2 * n :]
        spread = TeamSpread(row_a, spread_out, rest[:4])
        out = Pass(row_b, out_all, rest[4:6])

        def product(left, right, dst):
            def one(block):
                dst[block] = mm_tn(row_block(left, block, count), right[...]).astype(BF)

            return one

        fetches[0].wait()
        fetches[1].wait()
        rings[0].start_with(product(x, d0, g0))
        fetches[2].wait()
        team_a.swap_all()
        fetches[3].wait()
        team_b.swap_all()
        team_a.add_all()
        fetches[4].wait()
        rings[1].start_with(product(x, d1, g1))
        rings[0].middle()
        team_a.total1(total_a)
        team_b.add_all()
        after = after_ref[...]
        normed_own = (after * rms_scale(after) * small_ref[1:2]).astype(BF)
        seq, quarter = own_tile()
        team_a.total2(total_a)
        inner, gain_grad, router_grad = back_through_norm(
            total_a[...], after, small_ref[1:2], gates_ref[seq * 4 + quarter], normed_own, router_ref[...]
        )
        grad_mid = own_ref[...].astype(F32) + inner
        mid_out[...] = grad_mid
        row_a[...] = grad_mid.astype(BF)
        spread.start()
        rings[1].middle()
        small_out[:8] = jnp.zeros((8, width), F32)
        small_out[0:1] = gain_grad
        small_out[8:] = router_grad
        fetches[5].wait()
        fetches[6].wait()

        def down(block, _):
            product(cot, d2, g2)(block)
            return 0

        lax.fori_loop(0, 4, down, 0)
        spread.middle()
        team_b.total1(total_b)
        spread.finish()
        team_b.total2(total_b)
        row_b[...] = in_order((after + total_b[...]).astype(BF))
        out.start()
        rings[0].finish(s0)
        rings[1].finish(s1)
        out.finish()
        team_a.close()
        team_b.close()

    return pl.pallas_call(
        kernel,
        out_shape=[
            jax.ShapeDtypeStruct((own, width), F32),
            jax.ShapeDtypeStruct((16, width), F32),
            jax.ShapeDtypeStruct((2, 4, 2, 2, own, width), BF),
            jax.ShapeDtypeStruct((8, rows // 8, cols), BF),
            jax.ShapeDtypeStruct((8, rows // 8, cols), BF),
            jax.ShapeDtypeStruct((4, rows, cols), BF),
            jax.ShapeDtypeStruct((2, 2, own, width), BF),
        ],
        in_specs=[ANY] * 7 + [VMEM] * 5,
        out_specs=[VMEM] * 2 + [ANY] + [VMEM] * 3 + [ANY],
        scratch_shapes=[
            pltpu.VMEM((count, width), BF),
            pltpu.VMEM((count, width), BF),
            pltpu.VMEM((count, cols), BF),
            pltpu.VMEM((count, cols), BF),
            pltpu.VMEM((count, cols), BF),
            pltpu.VMEM((4, rows, cols), BF),
            pltpu.VMEM((4, rows, cols), BF),
            pltpu.VMEM((2, 4, 2, 2, own, width + LANE), BF),
            pltpu.VMEM((2, 4, 2, 2, own, width), BF),
            pltpu.SemaphoreType.DMA((7,)),
            pltpu.VMEM((own, width + LANE), F32),
            pltpu.VMEM((own, width), F32),
            pltpu.VMEM((own, width), BF),
            pltpu.VMEM((own, width), BF),
        ]
        + TeamSum.scratch(own, width + LANE)
        + TeamSum.scratch(own, width)
        + RingSum.scratch(rows, cols) * 2
        + TeamSpread.sems
        + Pass.sems,
        name="middle",
        **settings(collective, 200 << 20, 58),
    )(
        back.reshape(2, 4, 2, 2, own, width + LANE), branch.reshape(2, 4, 2, 2, own, width),
        normed, cotangent, *grads, after, small, gates.reshape(-1, own, LANE), routers, cot_own,
    )


def in_order(values):
    block = values.shape[1] // 8
    order = [(b % 4) * 2 + b // 4 for b in range(8)]
    return jnp.concatenate([values[:, k * block : (k + 1) * block] for k in order], axis=1)


def attn_backward(
    collective, grad_mid, qkv, gated, normed, gates, weights, cosines, sines, mid_own, entered, gains, routers, small, summed, grads
):
    own, width = mid_own.shape
    seq = qkv.shape[1]
    rows, cols = grads.shape[1:]
    shard = rows // 8
    scale = HEAD ** (-0.5)
    stages = [X_MOVES, Y_MOVES, Z_MOVES]

    def kernel(
        gm_ref, w_ref, x_ref, g2_ref, y0, y1, qkv_ref, gated_ref, gates_ref, cos_ref, sin_ref,
        mid_ref, in_ref, gain_ref, router_ref, small_ref,
        grad_all, gain_a, gain_m, router_a, router_m, s0, s1, s2, s3,
        gm, w, x, g2, g3, y2, y3, proj, part, load, total, row,
        acc, got, other, rest_rows, csem, ssend, srecv, *rest,
    ):
        loads = [(gm_ref, gm), (w_ref, w), (g2_ref, g2), (x_ref, x)]
        fetches = [pltpu.make_async_copy(a, b, load.at[k]) for k, (a, b) in enumerate(loads)]
        for fetch in fetches:
            fetch.start()
        meet([place(m) for m in TEAM_MOVES[1:] + Y_MOVES[1:]] + [sibling()])
        n = TeamSum.count
        team, rest = TeamSum(part, rest[:n]), rest[n:]
        n = RingSum.count
        rings, rest = [RingSum(g2, rest[:n]), RingSum(g3, rest[n : 2 * n])], rest[2 * n :]
        swaps_back = [
            Swap(y, s, rest[2 * k : 2 * k + 2]) for k, (y, s) in enumerate(((y0, s0), (y1, s1), (y2, s2)))
        ]
        last_swap = ColumnSwap(y3, s3, rest[6:8])
        out = Pass(row, grad_all, rest[8:10])
        first = 2 * team.zl
        causal = causal_mask(2, seq)
        swaps_back[0].start()
        swaps_back[1].start()
        fetches[0].wait()
        fetches[1].wait()

        def step(i, _):
            pair = team.pair(i)
            grads = mm(gm[pl.ds(pair * 2, 2)].reshape(2 * seq, width), w[:, 4 * HEAD :])
            both = []
            for j in range(2):
                at = pair * 2 + j
                here = slice(j * seq, (j + 1) * seq)
                query = jnp.concatenate(
                    [qkv_ref[at, :, e * HEAD : (e + 1) * HEAD] for e in range(2)], axis=0
                )
                key = qkv_ref[at, :, 2 * HEAD : 3 * HEAD]
                value = qkv_ref[at, :, 3 * HEAD :]
                probs = soft(mm_nt(query, key) * scale, causal)
                probs_b = probs.astype(BF)
                attended = mm(probs_b, value)
                grad = jnp.concatenate(
                    [grads[here, e * HEAD : (e + 1) * HEAD] for e in range(2)], axis=0
                )
                gates = gates_ref[at]
                gate = jnp.concatenate([pick(gates, first + e) for e in range(2)], axis=0)
                each = jnp.sum(attended * grad, axis=1, keepdims=True)
                dots = jnp.where(lanes(seq) == first, each[:seq], 0.0)
                dots += jnp.where(lanes(seq) == first + 1, each[seq:], 0.0)
                grad = (grad * gate).astype(BF)
                grad_probs = mm_nt(grad, value)
                inner = jnp.sum(probs * grad_probs, axis=1, keepdims=True)
                grad_scores = (probs * (grad_probs - inner) * scale).astype(BF)
                turned = [mm(grad_scores, key), mm_tn(grad_scores, query)]
                turned = [turned[0][:seq], turned[0][seq:], turned[1]]
                turned = [rotate(t, cos_ref[...], -sin_ref[...]).astype(BF) for t in turned]
                grad_value = mm_tn(probs_b, grad).astype(BF)
                both.append(jnp.concatenate(turned + [grad_value], axis=1))
                proj[at] = both[-1]
                part[pair // 2, lax.rem(pair, 2) * 2 + j, :, :, :, width:] = dots.astype(BF).reshape(
                    2, 2, own, LANE
                )
            back = mm_nt(jnp.concatenate(both, axis=0), w[:, : 4 * HEAD])
            part[pair // 2, pl.ds(lax.rem(pair, 2) * 2, 2), :, :, :, :width] = back.astype(BF).reshape(
                2, 2, 2, own, width
            )
            for j in range(2):
                team.swap(pair * 2 + j).start()

            @pl.when(i == 0)
            def _():
                fetches[2].wait()
                rings[0].start()

            @pl.when(i > 0)
            def _():
                team.add_pair(i - 1)

            @pl.when(i == 2)
            def _():
                team.send_far_z()

            @pl.when(i == 3)
            def _():
                team.send_far_x()

            return 0

        lax.fori_loop(0, 4, step, 0)
        team.last()
        fetches[3].wait()

        def product(block):
            g3[block, :, : 4 * HEAD] = mm_tn(
                row_block(x, block, 8 * seq), proj[...].reshape(8 * seq, 4 * HEAD)
            ).astype(BF)
            g3[block, :, 4 * HEAD :] = mm_tn(
                row_block(gm, block, 8 * seq), gated_ref[...].reshape(8 * seq, 2 * HEAD)
            ).astype(BF)

        rings[1].start_with(product)
        rings[0].middle()
        inputs = in_ref[:, :width].astype(F32)
        normed_own = (inputs * rms_scale(inputs) * gain_ref[0:1]).astype(BF)
        own_seq, quarter = own_tile()
        gates_own = gates_ref[own_seq, pl.ds(pl.multiple_of(quarter * own, own), own)]
        team.total1(total)
        rings[1].middle()
        team.total2(total)
        inner, gain_grad, router_grad = back_through_norm(
            total[...], inputs, gain_ref[0:1], gates_own, normed_own, router_ref[...]
        )
        row[...] = in_order((mid_ref[...] + inner).astype(BF))
        out.start()
        acc[...] = small_ref[...]
        acc[1:2] = gain_grad
        acc[8:] += router_grad
        c = lax.axis_index("c")
        half = pl.ds(pl.multiple_of(c * 8, 8), 8)
        rest_half = pl.ds(pl.multiple_of((1 - c) * 8, 8), 8)
        over = push(acc.at[rest_half], other, csem.at[0], csem.at[1], sibling())
        over.start()
        over.wait()
        acc[half] = acc[half] + other[...]
        for s, stage in enumerate(stages):
            swaps = [
                push(acc.at[half], got.at[s, k - 1], ssend.at[s, k], srecv.at[s, k], place(stage[k]))
                for k in range(1, 4)
            ]
            for swap in swaps:
                swap.start()
            if s == 0:
                rings[0].finish(y2)
                swaps_back[2].start()
            if s == 1:
                rings[1].finish(y3)
                last_swap.start()
            for swap in swaps:
                swap.wait()
            acc[half] = acc[half] + got[s, 0] + got[s, 1] + got[s, 2]
        back_over = push(acc.at[half], rest_rows, csem.at[2], csem.at[3], sibling())
        back_over.start()
        out.finish()
        back_over.wait()
        acc[rest_half] = rest_rows[...]
        final = in_order(acc[...])
        for ref, at in ((gain_m, 0), (gain_a, 1)):
            for k in range(width // LANE):
                ref[k : k + 1] = final[at : at + 1, k * LANE : (k + 1) * LANE]
        router_a[...] = final[8 : 8 + EXPERTS]
        router_m[...] = final[8 + EXPERTS :]
        for swap in swaps_back + [last_swap]:
            swap.finish()
        team.close()

    block = jax.ShapeDtypeStruct((8, shard, cols), BF)
    heads = cols // HEAD
    return pl.pallas_call(
        kernel,
        out_shape=[
            jax.ShapeDtypeStruct((2, 2, own, width), BF),
            jax.ShapeDtypeStruct((width // LANE, LANE), F32),
            jax.ShapeDtypeStruct((width // LANE, LANE), F32),
            jax.ShapeDtypeStruct((EXPERTS, width), F32),
            jax.ShapeDtypeStruct((EXPERTS, width), F32),
            block, block, block,
            jax.ShapeDtypeStruct((2, heads, shard, 4 * HEAD), BF),
        ],
        in_specs=[ANY] * 6 + [VMEM] * 10,
        out_specs=[ANY] + [VMEM] * 4 + [ANY] * 4,
        scratch_shapes=[
            pltpu.VMEM((8, seq, width), BF),
            pltpu.VMEM(weights.shape, BF),
            pltpu.VMEM((8, seq, width), BF),
            pltpu.VMEM((4, rows, cols), BF),
            pltpu.VMEM((4, rows, cols), BF),
            pltpu.VMEM((8, shard, cols), BF),
            pltpu.VMEM((8, heads, shard, HEAD), BF),
            pltpu.VMEM((8, seq, 4 * HEAD), BF),
            pltpu.VMEM((2, 4, 2, 2, own, width + LANE), BF),
            pltpu.SemaphoreType.DMA((4,)),
            pltpu.VMEM((own, width + LANE), F32),
            pltpu.VMEM((own, width), BF),
            pltpu.VMEM((16, width), F32),
            pltpu.VMEM((3, 3, 8, width), F32),
            pltpu.VMEM((8, width), F32),
            pltpu.VMEM((8, width), F32),
            pltpu.SemaphoreType.DMA((4,)),
        ]
        + [pltpu.SemaphoreType.DMA((4, 4))] * 2
        + TeamSum.scratch(own, width + LANE)
        + RingSum.scratch(rows, cols) * 2
        + Swap.sems * 4
        + Pass.sems,
        name="attn_backward",
        **settings(collective, 200 << 20, 58),
    )(
        grad_mid.reshape(8, seq, width), weights, normed, grads, *summed, qkv, gated, gates, cosines, sines,
        mid_own, entered, gains, routers, small,
    )


def reorder(array, axis):
    shape = array.shape
    split = shape[:axis] + (2, 4, shape[axis] // 8) + shape[axis + 1 :]
    return jnp.swapaxes(array.reshape(split), axis, axis + 1).reshape(shape)


def local(
    hidden,
    cotangent,
    attn_gain,
    attn_router,
    qkv_weight,
    out_weight,
    mlp_gain,
    mlp_router,
    gate_up_weight,
    down_weight,
    attn_route,
    attn_slot,
    mlp_route,
    mlp_slot,
):
    seq, width = hidden.shape
    rows = qkv_weight.shape[0]
    features = down_weight.shape[2]
    part = (features // LANE + 1) // 2 * LANE
    low = features - part
    group = 8 * seq
    cosines, sines = rope_tables(seq)

    query_blocks = qkv_weight[:, :EXPERTS].reshape(rows, 2, 2, 4, HEAD).transpose(1, 3, 0, 2, 4)
    kv_blocks = qkv_weight[:, EXPERTS:].reshape(rows, 2, 4, HEAD).transpose(2, 0, 1, 3)
    kv_blocks = jnp.broadcast_to(kv_blocks[None], (2,) + kv_blocks.shape)
    out_blocks = out_weight.reshape(rows, 2, 2, 4, HEAD).transpose(1, 3, 0, 2, 4)
    attn_blocks = jnp.concatenate([query_blocks, kv_blocks, out_blocks], axis=3)
    attn_blocks = attn_blocks.reshape(8, rows, 6 * HEAD)

    def by_target(weight):
        weight = weight.transpose(1, 0, 2)
        return jnp.stack([weight[..., :part], weight[..., low:]], axis=0).reshape(8, rows, part)

    mlp_blocks = [
        by_target(w) for w in (gate_up_weight[:, :, 0], gate_up_weight[:, :, 1], down_weight)
    ]

    none = jnp.zeros((6, width), F32)
    routers = jnp.concatenate([attn_router, mlp_router], axis=1).astype(F32).T
    small = jnp.concatenate([attn_gain[None], mlp_gain[None], none, routers], axis=0)
    small = reorder(small, 1)
    routes = jnp.concatenate([attn_route, jnp.zeros_like(attn_route), mlp_route], axis=1)
    routes = jnp.pad(routes, ((0, 0), (0, LANE - 6))).astype(BF)

    (
        attn_w, normed_a, qkv, gated_att, gates_a, group_routes, after, entered, cot_own, routers,
        normed_m, group_cot, *mlp_w,
    ) = attn_forward(1, attn_blocks, mlp_blocks, hidden, cotangent, routes, small, cosines, sines)
    attn_w = attn_w.reshape(width, 6 * HEAD)
    mlp_w = [w.reshape(width, part) for w in mlp_w]
    group_cot = group_cot.reshape(group, width)
    normed_m = normed_m.reshape(group, width)

    h, grad_gate, grad_up, branch_m, back_m, gates_m = experts(
        normed_m, group_cot, group_routes.reshape(group, LANE), routers, mlp_w, 2 * part - features
    )
    grad_mid_own, small_m, grad_mid, gate_sum, up_sum, down_part, out_hidden = middle(
        2, back_m, branch_m, normed_m, group_cot, [grad_gate, grad_up, h], after, small, gates_m, routers, cot_own
    )
    grad_in, gain_a, gain_m, router_a, router_m, *mlp_grads, attn_grads = attn_backward(
        3, grad_mid, qkv, gated_att, normed_a, gates_a, attn_w, cosines, sines, grad_mid_own, entered, small,
        routers, small_m, [gate_sum, up_sum], down_part,
    )
    out_hidden = out_hidden.reshape(seq, width)
    grad_in = grad_in.reshape(seq, width).astype(F32)

    attn_grads = attn_grads.astype(F32)
    query_grad = attn_grads[:, :2].reshape(EXPERTS, rows, 4 * HEAD)
    kv_grad = attn_grads[0, 2:4] + attn_grads[1, 2:4]
    qkv_grad = jnp.concatenate([query_grad, kv_grad], axis=0).transpose(1, 0, 2)
    out_grad = attn_grads[:, 4:].reshape(EXPERTS, rows, 4 * HEAD).transpose(1, 0, 2)

    def placed_back(grad):
        grad = grad.reshape(2, EXPERTS, rows, part)
        return jnp.concatenate([grad[0], grad[1, ..., 2 * part - features :]], axis=-1).transpose(1, 0, 2)

    gate_grad, up_grad, down_grad = [placed_back(g) for g in mlp_grads]
    return (
        out_hidden,
        grad_in,
        gain_a.reshape(width),
        router_a.T,
        qkv_grad,
        out_grad,
        gain_m.reshape(width),
        router_m.T,
        jnp.stack([gate_grad, up_grad], axis=2).astype(F32),
        down_grad.astype(F32),
    )


def solution(mesh):
    fine = Mesh(mesh.devices.reshape(2, 4, 4, 2, 2), ALL)
    dp, tensor = ("zl", "y", "x"), ("zh", "c")
    placed = (
        P(dp, None),
        P(dp, None),
        P(),
        P(),
        P(dp, None, tensor),
        P(dp, None, tensor),
        P(),
        P(),
        P(dp, None, None, tensor),
        P(dp, None, tensor),
        P(dp, None),
        P(dp, None),
        P(dp, None),
        P(dp, None),
    )
    return jax.shard_map(
        local,
        mesh=fine,
        in_specs=placed,
        out_specs=(
            P(dp, None),
            P(dp, None),
            P(),
            P(),
            P(dp, None, tensor),
            P(dp, None, tensor),
            P(),
            P(),
            P(dp, None, None, tensor),
            P(dp, None, tensor),
        ),
        check_vma=False,
    )
```

```python
import itertools

import jax
import jax.numpy as jnp
import numpy as np
from jax import lax
from jax.experimental import pallas as pl
from jax.experimental.pallas import tpu as pltpu
from jax.sharding import Mesh, PartitionSpec as P

HEAD = 128
LANE = 128
EPS = 1e-05
THETA = 10000.0
NEG = -1e30
EXPERTS = 4
GROUP = ("zl", "x")
TEAM = ("zl", "x", "zh", "c")
ALL = ("zl", "y", "x", "zh", "c")
SIZES = dict(zl=2, y=4, x=4, zh=2, c=2)
BF = jnp.bfloat16
F32 = jnp.float32
MESH = pl.DeviceIdType.MESH
ANY = pl.BlockSpec(memory_space=pl.ANY)
VMEM = pl.BlockSpec(memory_space=pltpu.VMEM)


def dot(a, b, dims):
    return lax.dot_general(a, b, (dims, ((), ())), preferred_element_type=F32)


def mm(a, b):
    return dot(a, b, ((1,), (0,)))


def mm_nt(a, b):
    return dot(a, b, ((1,), (1,)))


def mm_tn(a, b):
    return dot(a, b, ((0,), (0,)))


def rms_scale(values):
    return lax.rsqrt(jnp.mean(values * values, axis=-1, keepdims=True) + EPS)


def lanes(rows):
    return lax.broadcasted_iota(jnp.int32, (rows, LANE), 1)


def chosen(routes, first):
    lane = lanes(routes.shape[0])
    named = [pick(routes, first + c).astype(jnp.int32) + first for c in range(2)]
    return (lane == named[0]) | (lane == named[1])


def dense_gates(logits, mask):
    top = jnp.max(jnp.where(mask, logits, NEG), axis=1, keepdims=True)
    expon = jnp.where(mask, jnp.exp(jnp.where(mask, logits - top, 0.0)), 0.0)
    return expon / jnp.sum(expon, axis=1, keepdims=True)


def pick(values, lane):
    return jnp.sum(jnp.where(lanes(values.shape[0]) == lane, values, 0.0), axis=1, keepdims=True)


def gates_back(gates, dots):
    return gates * (dots - jnp.sum(gates * dots, axis=1, keepdims=True))


def rope_tables(count):
    frequency = THETA ** (-(np.arange(HEAD // 2).astype(np.float32) * 2.0 / HEAD))
    angles = np.arange(count).astype(np.float32)[:, None] * frequency[None, :].astype(np.float32)
    cosines, sines = np.cos(angles), np.sin(angles)
    return (
        jnp.asarray(np.concatenate([cosines, cosines], axis=1), F32),
        jnp.asarray(np.concatenate([-sines, sines], axis=1), F32),
    )


def rotate(values, cosines, sines):
    return values * cosines + pltpu.roll(values, HEAD // 2, 1) * sines


def norm_back(inputs, gain, grad_normed):
    scale = rms_scale(inputs)
    scaled = inputs * scale
    grad_scaled = grad_normed * gain
    grad_inputs = scale * (
        grad_scaled - scaled * jnp.mean(grad_scaled * scaled, axis=-1, keepdims=True)
    )
    return grad_inputs, jnp.sum(grad_normed * scaled, axis=0, keepdims=True)


def moves(*axes):
    return [dict(zip(axes, steps)) for steps in itertools.product(*[range(SIZES[a]) for a in axes])]


def place(move, sign=1):
    return {a: lax.rem(lax.axis_index(a) + sign * v + SIZES[a], SIZES[a]) for a, v in move.items()}


def number(coords):
    total = 0
    for axis, value in coords.items():
        total = total * SIZES[axis] + value
    return total


def meet(partners):
    barrier = pltpu.get_barrier_semaphore()
    for partner in partners:
        pl.semaphore_signal(barrier, inc=1, device_id=partner, device_id_type=MESH)
    pl.semaphore_wait(barrier, len(partners))


def push(src, dst, send, recv, to):
    return pltpu.make_async_remote_copy(
        src_ref=src, dst_ref=dst, send_sem=send, recv_sem=recv, device_id=to, device_id_type=MESH
    )


def settings(number, moved, vmem=32):
    return dict(
        compiler_params=pltpu.CompilerParams(
            collective_id=number, has_side_effects=True, vmem_limit_bytes=vmem << 20
        ),
        cost_estimate=pl.CostEstimate(flops=0, bytes_accessed=moved, transcendentals=0),
    )


GROUP_MOVES = moves("zl", "x")
TEAM_MOVES = moves("zl", "x", "zh")
X_MOVES = moves("x")
Y_MOVES = moves("y")
Z_MOVES = moves("zl", "zh")


def sibling():
    return {"c": 1 - lax.axis_index("c")}


class RingY:
    sems = [pltpu.SemaphoreType.DMA((5,)), pltpu.SemaphoreType.DMA((5,))]

    def __init__(self, src, out, sems):
        self.src, self.out = src, out
        self.send, self.recv = sems
        self.y = lax.axis_index("y")
        self.half = src.shape[0] // 2

    def line(self, step):
        return lax.rem(self.y + step, 4)

    def copy(self, k):
        y = self.y
        if k < 2:
            src, dst, to = self.src, self.out.at[y], self.line((1, 3)[k])
        else:
            half = pl.ds((k - 2) * self.half, self.half)
            src = dst = self.out.at[self.line((3, 1)[k - 2]), half]
            to = self.line((1, 3)[k - 2])
        return push(src, dst, self.send.at[k], self.recv.at[k], {"y": to})

    def start(self):
        self.stay = pltpu.make_async_copy(self.src, self.out.at[self.y], self.send.at[4])
        for k in range(2):
            self.copy(k).start()
        self.stay.start()

    def forward(self):
        for k in range(2):
            self.copy(k).wait_recv()
            self.copy(k + 2).start()

    def finish(self):
        for k in range(2):
            self.copy(k + 2).wait_recv()
        for k in range(4):
            self.copy(k).wait_send()
        self.stay.wait()


class Swap:
    sems = [pltpu.SemaphoreType.DMA((8,))] * 2

    def __init__(self, src, dst, sems):
        self.src, self.dst = src, dst
        self.send, self.recv = sems

    def start(self):
        me = number(place(GROUP_MOVES[0]))
        self.copies = [
            pltpu.make_async_copy(self.src.at[me], self.dst.at[me], self.send.at[0])
        ]
        for k, move in enumerate(GROUP_MOVES):
            if k:
                to = place(move)
                self.copies.append(
                    push(
                        self.src.at[number(to)],
                        self.dst.at[me],
                        self.send.at[k],
                        self.recv.at[k],
                        to,
                    )
                )
        for copy in self.copies:
            copy.start()

    def finish(self):
        for copy in self.copies:
            copy.wait()


class ColumnSwap(Swap):
    def start(self):
        zl, x = lax.axis_index("zl"), lax.axis_index("x")
        mine = self.dst.at[zl, :, :, pl.ds(pl.multiple_of(x * HEAD, HEAD), HEAD)]
        self.copies = [
            pltpu.make_async_copy(self.src.at[zl * 4 + x], mine, self.send.at[0])
        ]
        for k, move in enumerate(GROUP_MOVES):
            if k:
                to = place(move)
                block = self.src.at[number(to)]
                self.copies.append(push(block, mine, self.send.at[k], self.recv.at[k], to))
        for copy in self.copies:
            copy.start()


class RingSum:
    @staticmethod
    def scratch(rows, cols):
        return [
            pltpu.VMEM((2, rows // 2, cols), BF),
            pltpu.VMEM((2, rows // 2, cols), BF),
            pltpu.VMEM((2, rows, cols), BF),
            pltpu.SemaphoreType.DMA((6,)),
            pltpu.SemaphoreType.DMA((6,)),
        ]

    count = 5

    def __init__(self, part, scratch):
        self.part = part
        self.got, self.mix, self.sums, self.send, self.recv = scratch
        self.y = lax.axis_index("y")
        half = part.shape[1] // 2
        self.halves = [pl.ds(0, half), pl.ds(half, half)]

    def line(self, step):
        return lax.rem(self.y + step, 4)

    def copy(self, k):
        kind, way = k // 2, k % 2
        step = (1, 3)[way]
        top, low = self.halves[way], self.halves[1 - way]
        if kind == 0:
            src, dst = self.part.at[self.line(2), top], self.got.at[way]
        elif kind == 1:
            src, dst = self.part.at[self.line(step), low], self.sums.at[way, low]
        else:
            src, dst = self.mix.at[way], self.sums.at[way, top]
        return push(src, dst, self.send.at[k], self.recv.at[k], {"y": self.line(step)})

    def start(self):
        for k in range(4):
            self.copy(k).start()

    def start_with(self, product):
        product(self.line(2))
        self.copy(0).start()
        self.copy(1).start()
        product(self.line(1))
        self.copy(2).start()
        product(self.line(3))
        self.copy(3).start()
        product(self.y)

    def middle(self):
        for way in range(2):
            self.copy(way).wait_recv()
            mine = self.part[self.line((1, 3)[way]), self.halves[way]].astype(F32)
            self.mix[way] = (mine + self.got[way].astype(F32)).astype(BF)
            self.copy(4 + way).start()

    def finish(self, out):
        for k in range(2, 6):
            self.copy(k).wait_recv()
        total = self.part[self.y].astype(F32) + self.sums[0].astype(F32) + self.sums[1].astype(F32)
        total = total.astype(BF)
        if len(out.shape) < 4:
            out[...] = total.reshape(out.shape)
        else:
            targets, count, rows, cols = out.shape
            for t in range(targets):
                for n in range(count):
                    out[t, n] = total[t * rows : (t + 1) * rows, n * cols : (n + 1) * cols]
        for k in range(6):
            self.copy(k).wait_send()


class TeamSum:
    @staticmethod
    def scratch(own, width):
        half = own // 2
        return [
            pltpu.VMEM((8, 2, own, width), BF),
            pltpu.VMEM((3, 2, 2, half, width), BF),
            pltpu.VMEM((3, 4, half, width), BF),
            pltpu.VMEM((6, half, width), BF),
            pltpu.SemaphoreType.DMA((8,)),
            pltpu.SemaphoreType.DMA((8,)),
            pltpu.SemaphoreType.DMA((6,)),
            pltpu.SemaphoreType.DMA((6,)),
            pltpu.SemaphoreType.DMA((6,)),
            pltpu.SemaphoreType.DMA((6,)),
        ]

    count = 10

    def __init__(self, part, scratch):
        self.part = part
        self.other, self.got_x, self.got_z, self.late = scratch[:4]
        self.ssem, self.rsem, self.send1, self.recv1, self.send2, self.recv2 = scratch[4:]
        self.zl, self.x, self.zh, self.c = (lax.axis_index(a) for a in TEAM)
        self.half = part.shape[4] // 2
        self.top, self.low = pl.ds(0, self.half), pl.ds(self.half, self.half)

    def swap(self, seq):
        return push(
            self.part.at[seq // 4, lax.rem(seq, 4), :, 1 - self.c],
            self.other.at[seq],
            self.ssem.at[seq],
            self.rsem.at[seq],
            sibling(),
        )

    def send_x(self, x):
        slot = lax.rem(x - self.x + 4, 4) - 1
        return push(
            self.part.at[:, x, :, self.c, self.top],
            self.got_x.at[slot],
            self.send1.at[slot],
            self.recv1.at[slot],
            {"x": x},
        )

    def send_z(self, zl, zh):
        slot = lax.rem(zl - self.zl + 2, 2) * 2 + lax.rem(zh - self.zh + 2, 2) - 1
        return push(
            self.part.at[zl, :, zh, self.c, self.low],
            self.got_z.at[slot],
            self.send1.at[3 + slot],
            self.recv1.at[3 + slot],
            {"zl": zl, "zh": zh},
        )

    def late_z(self, k):
        to = place(Z_MOVES[k])
        return push(
            self.part.at[to["zl"], self.x, to["zh"], self.c, self.top],
            self.late.at[k - 1],
            self.send2.at[k - 1],
            self.recv2.at[k - 1],
            to,
        )

    def late_x(self, k):
        to = place(X_MOVES[k])
        return push(
            self.part.at[self.zl, to["x"], self.zh, self.c, self.low],
            self.late.at[2 + k],
            self.send2.at[2 + k],
            self.recv2.at[2 + k],
            to,
        )

    def add(self, seq):
        self.swap(seq).wait_recv()
        zl, x = seq // 4, lax.rem(seq, 4)
        for zh in range(2):
            mine = self.part[zl, x, zh, self.c].astype(F32)
            self.part[zl, x, zh, self.c] = (mine + self.other[seq, zh].astype(F32)).astype(BF)

    def pair(self, step):
        back = 3 - step
        return lax.rem(self.zl + back // 2, 2) * 2 + lax.rem(self.x // 2 + back, 2)

    def add_pair(self, step):
        for j in range(2):
            self.add(self.pair(step) * 2 + j)

    def send_far_z(self):
        for zh in range(2):
            self.send_z(1 - self.zl, zh).start()

    def send_far_x(self):
        for j in range(2):
            self.send_x((1 - self.x // 2) * 2 + j).start()

    def last(self):
        self.add_pair(3)
        self.send_x(self.x + 1 - 2 * lax.rem(self.x, 2)).start()
        self.send_z(self.zl, 1 - self.zh).start()

    def got(self, ref, sem):
        pltpu.make_async_copy(ref, ref, sem).wait()

    def total(self, total_ref):
        self.total1(total_ref)
        self.total2(total_ref)

    def total1(self, total_ref):
        half, c = self.half, self.c
        for k in range(3):
            self.got(self.got_x.at[k], self.recv1.at[k])
        for k, move in reversed(list(enumerate(Z_MOVES))):
            at = place(move)
            rows = self.part[at["zl"], self.x, at["zh"], c, :half].astype(F32)
            for j in range(3):
                rows += self.got_x[j, at["zl"], at["zh"]].astype(F32)
            if k:
                self.part[at["zl"], self.x, at["zh"], c, :half] = rows.astype(BF)
                self.late_z(k).start()
            else:
                total_ref[:half] = rows
        for k in range(3):
            self.got(self.got_z.at[k], self.recv1.at[3 + k])
        for k, move in reversed(list(enumerate(X_MOVES))):
            at = place(move)
            rows = self.part[self.zl, at["x"], self.zh, c, half:].astype(F32)
            for j in range(3):
                rows += self.got_z[j, at["x"]].astype(F32)
            if k:
                self.part[self.zl, at["x"], self.zh, c, half:] = rows.astype(BF)
                self.late_x(k).start()
            else:
                total_ref[half:] = rows

    def total2(self, total_ref):
        half = self.half
        for k in range(3):
            self.got(self.late.at[k], self.recv2.at[k])
            total_ref[:half] += self.late[k].astype(F32)
        for k in range(3):
            self.got(self.late.at[3 + k], self.recv2.at[3 + k])
            total_ref[half:] += self.late[3 + k].astype(F32)

    def close(self):
        for seq in range(8):
            self.swap(seq).wait_send()
        for k in range(1, 4):
            x, z = place(X_MOVES[k])["x"], place(Z_MOVES[k])
            self.send_x(x).wait_send()
            self.send_z(z["zl"], z["zh"]).wait_send()
            self.late_z(k).wait_send()
            self.late_x(k).wait_send()

    def swap_all(self):
        for step in range(4):
            for j in range(2):
                self.swap(self.pair(step) * 2 + j).start()

    def add_all(self):
        self.add_pair(0)
        self.add_pair(1)
        self.send_far_z()
        self.add_pair(2)
        self.send_far_x()
        self.last()


class TeamSpread:
    sems = [pltpu.SemaphoreType.DMA((12,))] * 2 + [pltpu.SemaphoreType.DMA((9,))] * 2

    def __init__(self, rows, out, sems):
        self.rows, self.out = rows, out
        self.send, self.recv, self.fsend, self.frecv = sems
        self.zl, self.x, self.zh, self.c = (lax.axis_index(a) for a in TEAM)
        self.half = rows.shape[0] // 2
        self.top, self.low = pl.ds(0, self.half), pl.ds(self.half, self.half)

    def tops(self, zl, zh):
        return self.out.at[zl, :, zh, self.c, self.top]

    def lows(self, x):
        return self.out.at[:, x, :, self.c, self.low]

    def hop(self, k, src, dst, to):
        return push(src, dst, self.send.at[k], self.recv.at[k], to)

    def first(self, k):
        here = (self.zl, self.x, self.zh, self.c)
        if k < 3:
            return self.hop(k, self.rows.at[self.top], self.out.at[(*here, self.top)], place(X_MOVES[k + 1]))
        return self.hop(k, self.rows.at[self.low], self.out.at[(*here, self.low)], place(Z_MOVES[k - 2]))

    def second(self, k):
        if k < 3:
            block = self.tops(self.zl, self.zh)
            return self.hop(6 + k, block, block, place(Z_MOVES[k + 1]))
        block = self.lows(self.x)
        return self.hop(6 + k, block, block, place(X_MOVES[k - 2]))

    def forward(self, k, block):
        return push(block, block, self.fsend.at[k], self.frecv.at[k], sibling())

    def start(self):
        self.stay = pltpu.make_async_copy(
            self.rows, self.out.at[self.zl, self.x, self.zh, self.c], self.fsend.at[8]
        )
        for k in range(6):
            self.first(k).start()
        self.stay.start()

    def middle(self):
        self.stay.wait()
        for k in range(3):
            self.first(k).wait_recv()
        for k in range(3):
            self.second(k).start()
        self.forward(0, self.tops(self.zl, self.zh)).start()
        for k in range(3, 6):
            self.first(k).wait_recv()
        for k in range(3, 6):
            self.second(k).start()
        self.forward(1, self.lows(self.x)).start()

    def block(self, k):
        if k < 3:
            at = place(Z_MOVES[k + 1], -1)
            return self.tops(at["zl"], at["zh"])
        return self.lows(place(X_MOVES[k - 2], -1)["x"])

    def finish(self):
        for k in range(6):
            self.second(k).wait_recv()
            self.forward(2 + k, self.block(k)).start()
        blocks = [self.tops(self.zl, self.zh), self.lows(self.x)] + [self.block(k) for k in range(6)]
        for k in range(8):
            self.forward(k, blocks[k]).wait()
        for k in range(6):
            self.first(k).wait_send()
            self.second(k).wait_send()


def soft(scores, causal):
    scores = jnp.where(causal, scores, NEG)
    expon = jnp.exp(scores - jnp.max(scores, axis=-1, keepdims=True))
    return expon / jnp.sum(expon, axis=-1, keepdims=True)


def causal_mask(copies, seq):
    rows = lax.rem(lax.broadcasted_iota(jnp.int32, (copies * seq, seq), 0), seq)
    return lax.broadcasted_iota(jnp.int32, (copies * seq, seq), 1) <= rows


def attn_forward(
    collective, attn_blocks, blocks, hidden, cotangent, routes, small, cosines, sines
):
    seq, width = hidden.shape
    own = seq // 4
    piece = width // 8
    scale = HEAD ** (-0.5)

    def kernel(
        a_ref, b0, b1, b2, hidden_ref, cotangent_ref, route_ref, small_ref, cos_ref, sin_ref,
        w_out, normed_out, qkv_out, gated_out, gates_out, routes_out, after_out, enter_row, cot_row, router_ref,
        spread_out, cot_out, w0, w1, w2, a_mid, m0, m1, m2,
        load, hid, part, total, row, *rest,
    ):
        mine = pl.ds(pl.multiple_of((lax.axis_index("zh") * 2 + lax.axis_index("c")) * own, own), own)
        loads = []
        for b in range(8):
            here, there = pl.ds(b * piece, piece), pl.ds(((b % 4) * 2 + b // 4) * piece, piece)
            loads.append((hidden_ref.at[mine, here], enter_row.at[:, there]))
            loads.append((cotangent_ref.at[mine, here], cot_row.at[:, there]))
        loads.append((route_ref.at[mine], enter_row.at[:, pl.ds(width, LANE)]))
        fetches = [pltpu.make_async_copy(a, b, load.at[k]) for k, (a, b) in enumerate(loads)]
        for fetch in fetches:
            fetch.start()
        meet([place(m) for m in TEAM_MOVES[1:] + [Y_MOVES[1], Y_MOVES[3]]] + [sibling()])
        n = TeamSum.count
        team, rest = TeamSum(part, rest[:n]), rest[n:]
        enters = TeamSpread(enter_row, hid, rest[:4])
        cot = TeamSpread(cot_row, cot_out, rest[4:8])
        spread = TeamSpread(row, spread_out, rest[8:12])
        rest = rest[12:]
        swaps = [
            Swap(b, m, rest[2 * k : 2 * k + 2])
            for k, (b, m) in enumerate(((a_ref, a_mid), (b0, m0), (b1, m1), (b2, m2)))
        ]
        rings = [
            RingY(m, w, rest[8 + 2 * k : 10 + 2 * k])
            for k, (m, w) in enumerate(((a_mid, w_out), (m0, w0), (m1, w1), (m2, w2)))
        ]
        swaps[0].start()
        for fetch in fetches:
            fetch.wait()
        enters.start()
        router_ref[...] = jnp.zeros_like(router_ref)
        router_ref[:8] = small_ref[8:].astype(BF)
        swaps[0].finish()
        rings[0].start()
        swaps[1].start()
        enters.middle()
        swaps[2].start()
        rings[0].forward()
        swaps[1].finish()
        rings[1].start()
        swaps[3].start()
        enters.finish()
        rings[0].finish()
        first = 2 * team.zl
        causal = causal_mask(2, seq)

        def step(i, _):
            pair = team.pair(i)
            zl, x = pair // 2, lax.rem(pair, 2) * 2
            routes = []
            for j in range(2):
                entered = hid[zl, x + j].reshape(seq, width + LANE)
                values = entered[:, :width].astype(F32)
                normed_out[pair * 2 + j] = (values * rms_scale(values) * small_ref[0:1]).astype(BF)
                routes.append(entered[:, width:])
                routes_out[pair * 2 + j] = routes[j]
            normed = normed_out[pl.ds(pair * 2, 2)].reshape(2 * seq, width)
            weights = w_out.reshape(width, 6 * HEAD)
            logits = mm_nt(normed, router_ref[...])
            proj = mm(normed, weights[:, : 4 * HEAD])
            gates = dense_gates(logits, chosen(jnp.concatenate(routes, axis=0).astype(F32), 0))
            gates_out[pl.ds(pair * 2, 2)] = gates.reshape(2, seq, LANE)
            gated = []
            for j in range(2):
                rows = slice(j * seq, (j + 1) * seq)
                query = [
                    rotate(proj[rows, e * HEAD : (e + 1) * HEAD], cos_ref[...], sin_ref[...]).astype(BF)
                    for e in range(2)
                ]
                key = rotate(proj[rows, 2 * HEAD : 3 * HEAD], cos_ref[...], sin_ref[...]).astype(BF)
                value = proj[rows, 3 * HEAD :].astype(BF)
                probs = soft(mm_nt(jnp.concatenate(query, axis=0), key) * scale, causal)
                attended = mm(probs.astype(BF), value)
                out = [
                    (attended[e * seq : (e + 1) * seq] * pick(gates[rows], first + e)).astype(BF)
                    for e in range(2)
                ]
                qkv_out[pair * 2 + j] = jnp.concatenate(query + [key, value], axis=1)
                gated.append(jnp.concatenate(out, axis=1))
                gated_out[pair * 2 + j] = gated[-1]
            branch = mm_nt(jnp.concatenate(gated, axis=0), weights[:, 4 * HEAD :])
            part[zl, pl.ds(x, 2)] = branch.astype(BF).reshape(2, 2, 2, own, width)
            for j in range(2):
                team.swap(pair * 2 + j).start()

            @pl.when(i > 0)
            def _():
                team.add_pair(i - 1)

            @pl.when(i == 2)
            def _():
                team.send_far_z()

            @pl.when(i == 3)
            def _():
                team.send_far_x()

            return 0

        lax.fori_loop(0, 4, step, 0)
        team.last()
        swaps[2].finish()
        cot.start()
        rings[1].forward()
        rings[2].start()
        swaps[3].finish()
        team.total1(total)
        cot.middle()
        team.total2(total)
        after = total[...] + enter_row[:, :width].astype(F32)
        after_out[...] = after
        row[...] = (after * rms_scale(after) * small_ref[1:2]).astype(BF)
        spread.start()
        rings[2].forward()
        rings[3].start()
        spread.middle()
        cot.finish()
        spread.finish()
        rings[3].forward()
        team.close()
        for ring in rings[1:]:
            ring.finish()

    block = jax.ShapeDtypeStruct(attn_blocks.shape, BF)
    four = jax.ShapeDtypeStruct((4,) + attn_blocks.shape, BF)
    rows = jax.ShapeDtypeStruct((2, 4, 2, 2, own, width), BF)
    return pl.pallas_call(
        kernel,
        out_shape=[
            four,
            jax.ShapeDtypeStruct((8, seq, width), BF),
            jax.ShapeDtypeStruct((8, seq, 4 * HEAD), BF),
            jax.ShapeDtypeStruct((8, seq, 2 * HEAD), BF),
            jax.ShapeDtypeStruct((8, seq, LANE), F32),
            jax.ShapeDtypeStruct((8, seq, LANE), BF),
            jax.ShapeDtypeStruct((own, width), F32),
            jax.ShapeDtypeStruct((own, width + LANE), BF),
            jax.ShapeDtypeStruct((own, width), BF),
            jax.ShapeDtypeStruct((LANE, width), BF),
            rows, rows, four, four, four, block, block, block, block,
        ],
        in_specs=[ANY] * 7 + [VMEM] * 3,
        out_specs=[VMEM] * 10 + [ANY] * 9,
        scratch_shapes=[
            pltpu.SemaphoreType.DMA((17,)),
            pltpu.VMEM((2, 4, 2, 2, own, width + LANE), BF),
            pltpu.VMEM((2, 4, 2, 2, own, width), BF),
            pltpu.VMEM((own, width), F32),
            pltpu.VMEM((own, width), BF),
        ]
        + TeamSum.scratch(own, width)
        + TeamSpread.sems * 3
        + Swap.sems * 4
        + RingY.sems * 4,
        name="attn_forward",
        **settings(collective, 200 << 20, 56),
    )(attn_blocks, *blocks, hidden, cotangent, routes, small, cosines, sines)[:15]


def back_through_norm(total, inputs, gain, gates, normed, routers):
    width = inputs.shape[1]
    logits_back = gates_back(gates, total[:, width:])
    full = total[:, :width] + mm(logits_back.astype(BF), routers)
    inner, gain_grad = norm_back(inputs, gain, full)
    return inner, gain_grad, mm_tn(logits_back.astype(BF), normed)[:8]


def row_block(array, block, count):
    cols = array.shape[-1] // 4
    part = array[..., pl.ds(pl.multiple_of(block * cols, cols), cols)]
    return part.reshape(count, cols)


class Pass:
    sems = [pltpu.SemaphoreType.DMA((4,))] * 2

    def __init__(self, src, dst, sems):
        send, recv = sems
        zh, c = lax.axis_index("zh"), lax.axis_index("c")
        mine, far = dst.at[zh, c], dst.at[1 - zh, c]
        self.copies = [
            pltpu.make_async_copy(src, mine, send.at[0]),
            push(src, mine, send.at[1], recv.at[1], {"zh": 1 - zh}),
            push(src, mine, send.at[2], recv.at[2], sibling()),
            push(far, far, send.at[3], recv.at[3], sibling()),
        ]

    def start(self):
        for copy in self.copies[:3]:
            copy.start()

    def finish(self):
        self.copies[1].wait_recv()
        self.copies[3].start()
        self.copies[0].wait()
        self.copies[1].wait_send()
        self.copies[2].wait()
        self.copies[3].wait()


def own_tile():
    zl, x, zh, c = (lax.axis_index(a) for a in TEAM)
    return zl * 4 + x, zh * 2 + c


def experts(collective, normed, cotangent, routes, weights, after, small, routers, cot_own, extra):
    own, width = after.shape
    count = normed.shape[0]
    cols = weights[0].shape[1]
    rows = width // 4
    tile = count // 4

    def kernel(
        x_ref, cot_ref, wg_ref, wu_ref, wd_ref, route_ref, after_ref, small_ref, router_ref, own_ref,
        mid_out, small_out, spread_out, s0, s1, g2, out_all,
        x, cot, wg, wu, wd, h, dg, du, g0, gates, part_a, part_b, load, total_a, total_b, row_a, row_b, *rest,
    ):
        loads = [(x_ref, x), (wg_ref, wg), (wu_ref, wu), (cot_ref, cot), (wd_ref, wd)]
        fetches = [pltpu.make_async_copy(a, b, load.at[k]) for k, (a, b) in enumerate(loads)]
        for fetch in fetches:
            fetch.start()
        meet([place(m) for m in TEAM_MOVES[1:] + [Y_MOVES[1], Y_MOVES[3]]] + [sibling()])
        n = TeamSum.count
        team_a, team_b = TeamSum(part_a, rest[:n]), TeamSum(part_b, rest[n : 2 * n])
        rest = rest[2 * n :]
        n = RingSum.count
        rings = [RingSum(g0, rest[:n]), RingSum(wg, rest[n : 2 * n])]
        rest = rest[2 * n :]
        spread = TeamSpread(row_a, spread_out, rest[:4])
        out = Pass(row_b, out_all, rest[4:6])
        gate_w, up_w = wg.reshape(width, cols), wu.reshape(width, cols)
        lane = EXPERTS + lax.axis_index("x")
        skip = lax.axis_index("zl") * extra

        def tokens(pair):
            return pl.ds(pl.multiple_of(pair * tile, tile), tile)

        def forward(pair, _):
            at = tokens(pair)
            x_t = x[at]
            gates_t = dense_gates(mm_nt(x_t, router_ref[...]), chosen(route_ref[at].astype(F32), EXPERTS))
            gates[at] = gates_t
            valid = (lax.broadcasted_iota(jnp.int32, (1, cols), 1) >= skip).astype(F32)
            gate = pick(gates_t, lane) * valid
            gate_part = mm(x_t, gate_w[...])
            up_part = mm(x_t, up_w[...])
            sigma = 1.0 / (1.0 + jnp.exp(-gate_part))
            silu = gate_part * sigma
            activated = silu * up_part
            h[at] = (activated * gate).astype(BF)

            @pl.when(pair == 0)
            def _():
                fetches[3].wait()
                fetches[4].wait()

            cot_down = mm(cot[at], wd[...])
            dots = jnp.sum(activated * valid * cot_down, axis=1, keepdims=True)
            grad_act = cot_down * gate
            dg[at] = (grad_act * up_part * sigma * (1.0 + gate_part * (1.0 - sigma))).astype(BF)
            du[at] = (grad_act * silu).astype(BF)
            hot = jnp.where(lanes(tile) == lane, dots, 0.0).astype(BF)
            part_a[pair // 2, pl.ds(lax.rem(pair, 2) * 2, 2), :, :, :, width:] = hot.reshape(
                2, 2, 2, own, LANE
            )
            return 0

        def summed(team, columns, values):
            def step(i, _):
                pair = team.pair(i)
                at = (pair // 2, pl.ds(lax.rem(pair, 2) * 2, 2), slice(None), slice(None), slice(None), columns)
                team.part[at] = values(tokens(pair)).astype(BF).reshape(2, 2, 2, own, width)
                for j in range(2):
                    team.swap(pair * 2 + j).start()

                @pl.when(i > 0)
                def _():
                    team.add_pair(i - 1)

                @pl.when(i == 2)
                def _():
                    team.send_far_z()

                @pl.when(i == 3)
                def _():
                    team.send_far_x()

                return 0

            lax.fori_loop(0, 4, step, 0)
            team.last()

        def product(left, right, dst):
            def one(block):
                dst[block] = mm_tn(row_block(left, block, count), right[...]).astype(BF)

            return one

        for fetch in fetches[:3]:
            fetch.wait()
        lax.fori_loop(0, 4, forward, 0)
        rings[0].start_with(product(x, dg, g0))
        summed(team_a, slice(0, width), lambda at: mm_nt(dg[at], gate_w[...]) + mm_nt(du[at], up_w[...]))
        rings[0].middle()
        rings[1].start_with(product(x, du, wg))
        team_a.total1(total_a)
        summed(team_b, slice(0, width), lambda at: mm_nt(h[at], wd[...]))
        after = after_ref[...]
        normed_own = (after * rms_scale(after) * small_ref[1:2]).astype(BF)
        seq, quarter = own_tile()
        gates_own = gates[pl.ds(pl.multiple_of((seq * 4 + quarter) * own, own), own)]
        team_a.total2(total_a)
        inner, gain_grad, router_grad = back_through_norm(
            total_a[...], after, small_ref[1:2], gates_own, normed_own, router_ref[...]
        )
        grad_mid = own_ref[...].astype(F32) + inner
        mid_out[...] = grad_mid
        row_a[...] = grad_mid.astype(BF)
        spread.start()
        rings[1].middle()
        small_out[:8] = jnp.zeros((8, width), F32)
        small_out[0:1] = gain_grad
        small_out[8:] = router_grad

        def down(block, _):
            product(cot, h, wu)(block)
            return 0

        lax.fori_loop(0, 4, down, 0)
        keep = pltpu.make_async_copy(wu, g2, load.at[0])
        keep.start()
        spread.middle()
        team_b.total1(total_b)
        spread.finish()
        team_b.total2(total_b)
        row_b[...] = in_order((after + total_b[...]).astype(BF))
        out.start()
        stores = []
        for ring, buffer, dst, k in ((rings[0], dg, s0, 1), (rings[1], du, s1, 2)):
            ring.finish(buffer.at[pl.ds(0, rows)])
            stores.append(pltpu.make_async_copy(buffer.at[pl.ds(0, rows)], dst, load.at[k]))
            stores[-1].start()
        out.finish()
        keep.wait()
        for store in stores:
            store.wait()
        team_a.close()
        team_b.close()

    return pl.pallas_call(
        kernel,
        out_shape=[
            jax.ShapeDtypeStruct((own, width), F32),
            jax.ShapeDtypeStruct((16, width), F32),
            jax.ShapeDtypeStruct((2, 4, 2, 2, own, width), BF),
            jax.ShapeDtypeStruct((rows, cols), BF),
            jax.ShapeDtypeStruct((rows, cols), BF),
            jax.ShapeDtypeStruct((4, rows, cols), BF),
            jax.ShapeDtypeStruct((2, 2, own, width), BF),
        ],
        in_specs=[ANY] * 5 + [VMEM] * 5,
        out_specs=[VMEM] * 2 + [ANY] * 5,
        scratch_shapes=[
            pltpu.VMEM((count, width), BF),
            pltpu.VMEM((count, width), BF),
            pltpu.VMEM((4, rows, cols), BF),
            pltpu.VMEM((4, rows, cols), BF),
            pltpu.VMEM((width, cols), BF),
            pltpu.VMEM((count, cols), BF),
            pltpu.VMEM((count, cols), BF),
            pltpu.VMEM((count, cols), BF),
            pltpu.VMEM((4, rows, cols), BF),
            pltpu.VMEM((count, LANE), F32),
            pltpu.VMEM((2, 4, 2, 2, own, width + LANE), BF),
            pltpu.VMEM((2, 4, 2, 2, own, width), BF),
            pltpu.SemaphoreType.DMA((5,)),
            pltpu.VMEM((own, width + LANE), F32),
            pltpu.VMEM((own, width), F32),
            pltpu.VMEM((own, width), BF),
            pltpu.VMEM((own, width), BF),
        ]
        + TeamSum.scratch(own, width + LANE)
        + TeamSum.scratch(own, width)
        + RingSum.scratch(rows, cols) * 2
        + TeamSpread.sems
        + Pass.sems,
        name="experts",
        **settings(collective, 300 << 20, 61),
    )(
        normed, cotangent, *[w.reshape(4, rows, cols) for w in weights[:2]], weights[2], routes,
        after, small, routers, cot_own,
    )


def in_order(values):
    block = values.shape[1] // 8
    order = [(b % 4) * 2 + b // 4 for b in range(8)]
    return jnp.concatenate([values[:, k * block : (k + 1) * block] for k in order], axis=1)


def attn_backward(
    collective, grad_mid, qkv, gated, normed, gates, weights, cosines, sines, mid_own, entered, gains, routers, small, summed, grads
):
    own, width = mid_own.shape
    seq = qkv.shape[1]
    rows, cols = grads.shape[1:]
    shard = rows // 8
    scale = HEAD ** (-0.5)
    stages = [X_MOVES, Y_MOVES, Z_MOVES]

    def kernel(
        gm_ref, w_ref, x_ref, g2_ref, y0, y1, qkv_ref, gated_ref, gates_ref, cos_ref, sin_ref,
        mid_ref, in_ref, gain_ref, router_ref, small_ref,
        grad_all, gain_a, gain_m, router_a, router_m, s0, s1, s2, s3,
        gm, w, x, g2, g3, y2, y3, proj, part, load, total, row,
        acc, got, other, rest_rows, csem, ssend, srecv, *rest,
    ):
        loads = [(gm_ref, gm), (w_ref, w), (g2_ref, g2), (x_ref, x)]
        fetches = [pltpu.make_async_copy(a, b, load.at[k]) for k, (a, b) in enumerate(loads)]
        for fetch in fetches:
            fetch.start()
        meet([place(m) for m in TEAM_MOVES[1:] + Y_MOVES[1:]] + [sibling()])
        n = TeamSum.count
        team, rest = TeamSum(part, rest[:n]), rest[n:]
        n = RingSum.count
        rings, rest = [RingSum(g2, rest[:n]), RingSum(g3, rest[n : 2 * n])], rest[2 * n :]
        swaps_back = [
            Swap(y, s, rest[2 * k : 2 * k + 2]) for k, (y, s) in enumerate(((y0, s0), (y1, s1), (y2, s2)))
        ]
        last_swap = ColumnSwap(y3, s3, rest[6:8])
        out = Pass(row, grad_all, rest[8:10])
        first = 2 * team.zl
        causal = causal_mask(2, seq)
        swaps_back[0].start()
        swaps_back[1].start()
        fetches[0].wait()
        fetches[1].wait()

        def step(i, _):
            pair = team.pair(i)
            grads = mm(gm[pl.ds(pair * 2, 2)].reshape(2 * seq, width), w[:, 4 * HEAD :])
            both = []
            for j in range(2):
                at = pair * 2 + j
                here = slice(j * seq, (j + 1) * seq)
                query = jnp.concatenate(
                    [qkv_ref[at, :, e * HEAD : (e + 1) * HEAD] for e in range(2)], axis=0
                )
                key = qkv_ref[at, :, 2 * HEAD : 3 * HEAD]
                value = qkv_ref[at, :, 3 * HEAD :]
                probs = soft(mm_nt(query, key) * scale, causal)
                probs_b = probs.astype(BF)
                attended = mm(probs_b, value)
                grad = jnp.concatenate(
                    [grads[here, e * HEAD : (e + 1) * HEAD] for e in range(2)], axis=0
                )
                gates = gates_ref[at]
                gate = jnp.concatenate([pick(gates, first + e) for e in range(2)], axis=0)
                each = jnp.sum(attended * grad, axis=1, keepdims=True)
                dots = jnp.where(lanes(seq) == first, each[:seq], 0.0)
                dots += jnp.where(lanes(seq) == first + 1, each[seq:], 0.0)
                grad = (grad * gate).astype(BF)
                grad_probs = mm_nt(grad, value)
                inner = jnp.sum(probs * grad_probs, axis=1, keepdims=True)
                grad_scores = (probs * (grad_probs - inner) * scale).astype(BF)
                turned = [mm(grad_scores, key), mm_tn(grad_scores, query)]
                turned = [turned[0][:seq], turned[0][seq:], turned[1]]
                turned = [rotate(t, cos_ref[...], -sin_ref[...]).astype(BF) for t in turned]
                grad_value = mm_tn(probs_b, grad).astype(BF)
                both.append(jnp.concatenate(turned + [grad_value], axis=1))
                proj[at] = both[-1]
                part[pair // 2, lax.rem(pair, 2) * 2 + j, :, :, :, width:] = dots.astype(BF).reshape(
                    2, 2, own, LANE
                )
            back = mm_nt(jnp.concatenate(both, axis=0), w[:, : 4 * HEAD])
            part[pair // 2, pl.ds(lax.rem(pair, 2) * 2, 2), :, :, :, :width] = back.astype(BF).reshape(
                2, 2, 2, own, width
            )
            for j in range(2):
                team.swap(pair * 2 + j).start()

            @pl.when(i == 0)
            def _():
                fetches[2].wait()
                rings[0].start()

            @pl.when(i > 0)
            def _():
                team.add_pair(i - 1)

            @pl.when(i == 2)
            def _():
                team.send_far_z()

            @pl.when(i == 3)
            def _():
                team.send_far_x()

            return 0

        lax.fori_loop(0, 4, step, 0)
        team.last()
        fetches[3].wait()

        def product(block):
            g3[block, :, : 4 * HEAD] = mm_tn(
                row_block(x, block, 8 * seq), proj[...].reshape(8 * seq, 4 * HEAD)
            ).astype(BF)
            g3[block, :, 4 * HEAD :] = mm_tn(
                row_block(gm, block, 8 * seq), gated_ref[...].reshape(8 * seq, 2 * HEAD)
            ).astype(BF)

        rings[1].start_with(product)
        rings[0].middle()
        inputs = in_ref[:, :width].astype(F32)
        normed_own = (inputs * rms_scale(inputs) * gain_ref[0:1]).astype(BF)
        own_seq, quarter = own_tile()
        gates_own = gates_ref[own_seq, pl.ds(pl.multiple_of(quarter * own, own), own)]
        team.total1(total)
        rings[1].middle()
        team.total2(total)
        inner, gain_grad, router_grad = back_through_norm(
            total[...], inputs, gain_ref[0:1], gates_own, normed_own, router_ref[...]
        )
        row[...] = in_order((mid_ref[...] + inner).astype(BF))
        out.start()
        acc[...] = small_ref[...]
        acc[1:2] = gain_grad
        acc[8:] += router_grad
        c = lax.axis_index("c")
        half = pl.ds(pl.multiple_of(c * 8, 8), 8)
        rest_half = pl.ds(pl.multiple_of((1 - c) * 8, 8), 8)
        over = push(acc.at[rest_half], other, csem.at[0], csem.at[1], sibling())
        over.start()
        over.wait()
        acc[half] = acc[half] + other[...]
        for s, stage in enumerate(stages):
            swaps = [
                push(acc.at[half], got.at[s, k - 1], ssend.at[s, k], srecv.at[s, k], place(stage[k]))
                for k in range(1, 4)
            ]
            for swap in swaps:
                swap.start()
            if s == 0:
                rings[0].finish(y2)
                swaps_back[2].start()
            if s == 1:
                rings[1].finish(y3)
                last_swap.start()
            for swap in swaps:
                swap.wait()
            acc[half] = acc[half] + got[s, 0] + got[s, 1] + got[s, 2]
        back_over = push(acc.at[half], rest_rows, csem.at[2], csem.at[3], sibling())
        back_over.start()
        out.finish()
        back_over.wait()
        acc[rest_half] = rest_rows[...]
        final = in_order(acc[...])
        for ref, at in ((gain_m, 0), (gain_a, 1)):
            for k in range(width // LANE):
                ref[k : k + 1] = final[at : at + 1, k * LANE : (k + 1) * LANE]
        router_a[...] = final[8 : 8 + EXPERTS]
        router_m[...] = final[8 + EXPERTS :]
        for swap in swaps_back + [last_swap]:
            swap.finish()
        team.close()

    block = jax.ShapeDtypeStruct((8, shard, cols), BF)
    heads = cols // HEAD
    return pl.pallas_call(
        kernel,
        out_shape=[
            jax.ShapeDtypeStruct((2, 2, own, width), BF),
            jax.ShapeDtypeStruct((width // LANE, LANE), F32),
            jax.ShapeDtypeStruct((width // LANE, LANE), F32),
            jax.ShapeDtypeStruct((EXPERTS, width), F32),
            jax.ShapeDtypeStruct((EXPERTS, width), F32),
            block, block, block,
            jax.ShapeDtypeStruct((2, heads, shard, 4 * HEAD), BF),
        ],
        in_specs=[ANY] * 6 + [VMEM] * 10,
        out_specs=[ANY] + [VMEM] * 4 + [ANY] * 4,
        scratch_shapes=[
            pltpu.VMEM((8, seq, width), BF),
            pltpu.VMEM(weights.shape, BF),
            pltpu.VMEM((8, seq, width), BF),
            pltpu.VMEM((4, rows, cols), BF),
            pltpu.VMEM((4, rows, cols), BF),
            pltpu.VMEM((8, shard, cols), BF),
            pltpu.VMEM((8, heads, shard, HEAD), BF),
            pltpu.VMEM((8, seq, 4 * HEAD), BF),
            pltpu.VMEM((2, 4, 2, 2, own, width + LANE), BF),
            pltpu.SemaphoreType.DMA((4,)),
            pltpu.VMEM((own, width + LANE), F32),
            pltpu.VMEM((own, width), BF),
            pltpu.VMEM((16, width), F32),
            pltpu.VMEM((3, 3, 8, width), F32),
            pltpu.VMEM((8, width), F32),
            pltpu.VMEM((8, width), F32),
            pltpu.SemaphoreType.DMA((4,)),
        ]
        + [pltpu.SemaphoreType.DMA((4, 4))] * 2
        + TeamSum.scratch(own, width + LANE)
        + RingSum.scratch(rows, cols) * 2
        + Swap.sems * 4
        + Pass.sems,
        name="attn_backward",
        **settings(collective, 200 << 20, 58),
    )(
        grad_mid.reshape(8, seq, width), weights, normed, grads, *summed, qkv, gated, gates, cosines, sines,
        mid_own, entered, gains, routers, small,
    )


def reorder(array, axis):
    shape = array.shape
    split = shape[:axis] + (2, 4, shape[axis] // 8) + shape[axis + 1 :]
    return jnp.swapaxes(array.reshape(split), axis, axis + 1).reshape(shape)


def local(
    hidden,
    cotangent,
    attn_gain,
    attn_router,
    qkv_weight,
    out_weight,
    mlp_gain,
    mlp_router,
    gate_up_weight,
    down_weight,
    attn_route,
    attn_slot,
    mlp_route,
    mlp_slot,
):
    seq, width = hidden.shape
    rows = qkv_weight.shape[0]
    features = down_weight.shape[2]
    part = (features // LANE + 1) // 2 * LANE
    low = features - part
    group = 8 * seq
    cosines, sines = rope_tables(seq)

    query_blocks = qkv_weight[:, :EXPERTS].reshape(rows, 2, 2, 4, HEAD).transpose(1, 3, 0, 2, 4)
    kv_blocks = qkv_weight[:, EXPERTS:].reshape(rows, 2, 4, HEAD).transpose(2, 0, 1, 3)
    kv_blocks = jnp.broadcast_to(kv_blocks[None], (2,) + kv_blocks.shape)
    out_blocks = out_weight.reshape(rows, 2, 2, 4, HEAD).transpose(1, 3, 0, 2, 4)
    attn_blocks = jnp.concatenate([query_blocks, kv_blocks, out_blocks], axis=3)
    attn_blocks = attn_blocks.reshape(8, rows, 6 * HEAD)

    def by_target(weight):
        weight = weight.transpose(1, 0, 2)
        return jnp.stack([weight[..., :part], weight[..., low:]], axis=0).reshape(8, rows, part)

    mlp_blocks = [
        by_target(w) for w in (gate_up_weight[:, :, 0], gate_up_weight[:, :, 1], down_weight)
    ]

    none = jnp.zeros((6, width), F32)
    routers = jnp.concatenate([attn_router, mlp_router], axis=1).astype(F32).T
    small = jnp.concatenate([attn_gain[None], mlp_gain[None], none, routers], axis=0)
    small = reorder(small, 1)
    routes = jnp.concatenate([attn_route, jnp.zeros_like(attn_route), mlp_route], axis=1)
    routes = jnp.pad(routes, ((0, 0), (0, LANE - 6))).astype(BF)

    (
        attn_w, normed_a, qkv, gated_att, gates_a, group_routes, after, entered, cot_own, routers,
        normed_m, group_cot, *mlp_w,
    ) = attn_forward(1, attn_blocks, mlp_blocks, hidden, cotangent, routes, small, cosines, sines)
    attn_w = attn_w.reshape(width, 6 * HEAD)
    mlp_w = [w.reshape(width, part) for w in mlp_w]
    group_cot = group_cot.reshape(group, width)
    normed_m = normed_m.reshape(group, width)

    grad_mid_own, small_m, grad_mid, gate_sum, up_sum, down_part, out_hidden = experts(
        2, normed_m, group_cot, group_routes.reshape(group, LANE), mlp_w, after, small, routers, cot_own,
        2 * part - features,
    )
    gate_sum, up_sum = (a.reshape(8, rows, part) for a in (gate_sum, up_sum))
    grad_in, gain_a, gain_m, router_a, router_m, *mlp_grads, attn_grads = attn_backward(
        3, grad_mid, qkv, gated_att, normed_a, gates_a, attn_w, cosines, sines, grad_mid_own, entered, small,
        routers, small_m, [gate_sum, up_sum], down_part,
    )
    out_hidden = out_hidden.reshape(seq, width)
    grad_in = grad_in.reshape(seq, width).astype(F32)

    attn_grads = attn_grads.astype(F32)
    query_grad = attn_grads[:, :2].reshape(EXPERTS, rows, 4 * HEAD)
    kv_grad = attn_grads[0, 2:4] + attn_grads[1, 2:4]
    qkv_grad = jnp.concatenate([query_grad, kv_grad], axis=0).transpose(1, 0, 2)
    out_grad = attn_grads[:, 4:].reshape(EXPERTS, rows, 4 * HEAD).transpose(1, 0, 2)

    def placed_back(grad):
        grad = grad.reshape(2, EXPERTS, rows, part)
        return jnp.concatenate([grad[0], grad[1, ..., 2 * part - features :]], axis=-1).transpose(1, 0, 2)

    gate_grad, up_grad, down_grad = [placed_back(g) for g in mlp_grads]
    return (
        out_hidden,
        grad_in,
        gain_a.reshape(width),
        router_a.T,
        qkv_grad,
        out_grad,
        gain_m.reshape(width),
        router_m.T,
        jnp.stack([gate_grad, up_grad], axis=2).astype(F32),
        down_grad.astype(F32),
    )


def solution(mesh):
    fine = Mesh(mesh.devices.reshape(2, 4, 4, 2, 2), ALL)
    dp, tensor = ("zl", "y", "x"), ("zh", "c")
    placed = (
        P(dp, None),
        P(dp, None),
        P(),
        P(),
        P(dp, None, tensor),
        P(dp, None, tensor),
        P(),
        P(),
        P(dp, None, None, tensor),
        P(dp, None, tensor),
        P(dp, None),
        P(dp, None),
        P(dp, None),
        P(dp, None),
    )
    return jax.shard_map(
        local,
        mesh=fine,
        in_specs=placed,
        out_specs=(
            P(dp, None),
            P(dp, None),
            P(),
            P(),
            P(dp, None, tensor),
            P(dp, None, tensor),
            P(),
            P(),
            P(dp, None, None, tensor),
            P(dp, None, tensor),
        ),
        check_vma=False,
    )
```

```python
import itertools

import jax
import jax.numpy as jnp
import numpy as np
from jax import lax
from jax.experimental import pallas as pl
from jax.experimental.pallas import tpu as pltpu
from jax.sharding import Mesh, PartitionSpec as P

HEAD = 128
LANE = 128
EPS = 1e-05
THETA = 10000.0
NEG = -1e30
EXPERTS = 4
GROUP = ("zl", "x")
TEAM = ("zl", "x", "zh", "c")
ALL = ("zl", "y", "x", "zh", "c")
SIZES = dict(zl=2, y=4, x=4, zh=2, c=2)
BF = jnp.bfloat16
F32 = jnp.float32
MESH = pl.DeviceIdType.MESH
ANY = pl.BlockSpec(memory_space=pl.ANY)
VMEM = pl.BlockSpec(memory_space=pltpu.VMEM)


def dot(a, b, dims):
    return lax.dot_general(a, b, (dims, ((), ())), preferred_element_type=F32)


def mm(a, b):
    return dot(a, b, ((1,), (0,)))


def mm_nt(a, b):
    return dot(a, b, ((1,), (1,)))


def mm_tn(a, b):
    return dot(a, b, ((0,), (0,)))


def rms_scale(values):
    return lax.rsqrt(jnp.mean(values * values, axis=-1, keepdims=True) + EPS)


def lanes(rows):
    return lax.broadcasted_iota(jnp.int32, (rows, LANE), 1)


def chosen(routes, first):
    lane = lanes(routes.shape[0])
    named = [pick(routes, first + c).astype(jnp.int32) + first for c in range(2)]
    return (lane == named[0]) | (lane == named[1])


def dense_gates(logits, mask):
    top = jnp.max(jnp.where(mask, logits, NEG), axis=1, keepdims=True)
    expon = jnp.where(mask, jnp.exp(jnp.where(mask, logits - top, 0.0)), 0.0)
    return expon / jnp.sum(expon, axis=1, keepdims=True)


def pick(values, lane):
    return jnp.sum(jnp.where(lanes(values.shape[0]) == lane, values, 0.0), axis=1, keepdims=True)


def gates_back(gates, gated_dots):
    return gated_dots - gates * jnp.sum(gated_dots, axis=1, keepdims=True)


def rope_tables(count):
    frequency = THETA ** (-(np.arange(HEAD // 2).astype(np.float32) * 2.0 / HEAD))
    angles = np.arange(count).astype(np.float32)[:, None] * frequency[None, :].astype(np.float32)
    cosines, sines = np.cos(angles), np.sin(angles)
    return (
        jnp.asarray(np.concatenate([cosines, cosines], axis=1), F32),
        jnp.asarray(np.concatenate([-sines, sines], axis=1), F32),
    )


def rotate(values, cosines, sines):
    return values * cosines + pltpu.roll(values, HEAD // 2, 1) * sines


def norm_back(inputs, gain, grad_normed):
    scale = rms_scale(inputs)
    scaled = inputs * scale
    grad_scaled = grad_normed * gain
    grad_inputs = scale * (
        grad_scaled - scaled * jnp.mean(grad_scaled * scaled, axis=-1, keepdims=True)
    )
    return grad_inputs, jnp.sum(grad_normed * scaled, axis=0, keepdims=True)


def moves(*axes):
    return [dict(zip(axes, steps)) for steps in itertools.product(*[range(SIZES[a]) for a in axes])]


def place(move, sign=1):
    return {a: lax.rem(lax.axis_index(a) + sign * v + SIZES[a], SIZES[a]) for a, v in move.items()}


def number(coords):
    total = 0
    for axis, value in coords.items():
        total = total * SIZES[axis] + value
    return total


def meet(partners):
    barrier = pltpu.get_barrier_semaphore()
    for partner in partners:
        pl.semaphore_signal(barrier, inc=1, device_id=partner, device_id_type=MESH)
    pl.semaphore_wait(barrier, len(partners))


def push(src, dst, send, recv, to):
    return pltpu.make_async_remote_copy(
        src_ref=src, dst_ref=dst, send_sem=send, recv_sem=recv, device_id=to, device_id_type=MESH
    )


def settings(number, moved, vmem=32):
    return dict(
        compiler_params=pltpu.CompilerParams(
            collective_id=number, has_side_effects=True, vmem_limit_bytes=vmem << 20
        ),
        cost_estimate=pl.CostEstimate(flops=0, bytes_accessed=moved, transcendentals=0),
    )


GROUP_MOVES = moves("zl", "x")
TEAM_MOVES = moves("zl", "x", "zh")
X_MOVES = moves("x")
Y_MOVES = moves("y")
Z_MOVES = moves("zl", "zh")


def sibling():
    return {"c": 1 - lax.axis_index("c")}


class RingY:
    sems = [pltpu.SemaphoreType.DMA((5,)), pltpu.SemaphoreType.DMA((5,))]

    def __init__(self, src, out, sems):
        self.src, self.out = src, out
        self.send, self.recv = sems
        self.y = lax.axis_index("y")
        self.half = src.shape[0] // 2

    def line(self, step):
        return lax.rem(self.y + step, 4)

    def copy(self, k):
        y = self.y
        if k < 2:
            src, dst, to = self.src, self.out.at[y], self.line((1, 3)[k])
        else:
            half = pl.ds((k - 2) * self.half, self.half)
            src = dst = self.out.at[self.line((3, 1)[k - 2]), half]
            to = self.line((1, 3)[k - 2])
        return push(src, dst, self.send.at[k], self.recv.at[k], {"y": to})

    def start(self):
        self.stay = pltpu.make_async_copy(self.src, self.out.at[self.y], self.send.at[4])
        for k in range(2):
            self.copy(k).start()
        self.stay.start()

    def forward(self):
        for k in range(2):
            self.copy(k).wait_recv()
            self.copy(k + 2).start()

    def finish(self):
        for k in range(2):
            self.copy(k + 2).wait_recv()
        for k in range(4):
            self.copy(k).wait_send()
        self.stay.wait()

    def finish_first(self):
        for k in range(2):
            self.copy(k).wait()
        self.stay.wait()


class RingRest:
    sems = [pltpu.SemaphoreType.DMA((5,)), pltpu.SemaphoreType.DMA((2,))]

    def __init__(self, src, out, sems):
        self.y = lax.axis_index("y")
        rows = src.shape[1] // 2
        send, recv = sems
        self.copies = [
            pltpu.make_async_copy(src.at[self.line(step)], out.at[self.line(step)], send.at[2 + k])
            for k, step in enumerate((0, 1, 3))
        ]
        for k in range(2):
            here = (self.line((3, 1)[k]), pl.ds(k * rows, rows))
            to = {"y": self.line((1, 3)[k])}
            self.copies.append(push(src.at[here], out.at[here], send.at[k], recv.at[k], to))

    def line(self, step):
        return lax.rem(self.y + step, 4)

    def start_here(self):
        for copy in self.copies[:3]:
            copy.start()

    def start(self):
        for copy in self.copies[3:]:
            copy.start()

    def finish(self):
        for copy in self.copies:
            copy.wait()


class Swap:
    sems = [pltpu.SemaphoreType.DMA((8,))] * 2

    def __init__(self, src, dst, sems):
        self.src, self.dst = src, dst
        self.send, self.recv = sems

    def start(self):
        me = number(place(GROUP_MOVES[0]))
        self.copies = [
            pltpu.make_async_copy(self.src.at[me], self.dst.at[me], self.send.at[0])
        ]
        for k, move in enumerate(GROUP_MOVES):
            if k:
                to = place(move)
                self.copies.append(
                    push(
                        self.src.at[number(to)],
                        self.dst.at[me],
                        self.send.at[k],
                        self.recv.at[k],
                        to,
                    )
                )
        for copy in self.copies:
            copy.start()

    def finish(self):
        for copy in self.copies:
            copy.wait()


class ExpertSwap(Swap):
    def start(self):
        me = number(place(GROUP_MOVES[0]))
        part = self.dst.shape[2]
        low = self.src.shape[2] - part
        self.copies = []
        for k, move in enumerate(GROUP_MOVES):
            to = place(move)
            block = self.src.at[to["x"], :, pl.ds(pl.multiple_of(to["zl"] * low, LANE), part)]
            if k:
                self.copies.append(
                    push(block, self.dst.at[me], self.send.at[k], self.recv.at[k], to)
                )
            else:
                self.copies.append(pltpu.make_async_copy(block, self.dst.at[me], self.send.at[0]))
        for copy in self.copies:
            copy.start()


class ColumnSwap(Swap):
    def start(self):
        zl, x = lax.axis_index("zl"), lax.axis_index("x")
        mine = self.dst.at[zl, :, :, pl.ds(pl.multiple_of(x * HEAD, HEAD), HEAD)]
        self.copies = [
            pltpu.make_async_copy(self.src.at[zl * 4 + x], mine, self.send.at[0])
        ]
        for k, move in enumerate(GROUP_MOVES):
            if k:
                to = place(move)
                block = self.src.at[number(to)]
                self.copies.append(push(block, mine, self.send.at[k], self.recv.at[k], to))
        for copy in self.copies:
            copy.start()


class RingSum:
    @staticmethod
    def scratch(rows, cols):
        return [
            pltpu.VMEM((2, rows // 2, cols), BF),
            pltpu.VMEM((2, rows // 2, cols), BF),
            pltpu.VMEM((2, rows, cols), BF),
            pltpu.SemaphoreType.DMA((6,)),
            pltpu.SemaphoreType.DMA((6,)),
        ]

    count = 5

    def __init__(self, part, scratch):
        self.part = part
        self.got, self.mix, self.sums, self.send, self.recv = scratch
        self.y = lax.axis_index("y")
        half = part.shape[1] // 2
        self.halves = [pl.ds(0, half), pl.ds(half, half)]

    def line(self, step):
        return lax.rem(self.y + step, 4)

    def copy(self, k):
        kind, way = k // 2, k % 2
        step = (1, 3)[way]
        top, low = self.halves[way], self.halves[1 - way]
        if kind == 0:
            src, dst = self.part.at[self.line(2), top], self.got.at[way]
        elif kind == 1:
            src, dst = self.part.at[self.line(step), low], self.sums.at[way, low]
        else:
            src, dst = self.mix.at[way], self.sums.at[way, top]
        return push(src, dst, self.send.at[k], self.recv.at[k], {"y": self.line(step)})

    def start(self):
        for k in range(4):
            self.copy(k).start()

    def start_with(self, product):
        product(self.line(2))
        self.copy(0).start()
        self.copy(1).start()
        product(self.line(1))
        self.copy(2).start()
        product(self.line(3))
        self.copy(3).start()
        product(self.y)

    def middle(self):
        for way in range(2):
            self.copy(way).wait_recv()
            mine = self.part[self.line((1, 3)[way]), self.halves[way]].astype(F32)
            self.mix[way] = (mine + self.got[way].astype(F32)).astype(BF)
            self.copy(4 + way).start()

    def finish(self, out):
        for k in range(2, 6):
            self.copy(k).wait_recv()
        total = self.part[self.y].astype(F32) + self.sums[0].astype(F32) + self.sums[1].astype(F32)
        total = total.astype(BF)
        if len(out.shape) < 4:
            out[...] = total.reshape(out.shape)
        else:
            targets, count, rows, cols = out.shape
            for t in range(targets):
                for n in range(count):
                    out[t, n] = total[t * rows : (t + 1) * rows, n * cols : (n + 1) * cols]
        for k in range(6):
            self.copy(k).wait_send()


class TeamSum:
    @staticmethod
    def scratch(own, width):
        half = own // 2
        return [
            pltpu.VMEM((8, 2, own, width), BF),
            pltpu.VMEM((3, 2, 2, half, width), BF),
            pltpu.VMEM((3, 4, half, width), BF),
            pltpu.VMEM((6, half, width), BF),
            pltpu.SemaphoreType.DMA((8,)),
            pltpu.SemaphoreType.DMA((8,)),
            pltpu.SemaphoreType.DMA((6,)),
            pltpu.SemaphoreType.DMA((6,)),
            pltpu.SemaphoreType.DMA((6,)),
            pltpu.SemaphoreType.DMA((6,)),
        ]

    count = 10

    def __init__(self, part, scratch):
        self.part = part
        self.other, self.got_x, self.got_z, self.late = scratch[:4]
        self.ssem, self.rsem, self.send1, self.recv1, self.send2, self.recv2 = scratch[4:]
        self.zl, self.x, self.zh, self.c = (lax.axis_index(a) for a in TEAM)
        self.half = part.shape[4] // 2
        self.top, self.low = pl.ds(0, self.half), pl.ds(self.half, self.half)

    def swap(self, seq):
        return push(
            self.part.at[seq // 4, lax.rem(seq, 4), :, 1 - self.c],
            self.other.at[seq],
            self.ssem.at[seq],
            self.rsem.at[seq],
            sibling(),
        )

    def send_x(self, x):
        slot = lax.rem(x - self.x + 4, 4) - 1
        return push(
            self.part.at[:, x, :, self.c, self.top],
            self.got_x.at[slot],
            self.send1.at[slot],
            self.recv1.at[slot],
            {"x": x},
        )

    def send_z(self, zl, zh):
        slot = lax.rem(zl - self.zl + 2, 2) * 2 + lax.rem(zh - self.zh + 2, 2) - 1
        return push(
            self.part.at[zl, :, zh, self.c, self.low],
            self.got_z.at[slot],
            self.send1.at[3 + slot],
            self.recv1.at[3 + slot],
            {"zl": zl, "zh": zh},
        )

    def late_z(self, k):
        to = place(Z_MOVES[k])
        return push(
            self.part.at[to["zl"], self.x, to["zh"], self.c, self.top],
            self.late.at[k - 1],
            self.send2.at[k - 1],
            self.recv2.at[k - 1],
            to,
        )

    def late_x(self, k):
        to = place(X_MOVES[k])
        return push(
            self.part.at[self.zl, to["x"], self.zh, self.c, self.low],
            self.late.at[2 + k],
            self.send2.at[2 + k],
            self.recv2.at[2 + k],
            to,
        )

    def add(self, seq):
        self.swap(seq).wait_recv()
        zl, x = seq // 4, lax.rem(seq, 4)
        for zh in range(2):
            mine = self.part[zl, x, zh, self.c].astype(F32)
            self.part[zl, x, zh, self.c] = (mine + self.other[seq, zh].astype(F32)).astype(BF)

    def pair(self, step):
        back = 3 - step
        return lax.rem(self.zl + back // 2, 2) * 2 + lax.rem(self.x // 2 + back, 2)

    def add_pair(self, step):
        for j in range(2):
            self.add(self.pair(step) * 2 + j)

    def send_far_z(self):
        for zh in range(2):
            self.send_z(1 - self.zl, zh).start()

    def send_far_x(self):
        for j in range(2):
            self.send_x((1 - self.x // 2) * 2 + j).start()

    def last(self):
        self.add_pair(3)
        self.send_x(self.x + 1 - 2 * lax.rem(self.x, 2)).start()
        self.send_z(self.zl, 1 - self.zh).start()

    def got(self, ref, sem):
        pltpu.make_async_copy(ref, ref, sem).wait()

    def total(self, total_ref):
        self.total1(total_ref)
        self.total2(total_ref)

    def total1(self, total_ref):
        half, c = self.half, self.c
        for k in range(3):
            self.got(self.got_x.at[k], self.recv1.at[k])
        for k, move in reversed(list(enumerate(Z_MOVES))):
            at = place(move)
            rows = self.part[at["zl"], self.x, at["zh"], c, :half].astype(F32)
            for j in range(3):
                rows += self.got_x[j, at["zl"], at["zh"]].astype(F32)
            if k:
                self.part[at["zl"], self.x, at["zh"], c, :half] = rows.astype(BF)
                self.late_z(k).start()
            else:
                total_ref[:half] = rows
        for k in range(3):
            self.got(self.got_z.at[k], self.recv1.at[3 + k])
        for k, move in reversed(list(enumerate(X_MOVES))):
            at = place(move)
            rows = self.part[self.zl, at["x"], self.zh, c, half:].astype(F32)
            for j in range(3):
                rows += self.got_z[j, at["x"]].astype(F32)
            if k:
                self.part[self.zl, at["x"], self.zh, c, half:] = rows.astype(BF)
                self.late_x(k).start()
            else:
                total_ref[half:] = rows

    def total2(self, total_ref):
        half = self.half
        for k in range(3):
            self.got(self.late.at[k], self.recv2.at[k])
            total_ref[:half] += self.late[k].astype(F32)
        for k in range(3):
            self.got(self.late.at[3 + k], self.recv2.at[3 + k])
            total_ref[half:] += self.late[3 + k].astype(F32)

    def close(self):
        for seq in range(8):
            self.swap(seq).wait_send()
        for k in range(1, 4):
            x, z = place(X_MOVES[k])["x"], place(Z_MOVES[k])
            self.send_x(x).wait_send()
            self.send_z(z["zl"], z["zh"]).wait_send()
            self.late_z(k).wait_send()
            self.late_x(k).wait_send()

    def swap_all(self):
        for step in range(4):
            for j in range(2):
                self.swap(self.pair(step) * 2 + j).start()

    def add_all(self):
        self.add_pair(0)
        self.add_pair(1)
        self.send_far_z()
        self.add_pair(2)
        self.send_far_x()
        self.last()


class TeamSpread:
    sems = [pltpu.SemaphoreType.DMA((12,))] * 2 + [pltpu.SemaphoreType.DMA((9,))] * 2

    def __init__(self, rows, out, sems):
        self.rows, self.out = rows, out
        self.send, self.recv, self.fsend, self.frecv = sems
        self.zl, self.x, self.zh, self.c = (lax.axis_index(a) for a in TEAM)
        self.half = rows.shape[0] // 2
        self.top, self.low = pl.ds(0, self.half), pl.ds(self.half, self.half)

    def tops(self, zl, zh):
        return self.out.at[zl, :, zh, self.c, self.top]

    def lows(self, x):
        return self.out.at[:, x, :, self.c, self.low]

    def hop(self, k, src, dst, to):
        return push(src, dst, self.send.at[k], self.recv.at[k], to)

    def first(self, k):
        here = (self.zl, self.x, self.zh, self.c)
        if k < 3:
            return self.hop(k, self.rows.at[self.top], self.out.at[(*here, self.top)], place(X_MOVES[k + 1]))
        return self.hop(k, self.rows.at[self.low], self.out.at[(*here, self.low)], place(Z_MOVES[k - 2]))

    def second(self, k):
        if k < 3:
            block = self.tops(self.zl, self.zh)
            return self.hop(6 + k, block, block, place(Z_MOVES[k + 1]))
        block = self.lows(self.x)
        return self.hop(6 + k, block, block, place(X_MOVES[k - 2]))

    def forward(self, k, block):
        return push(block, block, self.fsend.at[k], self.frecv.at[k], sibling())

    def start(self):
        self.stay = pltpu.make_async_copy(
            self.rows, self.out.at[self.zl, self.x, self.zh, self.c], self.fsend.at[8]
        )
        for k in range(6):
            self.first(k).start()
        self.stay.start()

    def middle(self):
        self.stay.wait()
        for k in range(3):
            self.first(k).wait_recv()
        for k in range(3):
            self.second(k).start()
        self.forward(0, self.tops(self.zl, self.zh)).start()
        for k in range(3, 6):
            self.first(k).wait_recv()
        for k in range(3, 6):
            self.second(k).start()
        self.forward(1, self.lows(self.x)).start()

    def block(self, k):
        if k < 3:
            at = place(Z_MOVES[k + 1], -1)
            return self.tops(at["zl"], at["zh"])
        return self.lows(place(X_MOVES[k - 2], -1)["x"])

    def finish(self):
        for k in range(6):
            self.second(k).wait_recv()
            self.forward(2 + k, self.block(k)).start()
        blocks = [self.tops(self.zl, self.zh), self.lows(self.x)] + [self.block(k) for k in range(6)]
        for k in range(8):
            self.forward(k, blocks[k]).wait()
        for k in range(6):
            self.first(k).wait_send()
            self.second(k).wait_send()


def soft(scores, causal):
    scores = jnp.where(causal, scores, NEG)
    expon = jnp.exp(scores - jnp.max(scores, axis=-1, keepdims=True))
    return expon / jnp.sum(expon, axis=-1, keepdims=True)


def causal_mask(copies, seq):
    rows = lax.rem(lax.broadcasted_iota(jnp.int32, (copies * seq, seq), 0), seq)
    return lax.broadcasted_iota(jnp.int32, (copies * seq, seq), 1) <= rows


def attn_forward(
    collective, attn_blocks, blocks, part_cols, hidden, cotangent, gains, routers, routes, cosines, sines
):
    seq, width = hidden.shape
    own = seq // 4
    piece = width // 8
    scale = HEAD ** (-0.5)

    def kernel(
        a_ref, b0, b1, b2, hidden_ref, cotangent_ref,
        gain_a, gain_m, router_a, router_m, route_a, route_m, cos_ref, sin_ref,
        w_out, normed_out, qkv_out, gated_out, gates_out, routes_out, after_out, enter_row, cot_row, router_ref, small_ref,
        spread_out, cot_out, w0, w1, w2, a_mid, m0, m1, m2,
        turned, load, hid, part, total, row, *rest,
    ):
        mine = pl.ds(pl.multiple_of(own_tile()[1] * own, own), own)
        loads = []
        for b in range(8):
            here, there = pl.ds(b * piece, piece), pl.ds(((b % 4) * 2 + b // 4) * piece, piece)
            loads.append((hidden_ref.at[mine, here], enter_row.at[:, there]))
            loads.append((cotangent_ref.at[mine, here], cot_row.at[:, there]))
        fetches = [pltpu.make_async_copy(a, b, load.at[k]) for k, (a, b) in enumerate(loads)]
        for fetch in fetches:
            fetch.start()
        meet([place(m) for m in TEAM_MOVES[1:] + [Y_MOVES[1], Y_MOVES[3]]] + [sibling()])
        n = TeamSum.count
        team, rest = TeamSum(part, rest[:n]), rest[n:]
        enters = TeamSpread(enter_row, hid, rest[:4])
        cot = TeamSpread(cot_row, cot_out, rest[4:8])
        spread = TeamSpread(row, spread_out, rest[8:12])
        rest = rest[12:]
        swaps = [Swap(a_ref, a_mid, rest[:2])] + [
            ExpertSwap(b, m, rest[2 * k : 2 * k + 2])
            for k, (b, m) in ((1, (b0, m0)), (2, (b1, m1)), (3, (b2, m2)))
        ]
        rings = [
            RingY(m, w, rest[8 + 2 * k : 10 + 2 * k])
            for k, (m, w) in enumerate(((a_mid, w_out), (m0, w0), (m1, w1), (m2, w2)))
        ]
        swaps[0].start()
        named = [route_a[...], jnp.zeros_like(route_a), route_m[...], jnp.zeros((LANE - 6, seq), jnp.int32)]
        turned[...] = jnp.concatenate(named, axis=0).astype(F32).T.astype(BF)
        enter_row[:, width:] = turned[mine]
        for fetch in fetches:
            fetch.wait()
        enters.start()
        small_ref[...] = jnp.zeros_like(small_ref)
        for at, gain in ((0, gain_a), (1, gain_m)):
            for b in range(8):
                for i in range(piece // LANE):
                    there = ((b % 4) * 2 + b // 4) * piece + i * LANE
                    row_at = b * (piece // LANE) + i
                    small_ref[at : at + 1, there : there + LANE] = gain[row_at : row_at + 1]
        columns = jnp.concatenate([router_a[...].astype(F32), router_m[...].astype(F32)], axis=0)
        columns = [columns[:, b * piece : (b + 1) * piece] for b in ((k % 2) * 4 + k // 2 for k in range(8))]
        router_ref[...] = jnp.zeros_like(router_ref)
        router_ref[:8] = jnp.concatenate(columns, axis=1).astype(BF)
        swaps[0].finish()
        rings[0].start()
        swaps[1].start()
        enters.middle()
        swaps[2].start()
        rings[0].forward()
        swaps[1].finish()
        rings[1].start()
        swaps[3].start()
        enters.finish()

        def ahead(pair, _):
            routes = []
            for j in range(2):
                entered = hid[pair // 2, lax.rem(pair, 2) * 2 + j].reshape(seq, width + LANE)
                values = entered[:, :width].astype(F32)
                normed_out[pair * 2 + j] = (values * rms_scale(values) * small_ref[0:1]).astype(BF)
                routes.append(entered[:, width:])
                routes_out[pair * 2 + j] = routes[j]
            logits = mm_nt(normed_out[pl.ds(pair * 2, 2)].reshape(2 * seq, width), router_ref[...])
            gates = dense_gates(logits, chosen(jnp.concatenate(routes, axis=0).astype(F32), 0))
            gates_out[pl.ds(pair * 2, 2)] = gates.reshape(2, seq, LANE)
            return 0

        lax.fori_loop(0, 4, ahead, 0)
        rings[0].finish()
        swaps[2].finish()
        rings[2].start()
        first = 2 * team.zl
        causal = causal_mask(2, seq)

        def step(i, _):
            pair = team.pair(i)
            zl, x = pair // 2, lax.rem(pair, 2) * 2
            normed = normed_out[pl.ds(pair * 2, 2)].reshape(2 * seq, width)
            weights = w_out.reshape(width, 6 * HEAD)
            proj = mm(normed, weights[:, : 4 * HEAD])
            gates = gates_out[pl.ds(pair * 2, 2)].reshape(2 * seq, LANE)
            gated = []
            for j in range(2):
                rows = slice(j * seq, (j + 1) * seq)
                query = [
                    rotate(proj[rows, e * HEAD : (e + 1) * HEAD], cos_ref[...], sin_ref[...]).astype(BF)
                    for e in range(2)
                ]
                key = rotate(proj[rows, 2 * HEAD : 3 * HEAD], cos_ref[...], sin_ref[...]).astype(BF)
                value = proj[rows, 3 * HEAD :].astype(BF)
                probs = soft(mm_nt(jnp.concatenate(query, axis=0), key) * scale, causal)
                attended = mm(probs.astype(BF), value)
                out = [
                    (attended[e * seq : (e + 1) * seq] * pick(gates[rows], first + e)).astype(BF)
                    for e in range(2)
                ]
                qkv_out[pair * 2 + j] = jnp.concatenate(query + [key, value], axis=1)
                gated.append(jnp.concatenate(out, axis=1))
                gated_out[pair * 2 + j] = gated[-1]
            branch = mm_nt(jnp.concatenate(gated, axis=0), weights[:, 4 * HEAD :])
            part[zl, pl.ds(x, 2)] = branch.astype(BF).reshape(2, 2, 2, own, width)
            for j in range(2):
                team.swap(pair * 2 + j).start()

            @pl.when(i > 0)
            def _():
                team.add_pair(i - 1)

            @pl.when(i == 2)
            def _():
                team.send_far_z()
                rings[1].forward()

            @pl.when(i == 3)
            def _():
                team.send_far_x()

            return 0

        lax.fori_loop(0, 4, step, 0)
        team.last()
        cot.start()
        swaps[3].finish()
        team.total1(total)
        cot.middle()
        team.total2(total)
        after = total[...] + enter_row[:, :width].astype(F32)
        after_out[...] = after
        row[...] = (after * rms_scale(after) * small_ref[1:2]).astype(BF)
        spread.start()
        rings[2].forward()
        rings[3].start()
        spread.middle()
        cot.finish()
        spread.finish()
        team.close()
        for ring in rings[1:3]:
            ring.finish()
        rings[3].finish_first()

    block = jax.ShapeDtypeStruct(attn_blocks.shape, BF)
    block_m = jax.ShapeDtypeStruct(attn_blocks.shape[:2] + (part_cols,), BF)
    four = jax.ShapeDtypeStruct((4,) + attn_blocks.shape, BF)
    four_m = jax.ShapeDtypeStruct((4,) + block_m.shape, BF)
    rows = jax.ShapeDtypeStruct((2, 4, 2, 2, own, width), BF)
    return pl.pallas_call(
        kernel,
        out_shape=[
            four,
            jax.ShapeDtypeStruct((8, seq, width), BF),
            jax.ShapeDtypeStruct((8, seq, 4 * HEAD), BF),
            jax.ShapeDtypeStruct((8, seq, 2 * HEAD), BF),
            jax.ShapeDtypeStruct((8, seq, LANE), F32),
            jax.ShapeDtypeStruct((8, seq, LANE), BF),
            jax.ShapeDtypeStruct((own, width), F32),
            jax.ShapeDtypeStruct((own, width + LANE), BF),
            jax.ShapeDtypeStruct((own, width), BF),
            jax.ShapeDtypeStruct((LANE, width), BF),
            jax.ShapeDtypeStruct((16, width), F32),
            rows, rows, four_m, four_m, four_m, block, block_m, block_m, block_m,
        ],
        in_specs=[ANY] * 6 + [VMEM] * 8,
        out_specs=[VMEM] * 11 + [ANY] * 9,
        scratch_shapes=[
            pltpu.VMEM((seq, LANE), BF),
            pltpu.SemaphoreType.DMA((16,)),
            pltpu.VMEM((2, 4, 2, 2, own, width + LANE), BF),
            pltpu.VMEM((2, 4, 2, 2, own, width), BF),
            pltpu.VMEM((own, width), F32),
            pltpu.VMEM((own, width), BF),
        ]
        + TeamSum.scratch(own, width)
        + TeamSpread.sems * 3
        + Swap.sems * 4
        + RingY.sems * 4,
        name="attn_forward",
        **settings(collective, 200 << 20, 56),
    )(attn_blocks, *blocks, hidden, cotangent, *gains, *routers, *routes, cosines, sines)[:16]


def back_through_norm(total, inputs, gain, gates, normed, routers):
    width = inputs.shape[1]
    logits_back = gates_back(gates, total[:, width:])
    full = total[:, :width] + mm(logits_back.astype(BF), routers)
    inner, gain_grad = norm_back(inputs, gain, full)
    return inner, gain_grad, mm_tn(logits_back.astype(BF), normed)[:8]


def row_block(array, block, count):
    cols = array.shape[-1] // 4
    part = array[..., pl.ds(pl.multiple_of(block * cols, cols), cols)]
    return part.reshape(count, cols)


class Pass:
    sems = [pltpu.SemaphoreType.DMA((4,))] * 2

    def __init__(self, src, dst, sems):
        send, recv = sems
        zh, c = lax.axis_index("zh"), lax.axis_index("c")
        mine, far = dst.at[zh, c], dst.at[1 - zh, c]
        self.copies = [
            pltpu.make_async_copy(src, mine, send.at[0]),
            push(src, mine, send.at[1], recv.at[1], {"zh": 1 - zh}),
            push(src, mine, send.at[2], recv.at[2], sibling()),
            push(far, far, send.at[3], recv.at[3], sibling()),
        ]

    def start(self):
        for copy in self.copies[:3]:
            copy.start()

    def finish(self):
        self.copies[1].wait_recv()
        self.copies[3].start()
        self.copies[0].wait()
        self.copies[1].wait_send()
        self.copies[2].wait()
        self.copies[3].wait()


def own_tile():
    zl, x, zh, c = (lax.axis_index(a) for a in TEAM)
    return zl * 4 + x, zh * 2 + c


def experts(collective, normed, cotangent, routes, weights, after, small, routers, cot_own, extra):
    own, width = after.shape
    count = normed.shape[0]
    cols = weights[0].shape[1]
    rows = width // 4
    tile = count // 4

    def kernel(
        x_ref, cot_ref, wg_ref, wu_ref, wd_ref, route_ref, after_ref, small_ref, router_ref, own_ref,
        mid_out, small_out, spread_out, s0, s1, g2, out_all,
        x, cot, wg, wu, wd, h, dg, du, g0, gates, part_a, part_b, load, total_a, total_b, row_a, row_b, *rest,
    ):
        loads = [(x_ref, x), (wg_ref, wg), (wu_ref, wu), (cot_ref, cot)]
        fetches = [pltpu.make_async_copy(a, b, load.at[k]) for k, (a, b) in enumerate(loads)]
        for fetch in fetches:
            fetch.start()
        down_rest = RingRest(wd_ref, wd, rest[:2])
        rest = rest[2:]
        down_rest.start_here()
        meet([place(m) for m in TEAM_MOVES[1:] + [Y_MOVES[1], Y_MOVES[3]]] + [sibling()])
        down_rest.start()
        n = TeamSum.count
        team_a, team_b = TeamSum(part_a, rest[:n]), TeamSum(part_b, rest[n : 2 * n])
        rest = rest[2 * n :]
        n = RingSum.count
        rings = [RingSum(g0, rest[:n]), RingSum(wg, rest[n : 2 * n])]
        rest = rest[2 * n :]
        spread = TeamSpread(row_a, spread_out, rest[:4])
        out = Pass(row_b, out_all, rest[4:6])
        gate_w, up_w, down_w = (w.reshape(width, cols) for w in (wg, wu, wd))
        lane = EXPERTS + lax.axis_index("x")
        skip = lax.axis_index("zl") * extra

        def tokens(pair):
            return pl.ds(pl.multiple_of(pair * tile, tile), tile)

        def forward(pair, _):
            at = tokens(pair)
            x_t = x[at]
            gates_t = dense_gates(mm_nt(x_t, router_ref[...]), chosen(route_ref[at].astype(F32), EXPERTS))
            gates[at] = gates_t
            valid = (lax.broadcasted_iota(jnp.int32, (1, cols), 1) >= skip).astype(F32)
            gate = pick(gates_t, lane) * valid
            gate_part = mm(x_t, gate_w[...])
            up_part = mm(x_t, up_w[...])
            sigma = 1.0 / (1.0 + jnp.exp(-gate_part))
            silu = gate_part * sigma
            h[at] = (silu * up_part * gate).astype(BF)
            dg[at] = (up_part * sigma * (1.0 + gate_part * (1.0 - sigma)) * gate).astype(BF)
            du[at] = (silu * gate).astype(BF)
            return 0

        def backward(pair, _):
            at = tokens(pair)
            cot_down = mm(cot[at], down_w[...])
            dots = jnp.sum(h[at].astype(F32) * cot_down, axis=1, keepdims=True)
            dg[at] = (dg[at].astype(F32) * cot_down).astype(BF)
            du[at] = (du[at].astype(F32) * cot_down).astype(BF)
            hot = jnp.where(lanes(tile) == lane, dots, 0.0).astype(BF)
            part_a[pair // 2, pl.ds(lax.rem(pair, 2) * 2, 2), :, :, :, width:] = hot.reshape(
                2, 2, 2, own, LANE
            )
            return 0

        def summed(team, columns, values):
            def step(i, _):
                pair = team.pair(i)
                at = (pair // 2, pl.ds(lax.rem(pair, 2) * 2, 2), slice(None), slice(None), slice(None), columns)
                team.part[at] = values(tokens(pair)).astype(BF).reshape(2, 2, 2, own, width)
                for j in range(2):
                    team.swap(pair * 2 + j).start()

                @pl.when(i > 0)
                def _():
                    team.add_pair(i - 1)

                @pl.when(i == 2)
                def _():
                    team.send_far_z()

                @pl.when(i == 3)
                def _():
                    team.send_far_x()

                return 0

            lax.fori_loop(0, 4, step, 0)
            team.last()

        def product(left, right, dst):
            def one(block):
                dst[block] = mm_tn(row_block(left, block, count), right[...]).astype(BF)

            return one

        for fetch in fetches[:3]:
            fetch.wait()
        lax.fori_loop(0, 4, forward, 0)
        fetches[3].wait()
        down_rest.finish()
        lax.fori_loop(0, 4, backward, 0)
        rings[0].start_with(product(x, dg, g0))
        summed(team_a, slice(0, width), lambda at: mm_nt(dg[at], gate_w[...]) + mm_nt(du[at], up_w[...]))
        rings[0].middle()
        rings[1].start_with(product(x, du, wg))
        team_a.total1(total_a)
        summed(team_b, slice(0, width), lambda at: mm_nt(h[at], down_w[...]))
        after = after_ref[...]
        normed_own = (after * rms_scale(after) * small_ref[1:2]).astype(BF)
        seq, quarter = own_tile()
        gates_own = gates[pl.ds(pl.multiple_of((seq * 4 + quarter) * own, own), own)]
        team_a.total2(total_a)
        inner, gain_grad, router_grad = back_through_norm(
            total_a[...], after, small_ref[1:2], gates_own, normed_own, router_ref[...]
        )
        grad_mid = own_ref[...].astype(F32) + inner
        mid_out[...] = grad_mid
        row_a[...] = grad_mid.astype(BF)
        spread.start()
        rings[1].middle()
        small_out[:8] = jnp.zeros((8, width), F32)
        small_out[0:1] = gain_grad
        small_out[8:] = router_grad

        def down(block, _):
            product(cot, h, wu)(block)
            return 0

        lax.fori_loop(0, 4, down, 0)
        keep = pltpu.make_async_copy(wu, g2, load.at[0])
        keep.start()
        spread.middle()
        team_b.total1(total_b)
        spread.finish()
        team_b.total2(total_b)
        row_b[...] = in_order((after + total_b[...]).astype(BF))
        out.start()
        stores = []
        for ring, buffer, dst, k in ((rings[0], dg, s0, 1), (rings[1], du, s1, 2)):
            ring.finish(buffer.at[pl.ds(0, rows)])
            stores.append(pltpu.make_async_copy(buffer.at[pl.ds(0, rows)], dst, load.at[k]))
            stores[-1].start()
        out.finish()
        keep.wait()
        for store in stores:
            store.wait()
        team_a.close()
        team_b.close()

    return pl.pallas_call(
        kernel,
        out_shape=[
            jax.ShapeDtypeStruct((own, width), F32),
            jax.ShapeDtypeStruct((16, width), F32),
            jax.ShapeDtypeStruct((2, 4, 2, 2, own, width), BF),
            jax.ShapeDtypeStruct((rows, cols), BF),
            jax.ShapeDtypeStruct((rows, cols), BF),
            jax.ShapeDtypeStruct((4, rows, cols), BF),
            jax.ShapeDtypeStruct((2, 2, own, width), BF),
        ],
        in_specs=[ANY] * 5 + [VMEM] * 5,
        out_specs=[VMEM] * 2 + [ANY] * 5,
        scratch_shapes=[
            pltpu.VMEM((count, width), BF),
            pltpu.VMEM((count, width), BF),
            pltpu.VMEM((4, rows, cols), BF),
            pltpu.VMEM((4, rows, cols), BF),
            pltpu.VMEM((4, rows, cols), BF),
            pltpu.VMEM((count, cols), BF),
            pltpu.VMEM((count, cols), BF),
            pltpu.VMEM((count, cols), BF),
            pltpu.VMEM((4, rows, cols), BF),
            pltpu.VMEM((count, LANE), F32),
            pltpu.VMEM((2, 4, 2, 2, own, width + LANE), BF),
            pltpu.VMEM((2, 4, 2, 2, own, width), BF),
            pltpu.SemaphoreType.DMA((4,)),
            pltpu.VMEM((own, width + LANE), F32),
            pltpu.VMEM((own, width), F32),
            pltpu.VMEM((own, width), BF),
            pltpu.VMEM((own, width), BF),
        ]
        + RingRest.sems
        + TeamSum.scratch(own, width + LANE)
        + TeamSum.scratch(own, width)
        + RingSum.scratch(rows, cols) * 2
        + TeamSpread.sems
        + Pass.sems,
        name="experts",
        **settings(collective, 300 << 20, 61),
    )(
        normed, cotangent, *[w.reshape(4, rows, cols) for w in weights], routes,
        after, small, routers, cot_own,
    )


def in_order(values):
    block = values.shape[1] // 8
    order = [(b % 4) * 2 + b // 4 for b in range(8)]
    return jnp.concatenate([values[:, k * block : (k + 1) * block] for k in order], axis=1)


def attn_backward(
    collective, grad_mid, qkv, gated, normed, gates, weights, cosines, sines, mid_own, entered, gains, routers, small, summed, grads
):
    own, width = mid_own.shape
    seq = qkv.shape[1]
    rows, cols = grads.shape[1:]
    shard = rows // 8
    scale = HEAD ** (-0.5)
    stages = [X_MOVES, Y_MOVES, Z_MOVES]

    def kernel(
        gm_ref, w_ref, x_ref, g2_ref, y0, y1, qkv_ref, gated_ref, gates_ref, cos_ref, sin_ref,
        mid_ref, in_ref, gain_ref, router_ref, small_ref,
        grad_all, gain_a, gain_m, router_a, router_m, s0, s1, s2, s3,
        gm, w, x, g2, g3, y2, y3, proj, part, load, total, row,
        acc, got, other, rest_rows, csem, ssend, srecv, *rest,
    ):
        loads = [(gm_ref, gm), (w_ref, w), (g2_ref, g2), (x_ref, x)]
        fetches = [pltpu.make_async_copy(a, b, load.at[k]) for k, (a, b) in enumerate(loads)]
        for fetch in fetches:
            fetch.start()
        meet([place(m) for m in TEAM_MOVES[1:] + Y_MOVES[1:]] + [sibling()])
        n = TeamSum.count
        team, rest = TeamSum(part, rest[:n]), rest[n:]
        n = RingSum.count
        rings, rest = [RingSum(g2, rest[:n]), RingSum(g3, rest[n : 2 * n])], rest[2 * n :]
        swaps_back = [
            Swap(y, s, rest[2 * k : 2 * k + 2]) for k, (y, s) in enumerate(((y0, s0), (y1, s1), (y2, s2)))
        ]
        last_swap = ColumnSwap(y3, s3, rest[6:8])
        out = Pass(row, grad_all, rest[8:10])
        first = 2 * team.zl
        causal = causal_mask(2, seq)
        swaps_back[0].start()
        swaps_back[1].start()
        fetches[0].wait()
        fetches[1].wait()

        def step(i, _):
            pair = team.pair(i)
            grads = mm(gm[pl.ds(pair * 2, 2)].reshape(2 * seq, width), w[:, 4 * HEAD :])
            both = []
            for j in range(2):
                at = pair * 2 + j
                here = slice(j * seq, (j + 1) * seq)
                query = jnp.concatenate(
                    [qkv_ref[at, :, e * HEAD : (e + 1) * HEAD] for e in range(2)], axis=0
                )
                key = qkv_ref[at, :, 2 * HEAD : 3 * HEAD]
                value = qkv_ref[at, :, 3 * HEAD :]
                probs = soft(mm_nt(query, key) * scale, causal)
                probs_b = probs.astype(BF)
                attended = mm(probs_b, value)
                grad = jnp.concatenate(
                    [grads[here, e * HEAD : (e + 1) * HEAD] for e in range(2)], axis=0
                )
                gates = gates_ref[at]
                gate = jnp.concatenate([pick(gates, first + e) for e in range(2)], axis=0)
                each = jnp.sum(attended * grad, axis=1, keepdims=True) * gate
                dots = jnp.where(lanes(seq) == first, each[:seq], 0.0)
                dots += jnp.where(lanes(seq) == first + 1, each[seq:], 0.0)
                grad = (grad * gate).astype(BF)
                grad_probs = mm_nt(grad, value)
                inner = jnp.sum(probs * grad_probs, axis=1, keepdims=True)
                grad_scores = (probs * (grad_probs - inner) * scale).astype(BF)
                turned = [mm(grad_scores, key), mm_tn(grad_scores, query)]
                turned = [turned[0][:seq], turned[0][seq:], turned[1]]
                turned = [rotate(t, cos_ref[...], -sin_ref[...]).astype(BF) for t in turned]
                grad_value = mm_tn(probs_b, grad).astype(BF)
                both.append(jnp.concatenate(turned + [grad_value], axis=1))
                proj[at] = both[-1]
                part[pair // 2, lax.rem(pair, 2) * 2 + j, :, :, :, width:] = dots.astype(BF).reshape(
                    2, 2, own, LANE
                )
            back = mm_nt(jnp.concatenate(both, axis=0), w[:, : 4 * HEAD])
            part[pair // 2, pl.ds(lax.rem(pair, 2) * 2, 2), :, :, :, :width] = back.astype(BF).reshape(
                2, 2, 2, own, width
            )
            for j in range(2):
                team.swap(pair * 2 + j).start()

            @pl.when(i == 0)
            def _():
                fetches[2].wait()
                rings[0].start()

            @pl.when(i > 0)
            def _():
                team.add_pair(i - 1)

            @pl.when(i == 2)
            def _():
                team.send_far_z()

            @pl.when(i == 3)
            def _():
                team.send_far_x()

            return 0

        lax.fori_loop(0, 4, step, 0)
        team.last()
        fetches[3].wait()

        def product(block):
            g3[block, :, : 4 * HEAD] = mm_tn(
                row_block(x, block, 8 * seq), proj[...].reshape(8 * seq, 4 * HEAD)
            ).astype(BF)
            g3[block, :, 4 * HEAD :] = mm_tn(
                row_block(gm, block, 8 * seq), gated_ref[...].reshape(8 * seq, 2 * HEAD)
            ).astype(BF)

        rings[1].start_with(product)
        rings[0].middle()
        inputs = in_ref[:, :width].astype(F32)
        normed_own = (inputs * rms_scale(inputs) * gain_ref[0:1]).astype(BF)
        own_seq, quarter = own_tile()
        gates_own = gates_ref[own_seq, pl.ds(pl.multiple_of(quarter * own, own), own)]
        team.total1(total)
        rings[1].middle()
        team.total2(total)
        inner, gain_grad, router_grad = back_through_norm(
            total[...], inputs, gain_ref[0:1], gates_own, normed_own, router_ref[...]
        )
        row[...] = in_order((mid_ref[...] + inner).astype(BF))
        out.start()
        acc[...] = small_ref[...]
        acc[1:2] = gain_grad
        acc[8:] += router_grad
        c = lax.axis_index("c")
        half = pl.ds(pl.multiple_of(c * 8, 8), 8)
        rest_half = pl.ds(pl.multiple_of((1 - c) * 8, 8), 8)
        over = push(acc.at[rest_half], other, csem.at[0], csem.at[1], sibling())
        over.start()
        over.wait()
        acc[half] = acc[half] + other[...]
        for s, stage in enumerate(stages):
            swaps = [
                push(acc.at[half], got.at[s, k - 1], ssend.at[s, k], srecv.at[s, k], place(stage[k]))
                for k in range(1, 4)
            ]
            for swap in swaps:
                swap.start()
            if s == 0:
                rings[0].finish(y2)
                swaps_back[2].start()
            if s == 1:
                rings[1].finish(y3)
                last_swap.start()
            for swap in swaps:
                swap.wait()
            acc[half] = acc[half] + got[s, 0] + got[s, 1] + got[s, 2]
        back_over = push(acc.at[half], rest_rows, csem.at[2], csem.at[3], sibling())
        back_over.start()
        out.finish()
        back_over.wait()
        acc[rest_half] = rest_rows[...]
        final = in_order(acc[...])
        for ref, at in ((gain_m, 0), (gain_a, 1)):
            for k in range(width // LANE):
                ref[k : k + 1] = final[at : at + 1, k * LANE : (k + 1) * LANE]
        router_a[...] = final[8 : 8 + EXPERTS]
        router_m[...] = final[8 + EXPERTS :]
        for swap in swaps_back + [last_swap]:
            swap.finish()
        team.close()

    block = jax.ShapeDtypeStruct((8, shard, cols), BF)
    heads = cols // HEAD
    return pl.pallas_call(
        kernel,
        out_shape=[
            jax.ShapeDtypeStruct((2, 2, own, width), BF),
            jax.ShapeDtypeStruct((width // LANE, LANE), F32),
            jax.ShapeDtypeStruct((width // LANE, LANE), F32),
            jax.ShapeDtypeStruct((EXPERTS, width), F32),
            jax.ShapeDtypeStruct((EXPERTS, width), F32),
            block, block, block,
            jax.ShapeDtypeStruct((2, heads, shard, 4 * HEAD), BF),
        ],
        in_specs=[ANY] * 6 + [VMEM] * 10,
        out_specs=[ANY] + [VMEM] * 4 + [ANY] * 4,
        scratch_shapes=[
            pltpu.VMEM((8, seq, width), BF),
            pltpu.VMEM(weights.shape, BF),
            pltpu.VMEM((8, seq, width), BF),
            pltpu.VMEM((4, rows, cols), BF),
            pltpu.VMEM((4, rows, cols), BF),
            pltpu.VMEM((8, shard, cols), BF),
            pltpu.VMEM((8, heads, shard, HEAD), BF),
            pltpu.VMEM((8, seq, 4 * HEAD), BF),
            pltpu.VMEM((2, 4, 2, 2, own, width + LANE), BF),
            pltpu.SemaphoreType.DMA((4,)),
            pltpu.VMEM((own, width + LANE), F32),
            pltpu.VMEM((own, width), BF),
            pltpu.VMEM((16, width), F32),
            pltpu.VMEM((3, 3, 8, width), F32),
            pltpu.VMEM((8, width), F32),
            pltpu.VMEM((8, width), F32),
            pltpu.SemaphoreType.DMA((4,)),
        ]
        + [pltpu.SemaphoreType.DMA((4, 4))] * 2
        + TeamSum.scratch(own, width + LANE)
        + RingSum.scratch(rows, cols) * 2
        + Swap.sems * 4
        + Pass.sems,
        name="attn_backward",
        **settings(collective, 200 << 20, 58),
    )(
        grad_mid.reshape(8, seq, width), weights, normed, grads, *summed, qkv, gated, gates, cosines, sines,
        mid_own, entered, gains, routers, small,
    )


def local(
    hidden,
    cotangent,
    attn_gain,
    attn_router,
    qkv_weight,
    out_weight,
    mlp_gain,
    mlp_router,
    gate_up_weight,
    down_weight,
    attn_route,
    attn_slot,
    mlp_route,
    mlp_slot,
):
    seq, width = hidden.shape
    rows = qkv_weight.shape[0]
    features = down_weight.shape[2]
    part = (features // LANE + 1) // 2 * LANE
    group = 8 * seq
    cosines, sines = rope_tables(seq)

    query_blocks = qkv_weight[:, :EXPERTS].reshape(rows, 2, 2, 4, HEAD).transpose(1, 3, 0, 2, 4)
    kv_blocks = qkv_weight[:, EXPERTS:].reshape(rows, 2, 4, HEAD).transpose(2, 0, 1, 3)
    kv_blocks = jnp.broadcast_to(kv_blocks[None], (2,) + kv_blocks.shape)
    out_blocks = out_weight.reshape(rows, 2, 2, 4, HEAD).transpose(1, 3, 0, 2, 4)
    attn_blocks = jnp.concatenate([query_blocks, kv_blocks, out_blocks], axis=3)
    attn_blocks = attn_blocks.reshape(8, rows, 6 * HEAD)

    mlp_blocks = [
        w.transpose(1, 0, 2) for w in (gate_up_weight[:, :, 0], gate_up_weight[:, :, 1], down_weight)
    ]
    gains = [g.reshape(width // LANE, LANE) for g in (attn_gain, mlp_gain)]

    (
        attn_w, normed_a, qkv, gated_att, gates_a, group_routes, after, entered, cot_own, routers, small,
        normed_m, group_cot, *mlp_w,
    ) = attn_forward(
        1, attn_blocks, mlp_blocks, part, hidden, cotangent, gains, [attn_router.T, mlp_router.T],
        [attn_route.T, mlp_route.T], cosines, sines,
    )
    attn_w = attn_w.reshape(width, 6 * HEAD)
    mlp_w = [w.reshape(width, part) for w in mlp_w]
    group_cot = group_cot.reshape(group, width)
    normed_m = normed_m.reshape(group, width)

    grad_mid_own, small_m, grad_mid, gate_sum, up_sum, down_part, out_hidden = experts(
        2, normed_m, group_cot, group_routes.reshape(group, LANE), mlp_w, after, small, routers, cot_own,
        2 * part - features,
    )
    gate_sum, up_sum = (a.reshape(8, rows, part) for a in (gate_sum, up_sum))
    grad_in, gain_a, gain_m, router_a, router_m, *mlp_grads, attn_grads = attn_backward(
        3, grad_mid, qkv, gated_att, normed_a, gates_a, attn_w, cosines, sines, grad_mid_own, entered, small,
        routers, small_m, [gate_sum, up_sum], down_part,
    )
    out_hidden = out_hidden.reshape(seq, width)
    grad_in = grad_in.reshape(seq, width).astype(F32)

    attn_grads = attn_grads.astype(F32)
    query_grad = attn_grads[:, :2].reshape(EXPERTS, rows, 4 * HEAD)
    kv_grad = attn_grads[0, 2:4] + attn_grads[1, 2:4]
    qkv_grad = jnp.concatenate([query_grad, kv_grad], axis=0).transpose(1, 0, 2)
    out_grad = attn_grads[:, 4:].reshape(EXPERTS, rows, 4 * HEAD).transpose(1, 0, 2)

    def placed_back(grad):
        grad = grad.reshape(2, EXPERTS, rows, part)
        return jnp.concatenate([grad[0], grad[1, ..., 2 * part - features :]], axis=-1).transpose(1, 0, 2)

    gate_grad, up_grad, down_grad = [placed_back(g) for g in mlp_grads]
    return (
        out_hidden,
        grad_in,
        gain_a.reshape(width),
        router_a.T,
        qkv_grad,
        out_grad,
        gain_m.reshape(width),
        router_m.T,
        jnp.stack([gate_grad, up_grad], axis=2).astype(F32),
        down_grad.astype(F32),
    )


def solution(mesh):
    fine = Mesh(mesh.devices.reshape(2, 4, 4, 2, 2), ALL)
    dp, tensor = ("zl", "y", "x"), ("zh", "c")
    placed = (
        P(dp, None),
        P(dp, None),
        P(),
        P(),
        P(dp, None, tensor),
        P(dp, None, tensor),
        P(),
        P(),
        P(dp, None, None, tensor),
        P(dp, None, tensor),
        P(dp, None),
        P(dp, None),
        P(dp, None),
        P(dp, None),
    )
    return jax.shard_map(
        local,
        mesh=fine,
        in_specs=placed,
        out_specs=(
            P(dp, None),
            P(dp, None),
            P(),
            P(),
            P(dp, None, tensor),
            P(dp, None, tensor),
            P(),
            P(),
            P(dp, None, None, tensor),
            P(dp, None, tensor),
        ),
        check_vma=False,
    )
```

```python
import itertools

import jax
import jax.numpy as jnp
import numpy as np
from jax import lax
from jax.experimental import pallas as pl
from jax.experimental.pallas import tpu as pltpu
from jax.sharding import Mesh, PartitionSpec as P

HEAD = 128
LANE = 128
EPS = 1e-05
THETA = 10000.0
NEG = -1e30
EXPERTS = 4
GROUP = ("zl", "x")
TEAM = ("zl", "x", "zh", "c")
ALL = ("zl", "y", "x", "zh", "c")
SIZES = dict(zl=2, y=4, x=4, zh=2, c=2)
BF = jnp.bfloat16
F32 = jnp.float32
MESH = pl.DeviceIdType.MESH
ANY = pl.BlockSpec(memory_space=pl.ANY)
VMEM = pl.BlockSpec(memory_space=pltpu.VMEM)


def dot(a, b, dims):
    return lax.dot_general(a, b, (dims, ((), ())), preferred_element_type=F32)


def mm(a, b):
    return dot(a, b, ((1,), (0,)))


def mm_nt(a, b):
    return dot(a, b, ((1,), (1,)))


def mm_tn(a, b):
    return dot(a, b, ((0,), (0,)))


def rms_scale(values):
    return lax.rsqrt(jnp.mean(values * values, axis=-1, keepdims=True) + EPS)


def lanes(rows):
    return lax.broadcasted_iota(jnp.int32, (rows, LANE), 1)


def chosen(routes, first):
    lane = lanes(routes.shape[0])
    named = [pick(routes, first + c).astype(jnp.int32) + first for c in range(2)]
    return (lane == named[0]) | (lane == named[1])


def dense_gates(logits, mask):
    top = jnp.max(jnp.where(mask, logits, NEG), axis=1, keepdims=True)
    expon = jnp.where(mask, jnp.exp(jnp.where(mask, logits - top, 0.0)), 0.0)
    return expon / jnp.sum(expon, axis=1, keepdims=True)


def pick(values, lane):
    return jnp.sum(jnp.where(lanes(values.shape[0]) == lane, values, 0.0), axis=1, keepdims=True)


def gates_back(gates, gated_dots):
    return gated_dots - gates * jnp.sum(gated_dots, axis=1, keepdims=True)


def rope_tables(count):
    frequency = THETA ** (-(np.arange(HEAD // 2).astype(np.float32) * 2.0 / HEAD))
    angles = np.arange(count).astype(np.float32)[:, None] * frequency[None, :].astype(np.float32)
    cosines, sines = np.cos(angles), np.sin(angles)
    return (
        jnp.asarray(np.concatenate([cosines, cosines], axis=1), F32),
        jnp.asarray(np.concatenate([-sines, sines], axis=1), F32),
    )


def rotate(values, cosines, sines):
    return values * cosines + pltpu.roll(values, HEAD // 2, 1) * sines


def norm_back(inputs, gain, grad_normed):
    scale = rms_scale(inputs)
    scaled = inputs * scale
    grad_scaled = grad_normed * gain
    grad_inputs = scale * (
        grad_scaled - scaled * jnp.mean(grad_scaled * scaled, axis=-1, keepdims=True)
    )
    return grad_inputs, jnp.sum(grad_normed * scaled, axis=0, keepdims=True)


def moves(*axes):
    return [dict(zip(axes, steps)) for steps in itertools.product(*[range(SIZES[a]) for a in axes])]


def place(move, sign=1):
    return {a: lax.rem(lax.axis_index(a) + sign * v + SIZES[a], SIZES[a]) for a, v in move.items()}


def number(coords):
    total = 0
    for axis, value in coords.items():
        total = total * SIZES[axis] + value
    return total


def meet(partners):
    barrier = pltpu.get_barrier_semaphore()
    for partner in partners:
        pl.semaphore_signal(barrier, inc=1, device_id=partner, device_id_type=MESH)
    pl.semaphore_wait(barrier, len(partners))


def push(src, dst, send, recv, to):
    return pltpu.make_async_remote_copy(
        src_ref=src, dst_ref=dst, send_sem=send, recv_sem=recv, device_id=to, device_id_type=MESH
    )


def settings(number, moved, vmem=32):
    return dict(
        compiler_params=pltpu.CompilerParams(
            collective_id=number, has_side_effects=True, vmem_limit_bytes=vmem << 20
        ),
        cost_estimate=pl.CostEstimate(flops=0, bytes_accessed=moved, transcendentals=0),
    )


GROUP_MOVES = moves("zl", "x")
TEAM_MOVES = moves("zl", "x", "zh")
X_MOVES = moves("x")
Y_MOVES = moves("y")
Z_MOVES = moves("zl", "zh")


def sibling():
    return {"c": 1 - lax.axis_index("c")}


class RingY:
    sems = [pltpu.SemaphoreType.DMA((5,)), pltpu.SemaphoreType.DMA((5,))]

    def __init__(self, src, out, sems):
        self.src, self.out = src, out
        self.send, self.recv = sems
        self.y = lax.axis_index("y")
        self.half = src.shape[0] // 2

    def line(self, step):
        return lax.rem(self.y + step, 4)

    def copy(self, k):
        y = self.y
        if k < 2:
            src, dst, to = self.src, self.out.at[y], self.line((1, 3)[k])
        else:
            half = pl.ds((k - 2) * self.half, self.half)
            src = dst = self.out.at[self.line((3, 1)[k - 2]), half]
            to = self.line((1, 3)[k - 2])
        return push(src, dst, self.send.at[k], self.recv.at[k], {"y": to})

    def start(self):
        self.stay = pltpu.make_async_copy(self.src, self.out.at[self.y], self.send.at[4])
        for k in range(2):
            self.copy(k).start()
        self.stay.start()

    def forward(self):
        for k in range(2):
            self.copy(k).wait_recv()
            self.copy(k + 2).start()

    def finish(self):
        for k in range(2):
            self.copy(k + 2).wait_recv()
        for k in range(4):
            self.copy(k).wait_send()
        self.stay.wait()

    def finish_first(self):
        for k in range(2):
            self.copy(k).wait()
        self.stay.wait()


class RingRest:
    sems = [pltpu.SemaphoreType.DMA((5,)), pltpu.SemaphoreType.DMA((2,))]

    def __init__(self, src, out, sems):
        self.y = lax.axis_index("y")
        rows = src.shape[1] // 2
        send, recv = sems
        self.copies = [
            pltpu.make_async_copy(src.at[self.line(step)], out.at[self.line(step)], send.at[2 + k])
            for k, step in enumerate((0, 1, 3))
        ]
        for k in range(2):
            here = (self.line((3, 1)[k]), pl.ds(k * rows, rows))
            to = {"y": self.line((1, 3)[k])}
            self.copies.append(push(src.at[here], out.at[here], send.at[k], recv.at[k], to))

    def line(self, step):
        return lax.rem(self.y + step, 4)

    def start_here(self):
        for copy in self.copies[:3]:
            copy.start()

    def start(self):
        for copy in self.copies[3:]:
            copy.start()

    def finish(self):
        for copy in self.copies:
            copy.wait()


class Swap:
    sems = [pltpu.SemaphoreType.DMA((8,))] * 2

    def __init__(self, src, dst, sems):
        self.src, self.dst = src, dst
        self.send, self.recv = sems

    def start(self):
        me = number(place(GROUP_MOVES[0]))
        self.copies = [
            pltpu.make_async_copy(self.src.at[me], self.dst.at[me], self.send.at[0])
        ]
        for k, move in enumerate(GROUP_MOVES):
            if k:
                to = place(move)
                self.copies.append(
                    push(
                        self.src.at[number(to)],
                        self.dst.at[me],
                        self.send.at[k],
                        self.recv.at[k],
                        to,
                    )
                )
        for copy in self.copies:
            copy.start()

    def finish(self):
        for copy in self.copies:
            copy.wait()


class ExpertSwap(Swap):
    def start(self):
        me = number(place(GROUP_MOVES[0]))
        part = self.dst.shape[2]
        low = self.src.shape[2] - part
        self.copies = []
        for k, move in enumerate(GROUP_MOVES):
            to = place(move)
            block = self.src.at[to["x"], :, pl.ds(pl.multiple_of(to["zl"] * low, LANE), part)]
            if k:
                self.copies.append(
                    push(block, self.dst.at[me], self.send.at[k], self.recv.at[k], to)
                )
            else:
                self.copies.append(pltpu.make_async_copy(block, self.dst.at[me], self.send.at[0]))
        for copy in self.copies:
            copy.start()


class ColumnSwap(Swap):
    def start(self):
        zl, x = lax.axis_index("zl"), lax.axis_index("x")
        mine = self.dst.at[zl, :, :, pl.ds(pl.multiple_of(x * HEAD, HEAD), HEAD)]
        self.copies = [
            pltpu.make_async_copy(self.src.at[zl * 4 + x], mine, self.send.at[0])
        ]
        for k, move in enumerate(GROUP_MOVES):
            if k:
                to = place(move)
                block = self.src.at[number(to)]
                self.copies.append(push(block, mine, self.send.at[k], self.recv.at[k], to))
        for copy in self.copies:
            copy.start()


class RingSum:
    @staticmethod
    def scratch(rows, cols):
        return [
            pltpu.VMEM((2, rows // 2, cols), BF),
            pltpu.VMEM((2, rows // 2, cols), BF),
            pltpu.VMEM((2, rows, cols), BF),
            pltpu.SemaphoreType.DMA((6,)),
            pltpu.SemaphoreType.DMA((6,)),
        ]

    count = 5

    def __init__(self, part, scratch):
        self.part = part
        self.got, self.mix, self.sums, self.send, self.recv = scratch
        self.y = lax.axis_index("y")
        half = part.shape[1] // 2
        self.halves = [pl.ds(0, half), pl.ds(half, half)]

    def line(self, step):
        return lax.rem(self.y + step, 4)

    def copy(self, k):
        kind, way = k // 2, k % 2
        step = (1, 3)[way]
        top, low = self.halves[way], self.halves[1 - way]
        if kind == 0:
            src, dst = self.part.at[self.line(2), top], self.got.at[way]
        elif kind == 1:
            src, dst = self.part.at[self.line(step), low], self.sums.at[way, low]
        else:
            src, dst = self.mix.at[way], self.sums.at[way, top]
        return push(src, dst, self.send.at[k], self.recv.at[k], {"y": self.line(step)})

    def start(self):
        for k in range(4):
            self.copy(k).start()

    def start_with(self, product):
        self.begin_with(product)
        self.go_on_with(product)

    def begin_with(self, product):
        product(self.line(2))
        self.copy(0).start()
        self.copy(1).start()
        product(self.line(1))
        self.copy(2).start()

    def go_on_with(self, product):
        product(self.line(3))
        self.copy(3).start()
        product(self.y)

    def middle(self):
        for way in range(2):
            self.copy(way).wait_recv()
            mine = self.part[self.line((1, 3)[way]), self.halves[way]].astype(F32)
            self.mix[way] = (mine + self.got[way].astype(F32)).astype(BF)
            self.copy(4 + way).start()

    def finish(self, out):
        for k in range(2, 6):
            self.copy(k).wait_recv()
        total = self.part[self.y].astype(F32) + self.sums[0].astype(F32) + self.sums[1].astype(F32)
        total = total.astype(BF)
        if len(out.shape) < 4:
            out[...] = total.reshape(out.shape)
        else:
            targets, count, rows, cols = out.shape
            for t in range(targets):
                for n in range(count):
                    out[t, n] = total[t * rows : (t + 1) * rows, n * cols : (n + 1) * cols]
        for k in range(6):
            self.copy(k).wait_send()


class TeamSum:
    @staticmethod
    def scratch(own, width):
        half = own // 2
        return [
            pltpu.VMEM((8, 2, own, width), BF),
            pltpu.VMEM((3, 2, 2, half, width), BF),
            pltpu.VMEM((3, 4, half, width), BF),
            pltpu.VMEM((6, half, width), BF),
            pltpu.SemaphoreType.DMA((8,)),
            pltpu.SemaphoreType.DMA((8,)),
            pltpu.SemaphoreType.DMA((6,)),
            pltpu.SemaphoreType.DMA((6,)),
            pltpu.SemaphoreType.DMA((6,)),
            pltpu.SemaphoreType.DMA((6,)),
        ]

    count = 10

    def __init__(self, part, scratch):
        self.part = part
        self.other, self.got_x, self.got_z, self.late = scratch[:4]
        self.ssem, self.rsem, self.send1, self.recv1, self.send2, self.recv2 = scratch[4:]
        self.zl, self.x, self.zh, self.c = (lax.axis_index(a) for a in TEAM)
        self.half = part.shape[4] // 2
        self.top, self.low = pl.ds(0, self.half), pl.ds(self.half, self.half)

    def swap(self, seq):
        return push(
            self.part.at[seq // 4, lax.rem(seq, 4), :, 1 - self.c],
            self.other.at[seq],
            self.ssem.at[seq],
            self.rsem.at[seq],
            sibling(),
        )

    def send_x(self, x):
        slot = lax.rem(x - self.x + 4, 4) - 1
        return push(
            self.part.at[:, x, :, self.c, self.top],
            self.got_x.at[slot],
            self.send1.at[slot],
            self.recv1.at[slot],
            {"x": x},
        )

    def send_z(self, zl, zh):
        slot = lax.rem(zl - self.zl + 2, 2) * 2 + lax.rem(zh - self.zh + 2, 2) - 1
        return push(
            self.part.at[zl, :, zh, self.c, self.low],
            self.got_z.at[slot],
            self.send1.at[3 + slot],
            self.recv1.at[3 + slot],
            {"zl": zl, "zh": zh},
        )

    def late_z(self, k):
        to = place(Z_MOVES[k])
        return push(
            self.part.at[to["zl"], self.x, to["zh"], self.c, self.top],
            self.late.at[k - 1],
            self.send2.at[k - 1],
            self.recv2.at[k - 1],
            to,
        )

    def late_x(self, k):
        to = place(X_MOVES[k])
        return push(
            self.part.at[self.zl, to["x"], self.zh, self.c, self.low],
            self.late.at[2 + k],
            self.send2.at[2 + k],
            self.recv2.at[2 + k],
            to,
        )

    def add(self, seq):
        self.swap(seq).wait_recv()
        zl, x = seq // 4, lax.rem(seq, 4)
        for zh in range(2):
            mine = self.part[zl, x, zh, self.c].astype(F32)
            self.part[zl, x, zh, self.c] = (mine + self.other[seq, zh].astype(F32)).astype(BF)

    def pair(self, step):
        back = 3 - step
        return lax.rem(self.zl + back // 2, 2) * 2 + lax.rem(self.x // 2 + back, 2)

    def add_pair(self, step):
        for j in range(2):
            self.add(self.pair(step) * 2 + j)

    def send_far_z(self):
        for zh in range(2):
            self.send_z(1 - self.zl, zh).start()

    def send_far_x(self):
        for j in range(2):
            self.send_x((1 - self.x // 2) * 2 + j).start()

    def last(self):
        self.add_pair(3)
        self.send_x(self.x + 1 - 2 * lax.rem(self.x, 2)).start()
        self.send_z(self.zl, 1 - self.zh).start()

    def got(self, ref, sem):
        pltpu.make_async_copy(ref, ref, sem).wait()

    def total(self, total_ref):
        self.total1(total_ref)
        self.total2(total_ref)

    def total1(self, total_ref):
        half, c = self.half, self.c
        for k in range(3):
            self.got(self.got_x.at[k], self.recv1.at[k])
        for k, move in reversed(list(enumerate(Z_MOVES))):
            at = place(move)
            rows = self.part[at["zl"], self.x, at["zh"], c, :half].astype(F32)
            for j in range(3):
                rows += self.got_x[j, at["zl"], at["zh"]].astype(F32)
            if k:
                self.part[at["zl"], self.x, at["zh"], c, :half] = rows.astype(BF)
                self.late_z(k).start()
            else:
                total_ref[:half] = rows
        for k in range(3):
            self.got(self.got_z.at[k], self.recv1.at[3 + k])
        for k, move in reversed(list(enumerate(X_MOVES))):
            at = place(move)
            rows = self.part[self.zl, at["x"], self.zh, c, half:].astype(F32)
            for j in range(3):
                rows += self.got_z[j, at["x"]].astype(F32)
            if k:
                self.part[self.zl, at["x"], self.zh, c, half:] = rows.astype(BF)
                self.late_x(k).start()
            else:
                total_ref[half:] = rows

    def total2(self, total_ref):
        half = self.half
        for k in range(3):
            self.got(self.late.at[k], self.recv2.at[k])
            total_ref[:half] += self.late[k].astype(F32)
        for k in range(3):
            self.got(self.late.at[3 + k], self.recv2.at[3 + k])
            total_ref[half:] += self.late[3 + k].astype(F32)

    def close(self):
        for seq in range(8):
            self.swap(seq).wait_send()
        for k in range(1, 4):
            x, z = place(X_MOVES[k])["x"], place(Z_MOVES[k])
            self.send_x(x).wait_send()
            self.send_z(z["zl"], z["zh"]).wait_send()
            self.late_z(k).wait_send()
            self.late_x(k).wait_send()

    def swap_all(self):
        for step in range(4):
            for j in range(2):
                self.swap(self.pair(step) * 2 + j).start()

    def add_all(self):
        self.add_pair(0)
        self.add_pair(1)
        self.send_far_z()
        self.add_pair(2)
        self.send_far_x()
        self.last()


class TeamSpread:
    sems = [pltpu.SemaphoreType.DMA((12,))] * 2 + [pltpu.SemaphoreType.DMA((9,))] * 2

    def __init__(self, rows, out, sems):
        self.rows, self.out = rows, out
        self.send, self.recv, self.fsend, self.frecv = sems
        self.zl, self.x, self.zh, self.c = (lax.axis_index(a) for a in TEAM)
        self.half = rows.shape[0] // 2
        self.top, self.low = pl.ds(0, self.half), pl.ds(self.half, self.half)

    def tops(self, zl, zh):
        return self.out.at[zl, :, zh, self.c, self.top]

    def lows(self, x):
        return self.out.at[:, x, :, self.c, self.low]

    def hop(self, k, src, dst, to):
        return push(src, dst, self.send.at[k], self.recv.at[k], to)

    def first(self, k):
        here = (self.zl, self.x, self.zh, self.c)
        if k < 3:
            return self.hop(k, self.rows.at[self.top], self.out.at[(*here, self.top)], place(X_MOVES[k + 1]))
        return self.hop(k, self.rows.at[self.low], self.out.at[(*here, self.low)], place(Z_MOVES[k - 2]))

    def second(self, k):
        if k < 3:
            block = self.tops(self.zl, self.zh)
            return self.hop(6 + k, block, block, place(Z_MOVES[k + 1]))
        block = self.lows(self.x)
        return self.hop(6 + k, block, block, place(X_MOVES[k - 2]))

    def forward(self, k, block):
        return push(block, block, self.fsend.at[k], self.frecv.at[k], sibling())

    def start(self):
        self.stay = pltpu.make_async_copy(
            self.rows, self.out.at[self.zl, self.x, self.zh, self.c], self.fsend.at[8]
        )
        for k in range(6):
            self.first(k).start()
        self.stay.start()

    def middle(self):
        self.stay.wait()
        for k in range(3):
            self.first(k).wait_recv()
        for k in range(3):
            self.second(k).start()
        self.forward(0, self.tops(self.zl, self.zh)).start()
        for k in range(3, 6):
            self.first(k).wait_recv()
        for k in range(3, 6):
            self.second(k).start()
        self.forward(1, self.lows(self.x)).start()

    def block(self, k):
        if k < 3:
            at = place(Z_MOVES[k + 1], -1)
            return self.tops(at["zl"], at["zh"])
        return self.lows(place(X_MOVES[k - 2], -1)["x"])

    def finish(self):
        for k in range(6):
            self.second(k).wait_recv()
            self.forward(2 + k, self.block(k)).start()
        blocks = [self.tops(self.zl, self.zh), self.lows(self.x)] + [self.block(k) for k in range(6)]
        for k in range(8):
            self.forward(k, blocks[k]).wait()
        for k in range(6):
            self.first(k).wait_send()
            self.second(k).wait_send()


def soft(scores, causal):
    scores = jnp.where(causal, scores, NEG)
    expon = jnp.exp(scores - jnp.max(scores, axis=-1, keepdims=True))
    return expon / jnp.sum(expon, axis=-1, keepdims=True)


def causal_mask(copies, seq):
    rows = lax.rem(lax.broadcasted_iota(jnp.int32, (copies * seq, seq), 0), seq)
    return lax.broadcasted_iota(jnp.int32, (copies * seq, seq), 1) <= rows


def attn_forward(
    collective, attn_blocks, blocks, part_cols, hidden, cotangent, gains, routers, routes, cosines, sines
):
    seq, width = hidden.shape
    own = seq // 4
    piece = width // 8
    scale = HEAD ** (-0.5)

    def kernel(
        a_ref, b0, b1, b2, hidden_ref, cotangent_ref,
        gain_a, gain_m, router_a, router_m, route_a, route_m, cos_ref, sin_ref,
        w_out, normed_out, qkv_out, gated_out, gates_out, routes_out, after_out, enter_row, cot_row, router_ref, small_ref,
        spread_out, cot_out, w0, w1, w2, a_mid, m0, m1, m2,
        turned, load, hid, part, total, row, *rest,
    ):
        mine = pl.ds(pl.multiple_of(own_tile()[1] * own, own), own)
        loads = []
        for b in range(8):
            here, there = pl.ds(b * piece, piece), pl.ds(((b % 4) * 2 + b // 4) * piece, piece)
            loads.append((hidden_ref.at[mine, here], enter_row.at[:, there]))
            loads.append((cotangent_ref.at[mine, here], cot_row.at[:, there]))
        fetches = [pltpu.make_async_copy(a, b, load.at[k]) for k, (a, b) in enumerate(loads)]
        for fetch in fetches:
            fetch.start()
        meet([place(m) for m in TEAM_MOVES[1:] + [Y_MOVES[1], Y_MOVES[3]]] + [sibling()])
        n = TeamSum.count
        team, rest = TeamSum(part, rest[:n]), rest[n:]
        enters = TeamSpread(enter_row, hid, rest[:4])
        cot = TeamSpread(cot_row, cot_out, rest[4:8])
        spread = TeamSpread(row, spread_out, rest[8:12])
        rest = rest[12:]
        swaps = [Swap(a_ref, a_mid, rest[:2])] + [
            ExpertSwap(b, m, rest[2 * k : 2 * k + 2])
            for k, (b, m) in ((1, (b0, m0)), (2, (b1, m1)), (3, (b2, m2)))
        ]
        rings = [
            RingY(m, w, rest[8 + 2 * k : 10 + 2 * k])
            for k, (m, w) in enumerate(((a_mid, w_out), (m0, w0), (m1, w1), (m2, w2)))
        ]
        swaps[0].start()
        named = [route_a[...], jnp.zeros_like(route_a), route_m[...], jnp.zeros((LANE - 6, seq), jnp.int32)]
        turned[...] = jnp.concatenate(named, axis=0).astype(F32).T.astype(BF)
        enter_row[:, width:] = turned[mine]
        for fetch in fetches:
            fetch.wait()
        enters.start()
        small_ref[...] = jnp.zeros_like(small_ref)
        for at, gain in ((0, gain_a), (1, gain_m)):
            for b in range(8):
                for i in range(piece // LANE):
                    there = ((b % 4) * 2 + b // 4) * piece + i * LANE
                    row_at = b * (piece // LANE) + i
                    small_ref[at : at + 1, there : there + LANE] = gain[row_at : row_at + 1]
        columns = jnp.concatenate([router_a[...].astype(F32), router_m[...].astype(F32)], axis=0)
        columns = [columns[:, b * piece : (b + 1) * piece] for b in ((k % 2) * 4 + k // 2 for k in range(8))]
        router_ref[...] = jnp.zeros_like(router_ref)
        router_ref[:8] = jnp.concatenate(columns, axis=1).astype(BF)
        swaps[0].finish()
        rings[0].start()
        swaps[1].start()
        enters.middle()
        swaps[2].start()
        rings[0].forward()
        swaps[1].finish()
        rings[1].start()
        swaps[3].start()
        enters.finish()

        def ahead(pair, _):
            routes = []
            for j in range(2):
                entered = hid[pair // 2, lax.rem(pair, 2) * 2 + j].reshape(seq, width + LANE)
                values = entered[:, :width].astype(F32)
                normed_out[pair * 2 + j] = (values * rms_scale(values) * small_ref[0:1]).astype(BF)
                routes.append(entered[:, width:])
                routes_out[pair * 2 + j] = routes[j]
            logits = mm_nt(normed_out[pl.ds(pair * 2, 2)].reshape(2 * seq, width), router_ref[...])
            gates = dense_gates(logits, chosen(jnp.concatenate(routes, axis=0).astype(F32), 0))
            gates_out[pl.ds(pair * 2, 2)] = gates.reshape(2, seq, LANE)
            return 0

        lax.fori_loop(0, 4, ahead, 0)
        rings[0].finish()
        swaps[2].finish()
        rings[2].start()
        first = 2 * team.zl
        causal = causal_mask(2, seq)

        def step(i, _):
            pair = team.pair(i)
            zl, x = pair // 2, lax.rem(pair, 2) * 2
            normed = normed_out[pl.ds(pair * 2, 2)].reshape(2 * seq, width)
            weights = w_out.reshape(width, 6 * HEAD)
            proj = mm(normed, weights[:, : 4 * HEAD])
            gates = gates_out[pl.ds(pair * 2, 2)].reshape(2 * seq, LANE)
            gated = []
            for j in range(2):
                rows = slice(j * seq, (j + 1) * seq)
                query = [
                    rotate(proj[rows, e * HEAD : (e + 1) * HEAD], cos_ref[...], sin_ref[...]).astype(BF)
                    for e in range(2)
                ]
                key = rotate(proj[rows, 2 * HEAD : 3 * HEAD], cos_ref[...], sin_ref[...]).astype(BF)
                value = proj[rows, 3 * HEAD :].astype(BF)
                probs = soft(mm_nt(jnp.concatenate(query, axis=0), key) * scale, causal)
                attended = mm(probs.astype(BF), value)
                out = [
                    (attended[e * seq : (e + 1) * seq] * pick(gates[rows], first + e)).astype(BF)
                    for e in range(2)
                ]
                qkv_out[pair * 2 + j] = jnp.concatenate(query + [key, value], axis=1)
                gated.append(jnp.concatenate(out, axis=1))
                gated_out[pair * 2 + j] = gated[-1]
            branch = mm_nt(jnp.concatenate(gated, axis=0), weights[:, 4 * HEAD :])
            part[zl, pl.ds(x, 2)] = branch.astype(BF).reshape(2, 2, 2, own, width)
            for j in range(2):
                team.swap(pair * 2 + j).start()

            @pl.when(i > 0)
            def _():
                team.add_pair(i - 1)

            @pl.when(i == 2)
            def _():
                team.send_far_z()
                rings[1].forward()

            @pl.when(i == 3)
            def _():
                team.send_far_x()

            return 0

        lax.fori_loop(0, 4, step, 0)
        team.last()
        cot.start()
        swaps[3].finish()
        team.total1(total)
        cot.middle()
        team.total2(total)
        after = total[...] + enter_row[:, :width].astype(F32)
        after_out[...] = after
        row[...] = (after * rms_scale(after) * small_ref[1:2]).astype(BF)
        spread.start()
        rings[2].forward()
        rings[3].start()
        spread.middle()
        cot.finish()
        spread.finish()
        team.close()
        for ring in rings[1:3]:
            ring.finish()
        rings[3].finish_first()

    block = jax.ShapeDtypeStruct(attn_blocks.shape, BF)
    block_m = jax.ShapeDtypeStruct(attn_blocks.shape[:2] + (part_cols,), BF)
    four = jax.ShapeDtypeStruct((4,) + attn_blocks.shape, BF)
    four_m = jax.ShapeDtypeStruct((4,) + block_m.shape, BF)
    rows = jax.ShapeDtypeStruct((2, 4, 2, 2, own, width), BF)
    return pl.pallas_call(
        kernel,
        out_shape=[
            four,
            jax.ShapeDtypeStruct((8, seq, width), BF),
            jax.ShapeDtypeStruct((8, seq, 4 * HEAD), BF),
            jax.ShapeDtypeStruct((8, seq, 2 * HEAD), BF),
            jax.ShapeDtypeStruct((8, seq, LANE), F32),
            jax.ShapeDtypeStruct((8, seq, LANE), BF),
            jax.ShapeDtypeStruct((own, width), F32),
            jax.ShapeDtypeStruct((own, width + LANE), BF),
            jax.ShapeDtypeStruct((own, width), BF),
            jax.ShapeDtypeStruct((LANE, width), BF),
            jax.ShapeDtypeStruct((16, width), F32),
            rows, rows, four_m, four_m, four_m, block, block_m, block_m, block_m,
        ],
        in_specs=[ANY] * 6 + [VMEM] * 8,
        out_specs=[VMEM] * 11 + [ANY] * 9,
        scratch_shapes=[
            pltpu.VMEM((seq, LANE), BF),
            pltpu.SemaphoreType.DMA((16,)),
            pltpu.VMEM((2, 4, 2, 2, own, width + LANE), BF),
            pltpu.VMEM((2, 4, 2, 2, own, width), BF),
            pltpu.VMEM((own, width), F32),
            pltpu.VMEM((own, width), BF),
        ]
        + TeamSum.scratch(own, width)
        + TeamSpread.sems * 3
        + Swap.sems * 4
        + RingY.sems * 4,
        name="attn_forward",
        **settings(collective, 200 << 20, 56),
    )(attn_blocks, *blocks, hidden, cotangent, *gains, *routers, *routes, cosines, sines)[:16]


def back_through_norm(total, inputs, gain, gates, normed, routers):
    width = inputs.shape[1]
    logits_back = gates_back(gates, total[:, width:])
    full = total[:, :width] + mm(logits_back.astype(BF), routers)
    inner, gain_grad = norm_back(inputs, gain, full)
    return inner, gain_grad, mm_tn(logits_back.astype(BF), normed)[:8]


def row_block(array, block, count):
    cols = array.shape[-1] // 4
    part = array[..., pl.ds(pl.multiple_of(block * cols, cols), cols)]
    return part.reshape(count, cols)


class Pass:
    sems = [pltpu.SemaphoreType.DMA((4,))] * 2

    def __init__(self, src, dst, sems):
        send, recv = sems
        zh, c = lax.axis_index("zh"), lax.axis_index("c")
        mine, far = dst.at[zh, c], dst.at[1 - zh, c]
        self.copies = [
            pltpu.make_async_copy(src, mine, send.at[0]),
            push(src, mine, send.at[1], recv.at[1], {"zh": 1 - zh}),
            push(src, mine, send.at[2], recv.at[2], sibling()),
            push(far, far, send.at[3], recv.at[3], sibling()),
        ]

    def start(self):
        for copy in self.copies[:3]:
            copy.start()

    def finish(self):
        self.copies[1].wait_recv()
        self.copies[3].start()
        self.copies[0].wait()
        self.copies[1].wait_send()
        self.copies[2].wait()
        self.copies[3].wait()


def own_tile():
    zl, x, zh, c = (lax.axis_index(a) for a in TEAM)
    return zl * 4 + x, zh * 2 + c


def experts(collective, normed, cotangent, routes, weights, after, small, routers, cot_own, extra):
    own, width = after.shape
    count = normed.shape[0]
    cols = weights[0].shape[1]
    rows = width // 4
    tile = count // 4

    def kernel(
        x_ref, cot_ref, wg_ref, wu_ref, wd_ref, route_ref, after_ref, small_ref, router_ref, own_ref,
        mid_out, small_out, spread_out, s0, s1, g2, out_all,
        x, cot, wg, wu, wd, h, dg, du, g0, gates, part_a, part_b, load, total_a, total_b, row_a, row_b, *rest,
    ):
        loads = [(x_ref, x), (wg_ref, wg), (wu_ref, wu), (cot_ref, cot)]
        fetches = [pltpu.make_async_copy(a, b, load.at[k]) for k, (a, b) in enumerate(loads)]
        for fetch in fetches:
            fetch.start()
        down_rest = RingRest(wd_ref, wd, rest[:2])
        rest = rest[2:]
        down_rest.start_here()
        meet([place(m) for m in TEAM_MOVES[1:] + [Y_MOVES[1], Y_MOVES[3]]] + [sibling()])
        down_rest.start()
        n = TeamSum.count
        team_a, team_b = TeamSum(part_a, rest[:n]), TeamSum(part_b, rest[n : 2 * n])
        rest = rest[2 * n :]
        n = RingSum.count
        rings = [RingSum(g0, rest[:n]), RingSum(wg, rest[n : 2 * n])]
        rest = rest[2 * n :]
        spread = TeamSpread(row_a, spread_out, rest[:4])
        out = Pass(row_b, out_all, rest[4:6])
        gate_w, up_w, down_w = (w.reshape(width, cols) for w in (wg, wu, wd))
        lane = EXPERTS + lax.axis_index("x")
        skip = lax.axis_index("zl") * extra

        def tokens(pair):
            return pl.ds(pl.multiple_of(pair * tile, tile), tile)

        def forward(pair, _):
            at = tokens(pair)
            x_t = x[at]
            gates_t = dense_gates(mm_nt(x_t, router_ref[...]), chosen(route_ref[at].astype(F32), EXPERTS))
            gates[at] = gates_t
            valid = (lax.broadcasted_iota(jnp.int32, (1, cols), 1) >= skip).astype(F32)
            gate = pick(gates_t, lane) * valid
            gate_part = mm(x_t, gate_w[...])
            up_part = mm(x_t, up_w[...])
            sigma = 1.0 / (1.0 + jnp.exp(-gate_part))
            silu = gate_part * sigma
            h[at] = (silu * up_part * gate).astype(BF)
            dg[at] = (up_part * sigma * (1.0 + gate_part * (1.0 - sigma)) * gate).astype(BF)
            du[at] = (silu * gate).astype(BF)
            return 0

        def backward(pair, _):
            at = tokens(pair)
            cot_down = mm(cot[at], down_w[...])
            dots = jnp.sum(h[at].astype(F32) * cot_down, axis=1, keepdims=True)
            dg[at] = (dg[at].astype(F32) * cot_down).astype(BF)
            du[at] = (du[at].astype(F32) * cot_down).astype(BF)
            hot = jnp.where(lanes(tile) == lane, dots, 0.0).astype(BF)
            part_a[pair // 2, pl.ds(lax.rem(pair, 2) * 2, 2), :, :, :, width:] = hot.reshape(
                2, 2, 2, own, LANE
            )
            return 0

        def summed(team, columns, values):
            def step(i, _):
                pair = team.pair(i)
                at = (pair // 2, pl.ds(lax.rem(pair, 2) * 2, 2), slice(None), slice(None), slice(None), columns)
                team.part[at] = values(tokens(pair)).astype(BF).reshape(2, 2, 2, own, width)
                for j in range(2):
                    team.swap(pair * 2 + j).start()

                @pl.when(i > 0)
                def _():
                    team.add_pair(i - 1)

                @pl.when(i == 2)
                def _():
                    team.send_far_z()

                @pl.when(i == 3)
                def _():
                    team.send_far_x()

                return 0

            lax.fori_loop(0, 4, step, 0)
            team.last()

        def product(left, right, dst):
            def one(block):
                dst[block] = mm_tn(row_block(left, block, count), right[...]).astype(BF)

            return one

        for fetch in fetches[:3]:
            fetch.wait()
        lax.fori_loop(0, 4, forward, 0)
        fetches[3].wait()
        down_rest.finish()
        lax.fori_loop(0, 4, backward, 0)
        rings[0].begin_with(product(x, dg, g0))
        summed(team_a, slice(0, width), lambda at: mm_nt(dg[at], gate_w[...]) + mm_nt(du[at], up_w[...]))
        rings[0].go_on_with(product(x, dg, g0))
        rings[0].middle()
        rings[1].start_with(product(x, du, wg))
        team_a.total1(total_a)
        summed(team_b, slice(0, width), lambda at: mm_nt(h[at], down_w[...]))
        after = after_ref[...]
        normed_own = (after * rms_scale(after) * small_ref[1:2]).astype(BF)
        seq, quarter = own_tile()
        gates_own = gates[pl.ds(pl.multiple_of((seq * 4 + quarter) * own, own), own)]
        team_a.total2(total_a)
        inner, gain_grad, router_grad = back_through_norm(
            total_a[...], after, small_ref[1:2], gates_own, normed_own, router_ref[...]
        )
        grad_mid = own_ref[...].astype(F32) + inner
        mid_out[...] = grad_mid
        row_a[...] = grad_mid.astype(BF)
        spread.start()
        rings[1].middle()
        small_out[:8] = jnp.zeros((8, width), F32)
        small_out[0:1] = gain_grad
        small_out[8:] = router_grad

        def down(block, _):
            product(cot, h, wu)(block)

            @pl.when(block == 1)
            def _():
                spread.middle()

            return 0

        lax.fori_loop(0, 4, down, 0)
        keep = pltpu.make_async_copy(wu, g2, load.at[0])
        keep.start()
        team_b.total1(total_b)
        spread.finish()
        team_b.total2(total_b)
        row_b[...] = in_order((after + total_b[...]).astype(BF))
        out.start()
        stores = []
        for ring, buffer, dst, k in ((rings[0], dg, s0, 1), (rings[1], du, s1, 2)):
            ring.finish(buffer.at[pl.ds(0, rows)])
            stores.append(pltpu.make_async_copy(buffer.at[pl.ds(0, rows)], dst, load.at[k]))
            stores[-1].start()
        out.finish()
        keep.wait()
        for store in stores:
            store.wait()
        team_a.close()
        team_b.close()

    return pl.pallas_call(
        kernel,
        out_shape=[
            jax.ShapeDtypeStruct((own, width), F32),
            jax.ShapeDtypeStruct((16, width), F32),
            jax.ShapeDtypeStruct((2, 4, 2, 2, own, width), BF),
            jax.ShapeDtypeStruct((rows, cols), BF),
            jax.ShapeDtypeStruct((rows, cols), BF),
            jax.ShapeDtypeStruct((4, rows, cols), BF),
            jax.ShapeDtypeStruct((2, 2, own, width), BF),
        ],
        in_specs=[ANY] * 5 + [VMEM] * 5,
        out_specs=[VMEM] * 2 + [ANY] * 5,
        scratch_shapes=[
            pltpu.VMEM((count, width), BF),
            pltpu.VMEM((count, width), BF),
            pltpu.VMEM((4, rows, cols), BF),
            pltpu.VMEM((4, rows, cols), BF),
            pltpu.VMEM((4, rows, cols), BF),
            pltpu.VMEM((count, cols), BF),
            pltpu.VMEM((count, cols), BF),
            pltpu.VMEM((count, cols), BF),
            pltpu.VMEM((4, rows, cols), BF),
            pltpu.VMEM((count, LANE), F32),
            pltpu.VMEM((2, 4, 2, 2, own, width + LANE), BF),
            pltpu.VMEM((2, 4, 2, 2, own, width), BF),
            pltpu.SemaphoreType.DMA((4,)),
            pltpu.VMEM((own, width + LANE), F32),
            pltpu.VMEM((own, width), F32),
            pltpu.VMEM((own, width), BF),
            pltpu.VMEM((own, width), BF),
        ]
        + RingRest.sems
        + TeamSum.scratch(own, width + LANE)
        + TeamSum.scratch(own, width)
        + RingSum.scratch(rows, cols) * 2
        + TeamSpread.sems
        + Pass.sems,
        name="experts",
        **settings(collective, 300 << 20, 61),
    )(
        normed, cotangent, *[w.reshape(4, rows, cols) for w in weights], routes,
        after, small, routers, cot_own,
    )


def in_order(values):
    block = values.shape[1] // 8
    order = [(b % 4) * 2 + b // 4 for b in range(8)]
    return jnp.concatenate([values[:, k * block : (k + 1) * block] for k in order], axis=1)


def attn_backward(
    collective, grad_mid, qkv, gated, normed, gates, weights, cosines, sines, mid_own, entered, gains, routers, small, summed, grads
):
    own, width = mid_own.shape
    seq = qkv.shape[1]
    rows, cols = grads.shape[1:]
    shard = rows // 8
    scale = HEAD ** (-0.5)
    stages = [X_MOVES, Y_MOVES, Z_MOVES]

    def kernel(
        gm_ref, w_ref, x_ref, g2_ref, y0, y1, qkv_ref, gated_ref, gates_ref, cos_ref, sin_ref,
        mid_ref, in_ref, gain_ref, router_ref, small_ref,
        grad_all, gain_a, gain_m, router_a, router_m, s0, s1, s2, s3,
        gm, w, x, g2, g3, y2, y3, proj, part, load, total, row,
        acc, got, other, rest_rows, csem, ssend, srecv, *rest,
    ):
        loads = [(gm_ref, gm), (w_ref, w), (g2_ref, g2), (x_ref, x)]
        fetches = [pltpu.make_async_copy(a, b, load.at[k]) for k, (a, b) in enumerate(loads)]
        for fetch in fetches:
            fetch.start()
        meet([place(m) for m in TEAM_MOVES[1:] + Y_MOVES[1:]] + [sibling()])
        n = TeamSum.count
        team, rest = TeamSum(part, rest[:n]), rest[n:]
        n = RingSum.count
        rings, rest = [RingSum(g2, rest[:n]), RingSum(g3, rest[n : 2 * n])], rest[2 * n :]
        swaps_back = [
            Swap(y, s, rest[2 * k : 2 * k + 2]) for k, (y, s) in enumerate(((y0, s0), (y1, s1), (y2, s2)))
        ]
        last_swap = ColumnSwap(y3, s3, rest[6:8])
        out = Pass(row, grad_all, rest[8:10])
        first = 2 * team.zl
        causal = causal_mask(2, seq)
        swaps_back[0].start()
        swaps_back[1].start()
        fetches[0].wait()
        fetches[1].wait()

        def step(i, _):
            pair = team.pair(i)
            grads = mm(gm[pl.ds(pair * 2, 2)].reshape(2 * seq, width), w[:, 4 * HEAD :])
            both = []
            for j in range(2):
                at = pair * 2 + j
                here = slice(j * seq, (j + 1) * seq)
                query = jnp.concatenate(
                    [qkv_ref[at, :, e * HEAD : (e + 1) * HEAD] for e in range(2)], axis=0
                )
                key = qkv_ref[at, :, 2 * HEAD : 3 * HEAD]
                value = qkv_ref[at, :, 3 * HEAD :]
                probs = soft(mm_nt(query, key) * scale, causal)
                probs_b = probs.astype(BF)
                attended = mm(probs_b, value)
                grad = jnp.concatenate(
                    [grads[here, e * HEAD : (e + 1) * HEAD] for e in range(2)], axis=0
                )
                gates = gates_ref[at]
                gate = jnp.concatenate([pick(gates, first + e) for e in range(2)], axis=0)
                each = jnp.sum(attended * grad, axis=1, keepdims=True) * gate
                dots = jnp.where(lanes(seq) == first, each[:seq], 0.0)
                dots += jnp.where(lanes(seq) == first + 1, each[seq:], 0.0)
                grad = (grad * gate).astype(BF)
                grad_probs = mm_nt(grad, value)
                inner = jnp.sum(probs * grad_probs, axis=1, keepdims=True)
                grad_scores = (probs * (grad_probs - inner) * scale).astype(BF)
                turned = [mm(grad_scores, key), mm_tn(grad_scores, query)]
                turned = [turned[0][:seq], turned[0][seq:], turned[1]]
                turned = [rotate(t, cos_ref[...], -sin_ref[...]).astype(BF) for t in turned]
                grad_value = mm_tn(probs_b, grad).astype(BF)
                both.append(jnp.concatenate(turned + [grad_value], axis=1))
                proj[at] = both[-1]
                part[pair // 2, lax.rem(pair, 2) * 2 + j, :, :, :, width:] = dots.astype(BF).reshape(
                    2, 2, own, LANE
                )
            back = mm_nt(jnp.concatenate(both, axis=0), w[:, : 4 * HEAD])
            part[pair // 2, pl.ds(lax.rem(pair, 2) * 2, 2), :, :, :, :width] = back.astype(BF).reshape(
                2, 2, 2, own, width
            )
            for j in range(2):
                team.swap(pair * 2 + j).start()

            @pl.when(i == 0)
            def _():
                fetches[2].wait()
                rings[0].start()

            @pl.when(i > 0)
            def _():
                team.add_pair(i - 1)

            @pl.when(i == 2)
            def _():
                team.send_far_z()

            @pl.when(i == 3)
            def _():
                team.send_far_x()

            return 0

        lax.fori_loop(0, 4, step, 0)
        team.last()
        fetches[3].wait()

        def product(block):
            g3[block, :, : 4 * HEAD] = mm_tn(
                row_block(x, block, 8 * seq), proj[...].reshape(8 * seq, 4 * HEAD)
            ).astype(BF)
            g3[block, :, 4 * HEAD :] = mm_tn(
                row_block(gm, block, 8 * seq), gated_ref[...].reshape(8 * seq, 2 * HEAD)
            ).astype(BF)

        rings[1].start_with(product)
        rings[0].middle()
        inputs = in_ref[:, :width].astype(F32)
        normed_own = (inputs * rms_scale(inputs) * gain_ref[0:1]).astype(BF)
        own_seq, quarter = own_tile()
        gates_own = gates_ref[own_seq, pl.ds(pl.multiple_of(quarter * own, own), own)]
        team.total1(total)
        rings[1].middle()
        team.total2(total)
        inner, gain_grad, router_grad = back_through_norm(
            total[...], inputs, gain_ref[0:1], gates_own, normed_own, router_ref[...]
        )
        row[...] = in_order((mid_ref[...] + inner).astype(BF))
        out.start()
        acc[...] = small_ref[...]
        acc[1:2] = gain_grad
        acc[8:] += router_grad
        c = lax.axis_index("c")
        half = pl.ds(pl.multiple_of(c * 8, 8), 8)
        rest_half = pl.ds(pl.multiple_of((1 - c) * 8, 8), 8)
        over = push(acc.at[rest_half], other, csem.at[0], csem.at[1], sibling())
        over.start()
        over.wait()
        acc[half] = acc[half] + other[...]
        for s, stage in enumerate(stages):
            swaps = [
                push(acc.at[half], got.at[s, k - 1], ssend.at[s, k], srecv.at[s, k], place(stage[k]))
                for k in range(1, 4)
            ]
            for swap in swaps:
                swap.start()
            if s == 0:
                rings[0].finish(y2)
                swaps_back[2].start()
            if s == 1:
                rings[1].finish(y3)
                last_swap.start()
            for swap in swaps:
                swap.wait()
            acc[half] = acc[half] + got[s, 0] + got[s, 1] + got[s, 2]
        back_over = push(acc.at[half], rest_rows, csem.at[2], csem.at[3], sibling())
        back_over.start()
        out.finish()
        back_over.wait()
        acc[rest_half] = rest_rows[...]
        final = in_order(acc[...])
        for ref, at in ((gain_m, 0), (gain_a, 1)):
            for k in range(width // LANE):
                ref[k : k + 1] = final[at : at + 1, k * LANE : (k + 1) * LANE]
        router_a[...] = final[8 : 8 + EXPERTS]
        router_m[...] = final[8 + EXPERTS :]
        for swap in swaps_back + [last_swap]:
            swap.finish()
        team.close()

    block = jax.ShapeDtypeStruct((8, shard, cols), BF)
    heads = cols // HEAD
    return pl.pallas_call(
        kernel,
        out_shape=[
            jax.ShapeDtypeStruct((2, 2, own, width), BF),
            jax.ShapeDtypeStruct((width // LANE, LANE), F32),
            jax.ShapeDtypeStruct((width // LANE, LANE), F32),
            jax.ShapeDtypeStruct((EXPERTS, width), F32),
            jax.ShapeDtypeStruct((EXPERTS, width), F32),
            block, block, block,
            jax.ShapeDtypeStruct((2, heads, shard, 4 * HEAD), BF),
        ],
        in_specs=[ANY] * 6 + [VMEM] * 10,
        out_specs=[ANY] + [VMEM] * 4 + [ANY] * 4,
        scratch_shapes=[
            pltpu.VMEM((8, seq, width), BF),
            pltpu.VMEM(weights.shape, BF),
            pltpu.VMEM((8, seq, width), BF),
            pltpu.VMEM((4, rows, cols), BF),
            pltpu.VMEM((4, rows, cols), BF),
            pltpu.VMEM((8, shard, cols), BF),
            pltpu.VMEM((8, heads, shard, HEAD), BF),
            pltpu.VMEM((8, seq, 4 * HEAD), BF),
            pltpu.VMEM((2, 4, 2, 2, own, width + LANE), BF),
            pltpu.SemaphoreType.DMA((4,)),
            pltpu.VMEM((own, width + LANE), F32),
            pltpu.VMEM((own, width), BF),
            pltpu.VMEM((16, width), F32),
            pltpu.VMEM((3, 3, 8, width), F32),
            pltpu.VMEM((8, width), F32),
            pltpu.VMEM((8, width), F32),
            pltpu.SemaphoreType.DMA((4,)),
        ]
        + [pltpu.SemaphoreType.DMA((4, 4))] * 2
        + TeamSum.scratch(own, width + LANE)
        + RingSum.scratch(rows, cols) * 2
        + Swap.sems * 4
        + Pass.sems,
        name="attn_backward",
        **settings(collective, 200 << 20, 58),
    )(
        grad_mid.reshape(8, seq, width), weights, normed, grads, *summed, qkv, gated, gates, cosines, sines,
        mid_own, entered, gains, routers, small,
    )


def local(
    hidden,
    cotangent,
    attn_gain,
    attn_router,
    qkv_weight,
    out_weight,
    mlp_gain,
    mlp_router,
    gate_up_weight,
    down_weight,
    attn_route,
    attn_slot,
    mlp_route,
    mlp_slot,
):
    seq, width = hidden.shape
    rows = qkv_weight.shape[0]
    features = down_weight.shape[2]
    part = (features // LANE + 1) // 2 * LANE
    group = 8 * seq
    cosines, sines = rope_tables(seq)

    qkv_rows, out_rows = qkv_weight.transpose(1, 0, 2), out_weight.transpose(1, 0, 2)

    def target(zl, x):
        head = slice(x * HEAD, (x + 1) * HEAD)
        first = 2 * zl
        pieces = [qkv_rows[n, :, head] for n in (first, first + 1, EXPERTS, EXPERTS + 1)]
        return jnp.concatenate(pieces + [out_rows[n, :, head] for n in (first, first + 1)], axis=1)

    attn_blocks = jnp.stack([target(zl, x) for zl in range(2) for x in range(4)], axis=0)

    mlp_blocks = [
        w.transpose(1, 0, 2) for w in (gate_up_weight[:, :, 0], gate_up_weight[:, :, 1], down_weight)
    ]
    gains = [g.reshape(width // LANE, LANE) for g in (attn_gain, mlp_gain)]

    (
        attn_w, normed_a, qkv, gated_att, gates_a, group_routes, after, entered, cot_own, routers, small,
        normed_m, group_cot, *mlp_w,
    ) = attn_forward(
        1, attn_blocks, mlp_blocks, part, hidden, cotangent, gains, [attn_router.T, mlp_router.T],
        [attn_route.T, mlp_route.T], cosines, sines,
    )
    attn_w = attn_w.reshape(width, 6 * HEAD)
    mlp_w = [w.reshape(width, part) for w in mlp_w]
    group_cot = group_cot.reshape(group, width)
    normed_m = normed_m.reshape(group, width)

    grad_mid_own, small_m, grad_mid, gate_sum, up_sum, down_part, out_hidden = experts(
        2, normed_m, group_cot, group_routes.reshape(group, LANE), mlp_w, after, small, routers, cot_own,
        2 * part - features,
    )
    gate_sum, up_sum = (a.reshape(8, rows, part) for a in (gate_sum, up_sum))
    grad_in, gain_a, gain_m, router_a, router_m, *mlp_grads, attn_grads = attn_backward(
        3, grad_mid, qkv, gated_att, normed_a, gates_a, attn_w, cosines, sines, grad_mid_own, entered, small,
        routers, small_m, [gate_sum, up_sum], down_part,
    )
    out_hidden = out_hidden.reshape(seq, width)
    grad_in = grad_in.reshape(seq, width).astype(F32)

    attn_grads = attn_grads.astype(F32)
    query_grad = attn_grads[:, :2].reshape(EXPERTS, rows, 4 * HEAD)
    kv_grad = attn_grads[0, 2:4] + attn_grads[1, 2:4]
    qkv_grad = jnp.concatenate([query_grad, kv_grad], axis=0).transpose(1, 0, 2)
    out_grad = attn_grads[:, 4:].reshape(EXPERTS, rows, 4 * HEAD).transpose(1, 0, 2)

    def placed_back(grad):
        grad = grad.reshape(2, EXPERTS, rows, part)
        return jnp.concatenate([grad[0], grad[1, ..., 2 * part - features :]], axis=-1).transpose(1, 0, 2)

    gate_grad, up_grad, down_grad = [placed_back(g) for g in mlp_grads]
    gate_up_grad = jnp.stack([gate_grad, up_grad], axis=2)
    gate_up_grad, down_grad = lax.optimization_barrier((gate_up_grad, down_grad))
    return (
        out_hidden,
        grad_in,
        gain_a.reshape(width),
        router_a.T,
        qkv_grad,
        out_grad,
        gain_m.reshape(width),
        router_m.T,
        gate_up_grad.astype(F32),
        down_grad.astype(F32),
    )


def solution(mesh):
    fine = Mesh(mesh.devices.reshape(2, 4, 4, 2, 2), ALL)
    dp, tensor = ("zl", "y", "x"), ("zh", "c")
    placed = (
        P(dp, None),
        P(dp, None),
        P(),
        P(),
        P(dp, None, tensor),
        P(dp, None, tensor),
        P(),
        P(),
        P(dp, None, None, tensor),
        P(dp, None, tensor),
        P(dp, None),
        P(dp, None),
        P(dp, None),
        P(dp, None),
    )
    return jax.shard_map(
        local,
        mesh=fine,
        in_specs=placed,
        out_specs=(
            P(dp, None),
            P(dp, None),
            P(),
            P(),
            P(dp, None, tensor),
            P(dp, None, tensor),
            P(),
            P(),
            P(dp, None, None, tensor),
            P(dp, None, tensor),
        ),
        check_vma=False,
    )
```
